32 devices in a mesh: gx: 4 (over y, core), gy: 8 (over z, x).
Axes of the slice: x: 2, y: 2, z: 4, core: 2. Of those that a mesh axis runs over, the one named last changes fastest.
Arguments:
- phase: float32 [32, 64, 256], P('gx', 'gy'), may hold values from -1 to 1
- solute: float32 [32, 64, 256], P('gx', 'gy'), may hold values from 0 to 1
- undercool: float32 [32, 64, 256], P('gx', 'gy'), may hold values from -1 to 1
- lift_weight: float32 [32, 2], replicated, may hold values from -4 to 4
- spectral_weight: float32 [2, 32, 32, 32, 1024], P(None, 'gx', 'gy'), may hold values from -6 to 6
- local_weight: float32 [32, 32], replicated, may hold values from -1 to 1
- local_bias: float32 [32], replicated, may hold values from -4 to 4
- proj_weight: float32 [32], replicated, may hold values from -1 to 1
- cotangent: float32 [32, 64, 256], P('gx', 'gy'), may hold values from -6 to 6
Outputs:
- phase_next: float32 [32, 64, 256], P('gx', 'gy')
- solute_next: float32 [32, 64, 256], P('gx', 'gy')
- predicted: float32 [32, 64, 256], P('gx', 'gy')
- grad_spectral: float32 [2, 32, 32, 32, 1024], P(None, 'gx', 'gy')
- grad_local: float32 [32, 32], replicated
- grad_proj: float32 [32], replicated
The draws below stay inside these ranges and needn't reach their ends.
All inputs are finite; a program needn't handle non-finite values.
Results may differ from the reference program's by a relative error of at most 0.00029.
Values sent between devices are 32-bit elements; how exact they have to be, the bound alone decides.
No kernel may reach another device: no remote copies, remote signals or barrier semaphores. Data moves between devices by JAX's collectives and lax.ppermute only.
A program may use at most 128 MiB of HBM per device.

```python
import math
from functools import reduce
import jax
import jax.numpy as jnp
from jax import lax

NZ = 256
WIDTH = 32
KX = 32
KY = 32
KZ = 32
NX = 32
NY = 64


def steps_of(rng, shape, pieces, smallest, high):
    def one(position, blocks):
        heights = jax.random.uniform(jax.random.fold_in(jax.random.fold_in(rng, 6), position), (blocks,), jnp.float32, smallest / len(pieces), high / len(pieces))
        return jnp.repeat(jnp.exp(heights), shape[position] // blocks).reshape((-1,) + (1,) * (len(shape) - position - 1))

    gain = one(*pieces[0])
    for cut in pieces[1:]:
        gain = gain * one(*cut)
    return gain


def normal_values(own_key, dims, deviation, limit, cuts=(), held_as=jnp.bfloat16):
    loudness = steps_of(own_key, dims, cuts, -0.22, 0.18) if cuts else 1.0
    entries = jax.random.normal(own_key, dims, jnp.float32) * deviation * loudness
    return jnp.minimum(jnp.maximum(entries, -limit), limit).astype(held_as)


def setup_inputs(seed: int = 0) -> dict:
    key_of = jax.random.split(jax.random.key(seed), 10)
    return {
        "phase": jnp.clip(jax.random.uniform(key_of[0], (NX, NY, NZ), jnp.float32, -1.0, 1.0) * steps_of(key_of[0], (NX, NY, NZ), ((0, 4), (1, 8)), -0.4, 0.0), -1.0, 1.0),
        "solute": jnp.clip(1.0 * jax.random.uniform(key_of[1], (NX, NY, NZ), jnp.float32) ** steps_of(key_of[1], (NX, NY, NZ), ((0, 4), (1, 8)), -0.2, 0.2), 0.0, 1.0),
        "undercool": jnp.clip(jax.random.uniform(key_of[2], (NX, NY, NZ), jnp.float32, -1.0, 1.0) * steps_of(key_of[2], (NX, NY, NZ), ((0, 4), (1, 8)), -0.4, 0.0), -1.0, 1.0),
        "lift_weight": normal_values(key_of[3], (WIDTH, 2), 2 ** -0.5, 4.0, (), jnp.float32),
        "spectral_weight": normal_values(key_of[4], (2, KX, KY, KZ, WIDTH * WIDTH), ((NX * NY * NZ / (2 * KX * KY * KZ * WIDTH)) ** 0.5), 6.0, ((1, 4), (2, 8)), jnp.float32),
        "local_weight": normal_values(key_of[5], (WIDTH, WIDTH), WIDTH ** -0.5, 1.0, (), jnp.float32),
        "local_bias": normal_values(key_of[6], (WIDTH,), 1.0, 4.0, (), jnp.float32),
        "proj_weight": normal_values(key_of[7], (WIDTH,), WIDTH ** -0.5, 1.0, (), jnp.float32),
        "cotangent": normal_values(key_of[8], (NX, NY, NZ), 1.0, 6.0, ((0, 4), (1, 8)), jnp.float32),
    }


TIME_STEP = 0.05
COUPLING = 2.0
SOLID_DIFF = 0.05
LIQUID_DIFF = 1.0
PARTITION = 0.15
TRAP_RATE = 4.0
SOLUTE_MEAN = 0.5

def diffusivity(phase_now):
    return SOLID_DIFF + (LIQUID_DIFF - SOLID_DIFF) * 0.5 * (1.0 - jnp.tanh(phase_now))

def update(phase_now, solute_now, undercool, phase_nb, solute_nb, diff_now, diff_nb):
    lap = reduce(jnp.add, phase_nb) - 6.0 * phase_now
    squares = 1.0 - phase_now * phase_now
    rate = lap + phase_now - phase_now * phase_now * phase_now + COUPLING * squares * squares * (undercool - solute_now)
    fluxes = [0.5 * (diff_now + diff_nb[index]) * (solute_nb[index] - solute_now) for index in range(6)]
    divergence = reduce(jnp.add, fluxes)
    speed = TRAP_RATE * jnp.abs(rate)
    keff = (PARTITION + speed) / (1.0 + speed)
    phase_new = phase_now + TIME_STEP * rate
    solute_new = solute_now + TIME_STEP * (divergence + 0.5 * (1.0 - keff) * solute_now * rate)
    return (phase_new, solute_new)

def neighbours(field):
    return [jnp.roll(field, -1, 0), jnp.roll(field, 1, 0), jnp.roll(field, -1, 1), jnp.roll(field, 1, 1), jnp.roll(field, -1, 2), jnp.roll(field, 1, 2)]

def phase_sweep(phase_now, solute_now, undercool):
    diff_now = diffusivity(phase_now)
    return update(phase_now, solute_now, undercool, neighbours(phase_now), neighbours(solute_now), diff_now, neighbours(diff_now))

def freq_index(amount, length):
    index = jnp.arange(amount, dtype=jnp.int32)
    return jnp.where(index < amount // 2, index, index + length - amount).astype(jnp.int32)

def forward_spec(field, zfactor, xfactor, yfactor):
    along_z = jnp.fft.rfft(field, axis=2)[:, :, :KZ] * zfactor
    along_x = jnp.take(jnp.fft.fft(along_z, axis=0), freq_index(KX, NX), axis=0) * xfactor
    along_y = jnp.take(jnp.fft.fft(along_x, axis=1), freq_index(KY, NY), axis=1) * yfactor
    return jnp.stack([jnp.real(along_y), jnp.imag(along_y)]).astype(jnp.float32)

def inverse_spec(spec):
    values = spec[0] + 1j * spec[1]
    full_y = jnp.zeros((KX, NY, KZ), values.dtype).at[:, freq_index(KY, NY)].set(values)
    back_y = jnp.fft.ifft(full_y, axis=1)
    full_x = jnp.zeros((NX, NY, KZ), values.dtype).at[freq_index(KX, NX)].set(back_y)
    back_x = jnp.fft.ifft(full_x, axis=0)
    full_z = jnp.zeros((NX, NY, NZ // 2 + 1), values.dtype).at[:, :, :KZ].set(back_x)
    return jnp.fft.irfft(full_z, n=NZ, axis=2).astype(jnp.float32)

def contract(weights, values):
    return jnp.einsum('abzoi,iabz->oabz', weights, values, precision=lax.Precision.HIGHEST)

def outer(left, right):
    return jnp.einsum('oabz,iabz->abzoi', left, right, precision=lax.Precision.HIGHEST)

def reference(phase, solute, undercool, lift_weight, spectral_weight, local_weight, local_bias, proj_weight, cotangent):
    phase_mid, solute_mid = phase_sweep(phase, solute, undercool)
    phase_next, solute_next = phase_sweep(phase_mid, solute_mid, undercool)
    centred = solute_next - SOLUTE_MEAN
    unit_z = jnp.ones((KZ,), jnp.float32)
    modes_z = jnp.arange(KZ, dtype=jnp.int32)
    weights_z = jnp.where(modes_z == 0, 1.0, 2.0).astype(jnp.float32) / NZ

    def lift_one(row):
        return forward_spec(row[0] * phase_next + row[1] * centred, unit_z, 1.0, 1.0)
    spectrum = lax.map(lift_one, lift_weight)
    spec_t = jnp.transpose(spectrum, (1, 0, 2, 3, 4))
    shaped = spectral_weight.reshape(2, KX, KY, KZ, WIDTH, WIDTH)
    out_real = contract(shaped[0], spec_t[0]) - contract(shaped[1], spec_t[1])
    out_imag = contract(shaped[0], spec_t[1]) + contract(shaped[1], spec_t[0])
    spectral_out = jnp.stack([out_real, out_imag], axis=1)
    mixed = jnp.dot(local_weight, lift_weight, precision=lax.Precision.HIGHEST)

    def channel(total, items):
        spec_o, mix_o, bias_o, proj_o = items
        spectral_field = inverse_spec(spec_o)
        pre_act = spectral_field + mix_o[0] * phase_next + mix_o[1] * centred + bias_o
        activated, gelu_back = jax.vjp(jax.nn.gelu, pre_act)
        grad_pre = gelu_back(proj_o * cotangent)[0]
        grad_modes = forward_spec(grad_pre, weights_z, 1.0 / NX, 1.0 / NY)
        sums = jnp.stack([jnp.sum(grad_pre * phase_next), jnp.sum(grad_pre * centred)])
        proj_sum = jnp.sum(activated * cotangent)
        return (total + proj_o * activated, (grad_modes, sums, proj_sum))
    predicted, (grad_modes, sums, proj_sums) = lax.scan(channel, jnp.zeros((NX, NY, NZ), jnp.float32), (spectral_out, mixed, local_bias, proj_weight))
    grad_t = jnp.transpose(grad_modes, (1, 0, 2, 3, 4))
    grad_real = outer(grad_t[0], spec_t[0]) + outer(grad_t[1], spec_t[1])
    grad_imag = outer(grad_t[1], spec_t[0]) - outer(grad_t[0], spec_t[1])
    grad_spectral = jnp.stack([grad_real, grad_imag]).reshape(2, KX, KY, KZ, WIDTH * WIDTH)
    scale = 1.0 / math.sqrt(NX * NY * NZ)
    grad_local = jnp.dot(sums, lift_weight.T, precision=lax.Precision.HIGHEST) * scale
    grad_proj = proj_sums * scale
    return (phase_next, solute_next, predicted, grad_spectral, grad_local, grad_proj)
```

```python
import functools
from functools import reduce
import math

import jax
import jax.numpy as jnp
import ml_dtypes
import numpy as np
from jax import lax
from jax.experimental import pallas as pl
from jax.experimental.pallas import tpu as pltpu
from jax.sharding import PartitionSpec as P

WIDTH = 32
KX = 32
KY = 32
KZ = 32


TIME_STEP = 0.05
COUPLING = 2.0
SOLID_DIFF = 0.05
LIQUID_DIFF = 1.0
PARTITION = 0.15
TRAP_RATE = 4.0
SOLUTE_MEAN = 0.5


def extended(cells, sides, width):
    for axis, dim in sides:
        count = lax.axis_size(axis)
        head = lax.slice_in_dim(cells, 0, width, axis=dim)
        tail = lax.slice_in_dim(cells, cells.shape[dim] - width, cells.shape[dim], axis=dim)
        cells = jnp.concatenate(
            [
                lax.ppermute(tail, axis, [(i, (i + 1) % count) for i in range(count)]),
                cells,
                lax.ppermute(head, axis, [((i + 1) % count, i) for i in range(count)]),
            ],
            axis=dim,
        )
    return cells


def diffusivity(phase_now):
    return SOLID_DIFF + (LIQUID_DIFF - SOLID_DIFF) * 0.5 * (1.0 - jnp.tanh(phase_now))


def update(phase_now, solute_now, undercool, phase_nb, solute_nb, diff_now, diff_nb):
    lap = reduce(jnp.add, phase_nb) - 6.0 * phase_now
    squares = 1.0 - phase_now * phase_now
    rate = (
        lap
        + phase_now
        - phase_now * phase_now * phase_now
        + COUPLING * squares * squares * (undercool - solute_now)
    )
    fluxes = [
        0.5 * (diff_now + diff_nb[index]) * (solute_nb[index] - solute_now) for index in range(6)
    ]
    divergence = reduce(jnp.add, fluxes)
    speed = TRAP_RATE * jnp.abs(rate)
    keff = (PARTITION + speed) / (1.0 + speed)
    phase_new = phase_now + TIME_STEP * rate
    solute_new = solute_now + TIME_STEP * (divergence + 0.5 * (1.0 - keff) * solute_now * rate)
    return (phase_new, solute_new)


def beside(padded):
    centre = padded[1:-1, 1:-1]
    return [
        padded[2:, 1:-1],
        padded[:-2, 1:-1],
        padded[1:-1, 2:],
        padded[1:-1, :-2],
        jnp.roll(centre, -1, 2),
        jnp.roll(centre, 1, 2),
    ]


def phase_sweep(phase_now, solute_now, undercool):
    padded = extended(jnp.stack([phase_now, solute_now]), (("gx", 1), ("gy", 2)), 1)
    phase_pad = padded[0]
    solute_pad = padded[1]
    diff_pad = diffusivity(phase_pad)
    return update(
        phase_now,
        solute_now,
        undercool,
        beside(phase_pad),
        beside(solute_pad),
        diff_pad[1:-1, 1:-1],
        beside(diff_pad),
    )


def signed_freq(indices, total):
    return jnp.where(indices < total // 2, indices, indices - total)


def wave_tables(freqs, positions, length, factor):
    product = freqs[:, None] * positions[None, :] % length
    angles = product.astype(jnp.float32) * (2.0 * math.pi / length)
    return (jnp.cos(angles) * factor, jnp.sin(angles) * factor)


def complex_mix(cosines, sines, data, pattern, orient):

    def apply(table, values):
        return jnp.einsum(pattern, table, values, precision=lax.Precision.HIGHEST)

    cos_real = apply(cosines, data[0])
    cos_imag = apply(cosines, data[1])
    sin_real = apply(sines, data[0])
    sin_imag = apply(sines, data[1])
    return jnp.stack([cos_real - orient * sin_imag, cos_imag + orient * sin_real])


def x_forward(data, factor):
    portion = lax.all_to_all(data, "gx", split_axis=1, concat_axis=2, tiled=True)
    length = portion.shape[2]
    cosines, sines = wave_tables(
        signed_freq(jnp.arange(KX, dtype=jnp.int32), KX),
        jnp.arange(length, dtype=jnp.int32),
        length,
        factor,
    )
    lines = complex_mix(cosines, sines, portion, "kx,wxyz->wkyz", -1.0)
    return lax.all_to_all(lines, "gx", split_axis=2, concat_axis=1, tiled=True)


def y_forward(data, factor):
    portion = lax.all_to_all(data, "gy", split_axis=1, concat_axis=3, tiled=True)
    length = portion.shape[3]
    cosines, sines = wave_tables(
        signed_freq(jnp.arange(KY, dtype=jnp.int32), KY),
        jnp.arange(length, dtype=jnp.int32),
        length,
        factor,
    )
    lines = complex_mix(cosines, sines, portion, "ky,wayz->wakz", -1.0)
    return lax.all_to_all(lines, "gy", split_axis=3, concat_axis=1, tiled=True)


def contract(weights, values):
    return jnp.einsum("abzoi,iabz->oabz", weights, values, precision=lax.Precision.HIGHEST)


def outer(left, right):
    return jnp.einsum("oabz,iabz->abzoi", left, right, precision=lax.Precision.HIGHEST)


def per_device_plain(
    phase,
    solute,
    undercool,
    lift_weight,
    spectral_weight,
    local_weight,
    local_bias,
    proj_weight,
    cotangent,
):
    phase_mid, solute_mid = phase_sweep(phase, solute, undercool)
    phase_next, solute_next = phase_sweep(phase_mid, solute_mid, undercool)
    cells_x, cells_y, depth = phase.shape
    total_x = cells_x * lax.axis_size("gx")
    total_y = cells_y * lax.axis_size("gy")
    fields = jnp.stack([phase_next, solute_next - SOLUTE_MEAN])
    modes_z = jnp.arange(KZ, dtype=jnp.int32)
    zpos = jnp.arange(depth, dtype=jnp.int32)
    unit_z = jnp.ones((KZ,), jnp.float32)
    weights_z = jnp.where(modes_z == 0, 1.0, 2.0).astype(jnp.float32) / depth

    def z_forward(field, zfactor):
        cosines, sines = wave_tables(modes_z, zpos, depth, zfactor[:, None])
        tables = jnp.stack([cosines, -sines])
        return jnp.einsum("wxyz,rkz->rwxyk", field, tables, precision=lax.Precision.HIGHEST)

    def spectral_forward(field, zfactor, xfactor, yfactor):
        return y_forward(x_forward(z_forward(field, zfactor), xfactor), yfactor)

    lifted = jnp.einsum("wc,cxyz->wxyz", lift_weight, fields, precision=lax.Precision.HIGHEST)
    spectrum = spectral_forward(lifted, unit_z, 1.0, 1.0)
    own_x = spectrum.shape[2]
    own_y = spectrum.shape[3]
    shaped = spectral_weight.reshape(2, own_x, own_y, KZ, WIDTH, WIDTH)
    out_real = contract(shaped[0], spectrum[0]) - contract(shaped[1], spectrum[1])
    out_imag = contract(shaped[0], spectrum[1]) + contract(shaped[1], spectrum[0])
    spectral_out = jnp.stack([out_real, out_imag])
    ypos = lax.axis_index("gy") * cells_y + jnp.arange(cells_y, dtype=jnp.int32)
    portion = lax.all_gather(spectral_out, "gy", axis=3, tiled=True)
    freqs = signed_freq(jnp.arange(portion.shape[3], dtype=jnp.int32), KY)
    cosines, sines = wave_tables(ypos, freqs, total_y, 1.0 / total_y)
    back_y = complex_mix(cosines, sines, portion, "yk,wakz->wayz", 1.0)
    cosines, sines = wave_tables(
        jnp.arange(total_x, dtype=jnp.int32),
        signed_freq(jnp.arange(KX, dtype=jnp.int32), KX),
        total_x,
        1.0 / total_x,
    )
    inverted = complex_mix(
        cosines,
        sines,
        lax.all_to_all(back_y, "gx", split_axis=1, concat_axis=2, tiled=True),
        "xk,wkyz->wxyz",
        1.0,
    )
    back_x = lax.all_to_all(inverted, "gx", split_axis=2, concat_axis=1, tiled=True)
    cos_back, sin_back = wave_tables(modes_z, zpos, depth, weights_z[:, None])
    back_tables = jnp.stack([cos_back, -sin_back])
    spectral_field = jnp.einsum(
        "rwxyk,rkz->wxyz", back_x, back_tables, precision=lax.Precision.HIGHEST
    )
    mixed = jnp.dot(local_weight, lift_weight, precision=lax.Precision.HIGHEST)
    pre_act = (
        spectral_field
        + jnp.einsum("wc,cxyz->wxyz", mixed, fields, precision=lax.Precision.HIGHEST)
        + local_bias[:, None, None, None]
    )
    activated, gelu_back = jax.vjp(jax.nn.gelu, pre_act)
    predicted = jnp.einsum("w,wxyz->xyz", proj_weight, activated, precision=lax.Precision.HIGHEST)
    grad_pre = gelu_back(proj_weight[:, None, None, None] * cotangent[None])[0]
    field_sums = jnp.einsum("wxyz,cxyz->wc", grad_pre, fields, precision=lax.Precision.HIGHEST)
    proj_sums = jnp.einsum("wxyz,xyz->w", activated, cotangent, precision=lax.Precision.HIGHEST)
    field_sums, proj_sums = lax.psum((field_sums, proj_sums), ("gx", "gy"))
    grad_modes = spectral_forward(grad_pre, weights_z, 1.0 / total_x, 1.0 / total_y)
    grad_real = outer(grad_modes[0], spectrum[0]) + outer(grad_modes[1], spectrum[1])
    grad_imag = outer(grad_modes[1], spectrum[0]) - outer(grad_modes[0], spectrum[1])
    grad_spectral = jnp.stack([grad_real, grad_imag]).reshape(2, own_x, own_y, KZ, WIDTH * WIDTH)
    scale = 1.0 / math.sqrt(total_x * total_y * depth)
    grad_local = jnp.dot(field_sums, lift_weight.T, precision=lax.Precision.HIGHEST) * scale
    grad_proj = proj_sums * scale
    return (phase_next, solute_next, predicted, grad_spectral, grad_local, grad_proj)


LANES = 128
SPREAD = LANES // WIDTH
NARROW = jnp.bfloat16
EXACT = lax.Precision.HIGHEST


def halves(table):
    head = table.astype(np.float32).astype(ml_dtypes.bfloat16)
    rest = (table - head.astype(np.float64)).astype(np.float32).astype(ml_dtypes.bfloat16)
    return head, rest


def left_table(table):
    head, rest = halves(table)
    return np.concatenate([head, head, rest], axis=1)


def right_table(table):
    head, rest = halves(table)
    return np.concatenate([head, head, rest], axis=0)


def parts_of(values):
    head = values.astype(NARROW)
    return head, (values - head.astype(jnp.float32)).astype(NARROW)


def thrice(values, axis):
    head, rest = parts_of(values)
    return jnp.concatenate([head, rest, head], axis=axis)


def mul(left, right):
    return jnp.dot(left, right, preferred_element_type=jnp.float32)


def mul_rows(left, right):
    return lax.dot_general(
        left, right, (((1,), (1,)), ((), ())), preferred_element_type=jnp.float32
    )


def angles(freqs, positions, length):
    return 2.0 * np.pi * ((freqs[:, None] * positions[None, :]) % length) / length


def signed(count):
    index = np.arange(count)
    return np.where(index < count // 2, index, index - count)


def rotation(theta, orient):
    cosines, sines = np.cos(theta), orient * np.sin(theta)
    return np.block([[cosines, -sines], [sines, cosines]])


def group_of(shape):
    return lax.broadcasted_iota(jnp.int32, shape, len(shape) - 1) // WIDTH


def pick(groups, choices):
    result = choices[-1]
    for index in range(len(choices) - 2, -1, -1):
        result = jnp.where(groups == index, choices[index], result)
    return result


def turn(values, shift):
    shift = shift % LANES
    return values if shift == 0 else pltpu.roll(values, shift, 1)


def swap_groups(pieces):
    groups = group_of(pieces[0].shape)
    return [
        pick(groups, [turn(pieces[i], WIDTH * (i - j)) for i in range(SPREAD)])
        for j in range(SPREAD)
    ]


def contract_kernel(weight_ref, lift_ref, out_ref, mix_ref):
    _, planes, own_y, modes_z, _ = weight_ref.shape
    own_x = pl.num_programs(0) * planes
    step = pl.program_id(0)

    @pl.when(step == 0)
    def _():
        shape = (WIDTH, LANES)
        lane = lax.broadcasted_iota(jnp.int32, shape, 1)
        base = jnp.where(
            lane % (2 * WIDTH) < WIDTH,
            jnp.broadcast_to(lift_ref[:, 0:1], shape),
            jnp.broadcast_to(lift_ref[:, 1:2], shape),
        )
        for channel in range(WIDTH):
            block = jnp.where(lane % WIDTH == channel, base, 0.0)
            head, rest = parts_of(block)
            both = jnp.where(lane < 2 * WIDTH, head.astype(jnp.float32), rest.astype(jnp.float32))
            mix_ref[channel * WIDTH : (channel + 1) * WIDTH, :] = both.astype(NARROW)

    mixing = mix_ref[...]
    rows = planes * own_y * modes_z
    sums = []
    for part in range(2):
        head, rest = parts_of(weight_ref[part].reshape(rows, WIDTH * WIDTH))
        total = mul(head, mixing) + mul(rest, mixing)
        sums.append(total + pltpu.roll(total, 2 * WIDTH, 1))
    lane = lax.broadcasted_iota(jnp.int32, (rows, LANES), 1)
    result = jnp.where(lane < 2 * WIDTH, sums[0], sums[1])
    for plane in range(planes):
        for row in range(own_y):
            first = (plane * own_y + row) * modes_z
            place = row * own_x + step * planes + plane
            out_ref[pl.ds(place, modes_z, stride=own_x * own_y), :] = result[
                first : first + modes_z
            ]


def pack_kernel(phase_ref, solute_ref, cool_ref, before_ref, after_ref, head_ref, tail_ref):
    cells_x, cells_y, _ = phase_ref.shape

    def put(target, phase, solute, cool):
        head_ref[target, 0:2] = phase[:, 0:2]
        head_ref[target, 2:4] = solute[:, 0:2]
        head_ref[target, 4:5] = cool[:, 0:1]
        tail_ref[target, 0:2] = phase[:, cells_y - 2 : cells_y]
        tail_ref[target, 2:4] = solute[:, cells_y - 2 : cells_y]
        tail_ref[target, 4:5] = cool[:, cells_y - 1 : cells_y]

    put(slice(0, 1), before_ref[1:2], before_ref[3:4], before_ref[4:5])
    put(slice(1, cells_x + 1), phase_ref[...], solute_ref[...], cool_ref[...])
    put(slice(cells_x + 1, cells_x + 2), after_ref[0:1], after_ref[2:3], after_ref[4:5])


def step_kernel(
    phase_ref,
    solute_ref,
    cool_ref,
    before_ref,
    after_ref,
    low_ref,
    high_ref,
    table_ref,
    phase_out,
    solute_out,
    spec_out,
    phase_ext,
    solute_ext,
    cool_ext,
    diff_ext,
    lines,
):
    cells_x, cells_y, depth = phase_ref.shape
    base = 8
    end = base + cells_y
    for ext, own, first in ((phase_ext, phase_ref, 0), (solute_ext, solute_ref, 2)):
        ext[2 : cells_x + 2, base:end] = own[...]
        ext[0:2, base:end] = before_ref[first : first + 2]
        ext[cells_x + 2 : cells_x + 4, base:end] = after_ref[first : first + 2]
        ext[1 : cells_x + 3, base - 2 : base] = low_ref[:, first : first + 2]
        ext[1 : cells_x + 3, end : end + 2] = high_ref[:, first : first + 2]
    cool_ext[2 : cells_x + 2, base:end] = cool_ref[...]
    cool_ext[1:2, base:end] = before_ref[4:5]
    cool_ext[cells_x + 2 : cells_x + 3, base:end] = after_ref[4:5]
    cool_ext[1 : cells_x + 3, base - 1 : base] = low_ref[:, 4:5]
    cool_ext[1 : cells_x + 3, end : end + 1] = high_ref[:, 4:5]

    def sweep(reach):
        diff_ext[...] = diffusivity(phase_ext[...])

        def window(ext, move_x, move_y):
            return ext[
                2 - reach + move_x : cells_x + 2 + reach + move_x,
                base - reach + move_y : end + reach + move_y,
            ]

        def around(ext, now):
            return [
                window(ext, 1, 0),
                window(ext, -1, 0),
                window(ext, 0, 1),
                window(ext, 0, -1),
                pltpu.roll(now, depth - 1, 2),
                pltpu.roll(now, 1, 2),
            ]

        phase_now = window(phase_ext, 0, 0)
        solute_now = window(solute_ext, 0, 0)
        diff_now = window(diff_ext, 0, 0)
        return update(
            phase_now,
            solute_now,
            window(cool_ext, 0, 0),
            around(phase_ext, phase_now),
            around(solute_ext, solute_now),
            diff_now,
            around(diff_ext, diff_now),
        )

    phase_mid, solute_mid = sweep(1)
    phase_ext[1 : cells_x + 3, base - 1 : end + 1] = phase_mid
    solute_ext[1 : cells_x + 3, base - 1 : end + 1] = solute_mid
    phase_next, solute_next = sweep(0)
    phase_out[...] = phase_next
    solute_out[...] = solute_next
    tile = cells_x * cells_y
    both = (phase_next.reshape(tile, depth), solute_next.reshape(tile, depth) - SOLUTE_MEAN)
    ordered = []
    for part in range(depth // LANES):
        for index, values in enumerate(both):
            lines[part, index * tile : (index + 1) * tile] = values[
                :, part * LANES : (part + 1) * LANES
            ]
        ordered.append(
            jnp.concatenate(
                [
                    lines[part, pl.ds(row, 2 * cells_x, stride=cells_y), :]
                    for row in range(cells_y)
                ],
                axis=0,
            )
        )
    ordered = jnp.concatenate(ordered, axis=1)
    spec_out[...] = mul_rows(table_ref[...], thrice(ordered, 1))


def spectral_kernel(
    shape,
    spec_ref,
    weight_ref,
    y_in_ref,
    x_in_ref,
    y_out_ref,
    x_out_ref,
    modes_ref,
    send_ref,
    lines_y,
    lines_x,
):
    count_x, count_y, cells_x, cells_y, own_x, own_y = shape
    modes_x, modes_y = count_x * own_x, count_y * own_y
    total_x, total_y = count_x * cells_x, count_y * cells_y
    tile = cells_x * cells_y
    narrow = 2 * cells_x
    rows = 2 * count_y
    lane = lax.broadcasted_iota(jnp.int32, (rows, LANES), 1)
    blocks = []
    for row in range(cells_y):
        block = jnp.zeros((rows, LANES), jnp.float32)
        for index in range(count_x):
            piece = turn(spec_ref[index * rows : (index + 1) * rows, :], narrow * (index - row))
            block = jnp.where(lane // narrow == index, piece, block)
        blocks.append(block)
    along_y = mul(y_in_ref[...], thrice(jnp.concatenate(blocks, axis=0), 0))
    half = lax.broadcasted_iota(jnp.int32, (modes_y, LANES), 1) < LANES // 2
    joined = jnp.where(half, along_y[0:modes_y], turn(along_y[modes_y:], LANES // 2))
    modes = mul(thrice(joined, 1), x_in_ref[...])
    modes_ref[...] = modes
    groups = group_of((modes_y, LANES))
    quads_y = total_y // SPREAD
    for quad in range(modes_x // SPREAD):
        reals, imags = [], []
        for index in range(SPREAD):
            freq = SPREAD * quad + index
            start = (freq // own_x) * count_y * own_y * own_x + freq % own_x
            weights = weight_ref[pl.ds(start, modes_y, stride=own_x), :]
            columns = [
                jnp.broadcast_to(
                    modes[:, k * modes_x + freq : k * modes_x + freq + 1], (modes_y, LANES)
                )
                for k in range(4)
            ]
            first = weights * pick(groups, [columns[0], columns[1], -columns[2], -columns[3]])
            second = weights * pick(groups, [columns[2], columns[3], columns[0], columns[1]])
            first = first + turn(first, 2 * WIDTH)
            second = second + turn(second, 2 * WIDTH)
            reals.append(first + turn(first, WIDTH))
            imags.append(second + turn(second, WIDTH))
        stacked = jnp.concatenate([pick(groups, reals), pick(groups, imags)], axis=0)
        lines_y[...] = mul(y_out_ref[...], thrice(stacked, 0))
        for part in range(2):
            pieces = [
                lines_y[pl.ds(part * total_y + i, quads_y, stride=SPREAD), :] for i in range(SPREAD)
            ]
            for index, piece in enumerate(swap_groups(pieces)):
                place = part * modes_x + SPREAD * quad + index
                lines_x[pl.ds(place, quads_y, stride=2 * modes_x), :] = piece
    per_tile = cells_y // SPREAD
    for quad in range(quads_y):
        block = lines_x[quad * 2 * modes_x : (quad + 1) * 2 * modes_x, :]
        back = mul(x_out_ref[...], thrice(block, 0))
        for part in range(2):
            for index in range(count_x):
                device = index * count_y + quad // per_tile
                place = (device * 2 + part) * per_tile + quad % per_tile
                first = part * total_x + index * cells_x
                send_ref[place * cells_x : (place + 1) * cells_x, :] = back[
                    first : first + cells_x
                ]


def field_kernel(
    shape,
    field_ref,
    phase_ref,
    solute_ref,
    cotangent_ref,
    vector_ref,
    back_ref,
    forth_ref,
    predicted_ref,
    send_ref,
    spread_ref,
):
    cells_x, cells_y, modes_z = shape
    tile = cells_x * cells_y
    depth = phase_ref.shape[1]
    wide = cells_y * WIDTH
    halves_y = cells_y // SPREAD
    stride = halves_y * cells_x
    for index, values in enumerate(
        (phase_ref[...], solute_ref[...] - SOLUTE_MEAN, cotangent_ref[...])
    ):
        head, rest = parts_of(values.T)
        spread_ref[index] = jnp.concatenate([head, rest], axis=1)
    mix_phase = vector_ref[0:1, :]
    mix_solute = vector_ref[1:2, :]
    bias = vector_ref[2:3, :]
    proj = vector_ref[3:4, :]
    root = math.sqrt(2.0 / math.pi)
    curve = 0.044715
    cell = lax.broadcasted_iota(jnp.int32, (2 * tile, wide), 0) % tile
    row = lax.broadcasted_iota(jnp.int32, (2 * tile, wide), 1) // WIDTH
    picker = (
        lax.broadcasted_iota(jnp.int32, (cells_y, 2 * wide), 0)
        == lax.broadcasted_iota(jnp.int32, (cells_y, 2 * wide), 1) % wide // WIDTH
    ).astype(jnp.float32).astype(NARROW)

    def fold(values):
        return jnp.sum(values.reshape(depth // 8, 8, wide), axis=0)

    def one(plane, sums):
        spectra = jnp.concatenate(
            [
                field_ref[pl.ds(part * cells_x + plane, 2 * modes_z, stride=stride), :]
                for part in range(halves_y)
            ],
            axis=1,
        )
        field = mul(back_ref[...], thrice(spectra, 0))
        chosen = (cell == plane * cells_y + row).astype(jnp.float32).astype(NARROW)
        phase = mul(spread_ref[0], chosen)
        solute = mul(spread_ref[1], chosen)
        cotangent = mul(spread_ref[2], chosen)
        pre = field + phase * mix_phase + solute * mix_solute + bias
        square = pre * pre
        bent = jnp.tanh(root * pre * (1.0 + curve * square))
        upper = 0.5 * (1.0 + bent)
        active = pre * upper
        slope = upper + 0.5 * pre * (1.0 - bent * bent) * (root * (1.0 + 3.0 * curve * square))
        grad = proj * cotangent * slope
        weighted = jnp.concatenate(parts_of(proj * active), axis=1)
        predicted_ref[pl.ds(pl.multiple_of(plane * cells_y, cells_y), cells_y), :] = mul_rows(
            picker, weighted
        )
        spectra = mul(forth_ref[...], thrice(grad, 0))
        for part in range(halves_y):
            send_ref[pl.ds(part * cells_x + plane, 2 * modes_z, stride=stride), :] = spectra[
                :, part * LANES : (part + 1) * LANES
            ]
        return (
            sums[0] + fold(grad * phase),
            sums[1] + fold(grad * solute),
            sums[2] + fold(active * cotangent),
        )

    zero = jnp.zeros((8, wide), jnp.float32)
    sums = lax.fori_loop(0, cells_x, one, (zero, zero, zero))
    for index, values in enumerate(sums):
        line = jnp.sum(values, axis=0, keepdims=True)
        line = sum(line[:, part * LANES : (part + 1) * LANES] for part in range(halves_y))
        send_ref[stride + index : stride + index + 1, :] = line


def gradient_kernel(
    shape, spectra_ref, modes_ref, x_in_ref, y_in_ref, send_ref, lines_x, lines_y
):
    count_x, count_y, cells_x, cells_y, own_x, own_y = shape
    modes_x, modes_y = count_x * own_x, count_y * own_y
    total_x, total_y = count_x * cells_x, count_y * cells_y
    per_tile = cells_y // SPREAD
    quads_y = total_y // SPREAD
    chunk = 2 * per_tile * cells_x
    first_device = (lax.axis_index("gx") == 0) & (lax.axis_index("gy") == 0)
    keep = jnp.where(first_device, 0.0, 1.0)
    for quad in range(quads_y):
        blocks = []
        for part in range(2):
            for index in range(count_x):
                device = index * count_y + quad // per_tile
                place = (device * 2 + part) * per_tile + quad % per_tile
                block = spectra_ref[place * cells_x : (place + 1) * cells_x, :]
                blocks.append(block * keep if part else block)
        lines_x[quad * 2 * modes_x : (quad + 1) * 2 * modes_x, :] = mul(
            x_in_ref[...], thrice(jnp.concatenate(blocks, axis=0), 0)
        )
    out_chunk = send_ref.shape[0] // (count_x * count_y)
    per_own = own_x // SPREAD
    for quad in range(modes_x // SPREAD):
        for part in range(2):
            pieces = [
                lines_x[
                    pl.ds(part * modes_x + SPREAD * quad + j, quads_y, stride=2 * modes_x), :
                ]
                for j in range(SPREAD)
            ]
            for index, piece in enumerate(swap_groups(pieces)):
                lines_y[pl.ds(part * total_y + index, quads_y, stride=SPREAD), :] = piece
        modes = mul(y_in_ref[...], thrice(lines_y[...], 0))
        for part in range(2):
            for index in range(count_y):
                device = (quad // per_own) * count_y + index
                place = device * out_chunk + (part * per_own + quad % per_own) * own_y
                first = part * modes_y + index * own_y
                send_ref[place : place + own_y, :] = modes[first : first + own_y]
    extra = 2 * per_own * own_y
    totals = []
    for index in range(3):
        start = chunk // 2 + index
        line = jnp.sum(
            spectra_ref[pl.ds(start, count_x * count_y, stride=chunk), :], axis=0, keepdims=True
        )
        line = line + turn(line, 2 * WIDTH)
        totals.append(line + turn(line, WIDTH))
    totals.append(jnp.zeros_like(totals[0]))
    totals = jnp.concatenate(totals, axis=0)
    for index_x in range(count_x):
        for index_y in range(count_y):
            place = (index_x * count_y + index_y) * out_chunk + extra
            send_ref[place : place + own_y, :] = modes_ref[
                index_y * own_y : (index_y + 1) * own_y, :
            ]
            send_ref[place + own_y : place + own_y + 4, :] = totals


def outer_kernel(scale, modes_x, modes_ref, lift_ref, grad_ref, local_ref, proj_ref, mix_ref):
    _, planes, own_y, modes_z, width = grad_ref.shape
    own_x = pl.num_programs(0) * planes
    step = pl.program_id(0)
    chunk = modes_ref.shape[0] // modes_z
    per_own = own_x // SPREAD
    extra = 2 * per_own * own_y

    @pl.when(step == 0)
    def _():
        shape = (2 * WIDTH, width)
        row = lax.broadcasted_iota(jnp.int32, shape, 0)
        column = lax.broadcasted_iota(jnp.int32, shape, 1)
        lift = jnp.where(row < WIDTH, lift_ref[0:1, :], lift_ref[1:2, :])
        head, rest = parts_of(jnp.where(column // WIDTH == row % WIDTH, lift, 0.0))
        mix_ref[0 : 2 * WIDTH] = head
        mix_ref[2 * WIDTH : 4 * WIDTH] = head
        mix_ref[4 * WIDTH : 6 * WIDTH] = rest
        mix_ref[6 * WIDTH : 8 * WIDTH] = jnp.zeros_like(rest)
        sums = modes_ref[extra : extra + 8, :]
        turned = sums.T[0:WIDTH]
        local_ref[...] = scale * (
            turned[:, own_y : own_y + 1] * lift_ref[0:1, 0:WIDTH]
            + turned[:, own_y + 1 : own_y + 2] * lift_ref[1:2, 0:WIDTH]
        )
        proj_ref[...] = scale * sums[own_y + 2 : own_y + 3, 0:WIDTH]

    lane = lax.broadcasted_iota(jnp.int32, (modes_z, LANES), 1)
    even = lane % (2 * WIDTH) < WIDTH
    low = lane < 2 * WIDTH

    def rows_of(values):
        head, rest = parts_of(values)
        both = jnp.where(low, head.astype(jnp.float32), rest.astype(jnp.float32)).astype(NARROW)
        return jnp.concatenate([both, head], axis=1)

    for plane in range(planes):
        freq = step * planes + plane
        reals, imags = [], []
        for row in range(own_y):
            modes = modes_ref[pl.ds(extra + row, modes_z, stride=chunk), :]
            modes = pltpu.roll(modes, LANES - (lax.axis_index("gx") * own_x + freq), 1)
            columns = [
                jnp.broadcast_to(modes[:, k * modes_x : k * modes_x + 1], (modes_z, LANES))
                for k in range(4)
            ]
            real = jnp.where(even, columns[0], columns[1])
            imag = jnp.where(even, columns[2], columns[3])
            grads = []
            for part in range(2):
                place = (part * per_own + freq // SPREAD) * own_y + row
                grad = modes_ref[pl.ds(place, modes_z, stride=chunk), :]
                grad = pltpu.roll(grad, (LANES - WIDTH * (freq % SPREAD)) % LANES, 1)
                grad = jnp.where(lane < WIDTH, grad, 0.0)
                grad = grad + turn(grad, WIDTH)
                grads.append(grad + turn(grad, 2 * WIDTH))
            reals.append(rows_of(grads[0] * real + grads[1] * imag))
            imags.append(rows_of(grads[1] * real - grads[0] * imag))
        result = mul(jnp.concatenate(reals + imags, axis=0), mix_ref[...])
        grad_ref[:, plane] = result.reshape(2, own_y, modes_z, width)


def tables(shape, depth, modes_z):
    count_x, count_y, cells_x, cells_y, own_x, own_y = shape
    modes_x, modes_y = count_x * own_x, count_y * own_y
    total_x, total_y = count_x * cells_x, count_y * cells_y
    theta_z = angles(np.arange(modes_z), np.arange(depth), depth)
    theta_x = angles(signed(modes_x), np.arange(total_x), total_x)
    theta_y = angles(signed(modes_y), np.arange(total_y), total_y)
    forth_z = np.stack([np.cos(theta_z), -np.sin(theta_z)], axis=1).reshape(2 * modes_z, depth)
    weight = np.where(np.arange(modes_z) == 0, 1.0, 2.0) / (total_x * total_y * depth)
    weighted_z = np.repeat(weight, 2)[:, None] * forth_z
    forth_x, back_x = rotation(theta_x, -1.0), rotation(theta_x.T, 1.0)
    forth_y, back_y = rotation(theta_y, -1.0), rotation(theta_y.T, 1.0)
    order_y = forth_y.reshape(2 * modes_y, 2, count_y, cells_y)
    order_y = order_y.transpose(0, 3, 2, 1).reshape(2 * modes_y, 2 * total_y)
    lines = forth_x.reshape(2, modes_x, 2, count_x, cells_x)
    both = np.zeros((2, count_x, 2, cells_x, 2, 2, modes_x))
    for field in range(2):
        both[:, :, field, :, :, field, :] = lines.transpose(2, 3, 4, 0, 1)
    both = both.reshape(4 * total_x, 4 * modes_x)
    return {
        "z_plain": left_table(forth_z),
        "z_forth": left_table(weighted_z),
        "z_back": left_table(weighted_z.T),
        "y_first": left_table(order_y),
        "x_first": right_table(both),
        "y_back": left_table(back_y),
        "x_back": left_table(back_x),
        "x_forth": left_table(forth_x),
        "y_forth": left_table(forth_y),
    }


def fits(count_x, count_y, phase, spectral_weight):
    cells_x, cells_y, depth = phase.shape
    _, own_x, own_y, modes_z, width = spectral_weight.shape
    return (
        width == WIDTH * WIDTH
        and modes_z == count_x * count_y
        and 4 * count_x * cells_x == LANES
        and 4 * count_x * own_x == LANES
        and 2 * cells_x * cells_y == LANES
        and cells_x == 8
        and cells_y % SPREAD == 0
        and own_x % SPREAD == 0
        and own_y == 4
        and depth % LANES == 0
    )


def call(kernel, outs, scratch, flops, moved, **more):
    return pl.pallas_call(
        kernel,
        out_shape=outs,
        scratch_shapes=scratch,
        compiler_params=pltpu.CompilerParams(vmem_limit_bytes=32 * 1024 * 1024),
        cost_estimate=pl.CostEstimate(flops=flops, bytes_accessed=moved, transcendentals=0),
        **more,
    )


def exchange(values):
    return lax.all_to_all(values, ("gx", "gy"), split_axis=0, concat_axis=0, tiled=True)


def per_device_fast(
    phase,
    solute,
    undercool,
    lift_weight,
    spectral_weight,
    local_weight,
    local_bias,
    proj_weight,
    cotangent,
):
    count_x, count_y = lax.axis_size("gx"), lax.axis_size("gy")
    cells_x, cells_y, depth = phase.shape
    _, own_x, own_y, modes_z, width = spectral_weight.shape
    shape = (count_x, count_y, cells_x, cells_y, own_x, own_y)
    devices = count_x * count_y
    tile = cells_x * cells_y
    modes_x, modes_y = count_x * own_x, count_y * own_y
    total_x, total_y = count_x * cells_x, count_y * cells_y
    table = tables(shape, depth, modes_z)
    real = jnp.float32

    def like(*dims):
        return jax.ShapeDtypeStruct(dims, real)

    planes = 2
    mixed_weights = call(
        contract_kernel,
        like(modes_z * own_x * own_y, LANES),
        [pltpu.VMEM((width, LANES), NARROW)],
        8 * own_x * own_y * modes_z * width * LANES,
        8 * own_x * own_y * modes_z * width,
        grid=(own_x // planes,),
        in_specs=[
            pl.BlockSpec((2, planes, own_y, modes_z, width), lambda i: (0, i, 0, 0, 0)),
            pl.BlockSpec(lift_weight.shape, lambda i: (0, 0)),
        ],
        out_specs=pl.BlockSpec((modes_z * own_x * own_y, LANES), lambda i: (0, 0)),
    )(spectral_weight, lift_weight)

    def ring(values, axis, step):
        count = lax.axis_size(axis)
        return lax.ppermute(values, axis, [(i, (i + step) % count) for i in range(count)])

    head = jnp.concatenate([phase[:2], solute[:2], undercool[:1]])
    tail = jnp.concatenate([phase[-2:], solute[-2:], undercool[-1:]])
    before, after = ring(tail, "gx", 1), ring(head, "gx", -1)
    head, tail = call(
        pack_kernel,
        (like(cells_x + 2, 8, depth), like(cells_x + 2, 8, depth)),
        [],
        1000,
        40 * cells_x * cells_y * depth,
    )(phase, solute, undercool, before, after)
    low, high = ring(tail, "gy", 1), ring(head, "gy", -1)
    extended_shape = pltpu.VMEM((cells_x + 4, cells_y + 16, depth), real)
    phase_next, solute_next, spectra = call(
        step_kernel,
        (like(*phase.shape), like(*phase.shape), like(2 * modes_z, LANES)),
        [extended_shape] * 4 + [pltpu.VMEM((depth // LANES, 2 * tile, LANES), real)],
        400 * tile * depth,
        80 * tile * depth,
    )(phase, solute, undercool, before, after, low, high, table["z_plain"])
    gathered_weights = exchange(mixed_weights)
    gathered = exchange(spectra)
    modes, fields = call(
        functools.partial(spectral_kernel, shape),
        (like(modes_y, LANES), like(devices * 2 * cells_x * (cells_y // SPREAD), LANES)),
        [
            pltpu.VMEM((2 * total_y, LANES), real),
            pltpu.VMEM((2 * modes_x * (total_y // SPREAD), LANES), real),
        ],
        100_000_000,
        2_000_000,
    )(
        gathered,
        gathered_weights,
        table["y_first"],
        table["x_first"],
        table["y_back"],
        table["x_back"],
    )
    fields = exchange(fields)
    mixed = jnp.dot(local_weight, lift_weight, precision=EXACT)
    vectors = jnp.tile(
        jnp.stack([mixed[:, 0], mixed[:, 1], local_bias, proj_weight]), (1, cells_y)
    )
    predicted, spectra = call(
        functools.partial(field_kernel, (cells_x, cells_y, modes_z)),
        (like(tile, depth), like(*fields.shape)),
        [pltpu.VMEM((3, depth, 2 * tile), NARROW)],
        1_000_000_000,
        2_000_000,
    )(
        fields,
        phase_next.reshape(tile, depth),
        solute_next.reshape(tile, depth),
        cotangent.reshape(tile, depth),
        vectors,
        table["z_back"],
        table["z_forth"],
    )
    spectra = exchange(spectra)
    chunk = 2 * own_x * own_y * WIDTH // LANES + 8
    gradients = call(
        functools.partial(gradient_kernel, shape),
        like(devices * chunk, LANES),
        [
            pltpu.VMEM((2 * modes_x * (total_y // SPREAD), LANES), real),
            pltpu.VMEM((2 * total_y, LANES), real),
        ],
        100_000_000,
        2_000_000,
    )(spectra, modes, table["x_forth"], table["y_forth"])
    gradients = exchange(gradients)
    planes = 1
    grad_spectral, grad_local, grad_proj = call(
        functools.partial(outer_kernel, 1.0 / math.sqrt(total_x * total_y * depth), modes_x),
        (like(*spectral_weight.shape), like(WIDTH, WIDTH), like(1, WIDTH)),
        [pltpu.VMEM((8 * WIDTH, width), NARROW)],
        4 * own_x * own_y * modes_z * width * 8 * WIDTH,
        8 * own_x * own_y * modes_z * width,
        grid=(own_x // planes,),
        in_specs=[
            pl.BlockSpec(gradients.shape, lambda i: (0, 0)),
            pl.BlockSpec((2, width), lambda i: (0, 0)),
        ],
        out_specs=(
            pl.BlockSpec((2, planes, own_y, modes_z, width), lambda i: (0, i, 0, 0, 0)),
            pl.BlockSpec((WIDTH, WIDTH), lambda i: (0, 0)),
            pl.BlockSpec((1, WIDTH), lambda i: (0, 0)),
        ),
    )(gradients, jnp.tile(lift_weight.T, (1, WIDTH)))
    return (
        phase_next,
        solute_next,
        predicted.reshape(phase.shape),
        grad_spectral,
        grad_local,
        grad_proj.reshape(WIDTH),
    )


def per_device(*arguments):
    count_x, count_y = lax.axis_size("gx"), lax.axis_size("gy")
    if fits(count_x, count_y, arguments[0], arguments[4]):
        return per_device_fast(*arguments)
    return per_device_plain(*arguments)


def solution(mesh):
    return jax.shard_map(
        per_device,
        mesh=mesh,
        in_specs=(
            P("gx", "gy", None),
            P("gx", "gy", None),
            P("gx", "gy", None),
            P(),
            P(None, "gx", "gy", None, None),
            P(),
            P(),
            P(),
            P("gx", "gy", None),
        ),
        out_specs=(
            P("gx", "gy", None),
            P("gx", "gy", None),
            P("gx", "gy", None),
            P(None, "gx", "gy", None, None),
            P(),
            P(),
        ),
        check_vma=False,
    )
```

```python
import functools
from functools import reduce
import math

import jax
import jax.numpy as jnp
import ml_dtypes
import numpy as np
from jax import lax
from jax.experimental import pallas as pl
from jax.experimental.pallas import tpu as pltpu
from jax.sharding import PartitionSpec as P

WIDTH = 32
KX = 32
KY = 32
KZ = 32


TIME_STEP = 0.05
COUPLING = 2.0
SOLID_DIFF = 0.05
LIQUID_DIFF = 1.0
PARTITION = 0.15
TRAP_RATE = 4.0
SOLUTE_MEAN = 0.5


def extended(cells, sides, width):
    for axis, dim in sides:
        count = lax.axis_size(axis)
        head = lax.slice_in_dim(cells, 0, width, axis=dim)
        tail = lax.slice_in_dim(cells, cells.shape[dim] - width, cells.shape[dim], axis=dim)
        cells = jnp.concatenate(
            [
                lax.ppermute(tail, axis, [(i, (i + 1) % count) for i in range(count)]),
                cells,
                lax.ppermute(head, axis, [((i + 1) % count, i) for i in range(count)]),
            ],
            axis=dim,
        )
    return cells


def diffusivity(phase_now):
    return SOLID_DIFF + (LIQUID_DIFF - SOLID_DIFF) * 0.5 * (1.0 - jnp.tanh(phase_now))


def update(phase_now, solute_now, undercool, phase_nb, solute_nb, diff_now, diff_nb):
    lap = reduce(jnp.add, phase_nb) - 6.0 * phase_now
    squares = 1.0 - phase_now * phase_now
    rate = (
        lap
        + phase_now
        - phase_now * phase_now * phase_now
        + COUPLING * squares * squares * (undercool - solute_now)
    )
    fluxes = [
        0.5 * (diff_now + diff_nb[index]) * (solute_nb[index] - solute_now) for index in range(6)
    ]
    divergence = reduce(jnp.add, fluxes)
    speed = TRAP_RATE * jnp.abs(rate)
    keff = (PARTITION + speed) / (1.0 + speed)
    phase_new = phase_now + TIME_STEP * rate
    solute_new = solute_now + TIME_STEP * (divergence + 0.5 * (1.0 - keff) * solute_now * rate)
    return (phase_new, solute_new)


def beside(padded):
    centre = padded[1:-1, 1:-1]
    return [
        padded[2:, 1:-1],
        padded[:-2, 1:-1],
        padded[1:-1, 2:],
        padded[1:-1, :-2],
        jnp.roll(centre, -1, 2),
        jnp.roll(centre, 1, 2),
    ]


def phase_sweep(phase_now, solute_now, undercool):
    padded = extended(jnp.stack([phase_now, solute_now]), (("gx", 1), ("gy", 2)), 1)
    phase_pad = padded[0]
    solute_pad = padded[1]
    diff_pad = diffusivity(phase_pad)
    return update(
        phase_now,
        solute_now,
        undercool,
        beside(phase_pad),
        beside(solute_pad),
        diff_pad[1:-1, 1:-1],
        beside(diff_pad),
    )


def signed_freq(indices, total):
    return jnp.where(indices < total // 2, indices, indices - total)


def wave_tables(freqs, positions, length, factor):
    product = freqs[:, None] * positions[None, :] % length
    angles = product.astype(jnp.float32) * (2.0 * math.pi / length)
    return (jnp.cos(angles) * factor, jnp.sin(angles) * factor)


def complex_mix(cosines, sines, data, pattern, orient):

    def apply(table, values):
        return jnp.einsum(pattern, table, values, precision=lax.Precision.HIGHEST)

    cos_real = apply(cosines, data[0])
    cos_imag = apply(cosines, data[1])
    sin_real = apply(sines, data[0])
    sin_imag = apply(sines, data[1])
    return jnp.stack([cos_real - orient * sin_imag, cos_imag + orient * sin_real])


def x_forward(data, factor):
    portion = lax.all_to_all(data, "gx", split_axis=1, concat_axis=2, tiled=True)
    length = portion.shape[2]
    cosines, sines = wave_tables(
        signed_freq(jnp.arange(KX, dtype=jnp.int32), KX),
        jnp.arange(length, dtype=jnp.int32),
        length,
        factor,
    )
    lines = complex_mix(cosines, sines, portion, "kx,wxyz->wkyz", -1.0)
    return lax.all_to_all(lines, "gx", split_axis=2, concat_axis=1, tiled=True)


def y_forward(data, factor):
    portion = lax.all_to_all(data, "gy", split_axis=1, concat_axis=3, tiled=True)
    length = portion.shape[3]
    cosines, sines = wave_tables(
        signed_freq(jnp.arange(KY, dtype=jnp.int32), KY),
        jnp.arange(length, dtype=jnp.int32),
        length,
        factor,
    )
    lines = complex_mix(cosines, sines, portion, "ky,wayz->wakz", -1.0)
    return lax.all_to_all(lines, "gy", split_axis=3, concat_axis=1, tiled=True)


def contract(weights, values):
    return jnp.einsum("abzoi,iabz->oabz", weights, values, precision=lax.Precision.HIGHEST)


def outer(left, right):
    return jnp.einsum("oabz,iabz->abzoi", left, right, precision=lax.Precision.HIGHEST)


def per_device_plain(
    phase,
    solute,
    undercool,
    lift_weight,
    spectral_weight,
    local_weight,
    local_bias,
    proj_weight,
    cotangent,
):
    phase_mid, solute_mid = phase_sweep(phase, solute, undercool)
    phase_next, solute_next = phase_sweep(phase_mid, solute_mid, undercool)
    cells_x, cells_y, depth = phase.shape
    total_x = cells_x * lax.axis_size("gx")
    total_y = cells_y * lax.axis_size("gy")
    fields = jnp.stack([phase_next, solute_next - SOLUTE_MEAN])
    modes_z = jnp.arange(KZ, dtype=jnp.int32)
    zpos = jnp.arange(depth, dtype=jnp.int32)
    unit_z = jnp.ones((KZ,), jnp.float32)
    weights_z = jnp.where(modes_z == 0, 1.0, 2.0).astype(jnp.float32) / depth

    def z_forward(field, zfactor):
        cosines, sines = wave_tables(modes_z, zpos, depth, zfactor[:, None])
        tables = jnp.stack([cosines, -sines])
        return jnp.einsum("wxyz,rkz->rwxyk", field, tables, precision=lax.Precision.HIGHEST)

    def spectral_forward(field, zfactor, xfactor, yfactor):
        return y_forward(x_forward(z_forward(field, zfactor), xfactor), yfactor)

    lifted = jnp.einsum("wc,cxyz->wxyz", lift_weight, fields, precision=lax.Precision.HIGHEST)
    spectrum = spectral_forward(lifted, unit_z, 1.0, 1.0)
    own_x = spectrum.shape[2]
    own_y = spectrum.shape[3]
    shaped = spectral_weight.reshape(2, own_x, own_y, KZ, WIDTH, WIDTH)
    out_real = contract(shaped[0], spectrum[0]) - contract(shaped[1], spectrum[1])
    out_imag = contract(shaped[0], spectrum[1]) + contract(shaped[1], spectrum[0])
    spectral_out = jnp.stack([out_real, out_imag])
    ypos = lax.axis_index("gy") * cells_y + jnp.arange(cells_y, dtype=jnp.int32)
    portion = lax.all_gather(spectral_out, "gy", axis=3, tiled=True)
    freqs = signed_freq(jnp.arange(portion.shape[3], dtype=jnp.int32), KY)
    cosines, sines = wave_tables(ypos, freqs, total_y, 1.0 / total_y)
    back_y = complex_mix(cosines, sines, portion, "yk,wakz->wayz", 1.0)
    cosines, sines = wave_tables(
        jnp.arange(total_x, dtype=jnp.int32),
        signed_freq(jnp.arange(KX, dtype=jnp.int32), KX),
        total_x,
        1.0 / total_x,
    )
    inverted = complex_mix(
        cosines,
        sines,
        lax.all_to_all(back_y, "gx", split_axis=1, concat_axis=2, tiled=True),
        "xk,wkyz->wxyz",
        1.0,
    )
    back_x = lax.all_to_all(inverted, "gx", split_axis=2, concat_axis=1, tiled=True)
    cos_back, sin_back = wave_tables(modes_z, zpos, depth, weights_z[:, None])
    back_tables = jnp.stack([cos_back, -sin_back])
    spectral_field = jnp.einsum(
        "rwxyk,rkz->wxyz", back_x, back_tables, precision=lax.Precision.HIGHEST
    )
    mixed = jnp.dot(local_weight, lift_weight, precision=lax.Precision.HIGHEST)
    pre_act = (
        spectral_field
        + jnp.einsum("wc,cxyz->wxyz", mixed, fields, precision=lax.Precision.HIGHEST)
        + local_bias[:, None, None, None]
    )
    activated, gelu_back = jax.vjp(jax.nn.gelu, pre_act)
    predicted = jnp.einsum("w,wxyz->xyz", proj_weight, activated, precision=lax.Precision.HIGHEST)
    grad_pre = gelu_back(proj_weight[:, None, None, None] * cotangent[None])[0]
    field_sums = jnp.einsum("wxyz,cxyz->wc", grad_pre, fields, precision=lax.Precision.HIGHEST)
    proj_sums = jnp.einsum("wxyz,xyz->w", activated, cotangent, precision=lax.Precision.HIGHEST)
    field_sums, proj_sums = lax.psum((field_sums, proj_sums), ("gx", "gy"))
    grad_modes = spectral_forward(grad_pre, weights_z, 1.0 / total_x, 1.0 / total_y)
    grad_real = outer(grad_modes[0], spectrum[0]) + outer(grad_modes[1], spectrum[1])
    grad_imag = outer(grad_modes[1], spectrum[0]) - outer(grad_modes[0], spectrum[1])
    grad_spectral = jnp.stack([grad_real, grad_imag]).reshape(2, own_x, own_y, KZ, WIDTH * WIDTH)
    scale = 1.0 / math.sqrt(total_x * total_y * depth)
    grad_local = jnp.dot(field_sums, lift_weight.T, precision=lax.Precision.HIGHEST) * scale
    grad_proj = proj_sums * scale
    return (phase_next, solute_next, predicted, grad_spectral, grad_local, grad_proj)


LANES = 128
SMALL_VMEM = 24 * 1024 * 1024
LARGE_VMEM = 56 * 1024 * 1024
PACK_COST = 50_000_000_000
SPREAD = LANES // WIDTH
NARROW = jnp.bfloat16
EXACT = lax.Precision.HIGHEST


def halves(table):
    head = table.astype(np.float32).astype(ml_dtypes.bfloat16)
    rest = (table - head.astype(np.float64)).astype(np.float32).astype(ml_dtypes.bfloat16)
    return head, rest


def left_table(table):
    head, rest = halves(table)
    return np.concatenate([head, head, rest], axis=1)


def right_table(table):
    head, rest = halves(table)
    return np.concatenate([head, head, rest], axis=0)


def parts_of(values):
    head = values.astype(NARROW)
    return head, (values - head.astype(jnp.float32)).astype(NARROW)


def thrice(values, axis):
    head, rest = parts_of(values)
    return jnp.concatenate([head, rest, head], axis=axis)


def one_where(mask):
    return mask.astype(jnp.float32).astype(NARROW)


def mul(left, right):
    return jnp.dot(left, right, preferred_element_type=jnp.float32)


def mul_rows(left, right):
    return lax.dot_general(
        left, right, (((1,), (1,)), ((), ())), preferred_element_type=jnp.float32
    )


def angles(freqs, positions, length):
    return 2.0 * np.pi * ((freqs[:, None] * positions[None, :]) % length) / length


def signed(count):
    index = np.arange(count)
    return np.where(index < count // 2, index, index - count)


def rotation(theta, orient):
    cosines, sines = np.cos(theta), orient * np.sin(theta)
    return np.block([[cosines, -sines], [sines, cosines]])


def group_of(shape):
    return lax.broadcasted_iota(jnp.int32, shape, len(shape) - 1) // WIDTH


def pick(groups, choices):
    result = choices[-1]
    for index in range(len(choices) - 2, -1, -1):
        result = jnp.where(groups == index, choices[index], result)
    return result


def turn(values, shift):
    shift = shift % LANES
    return values if shift == 0 else pltpu.roll(values, shift, 1)


def swap_groups(pieces):
    groups = group_of(pieces[0].shape)
    return [
        pick(groups, [turn(pieces[i], WIDTH * (i - j)) for i in range(SPREAD)])
        for j in range(SPREAD)
    ]


def contract_kernel(planes, lift_ref, weight_ref, out_ref, held, arrived):
    _, own_x, own_y, modes_z, width = weight_ref.shape
    chunk = out_ref.shape[0] // modes_z
    steps = own_x // planes

    def fetch(step):
        block = pl.ds(step * planes, planes)
        return pltpu.make_async_copy(
            weight_ref.at[:, block], held.at[:, block], arrived.at[step]
        )

    for step in range(steps):
        fetch(step).start()
    square = (WIDTH, WIDTH)
    diagonal = lax.broadcasted_iota(jnp.int32, square, 0) == lax.broadcasted_iota(
        jnp.int32, square, 1
    )
    columns = [
        jnp.sum(
            jnp.where(diagonal, jnp.broadcast_to(lift_ref[k : k + 1, :], square), 0.0),
            axis=1,
            keepdims=True,
        )
        for k in range(2)
    ]
    lane = lax.broadcasted_iota(jnp.int32, (WIDTH, LANES), 1)
    base = jnp.where(
        lane % (2 * WIDTH) < WIDTH,
        jnp.broadcast_to(columns[0], lane.shape),
        jnp.broadcast_to(columns[1], lane.shape),
    )
    head, rest = parts_of(base)
    base = jnp.where(lane < 2 * WIDTH, head.astype(jnp.float32), rest.astype(jnp.float32))
    mixing = jnp.concatenate(
        [jnp.where(lane % WIDTH == channel, base, 0.0) for channel in range(WIDTH)], axis=0
    ).astype(NARROW)
    rows = planes * own_y * modes_z
    low = lax.broadcasted_iota(jnp.int32, (rows, LANES), 1) < 2 * WIDTH
    for step in range(steps):
        fetch(step).wait()
        sums = []
        for part in range(2):
            block = held[part, step * planes : (step + 1) * planes]
            head, rest = parts_of(block.reshape(rows, width))
            total = mul(head, mixing) + mul(rest, mixing)
            sums.append(total + turn(total, 2 * WIDTH))
        result = jnp.where(low, sums[0], sums[1])
        for plane in range(planes):
            for row in range(own_y):
                first = (plane * own_y + row) * modes_z
                place = row * own_x + step * planes + plane
                out_ref[pl.ds(place, modes_z, stride=chunk), :] = result[
                    first : first + modes_z
                ]


def pack_kernel(held_ref, before_ref, after_ref, head_ref, tail_ref):
    _, cells_x, cells_y, _ = held_ref.shape

    def put(target, phase, solute, cool):
        head_ref[target, 0:2] = phase[:, 0:2]
        head_ref[target, 2:4] = solute[:, 0:2]
        head_ref[target, 4:5] = cool[:, 0:1]
        tail_ref[target, 0:2] = phase[:, cells_y - 2 : cells_y]
        tail_ref[target, 2:4] = solute[:, cells_y - 2 : cells_y]
        tail_ref[target, 4:5] = cool[:, cells_y - 1 : cells_y]

    put(slice(0, 1), before_ref[1:2], before_ref[3:4], before_ref[4:5])
    put(slice(1, cells_x + 1), held_ref[0], held_ref[1], held_ref[2])
    put(slice(cells_x + 1, cells_x + 2), after_ref[0:1], after_ref[2:3], after_ref[4:5])


def step_kernel(
    held_ref,
    before_ref,
    after_ref,
    low_ref,
    high_ref,
    table_ref,
    mixed_ref,
    phase_out,
    solute_out,
    send_ref,
    phase_ext,
    solute_ext,
    cool_ext,
    diff_ext,
    lines,
):
    _, cells_x, cells_y, depth = held_ref.shape
    base = 8
    end = base + cells_y
    for index, ext in enumerate((phase_ext, solute_ext)):
        first = 2 * index
        ext[2 : cells_x + 2, base:end] = held_ref[index]
        ext[0:2, base:end] = before_ref[first : first + 2]
        ext[cells_x + 2 : cells_x + 4, base:end] = after_ref[first : first + 2]
        ext[1 : cells_x + 3, base - 2 : base] = low_ref[:, first : first + 2]
        ext[1 : cells_x + 3, end : end + 2] = high_ref[:, first : first + 2]
    cool_ext[2 : cells_x + 2, base:end] = held_ref[2]
    cool_ext[1:2, base:end] = before_ref[4:5]
    cool_ext[cells_x + 2 : cells_x + 3, base:end] = after_ref[4:5]
    cool_ext[1 : cells_x + 3, base - 1 : base] = low_ref[:, 4:5]
    cool_ext[1 : cells_x + 3, end : end + 1] = high_ref[:, 4:5]

    def sweep(reach):
        diff_ext[...] = diffusivity(phase_ext[...])

        def window(ext, move_x, move_y):
            return ext[
                2 - reach + move_x : cells_x + 2 + reach + move_x,
                base - reach + move_y : end + reach + move_y,
            ]

        def around(ext, now):
            return [
                window(ext, 1, 0),
                window(ext, -1, 0),
                window(ext, 0, 1),
                window(ext, 0, -1),
                pltpu.roll(now, depth - 1, 2),
                pltpu.roll(now, 1, 2),
            ]

        phase_now = window(phase_ext, 0, 0)
        solute_now = window(solute_ext, 0, 0)
        diff_now = window(diff_ext, 0, 0)
        return update(
            phase_now,
            solute_now,
            window(cool_ext, 0, 0),
            around(phase_ext, phase_now),
            around(solute_ext, solute_now),
            diff_now,
            around(diff_ext, diff_now),
        )

    phase_mid, solute_mid = sweep(1)
    phase_ext[1 : cells_x + 3, base - 1 : end + 1] = phase_mid
    solute_ext[1 : cells_x + 3, base - 1 : end + 1] = solute_mid
    phase_next, solute_next = sweep(0)
    phase_out[...] = phase_next
    solute_out[...] = solute_next
    tile = cells_x * cells_y
    both = (phase_next.reshape(tile, depth), solute_next.reshape(tile, depth) - SOLUTE_MEAN)
    ordered = []
    for part in range(depth // LANES):
        for index, values in enumerate(both):
            lines[part, index * tile : (index + 1) * tile] = values[
                :, part * LANES : (part + 1) * LANES
            ]
        ordered.append(
            jnp.concatenate(
                [
                    lines[part, pl.ds(row, 2 * cells_x, stride=cells_y), :]
                    for row in range(cells_y)
                ],
                axis=0,
            )
        )
    ordered = jnp.concatenate(ordered, axis=1)
    spectra = mul_rows(table_ref[...], thrice(ordered, 1))
    send_ref[...] = mixed_ref[...]
    modes_z = spectra.shape[0] // 2
    chunk = send_ref.shape[0] // modes_z
    for part in range(2):
        send_ref[pl.ds(chunk - 2 + part, modes_z, stride=chunk), :] = spectra[
            part * modes_z : (part + 1) * modes_z
        ]


def pack_modes(shape, modes, modes_ref, rows_ref):
    count_x, count_y, _, _, own_x, own_y = shape
    modes_x, modes_y = count_x * own_x, count_y * own_y
    lane = lax.broadcasted_iota(jnp.int32, (modes_y, LANES), 1)
    for index in range(count_x):
        block = modes
        for k in range(4):
            shift = k * own_x - k * modes_x - index * own_x
            block = jnp.where(lane // own_x == k, turn(modes, shift), block)
        rows_ref[index] = block
        line = rows_ref[index, pl.ds(0, count_y, stride=own_y), :]
        groups = group_of(line.shape)
        for row in range(1, own_y):
            piece = rows_ref[index, pl.ds(row, count_y, stride=own_y), :]
            line = jnp.where(groups == row, turn(piece, row * WIDTH), line)
        modes_ref[index * count_y : (index + 1) * count_y] = line


def spectral_kernel(
    shape,
    mixed_ref,
    y_in_ref,
    x_in_ref,
    y_out_ref,
    x_out_ref,
    modes_ref,
    send_ref,
    lines_y,
    lines_x,
    rows_ref,
    weight_ref,
):
    count_x, count_y, cells_x, cells_y, own_x, own_y = shape
    modes_x, modes_y = count_x * own_x, count_y * own_y
    total_x, total_y = count_x * cells_x, count_y * cells_y
    tile = cells_x * cells_y
    narrow = 2 * cells_x
    rows = 2 * count_y
    devices = count_x * count_y
    own = own_x * own_y
    chunk = mixed_ref.shape[0] // devices
    spectra = [mixed_ref[pl.ds(own + part, devices, stride=chunk), :] for part in range(2)]
    for index in range(devices):
        weight_ref[index * own : (index + 1) * own, :] = mixed_ref[
            index * chunk : index * chunk + own, :
        ]
    lane = lax.broadcasted_iota(jnp.int32, (rows, LANES), 1)
    blocks = []
    for row in range(cells_y):
        block = jnp.zeros((rows, LANES), jnp.float32)
        for index in range(count_x):
            piece = jnp.concatenate(
                [values[index * count_y : (index + 1) * count_y] for values in spectra], axis=0
            )
            piece = turn(piece, narrow * (index - row))
            block = jnp.where(lane // narrow == index, piece, block)
        blocks.append(block)
    along_y = mul(y_in_ref[...], thrice(jnp.concatenate(blocks, axis=0), 0))
    half = lax.broadcasted_iota(jnp.int32, (modes_y, LANES), 1) < LANES // 2
    joined = jnp.where(half, along_y[0:modes_y], turn(along_y[modes_y:], LANES // 2))
    modes = mul(thrice(joined, 1), x_in_ref[...])
    quads_y = total_y // SPREAD
    quads_x = modes_x // SPREAD
    lane = lax.broadcasted_iota(jnp.int32, (modes_y, LANES), 1) % modes_x
    chosen = jnp.concatenate(
        [jnp.where(lane == freq, modes, 0.0) for freq in range(modes_x)], axis=0
    )
    place = lax.broadcasted_iota(jnp.int32, (2 * LANES, 2 * LANES), 0) % LANES // modes_x
    group = lax.broadcasted_iota(jnp.int32, (2 * LANES, 2 * LANES), 1) // WIDTH
    same = jnp.where(group < 4, group, (group + 2) % 4)
    signed_one = jnp.where((group == 2) | (group == 3), -1.0, 1.0)
    spread = jnp.where(place == same, signed_one, 0.0).astype(NARROW)
    columns = mul(jnp.concatenate(parts_of(chosen), axis=1), spread)
    products = [[], []]
    for quad in range(quads_x):
        lines = [[], []]
        for index in range(SPREAD):
            freq = SPREAD * quad + index
            start = (freq // own_x) * count_y * own_y * own_x + freq % own_x
            weights = weight_ref[pl.ds(start, modes_y, stride=own_x), :]
            for part in range(2):
                column = columns[
                    freq * modes_y : (freq + 1) * modes_y, part * LANES : (part + 1) * LANES
                ]
                lines[part].append(weights * column)
        for part in range(2):
            products[part].append(jnp.concatenate(lines[part], axis=1))
    products = jnp.concatenate(products[0] + products[1], axis=0)
    gather = lax.broadcasted_iota(jnp.int32, (2 * SPREAD * LANES, LANES), 0) % (SPREAD * LANES)
    column = lax.broadcasted_iota(jnp.int32, (2 * SPREAD * LANES, LANES), 1)
    gather = one_where(gather // LANES * WIDTH + gather % WIDTH == column)
    products = mul(jnp.concatenate(parts_of(products), axis=1), gather)
    stacked = [
        jnp.concatenate(
            [
                products[(part * quads_x + quad) * modes_y : (part * quads_x + quad + 1) * modes_y]
                for part in range(2)
            ],
            axis=0,
        )
        for quad in range(quads_x)
    ]
    back = mul(y_out_ref[...], thrice(jnp.concatenate(stacked, axis=1), 0))
    for quad in range(quads_x):
        lines_y[quad] = back[:, quad * LANES : (quad + 1) * LANES]
    for quad in range(quads_x):
        for part in range(2):
            pieces = [
                lines_y[quad, pl.ds(part * total_y + i, quads_y, stride=SPREAD), :]
                for i in range(SPREAD)
            ]
            for index, piece in enumerate(swap_groups(pieces)):
                place = part * modes_x + SPREAD * quad + index
                lines_x[pl.ds(place, quads_y, stride=2 * modes_x), :] = piece
    per_tile = cells_y // SPREAD
    blocks = [
        lines_x[quad * 2 * modes_x : (quad + 1) * 2 * modes_x, :] for quad in range(quads_y)
    ]
    back = mul(x_out_ref[...], thrice(jnp.concatenate(blocks, axis=1), 0))
    for quad in range(quads_y):
        for part in range(2):
            for index in range(count_x):
                device = index * count_y + quad // per_tile
                place = (device * 2 + part) * per_tile + quad % per_tile
                first = part * total_x + index * cells_x
                send_ref[place * cells_x : (place + 1) * cells_x, :] = back[
                    first : first + cells_x, quad * LANES : (quad + 1) * LANES
                ]
    pack_modes(shape, modes, modes_ref, rows_ref)


def prepare_kernel(
    phase_ref, solute_ref, cotangent_ref, vector_ref, base_ref, spread_ref, table_ref
):
    planes, depth, wide = base_ref.shape
    tile = phase_ref.shape[0]
    cells_y = tile // planes
    fields = (phase_ref[...], solute_ref[...] - SOLUTE_MEAN)
    spread = jnp.concatenate(
        [jnp.concatenate(parts_of(values.T), axis=1) for values in fields], axis=0
    )
    spread_ref[...] = jnp.concatenate(parts_of(cotangent_ref[...].T), axis=1)
    cell = lax.broadcasted_iota(jnp.int32, (2 * tile, wide), 0) % tile
    row = lax.broadcasted_iota(jnp.int32, (2 * tile, wide), 1) // WIDTH
    for plane in range(planes):
        values = mul(spread, one_where(cell == plane * cells_y + row))
        base_ref[plane] = (
            values[0:depth] * vector_ref[0:1, :]
            + values[depth:] * vector_ref[1:2, :]
            + vector_ref[2:3, :]
        )
        lines = [values[plane * cells_y : (plane + 1) * cells_y] for values in fields]
        head, rest = parts_of(jnp.concatenate(lines, axis=0))
        table_ref[plane] = jnp.concatenate([head, head, rest], axis=1)


def field_kernel(
    cells_y,
    field_ref,
    base_ref,
    spread_ref,
    table_ref,
    vector_ref,
    back_ref,
    forth_ref,
    predicted_ref,
    send_ref,
):
    planes, depth, wide = base_ref.shape
    rows = back_ref.shape[1] // 3
    halves_y = cells_y // SPREAD
    stride = halves_y * planes
    proj = vector_ref[3:4, :]
    root = math.sqrt(2.0 / math.pi)
    curve = 0.044715
    picker = one_where(
        lax.broadcasted_iota(jnp.int32, (cells_y, 2 * wide), 0)
        == lax.broadcasted_iota(jnp.int32, (cells_y, 2 * wide), 1) % wide // WIDTH
    )
    cell = lax.broadcasted_iota(jnp.int32, (2 * planes * cells_y, wide), 0) % (planes * cells_y)
    cell = cell - lax.broadcasted_iota(jnp.int32, cell.shape, 1) // WIDTH
    line_sums = jnp.zeros((2 * cells_y, wide), jnp.float32)
    proj_sums = jnp.zeros((8, wide), jnp.float32)
    for plane in range(planes):
        spectra = jnp.concatenate(
            [
                field_ref[pl.ds(part * planes + plane, rows, stride=stride), :]
                for part in range(halves_y)
            ],
            axis=1,
        )
        pre = mul(back_ref[...], thrice(spectra, 0)) + base_ref[plane]
        square = pre * pre
        bent = jnp.tanh(pre * (root + (root * curve) * square))
        upper = 0.5 + 0.5 * bent
        active = pre * upper
        slope = upper + (active - active * bent) * (root + (3.0 * root * curve) * square)
        cotangent = mul(spread_ref[...], one_where(cell == plane * cells_y))
        weighted = proj * cotangent
        grad = weighted * slope
        predicted_ref[plane * cells_y : (plane + 1) * cells_y, :] = mul_rows(
            picker, jnp.concatenate(parts_of(proj * active), axis=1)
        )
        table = jnp.concatenate([forth_ref[...], table_ref[plane]], axis=0)
        spectra = mul(table, thrice(grad, 0))
        for part in range(halves_y):
            send_ref[pl.ds(part * planes + plane, rows, stride=stride), :] = spectra[
                0:rows, part * LANES : (part + 1) * LANES
            ]
        line_sums = line_sums + spectra[rows:]
        proj_sums = proj_sums + jnp.sum(
            (active * cotangent).reshape(depth // 8, 8, wide), axis=0
        )
    shape = (cells_y, wide)
    own = lax.broadcasted_iota(jnp.int32, shape, 0) == (
        lax.broadcasted_iota(jnp.int32, shape, 1) // WIDTH
    )
    sums = [
        jnp.where(own, line_sums[0:cells_y], 0.0),
        jnp.where(own, line_sums[cells_y:], 0.0),
        proj_sums,
    ]
    for index, values in enumerate(sums):
        line = jnp.sum(values, axis=0, keepdims=True)
        line = sum(line[:, part * LANES : (part + 1) * LANES] for part in range(halves_y))
        send_ref[stride + index : stride + index + 1, :] = line


def gradient_kernel(
    shape, spectra_ref, modes_ref, x_in_ref, y_in_ref, send_ref, lines_x, lines_y
):
    count_x, count_y, cells_x, cells_y, own_x, own_y = shape
    modes_x, modes_y = count_x * own_x, count_y * own_y
    total_x, total_y = count_x * cells_x, count_y * cells_y
    per_tile = cells_y // SPREAD
    quads_y = total_y // SPREAD
    chunk = 2 * per_tile * cells_x
    first_device = (lax.axis_index("gx") == 0) & (lax.axis_index("gy") == 0)
    keep = jnp.where(first_device, 0.0, 1.0)
    blocks = []
    for quad in range(quads_y):
        block = []
        for part in range(2):
            for index in range(count_x):
                device = index * count_y + quad // per_tile
                place = (device * 2 + part) * per_tile + quad % per_tile
                piece = spectra_ref[place * cells_x : (place + 1) * cells_x, :]
                block.append(piece * keep if part else piece)
        blocks.append(jnp.concatenate(block, axis=0))
    forth = mul(x_in_ref[...], thrice(jnp.concatenate(blocks, axis=1), 0))
    for quad in range(quads_y):
        lines_x[quad * 2 * modes_x : (quad + 1) * 2 * modes_x, :] = forth[
            :, quad * LANES : (quad + 1) * LANES
        ]
    devices = count_x * count_y
    out_chunk = send_ref.shape[0] // devices
    per_own = own_x // SPREAD
    quads_x = modes_x // SPREAD
    for quad in range(quads_x):
        for part in range(2):
            pieces = [
                lines_x[
                    pl.ds(part * modes_x + SPREAD * quad + j, quads_y, stride=2 * modes_x), :
                ]
                for j in range(SPREAD)
            ]
            for index, piece in enumerate(swap_groups(pieces)):
                lines_y[quad, pl.ds(part * total_y + index, quads_y, stride=SPREAD), :] = piece
    lines = jnp.concatenate([lines_y[quad] for quad in range(quads_x)], axis=1)
    modes = mul(y_in_ref[...], thrice(lines, 0))
    for quad in range(quads_x):
        for part in range(2):
            for index in range(count_y):
                device = (quad // per_own) * count_y + index
                place = device * out_chunk + (part * per_own + quad % per_own) * own_y
                first = part * modes_y + index * own_y
                send_ref[place : place + own_y, :] = modes[
                    first : first + own_y, quad * LANES : (quad + 1) * LANES
                ]
    extra = 2 * per_own * own_y
    send_ref[pl.ds(extra, devices, stride=out_chunk), :] = modes_ref[...]
    groups = group_of((1, LANES))
    total = jnp.zeros((1, LANES), jnp.float32)
    for index in range(3):
        start = chunk // 2 + index
        line = jnp.sum(
            spectra_ref[pl.ds(start, devices, stride=chunk), :], axis=0, keepdims=True
        )
        line = line + turn(line, 2 * WIDTH)
        total = jnp.where(groups == index, line + turn(line, WIDTH), total)
    send_ref[pl.ds(extra + 1, devices, stride=out_chunk), :] = jnp.broadcast_to(
        total, (devices, LANES)
    )


def outer_kernel(scale, modes_ref, lift_ref, local_ref, proj_ref, grad_ref, mix_ref, held, sent):
    _, own_x, own_y, modes_z, width = held.shape
    chunk = modes_ref.shape[0] // modes_z
    per_own = own_x // SPREAD
    extra = 2 * per_own * own_y
    shape = (2 * WIDTH, width)
    row = lax.broadcasted_iota(jnp.int32, shape, 0)
    column = lax.broadcasted_iota(jnp.int32, shape, 1)
    lift = jnp.where(row < WIDTH, lift_ref[0:1, :], lift_ref[1:2, :])
    head, rest = parts_of(jnp.where(column // WIDTH == row % WIDTH, lift, 0.0))
    mix_ref[0 : 2 * WIDTH] = head
    mix_ref[2 * WIDTH : 4 * WIDTH] = head
    mix_ref[4 * WIDTH : 6 * WIDTH] = rest
    mix_ref[6 * WIDTH : 8 * WIDTH] = jnp.zeros_like(rest)
    lane = lax.broadcasted_iota(jnp.int32, (modes_z, LANES), 1)
    low = lane < 2 * WIDTH

    def rows_of(values):
        head, rest = parts_of(values)
        both = jnp.where(low, head.astype(jnp.float32), rest.astype(jnp.float32)).astype(NARROW)
        return jnp.concatenate([both, head], axis=1)

    grads = jnp.concatenate(
        [modes_ref[pl.ds(place, modes_z, stride=chunk), :] for place in range(extra)], axis=0
    )
    repeat = lax.broadcasted_iota(jnp.int32, (2 * LANES, SPREAD * LANES), 0) % LANES
    column = lax.broadcasted_iota(jnp.int32, (2 * LANES, SPREAD * LANES), 1)
    repeat = one_where(repeat == column // LANES * WIDTH + column % WIDTH)
    grads = mul(jnp.concatenate(parts_of(grads), axis=1), repeat)
    modes = modes_ref[pl.ds(extra, modes_z, stride=chunk), :]
    place = lax.broadcasted_iota(jnp.int32, (2 * LANES, 2 * LANES), 0) % LANES // own_x % 4
    column = lax.broadcasted_iota(jnp.int32, (2 * LANES, 2 * LANES), 1) // WIDTH
    spread = one_where(place == column // 4 * 2 + column % 2)
    own = lane // (4 * own_x) * own_x + lane % own_x
    copies = []
    for plane in range(own_x):
        chosen = jnp.concatenate(
            [jnp.where(own == row * own_x + plane, modes, 0.0) for row in range(own_y)], axis=0
        )
        columns = mul(jnp.concatenate(parts_of(chosen), axis=1), spread)
        reals, imags = [], []
        for row in range(own_y):
            real = columns[row * modes_z : (row + 1) * modes_z, 0:LANES]
            imag = columns[row * modes_z : (row + 1) * modes_z, LANES:]
            pair = []
            for part in range(2):
                first = ((part * per_own + plane // SPREAD) * own_y + row) * modes_z
                group = plane % SPREAD * LANES
                pair.append(grads[first : first + modes_z, group : group + LANES])
            reals.append(rows_of(pair[0] * real + pair[1] * imag))
            imags.append(rows_of(pair[1] * real - pair[0] * imag))
        result = mul(jnp.concatenate(reals + imags, axis=0), mix_ref[...])
        held[:, plane] = result.reshape(2, own_y, modes_z, width)
        copies.append(
            pltpu.make_async_copy(held.at[:, plane], grad_ref.at[:, plane], sent.at[plane])
        )
        copies[-1].start()
    line = modes_ref[extra + 1 : extra + 2, :]
    square = (WIDTH, WIDTH)
    diagonal = lax.broadcasted_iota(jnp.int32, square, 0) == lax.broadcasted_iota(
        jnp.int32, square, 1
    )
    local = jnp.zeros(square, jnp.float32)
    for k in range(2):
        sums = jnp.broadcast_to(line[:, k * WIDTH : (k + 1) * WIDTH], square)
        sums = jnp.sum(jnp.where(diagonal, sums, 0.0), axis=1, keepdims=True)
        local = local + sums * lift_ref[k : k + 1, 0:WIDTH]
    local_ref[...] = scale * local
    proj_ref[...] = scale * line[:, 2 * WIDTH : 3 * WIDTH]
    for copy in copies:
        copy.wait()


def tables(shape, depth, modes_z):
    count_x, count_y, cells_x, cells_y, own_x, own_y = shape
    modes_x, modes_y = count_x * own_x, count_y * own_y
    total_x, total_y = count_x * cells_x, count_y * cells_y
    theta_z = angles(np.arange(modes_z), np.arange(depth), depth)
    theta_x = angles(signed(modes_x), np.arange(total_x), total_x)
    theta_y = angles(signed(modes_y), np.arange(total_y), total_y)
    plain_z = np.concatenate([np.cos(theta_z), -np.sin(theta_z)], axis=0)
    forth_z = plain_z.reshape(2, modes_z, depth).transpose(1, 0, 2).reshape(2 * modes_z, depth)
    weight = np.where(np.arange(modes_z) == 0, 1.0, 2.0) / (total_x * total_y * depth)
    weighted_z = np.repeat(weight, 2)[:, None] * forth_z
    forth_x, back_x = rotation(theta_x, -1.0), rotation(theta_x.T, 1.0)
    forth_y, back_y = rotation(theta_y, -1.0), rotation(theta_y.T, 1.0)
    order_y = forth_y.reshape(2 * modes_y, 2, count_y, cells_y)
    order_y = order_y.transpose(0, 3, 1, 2).reshape(2 * modes_y, 2 * total_y)
    lines = forth_x.reshape(2, modes_x, 2, count_x, cells_x)
    both = np.zeros((2, count_x, 2, cells_x, 2, 2, modes_x))
    for field in range(2):
        both[:, :, field, :, :, field, :] = lines.transpose(2, 3, 4, 0, 1)
    both = both.reshape(4 * total_x, 4 * modes_x)
    return {
        "z_plain": left_table(plain_z),
        "z_forth": left_table(weighted_z),
        "z_back": left_table(weighted_z.T),
        "y_first": left_table(order_y),
        "x_first": right_table(both),
        "y_back": left_table(back_y),
        "x_back": left_table(back_x),
        "x_forth": left_table(forth_x),
        "y_forth": left_table(forth_y),
    }


def fits(count_x, count_y, phase, spectral_weight):
    cells_x, cells_y, depth = phase.shape
    _, own_x, own_y, modes_z, width = spectral_weight.shape
    return (
        width == WIDTH * WIDTH
        and modes_z == count_x * count_y
        and 4 * count_x * cells_x == LANES
        and 4 * count_x * own_x == LANES
        and 2 * cells_x * cells_y == LANES
        and cells_x == 8
        and cells_y % SPREAD == 0
        and own_x % SPREAD == 0
        and own_y * 4 * own_x == LANES
        and 3 * WIDTH <= LANES
        and cells_y == 8
        and depth % LANES == 0
    )


def call(kernel, outs, scratch, flops, moved, limit=SMALL_VMEM, **more):
    return pl.pallas_call(
        kernel,
        out_shape=outs,
        scratch_shapes=scratch,
        compiler_params=pltpu.CompilerParams(vmem_limit_bytes=limit),
        cost_estimate=pl.CostEstimate(flops=flops, bytes_accessed=moved, transcendentals=0),
        **more,
    )


def exchange(values):
    return lax.all_to_all(values, ("gx", "gy"), split_axis=0, concat_axis=0, tiled=True)


def per_device_fast(
    phase,
    solute,
    undercool,
    lift_weight,
    spectral_weight,
    local_weight,
    local_bias,
    proj_weight,
    cotangent,
):
    count_x, count_y = lax.axis_size("gx"), lax.axis_size("gy")
    cells_x, cells_y, depth = phase.shape
    _, own_x, own_y, modes_z, width = spectral_weight.shape
    shape = (count_x, count_y, cells_x, cells_y, own_x, own_y)
    devices = count_x * count_y
    tile = cells_x * cells_y
    modes_x, modes_y = count_x * own_x, count_y * own_y
    total_x, total_y = count_x * cells_x, count_y * cells_y
    table = tables(shape, depth, modes_z)
    real = jnp.float32

    def like(*dims):
        return jax.ShapeDtypeStruct(dims, real)

    far = pl.BlockSpec(memory_space=pltpu.HBM)
    near = pl.BlockSpec(memory_space=pltpu.VMEM)
    weight_bytes = 8 * own_x * own_y * modes_z * width
    head = jnp.concatenate([phase[:2], solute[:2], undercool[:1]])
    tail = jnp.concatenate([phase[-2:], solute[-2:], undercool[-1:]])
    held = jnp.stack([phase, solute, undercool])

    def ring(values, axis, step):
        count = lax.axis_size(axis)
        return lax.ppermute(values, axis, [(i, (i + step) % count) for i in range(count)])

    head, tail, lift = lax.optimization_barrier((head, tail, lift_weight.T))
    before, after = ring(tail, "gx", 1), ring(head, "gx", -1)
    planes = 2
    mixed_weights = call(
        functools.partial(contract_kernel, planes),
        like(modes_z * (own_x * own_y + 2), LANES),
        [
            pltpu.VMEM(spectral_weight.shape, real),
            pltpu.SemaphoreType.DMA((own_x // planes,)),
        ],
        weight_bytes * LANES,
        weight_bytes,
        limit=LARGE_VMEM,
        in_specs=[near, far],
    )(lift, spectral_weight)
    head, tail = call(
        pack_kernel,
        (like(cells_x + 2, 8, depth), like(cells_x + 2, 8, depth)),
        [],
        PACK_COST,
        40 * tile * depth,
    )(held, before, after)
    low, high = ring(tail, "gy", 1), ring(head, "gy", -1)
    extended_shape = pltpu.VMEM((cells_x + 4, cells_y + 16, depth), real)
    phase_next, solute_next, spectra = call(
        step_kernel,
        (like(*phase.shape), like(*phase.shape), like(*mixed_weights.shape)),
        [extended_shape] * 4 + [pltpu.VMEM((depth // LANES, 2 * tile, LANES), real)],
        400 * tile * depth,
        80 * tile * depth,
    )(held, before, after, low, high, table["z_plain"], mixed_weights)
    gathered = exchange(spectra.reshape(-1, 2, LANES)).reshape(spectra.shape)
    modes, fields = call(
        functools.partial(spectral_kernel, shape),
        (like(devices, LANES), like(devices * 2 * cells_x * (cells_y // SPREAD), LANES)),
        [
            pltpu.VMEM((modes_x // SPREAD, 2 * total_y, LANES), real),
            pltpu.VMEM((2 * modes_x * (total_y // SPREAD), LANES), real),
            pltpu.VMEM((count_x, modes_y, LANES), real),
            pltpu.VMEM((devices * own_x * own_y, LANES), real),
        ],
        100_000_000,
        2_000_000,
    )(
        gathered,
        table["y_first"],
        table["x_first"],
        table["y_back"],
        table["x_back"],
    )
    fields = exchange(fields)
    mixed = jnp.dot(local_weight, lift_weight, precision=EXACT)
    vectors = jnp.tile(
        jnp.stack([mixed[:, 0], mixed[:, 1], local_bias, proj_weight]), (1, cells_y)
    )
    spread_shape = (cells_x, depth, cells_y * WIDTH)
    base, spread, lines = call(
        prepare_kernel,
        (
            like(*spread_shape),
            jax.ShapeDtypeStruct((depth, 2 * tile), NARROW),
            jax.ShapeDtypeStruct((cells_x, 2 * cells_y, 3 * depth), NARROW),
        ),
        [],
        100_000_000,
        5_000_000,
    )(
        phase_next.reshape(tile, depth),
        solute_next.reshape(tile, depth),
        cotangent.reshape(tile, depth),
        vectors,
    )
    predicted, spectra = call(
        functools.partial(field_kernel, cells_y),
        (like(tile, depth), like(*fields.shape)),
        [],
        1_000_000_000,
        2_000_000,
    )(fields, base, spread, lines, vectors, table["z_back"], table["z_forth"])
    spectra = exchange(spectra)
    chunk = 2 * own_x * own_y * WIDTH // LANES + 2
    gradients = call(
        functools.partial(gradient_kernel, shape),
        like(devices * chunk, LANES),
        [
            pltpu.VMEM((2 * modes_x * (total_y // SPREAD), LANES), real),
            pltpu.VMEM((modes_x // SPREAD, 2 * total_y, LANES), real),
        ],
        100_000_000,
        2_000_000,
    )(spectra, modes, table["x_forth"], table["y_forth"])
    gradients = exchange(gradients.reshape(-1, 2, LANES)).reshape(gradients.shape)
    grad_local, grad_proj, grad_spectral = call(
        functools.partial(outer_kernel, 1.0 / math.sqrt(total_x * total_y * depth)),
        (like(WIDTH, WIDTH), like(1, WIDTH), like(*spectral_weight.shape)),
        [
            pltpu.VMEM((8 * WIDTH, width), NARROW),
            pltpu.VMEM(spectral_weight.shape, real),
            pltpu.SemaphoreType.DMA((own_x,)),
        ],
        weight_bytes * 4 * WIDTH,
        weight_bytes,
        limit=SMALL_VMEM,
        out_specs=(near, near, far),
    )(gradients, jnp.tile(lift_weight.T, (1, WIDTH)))
    return (
        phase_next,
        solute_next,
        predicted.reshape(phase.shape),
        grad_spectral,
        grad_local,
        grad_proj.reshape(WIDTH),
    )


def per_device(*arguments):
    count_x, count_y = lax.axis_size("gx"), lax.axis_size("gy")
    if fits(count_x, count_y, arguments[0], arguments[4]):
        return per_device_fast(*arguments)
    return per_device_plain(*arguments)


def solution(mesh):
    return jax.shard_map(
        per_device,
        mesh=mesh,
        in_specs=(
            P("gx", "gy", None),
            P("gx", "gy", None),
            P("gx", "gy", None),
            P(),
            P(None, "gx", "gy", None, None),
            P(),
            P(),
            P(),
            P("gx", "gy", None),
        ),
        out_specs=(
            P("gx", "gy", None),
            P("gx", "gy", None),
            P("gx", "gy", None),
            P(None, "gx", "gy", None, None),
            P(),
            P(),
        ),
        check_vma=False,
    )
```

```python
import functools
from functools import reduce
import math

import jax
import jax.numpy as jnp
import ml_dtypes
import numpy as np
from jax import lax
from jax.experimental import pallas as pl
from jax.experimental.pallas import tpu as pltpu
from jax.sharding import PartitionSpec as P

WIDTH = 32
KX = 32
KY = 32
KZ = 32


TIME_STEP = 0.05
COUPLING = 2.0
SOLID_DIFF = 0.05
LIQUID_DIFF = 1.0
PARTITION = 0.15
TRAP_RATE = 4.0
SOLUTE_MEAN = 0.5


def extended(cells, sides, width):
    for axis, dim in sides:
        count = lax.axis_size(axis)
        head = lax.slice_in_dim(cells, 0, width, axis=dim)
        tail = lax.slice_in_dim(cells, cells.shape[dim] - width, cells.shape[dim], axis=dim)
        cells = jnp.concatenate(
            [
                lax.ppermute(tail, axis, [(i, (i + 1) % count) for i in range(count)]),
                cells,
                lax.ppermute(head, axis, [((i + 1) % count, i) for i in range(count)]),
            ],
            axis=dim,
        )
    return cells


def diffusivity(phase_now):
    return SOLID_DIFF + (LIQUID_DIFF - SOLID_DIFF) * 0.5 * (1.0 - jnp.tanh(phase_now))


def update(phase_now, solute_now, undercool, phase_nb, solute_nb, diff_now, diff_nb):
    lap = reduce(jnp.add, phase_nb) - 6.0 * phase_now
    squares = 1.0 - phase_now * phase_now
    rate = (
        lap
        + phase_now
        - phase_now * phase_now * phase_now
        + COUPLING * squares * squares * (undercool - solute_now)
    )
    fluxes = [
        0.5 * (diff_now + diff_nb[index]) * (solute_nb[index] - solute_now) for index in range(6)
    ]
    divergence = reduce(jnp.add, fluxes)
    speed = TRAP_RATE * jnp.abs(rate)
    keff = (PARTITION + speed) / (1.0 + speed)
    phase_new = phase_now + TIME_STEP * rate
    solute_new = solute_now + TIME_STEP * (divergence + 0.5 * (1.0 - keff) * solute_now * rate)
    return (phase_new, solute_new)


def beside(padded):
    centre = padded[1:-1, 1:-1]
    return [
        padded[2:, 1:-1],
        padded[:-2, 1:-1],
        padded[1:-1, 2:],
        padded[1:-1, :-2],
        jnp.roll(centre, -1, 2),
        jnp.roll(centre, 1, 2),
    ]


def phase_sweep(phase_now, solute_now, undercool):
    padded = extended(jnp.stack([phase_now, solute_now]), (("gx", 1), ("gy", 2)), 1)
    phase_pad = padded[0]
    solute_pad = padded[1]
    diff_pad = diffusivity(phase_pad)
    return update(
        phase_now,
        solute_now,
        undercool,
        beside(phase_pad),
        beside(solute_pad),
        diff_pad[1:-1, 1:-1],
        beside(diff_pad),
    )


def signed_freq(indices, total):
    return jnp.where(indices < total // 2, indices, indices - total)


def wave_tables(freqs, positions, length, factor):
    product = freqs[:, None] * positions[None, :] % length
    angles = product.astype(jnp.float32) * (2.0 * math.pi / length)
    return (jnp.cos(angles) * factor, jnp.sin(angles) * factor)


def complex_mix(cosines, sines, data, pattern, orient):

    def apply(table, values):
        return jnp.einsum(pattern, table, values, precision=lax.Precision.HIGHEST)

    cos_real = apply(cosines, data[0])
    cos_imag = apply(cosines, data[1])
    sin_real = apply(sines, data[0])
    sin_imag = apply(sines, data[1])
    return jnp.stack([cos_real - orient * sin_imag, cos_imag + orient * sin_real])


def x_forward(data, factor):
    portion = lax.all_to_all(data, "gx", split_axis=1, concat_axis=2, tiled=True)
    length = portion.shape[2]
    cosines, sines = wave_tables(
        signed_freq(jnp.arange(KX, dtype=jnp.int32), KX),
        jnp.arange(length, dtype=jnp.int32),
        length,
        factor,
    )
    lines = complex_mix(cosines, sines, portion, "kx,wxyz->wkyz", -1.0)
    return lax.all_to_all(lines, "gx", split_axis=2, concat_axis=1, tiled=True)


def y_forward(data, factor):
    portion = lax.all_to_all(data, "gy", split_axis=1, concat_axis=3, tiled=True)
    length = portion.shape[3]
    cosines, sines = wave_tables(
        signed_freq(jnp.arange(KY, dtype=jnp.int32), KY),
        jnp.arange(length, dtype=jnp.int32),
        length,
        factor,
    )
    lines = complex_mix(cosines, sines, portion, "ky,wayz->wakz", -1.0)
    return lax.all_to_all(lines, "gy", split_axis=3, concat_axis=1, tiled=True)


def contract(weights, values):
    return jnp.einsum("abzoi,iabz->oabz", weights, values, precision=lax.Precision.HIGHEST)


def outer(left, right):
    return jnp.einsum("oabz,iabz->abzoi", left, right, precision=lax.Precision.HIGHEST)


def per_device_plain(
    phase,
    solute,
    undercool,
    lift_weight,
    spectral_weight,
    local_weight,
    local_bias,
    proj_weight,
    cotangent,
):
    phase_mid, solute_mid = phase_sweep(phase, solute, undercool)
    phase_next, solute_next = phase_sweep(phase_mid, solute_mid, undercool)
    cells_x, cells_y, depth = phase.shape
    total_x = cells_x * lax.axis_size("gx")
    total_y = cells_y * lax.axis_size("gy")
    fields = jnp.stack([phase_next, solute_next - SOLUTE_MEAN])
    modes_z = jnp.arange(KZ, dtype=jnp.int32)
    zpos = jnp.arange(depth, dtype=jnp.int32)
    unit_z = jnp.ones((KZ,), jnp.float32)
    weights_z = jnp.where(modes_z == 0, 1.0, 2.0).astype(jnp.float32) / depth

    def z_forward(field, zfactor):
        cosines, sines = wave_tables(modes_z, zpos, depth, zfactor[:, None])
        tables = jnp.stack([cosines, -sines])
        return jnp.einsum("wxyz,rkz->rwxyk", field, tables, precision=lax.Precision.HIGHEST)

    def spectral_forward(field, zfactor, xfactor, yfactor):
        return y_forward(x_forward(z_forward(field, zfactor), xfactor), yfactor)

    lifted = jnp.einsum("wc,cxyz->wxyz", lift_weight, fields, precision=lax.Precision.HIGHEST)
    spectrum = spectral_forward(lifted, unit_z, 1.0, 1.0)
    own_x = spectrum.shape[2]
    own_y = spectrum.shape[3]
    shaped = spectral_weight.reshape(2, own_x, own_y, KZ, WIDTH, WIDTH)
    out_real = contract(shaped[0], spectrum[0]) - contract(shaped[1], spectrum[1])
    out_imag = contract(shaped[0], spectrum[1]) + contract(shaped[1], spectrum[0])
    spectral_out = jnp.stack([out_real, out_imag])
    ypos = lax.axis_index("gy") * cells_y + jnp.arange(cells_y, dtype=jnp.int32)
    portion = lax.all_gather(spectral_out, "gy", axis=3, tiled=True)
    freqs = signed_freq(jnp.arange(portion.shape[3], dtype=jnp.int32), KY)
    cosines, sines = wave_tables(ypos, freqs, total_y, 1.0 / total_y)
    back_y = complex_mix(cosines, sines, portion, "yk,wakz->wayz", 1.0)
    cosines, sines = wave_tables(
        jnp.arange(total_x, dtype=jnp.int32),
        signed_freq(jnp.arange(KX, dtype=jnp.int32), KX),
        total_x,
        1.0 / total_x,
    )
    inverted = complex_mix(
        cosines,
        sines,
        lax.all_to_all(back_y, "gx", split_axis=1, concat_axis=2, tiled=True),
        "xk,wkyz->wxyz",
        1.0,
    )
    back_x = lax.all_to_all(inverted, "gx", split_axis=2, concat_axis=1, tiled=True)
    cos_back, sin_back = wave_tables(modes_z, zpos, depth, weights_z[:, None])
    back_tables = jnp.stack([cos_back, -sin_back])
    spectral_field = jnp.einsum(
        "rwxyk,rkz->wxyz", back_x, back_tables, precision=lax.Precision.HIGHEST
    )
    mixed = jnp.dot(local_weight, lift_weight, precision=lax.Precision.HIGHEST)
    pre_act = (
        spectral_field
        + jnp.einsum("wc,cxyz->wxyz", mixed, fields, precision=lax.Precision.HIGHEST)
        + local_bias[:, None, None, None]
    )
    activated, gelu_back = jax.vjp(jax.nn.gelu, pre_act)
    predicted = jnp.einsum("w,wxyz->xyz", proj_weight, activated, precision=lax.Precision.HIGHEST)
    grad_pre = gelu_back(proj_weight[:, None, None, None] * cotangent[None])[0]
    field_sums = jnp.einsum("wxyz,cxyz->wc", grad_pre, fields, precision=lax.Precision.HIGHEST)
    proj_sums = jnp.einsum("wxyz,xyz->w", activated, cotangent, precision=lax.Precision.HIGHEST)
    field_sums, proj_sums = lax.psum((field_sums, proj_sums), ("gx", "gy"))
    grad_modes = spectral_forward(grad_pre, weights_z, 1.0 / total_x, 1.0 / total_y)
    grad_real = outer(grad_modes[0], spectrum[0]) + outer(grad_modes[1], spectrum[1])
    grad_imag = outer(grad_modes[1], spectrum[0]) - outer(grad_modes[0], spectrum[1])
    grad_spectral = jnp.stack([grad_real, grad_imag]).reshape(2, own_x, own_y, KZ, WIDTH * WIDTH)
    scale = 1.0 / math.sqrt(total_x * total_y * depth)
    grad_local = jnp.dot(field_sums, lift_weight.T, precision=lax.Precision.HIGHEST) * scale
    grad_proj = proj_sums * scale
    return (phase_next, solute_next, predicted, grad_spectral, grad_local, grad_proj)


LANES = 128
SMALL_VMEM = 24 * 1024 * 1024
LARGE_VMEM = 50 * 1024 * 1024
PACK_COST = 50_000_000_000
SPREAD = LANES // WIDTH
NARROW = jnp.bfloat16
EXACT = lax.Precision.HIGHEST


def halves(table):
    head = table.astype(np.float32).astype(ml_dtypes.bfloat16)
    rest = (table - head.astype(np.float64)).astype(np.float32).astype(ml_dtypes.bfloat16)
    return head, rest


def left_table(table):
    head, rest = halves(table)
    return np.concatenate([head, head, rest], axis=1)


def right_table(table):
    head, rest = halves(table)
    return np.concatenate([head, head, rest], axis=0)


def parts_of(values):
    head = values.astype(NARROW)
    return head, (values - head.astype(jnp.float32)).astype(NARROW)


def thrice(values, axis):
    head, rest = parts_of(values)
    return jnp.concatenate([head, rest, head], axis=axis)


def one_where(mask):
    return mask.astype(jnp.float32).astype(NARROW)


def mul(left, right):
    return jnp.dot(left, right, preferred_element_type=jnp.float32)


def mul_rows(left, right):
    return lax.dot_general(
        left, right, (((1,), (1,)), ((), ())), preferred_element_type=jnp.float32
    )


def angles(freqs, positions, length):
    return 2.0 * np.pi * ((freqs[:, None] * positions[None, :]) % length) / length


def signed(count):
    index = np.arange(count)
    return np.where(index < count // 2, index, index - count)


def rotation(theta, orient):
    cosines, sines = np.cos(theta), orient * np.sin(theta)
    return np.block([[cosines, -sines], [sines, cosines]])


def group_of(shape):
    return lax.broadcasted_iota(jnp.int32, shape, len(shape) - 1) // WIDTH


def pick(groups, choices):
    result = choices[-1]
    for index in range(len(choices) - 2, -1, -1):
        result = jnp.where(groups == index, choices[index], result)
    return result


def turn(values, shift):
    shift = shift % LANES
    return values if shift == 0 else pltpu.roll(values, shift, 1)


def swap_groups(pieces):
    groups = group_of(pieces[0].shape)
    return [
        pick(groups, [turn(pieces[i], WIDTH * (i - j)) for i in range(SPREAD)])
        for j in range(SPREAD)
    ]


def contract_kernel(planes, lift_ref, weight_ref, out_ref, held, arrived):
    _, own_x, own_y, modes_z, width = weight_ref.shape
    chunk = out_ref.shape[0] // modes_z
    steps = own_x // planes

    def fetch(step):
        block = pl.ds(step * planes, planes)
        return pltpu.make_async_copy(
            weight_ref.at[:, block], held.at[:, block], arrived.at[step]
        )

    for step in range(steps):
        fetch(step).start()
    square = (WIDTH, WIDTH)
    diagonal = lax.broadcasted_iota(jnp.int32, square, 0) == lax.broadcasted_iota(
        jnp.int32, square, 1
    )
    columns = [
        jnp.sum(
            jnp.where(diagonal, jnp.broadcast_to(lift_ref[k : k + 1, :], square), 0.0),
            axis=1,
            keepdims=True,
        )
        for k in range(2)
    ]
    lane = lax.broadcasted_iota(jnp.int32, (WIDTH, LANES), 1)
    base = jnp.where(
        lane % (2 * WIDTH) < WIDTH,
        jnp.broadcast_to(columns[0], lane.shape),
        jnp.broadcast_to(columns[1], lane.shape),
    )
    head, rest = parts_of(base)
    base = jnp.where(lane < 2 * WIDTH, head.astype(jnp.float32), rest.astype(jnp.float32))
    mixing = jnp.concatenate(
        [jnp.where(lane % WIDTH == channel, base, 0.0) for channel in range(WIDTH)], axis=0
    ).astype(NARROW)
    rows = planes * own_y * modes_z
    low = lax.broadcasted_iota(jnp.int32, (rows, LANES), 1) < 2 * WIDTH
    for step in range(steps):
        fetch(step).wait()
        sums = []
        for part in range(2):
            block = held[part, step * planes : (step + 1) * planes]
            head, rest = parts_of(block.reshape(rows, width))
            total = mul(head, mixing) + mul(rest, mixing)
            sums.append(total + turn(total, 2 * WIDTH))
        result = jnp.where(low, sums[0], sums[1])
        for plane in range(planes):
            for row in range(own_y):
                first = (plane * own_y + row) * modes_z
                place = row * own_x + step * planes + plane
                out_ref[pl.ds(place, modes_z, stride=chunk), :] = result[
                    first : first + modes_z
                ]


def edge_kernel(held_ref, head_ref, tail_ref):
    cells_x = held_ref.shape[1]
    for index, reach in enumerate((2, 2, 1)):
        head_ref[2 * index : 2 * index + reach] = held_ref[index, 0:reach]
        tail_ref[2 * index : 2 * index + reach] = held_ref[index, cells_x - reach : cells_x]


def pack_kernel(held_ref, before_ref, after_ref, head_ref, tail_ref):
    _, cells_x, cells_y, _ = held_ref.shape

    def put(target, phase, solute, cool):
        head_ref[target, 0:2] = phase[:, 0:2]
        head_ref[target, 2:4] = solute[:, 0:2]
        head_ref[target, 4:5] = cool[:, 0:1]
        tail_ref[target, 0:2] = phase[:, cells_y - 2 : cells_y]
        tail_ref[target, 2:4] = solute[:, cells_y - 2 : cells_y]
        tail_ref[target, 4:5] = cool[:, cells_y - 1 : cells_y]

    put(slice(0, 1), before_ref[1:2], before_ref[3:4], before_ref[4:5])
    put(slice(1, cells_x + 1), held_ref[0], held_ref[1], held_ref[2])
    put(slice(cells_x + 1, cells_x + 2), after_ref[0:1], after_ref[2:3], after_ref[4:5])


def step_kernel(
    held_ref,
    before_ref,
    after_ref,
    low_ref,
    high_ref,
    table_ref,
    mixed_ref,
    fields_ref,
    send_ref,
    phase_ext,
    solute_ext,
    cool_ext,
    diff_ext,
    lines,
):
    _, cells_x, cells_y, depth = held_ref.shape
    base = 8
    end = base + cells_y
    for index, ext in enumerate((phase_ext, solute_ext)):
        first = 2 * index
        ext[2 : cells_x + 2, base:end] = held_ref[index]
        ext[0:2, base:end] = before_ref[first : first + 2]
        ext[cells_x + 2 : cells_x + 4, base:end] = after_ref[first : first + 2]
        ext[1 : cells_x + 3, base - 2 : base] = low_ref[:, first : first + 2]
        ext[1 : cells_x + 3, end : end + 2] = high_ref[:, first : first + 2]
    cool_ext[2 : cells_x + 2, base:end] = held_ref[2]
    cool_ext[1:2, base:end] = before_ref[4:5]
    cool_ext[cells_x + 2 : cells_x + 3, base:end] = after_ref[4:5]
    cool_ext[1 : cells_x + 3, base - 1 : base] = low_ref[:, 4:5]
    cool_ext[1 : cells_x + 3, end : end + 1] = high_ref[:, 4:5]

    def sweep(reach):
        diff_ext[...] = diffusivity(phase_ext[...])

        def window(ext, move_x, move_y):
            return ext[
                2 - reach + move_x : cells_x + 2 + reach + move_x,
                base - reach + move_y : end + reach + move_y,
            ]

        def around(ext, now):
            return [
                window(ext, 1, 0),
                window(ext, -1, 0),
                window(ext, 0, 1),
                window(ext, 0, -1),
                pltpu.roll(now, depth - 1, 2),
                pltpu.roll(now, 1, 2),
            ]

        phase_now = window(phase_ext, 0, 0)
        solute_now = window(solute_ext, 0, 0)
        diff_now = window(diff_ext, 0, 0)
        return update(
            phase_now,
            solute_now,
            window(cool_ext, 0, 0),
            around(phase_ext, phase_now),
            around(solute_ext, solute_now),
            diff_now,
            around(diff_ext, diff_now),
        )

    phase_mid, solute_mid = sweep(1)
    phase_ext[1 : cells_x + 3, base - 1 : end + 1] = phase_mid
    solute_ext[1 : cells_x + 3, base - 1 : end + 1] = solute_mid
    phase_next, solute_next = sweep(0)
    fields_ref[0] = phase_next
    fields_ref[1] = solute_next
    tile = cells_x * cells_y
    both = (phase_next.reshape(tile, depth), solute_next.reshape(tile, depth) - SOLUTE_MEAN)
    ordered = []
    for part in range(depth // LANES):
        for index, values in enumerate(both):
            lines[part, index * tile : (index + 1) * tile] = values[
                :, part * LANES : (part + 1) * LANES
            ]
        ordered.append(
            jnp.concatenate(
                [
                    lines[part, pl.ds(row, 2 * cells_x, stride=cells_y), :]
                    for row in range(cells_y)
                ],
                axis=0,
            )
        )
    ordered = jnp.concatenate(ordered, axis=1)
    spectra = mul_rows(table_ref[...], thrice(ordered, 1))
    send_ref[...] = mixed_ref[...]
    modes_z = spectra.shape[0] // 2
    chunk = send_ref.shape[0] // modes_z
    for part in range(2):
        send_ref[pl.ds(chunk - 2 + part, modes_z, stride=chunk), :] = spectra[
            part * modes_z : (part + 1) * modes_z
        ]


def pack_modes(shape, modes, modes_ref, rows_ref):
    count_x, count_y, _, _, own_x, own_y = shape
    modes_x, modes_y = count_x * own_x, count_y * own_y
    lane = lax.broadcasted_iota(jnp.int32, (modes_y, LANES), 1)
    for index in range(count_x):
        block = modes
        for k in range(4):
            shift = k * own_x - k * modes_x - index * own_x
            block = jnp.where(lane // own_x == k, turn(modes, shift), block)
        rows_ref[index] = block
        line = rows_ref[index, pl.ds(0, count_y, stride=own_y), :]
        groups = group_of(line.shape)
        for row in range(1, own_y):
            piece = rows_ref[index, pl.ds(row, count_y, stride=own_y), :]
            line = jnp.where(groups == row, turn(piece, row * WIDTH), line)
        modes_ref[index * count_y : (index + 1) * count_y] = line


def spectral_kernel(
    shape,
    mixed_ref,
    y_in_ref,
    x_in_ref,
    y_out_ref,
    x_out_ref,
    fields_ref,
    cotangent_ref,
    lift_ref,
    local_ref,
    bias_ref,
    proj_ref,
    modes_ref,
    send_ref,
    vector_ref,
    base_ref,
    spread_ref,
    table_ref,
    lines_y,
    lines_x,
    rows_ref,
    weight_ref,
):
    count_x, count_y, cells_x, cells_y, own_x, own_y = shape
    modes_x, modes_y = count_x * own_x, count_y * own_y
    total_x, total_y = count_x * cells_x, count_y * cells_y
    tile = cells_x * cells_y
    narrow = 2 * cells_x
    rows = 2 * count_y
    devices = count_x * count_y
    own = own_x * own_y
    chunk = mixed_ref.shape[0] // devices
    spectra = [mixed_ref[pl.ds(own + part, devices, stride=chunk), :] for part in range(2)]
    for index in range(devices):
        weight_ref[index * own : (index + 1) * own, :] = mixed_ref[
            index * chunk : index * chunk + own, :
        ]
    lane = lax.broadcasted_iota(jnp.int32, (rows, LANES), 1)
    blocks = []
    for row in range(cells_y):
        block = jnp.zeros((rows, LANES), jnp.float32)
        for index in range(count_x):
            piece = jnp.concatenate(
                [values[index * count_y : (index + 1) * count_y] for values in spectra], axis=0
            )
            piece = turn(piece, narrow * (index - row))
            block = jnp.where(lane // narrow == index, piece, block)
        blocks.append(block)
    along_y = mul(y_in_ref[...], thrice(jnp.concatenate(blocks, axis=0), 0))
    half = lax.broadcasted_iota(jnp.int32, (modes_y, LANES), 1) < LANES // 2
    joined = jnp.where(half, along_y[0:modes_y], turn(along_y[modes_y:], LANES // 2))
    modes = mul(thrice(joined, 1), x_in_ref[...])
    quads_y = total_y // SPREAD
    quads_x = modes_x // SPREAD
    lane = lax.broadcasted_iota(jnp.int32, (modes_y, LANES), 1) % modes_x
    chosen = jnp.concatenate(
        [jnp.where(lane == freq, modes, 0.0) for freq in range(modes_x)], axis=0
    )
    place = lax.broadcasted_iota(jnp.int32, (2 * LANES, 2 * LANES), 0) % LANES // modes_x
    group = lax.broadcasted_iota(jnp.int32, (2 * LANES, 2 * LANES), 1) // WIDTH
    same = jnp.where(group < 4, group, (group + 2) % 4)
    signed_one = jnp.where((group == 2) | (group == 3), -1.0, 1.0)
    spread = jnp.where(place == same, signed_one, 0.0).astype(NARROW)
    columns = mul(jnp.concatenate(parts_of(chosen), axis=1), spread)
    products = [[], []]
    for quad in range(quads_x):
        lines = [[], []]
        for index in range(SPREAD):
            freq = SPREAD * quad + index
            start = (freq // own_x) * count_y * own_y * own_x + freq % own_x
            weights = weight_ref[pl.ds(start, modes_y, stride=own_x), :]
            for part in range(2):
                column = columns[
                    freq * modes_y : (freq + 1) * modes_y, part * LANES : (part + 1) * LANES
                ]
                lines[part].append(weights * column)
        for part in range(2):
            products[part].append(jnp.concatenate(lines[part], axis=1))
    products = jnp.concatenate(products[0] + products[1], axis=0)
    gather = lax.broadcasted_iota(jnp.int32, (2 * SPREAD * LANES, LANES), 0) % (SPREAD * LANES)
    column = lax.broadcasted_iota(jnp.int32, (2 * SPREAD * LANES, LANES), 1)
    gather = one_where(gather // LANES * WIDTH + gather % WIDTH == column)
    products = mul(jnp.concatenate(parts_of(products), axis=1), gather)
    stacked = [
        jnp.concatenate(
            [
                products[(part * quads_x + quad) * modes_y : (part * quads_x + quad + 1) * modes_y]
                for part in range(2)
            ],
            axis=0,
        )
        for quad in range(quads_x)
    ]
    back = mul(y_out_ref[...], thrice(jnp.concatenate(stacked, axis=1), 0))
    for quad in range(quads_x):
        lines_y[quad] = back[:, quad * LANES : (quad + 1) * LANES]
    for quad in range(quads_x):
        for part in range(2):
            pieces = [
                lines_y[quad, pl.ds(part * total_y + i, quads_y, stride=SPREAD), :]
                for i in range(SPREAD)
            ]
            for index, piece in enumerate(swap_groups(pieces)):
                place = part * modes_x + SPREAD * quad + index
                lines_x[pl.ds(place, quads_y, stride=2 * modes_x), :] = piece
    per_tile = cells_y // SPREAD
    blocks = [
        lines_x[quad * 2 * modes_x : (quad + 1) * 2 * modes_x, :] for quad in range(quads_y)
    ]
    back = mul(x_out_ref[...], thrice(jnp.concatenate(blocks, axis=1), 0))
    for quad in range(quads_y):
        for part in range(2):
            for index in range(count_x):
                device = index * count_y + quad // per_tile
                place = (device * 2 + part) * per_tile + quad % per_tile
                first = part * total_x + index * cells_x
                send_ref[place * cells_x : (place + 1) * cells_x, :] = back[
                    first : first + cells_x, quad * LANES : (quad + 1) * LANES
                ]
    pack_modes(shape, modes, modes_ref, rows_ref)
    prepare(
        fields_ref,
        cotangent_ref,
        lift_ref,
        local_ref,
        bias_ref,
        proj_ref,
        vector_ref,
        base_ref,
        spread_ref,
        table_ref,
    )


def prepare(
    fields_ref,
    cotangent_ref,
    lift_ref,
    local_ref,
    bias_ref,
    proj_ref,
    vector_ref,
    base_ref,
    weight_ref,
    table_ref,
):
    planes, depth, wide = base_ref.shape
    tile = cotangent_ref.shape[0]
    cells_y = tile // planes
    lift, lift_rest = parts_of(lift_ref[...])
    local, local_rest = parts_of(local_ref[...])
    mixed = mul_rows(lift, local) + mul_rows(lift_rest, local) + mul_rows(lift, local_rest)
    for index in range(wide // WIDTH):
        place = slice(index * WIDTH, (index + 1) * WIDTH)
        vector_ref[0:2, place] = mixed
        vector_ref[2:3, place] = bias_ref[...]
        vector_ref[3:4, place] = proj_ref[...]
    fields = (
        fields_ref[0].reshape(tile, depth),
        fields_ref[1].reshape(tile, depth) - SOLUTE_MEAN,
        cotangent_ref[...],
    )
    spread = jnp.concatenate(
        [jnp.concatenate(parts_of(values.T), axis=1) for values in fields], axis=0
    )
    cell = lax.broadcasted_iota(jnp.int32, (2 * tile, wide), 0) % tile
    row = lax.broadcasted_iota(jnp.int32, (2 * tile, wide), 1) // WIDTH
    for plane in range(planes):
        values = mul(spread, one_where(cell == plane * cells_y + row))
        base_ref[plane] = (
            values[0:depth] * vector_ref[0:1, :]
            + values[depth : 2 * depth] * vector_ref[1:2, :]
            + vector_ref[2:3, :]
        )
        weight_ref[plane] = values[2 * depth :]
        lines = [values[plane * cells_y : (plane + 1) * cells_y] for values in fields[:2]]
        table_ref[plane] = jnp.concatenate(parts_of(jnp.concatenate(lines, axis=0)), axis=0)


def field_kernel(
    cells_y,
    field_ref,
    base_ref,
    weight_ref,
    table_ref,
    vector_ref,
    back_ref,
    forth_ref,
    predicted_ref,
    send_ref,
):
    planes, depth, wide = base_ref.shape
    rows = back_ref.shape[1] // 3
    halves_y = cells_y // SPREAD
    stride = halves_y * planes
    proj = vector_ref[3:4, :]
    root = math.sqrt(2.0 / math.pi)
    curve = 0.044715
    picker = one_where(
        lax.broadcasted_iota(jnp.int32, (cells_y, 2 * wide), 0)
        == lax.broadcasted_iota(jnp.int32, (cells_y, 2 * wide), 1) % wide // WIDTH
    )
    line_sums = jnp.zeros((2 * cells_y, wide), jnp.float32)
    proj_sums = jnp.zeros((8, wide), jnp.float32)
    for plane in range(planes):
        spectra = jnp.concatenate(
            [
                field_ref[pl.ds(part * planes + plane, rows, stride=stride), :]
                for part in range(halves_y)
            ],
            axis=1,
        )
        pre = mul(back_ref[...], thrice(spectra, 0)) + base_ref[plane]
        square = pre * pre
        bent = jnp.tanh(pre * (root + (root * curve) * square))
        upper = 0.5 + 0.5 * bent
        active = pre * upper
        slope = upper + (active - active * bent) * (root + (3.0 * root * curve) * square)
        cotangent = weight_ref[plane]
        weighted = proj * cotangent
        grad = weighted * slope
        predicted_ref[plane * cells_y : (plane + 1) * cells_y, :] = mul_rows(
            picker, jnp.concatenate(parts_of(proj * active), axis=1)
        )
        head, rest = parts_of(grad)
        lines = table_ref[plane]
        top = jnp.concatenate([forth_ref[0:rows], lines[0 : 2 * cells_y]], axis=0)
        low = jnp.concatenate([forth_ref[rows:], lines[2 * cells_y :]], axis=0)
        spectra = mul(jnp.concatenate([top, low], axis=0), head)
        spectra = spectra[0 : rows + 2 * cells_y] + spectra[rows + 2 * cells_y :] + mul(top, rest)
        for part in range(halves_y):
            send_ref[pl.ds(part * planes + plane, rows, stride=stride), :] = spectra[
                0:rows, part * LANES : (part + 1) * LANES
            ]
        line_sums = line_sums + spectra[rows:]
        proj_sums = proj_sums + jnp.sum(
            (active * cotangent).reshape(depth // 8, 8, wide), axis=0
        )
    shape = (cells_y, wide)
    own = lax.broadcasted_iota(jnp.int32, shape, 0) == (
        lax.broadcasted_iota(jnp.int32, shape, 1) // WIDTH
    )
    sums = [
        jnp.where(own, line_sums[0:cells_y], 0.0),
        jnp.where(own, line_sums[cells_y:], 0.0),
        proj_sums,
    ]
    for index, values in enumerate(sums):
        line = jnp.sum(values, axis=0, keepdims=True)
        line = sum(line[:, part * LANES : (part + 1) * LANES] for part in range(halves_y))
        send_ref[stride + index : stride + index + 1, :] = line


def gradient_kernel(
    shape, spectra_ref, modes_ref, x_in_ref, y_in_ref, send_ref, lines_x, lines_y
):
    count_x, count_y, cells_x, cells_y, own_x, own_y = shape
    modes_x, modes_y = count_x * own_x, count_y * own_y
    total_x, total_y = count_x * cells_x, count_y * cells_y
    per_tile = cells_y // SPREAD
    quads_y = total_y // SPREAD
    chunk = 2 * per_tile * cells_x
    first_device = (lax.axis_index("gx") == 0) & (lax.axis_index("gy") == 0)
    keep = jnp.where(first_device, 0.0, 1.0)
    blocks = []
    for quad in range(quads_y):
        block = []
        for part in range(2):
            for index in range(count_x):
                device = index * count_y + quad // per_tile
                place = (device * 2 + part) * per_tile + quad % per_tile
                piece = spectra_ref[place * cells_x : (place + 1) * cells_x, :]
                block.append(piece * keep if part else piece)
        blocks.append(jnp.concatenate(block, axis=0))
    forth = mul(x_in_ref[...], thrice(jnp.concatenate(blocks, axis=1), 0))
    for quad in range(quads_y):
        lines_x[quad * 2 * modes_x : (quad + 1) * 2 * modes_x, :] = forth[
            :, quad * LANES : (quad + 1) * LANES
        ]
    devices = count_x * count_y
    out_chunk = send_ref.shape[0] // devices
    per_own = own_x // SPREAD
    quads_x = modes_x // SPREAD
    for quad in range(quads_x):
        for part in range(2):
            pieces = [
                lines_x[
                    pl.ds(part * modes_x + SPREAD * quad + j, quads_y, stride=2 * modes_x), :
                ]
                for j in range(SPREAD)
            ]
            for index, piece in enumerate(swap_groups(pieces)):
                lines_y[quad, pl.ds(part * total_y + index, quads_y, stride=SPREAD), :] = piece
    lines = jnp.concatenate([lines_y[quad] for quad in range(quads_x)], axis=1)
    modes = mul(y_in_ref[...], thrice(lines, 0))
    for quad in range(quads_x):
        for part in range(2):
            for index in range(count_y):
                device = (quad // per_own) * count_y + index
                place = device * out_chunk + (part * per_own + quad % per_own) * own_y
                first = part * modes_y + index * own_y
                send_ref[place : place + own_y, :] = modes[
                    first : first + own_y, quad * LANES : (quad + 1) * LANES
                ]
    extra = 2 * per_own * own_y
    send_ref[pl.ds(extra, devices, stride=out_chunk), :] = modes_ref[...]
    groups = group_of((1, LANES))
    total = jnp.zeros((1, LANES), jnp.float32)
    for index in range(3):
        start = chunk // 2 + index
        line = jnp.sum(
            spectra_ref[pl.ds(start, devices, stride=chunk), :], axis=0, keepdims=True
        )
        line = line + turn(line, 2 * WIDTH)
        total = jnp.where(groups == index, line + turn(line, WIDTH), total)
    send_ref[pl.ds(extra + 1, devices, stride=out_chunk), :] = jnp.broadcast_to(
        total, (devices, LANES)
    )


def outer_kernel(
    scale,
    modes_ref,
    narrow_ref,
    predicted_ref,
    fields_ref,
    local_out,
    proj_out,
    predicted_out,
    phase_out,
    solute_out,
    grad_ref,
    mix_ref,
    local_ref,
    proj_ref,
    lift_ref,
    held,
    sent,
):
    _, own_x, own_y, modes_z, width = held.shape
    chunk = modes_ref.shape[0] // modes_z
    per_own = own_x // SPREAD
    extra = 2 * per_own * own_y
    copies = [
        pltpu.make_async_copy(predicted_ref, predicted_out, sent.at[own_x]),
        pltpu.make_async_copy(fields_ref.at[0], phase_out, sent.at[own_x + 1]),
        pltpu.make_async_copy(fields_ref.at[1], solute_out, sent.at[own_x + 2]),
    ]
    for copy in copies:
        copy.start()
    for index in range(SPREAD):
        lift_ref[:, index * WIDTH : (index + 1) * WIDTH] = narrow_ref[...]
    for index in range(1, width // LANES):
        lift_ref[:, index * LANES : (index + 1) * LANES] = lift_ref[:, 0:LANES]
    shape = (2 * WIDTH, width)
    row = lax.broadcasted_iota(jnp.int32, shape, 0)
    column = lax.broadcasted_iota(jnp.int32, shape, 1)
    lift = jnp.where(row < WIDTH, lift_ref[0:1, :], lift_ref[1:2, :])
    head, rest = parts_of(jnp.where(column // WIDTH == row % WIDTH, lift, 0.0))
    mix_ref[0 : 2 * WIDTH] = head
    mix_ref[2 * WIDTH : 4 * WIDTH] = head
    mix_ref[4 * WIDTH : 6 * WIDTH] = rest
    mix_ref[6 * WIDTH : 8 * WIDTH] = jnp.zeros_like(rest)
    lane = lax.broadcasted_iota(jnp.int32, (modes_z, LANES), 1)
    low = lane < 2 * WIDTH

    def rows_of(values):
        head, rest = parts_of(values)
        both = jnp.where(low, head.astype(jnp.float32), rest.astype(jnp.float32)).astype(NARROW)
        return jnp.concatenate([both, head], axis=1)

    line = modes_ref[extra + 1 : extra + 2, :]
    square = (WIDTH, WIDTH)
    diagonal = lax.broadcasted_iota(jnp.int32, square, 0) == lax.broadcasted_iota(
        jnp.int32, square, 1
    )
    local = jnp.zeros(square, jnp.float32)
    for k in range(2):
        sums = jnp.broadcast_to(line[:, k * WIDTH : (k + 1) * WIDTH], square)
        sums = jnp.sum(jnp.where(diagonal, sums, 0.0), axis=1, keepdims=True)
        local = local + sums * narrow_ref[k : k + 1, :]
    local_ref[...] = scale * local
    proj_ref[...] = scale * line[:, 2 * WIDTH : 3 * WIDTH]
    copies.append(pltpu.make_async_copy(local_ref, local_out, sent.at[own_x + 3]))
    copies.append(pltpu.make_async_copy(proj_ref, proj_out, sent.at[own_x + 4]))
    copies[3].start()
    copies[4].start()
    grads = jnp.concatenate(
        [modes_ref[pl.ds(place, modes_z, stride=chunk), :] for place in range(extra)], axis=0
    )
    repeat = lax.broadcasted_iota(jnp.int32, (2 * LANES, SPREAD * LANES), 0) % LANES
    column = lax.broadcasted_iota(jnp.int32, (2 * LANES, SPREAD * LANES), 1)
    repeat = one_where(repeat == column // LANES * WIDTH + column % WIDTH)
    grads = mul(jnp.concatenate(parts_of(grads), axis=1), repeat)
    modes = modes_ref[pl.ds(extra, modes_z, stride=chunk), :]
    place = lax.broadcasted_iota(jnp.int32, (2 * LANES, 2 * LANES), 0) % LANES // own_x % 4
    column = lax.broadcasted_iota(jnp.int32, (2 * LANES, 2 * LANES), 1) // WIDTH
    spread = one_where(place == column // 4 * 2 + column % 2)
    own = lane // (4 * own_x) * own_x + lane % own_x
    for plane in range(own_x):
        chosen = jnp.concatenate(
            [jnp.where(own == row * own_x + plane, modes, 0.0) for row in range(own_y)], axis=0
        )
        columns = mul(jnp.concatenate(parts_of(chosen), axis=1), spread)
        reals, imags = [], []
        for row in range(own_y):
            real = columns[row * modes_z : (row + 1) * modes_z, 0:LANES]
            imag = columns[row * modes_z : (row + 1) * modes_z, LANES:]
            pair = []
            for part in range(2):
                first = ((part * per_own + plane // SPREAD) * own_y + row) * modes_z
                group = plane % SPREAD * LANES
                pair.append(grads[first : first + modes_z, group : group + LANES])
            reals.append(rows_of(pair[0] * real + pair[1] * imag))
            imags.append(rows_of(pair[1] * real - pair[0] * imag))
        result = mul(jnp.concatenate(reals + imags, axis=0), mix_ref[...])
        held[:, plane] = result.reshape(2, own_y, modes_z, width)
        copies.append(
            pltpu.make_async_copy(held.at[:, plane], grad_ref.at[:, plane], sent.at[plane])
        )
        copies[-1].start()
    for copy in copies:
        copy.wait()


def tables(shape, depth, modes_z):
    count_x, count_y, cells_x, cells_y, own_x, own_y = shape
    modes_x, modes_y = count_x * own_x, count_y * own_y
    total_x, total_y = count_x * cells_x, count_y * cells_y
    theta_z = angles(np.arange(modes_z), np.arange(depth), depth)
    theta_x = angles(signed(modes_x), np.arange(total_x), total_x)
    theta_y = angles(signed(modes_y), np.arange(total_y), total_y)
    plain_z = np.concatenate([np.cos(theta_z), -np.sin(theta_z)], axis=0)
    forth_z = plain_z.reshape(2, modes_z, depth).transpose(1, 0, 2).reshape(2 * modes_z, depth)
    weight = np.where(np.arange(modes_z) == 0, 1.0, 2.0) / (total_x * total_y * depth)
    weighted_z = np.repeat(weight, 2)[:, None] * forth_z
    forth_x, back_x = rotation(theta_x, -1.0), rotation(theta_x.T, 1.0)
    forth_y, back_y = rotation(theta_y, -1.0), rotation(theta_y.T, 1.0)
    order_y = forth_y.reshape(2 * modes_y, 2, count_y, cells_y)
    order_y = order_y.transpose(0, 3, 1, 2).reshape(2 * modes_y, 2 * total_y)
    lines = forth_x.reshape(2, modes_x, 2, count_x, cells_x)
    both = np.zeros((2, count_x, 2, cells_x, 2, 2, modes_x))
    for field in range(2):
        both[:, :, field, :, :, field, :] = lines.transpose(2, 3, 4, 0, 1)
    both = both.reshape(4 * total_x, 4 * modes_x)
    return {
        "z_plain": left_table(plain_z),
        "z_forth": np.concatenate(halves(weighted_z), axis=0),
        "z_back": left_table(weighted_z.T),
        "y_first": left_table(order_y),
        "x_first": right_table(both),
        "y_back": left_table(back_y),
        "x_back": left_table(back_x),
        "x_forth": left_table(forth_x),
        "y_forth": left_table(forth_y),
    }


def fits(count_x, count_y, phase, spectral_weight):
    cells_x, cells_y, depth = phase.shape
    _, own_x, own_y, modes_z, width = spectral_weight.shape
    return (
        width == WIDTH * WIDTH
        and modes_z == count_x * count_y
        and 4 * count_x * cells_x == LANES
        and 4 * count_x * own_x == LANES
        and 2 * cells_x * cells_y == LANES
        and cells_x == 8
        and cells_y % SPREAD == 0
        and own_x % SPREAD == 0
        and own_y * 4 * own_x == LANES
        and 3 * WIDTH <= LANES
        and cells_y == 8
        and depth % LANES == 0
    )


def call(kernel, outs, scratch, flops, moved, limit=SMALL_VMEM, **more):
    return pl.pallas_call(
        kernel,
        out_shape=outs,
        scratch_shapes=scratch,
        compiler_params=pltpu.CompilerParams(vmem_limit_bytes=limit),
        cost_estimate=pl.CostEstimate(flops=flops, bytes_accessed=moved, transcendentals=0),
        **more,
    )


def exchange(values):
    return lax.all_to_all(values, ("gx", "gy"), split_axis=0, concat_axis=0, tiled=True)


def per_device_fast(
    phase,
    solute,
    undercool,
    lift_weight,
    spectral_weight,
    local_weight,
    local_bias,
    proj_weight,
    cotangent,
):
    count_x, count_y = lax.axis_size("gx"), lax.axis_size("gy")
    cells_x, cells_y, depth = phase.shape
    _, own_x, own_y, modes_z, width = spectral_weight.shape
    shape = (count_x, count_y, cells_x, cells_y, own_x, own_y)
    devices = count_x * count_y
    tile = cells_x * cells_y
    modes_x, modes_y = count_x * own_x, count_y * own_y
    total_x, total_y = count_x * cells_x, count_y * cells_y
    table = tables(shape, depth, modes_z)
    real = jnp.float32

    def like(*dims):
        return jax.ShapeDtypeStruct(dims, real)

    far = pl.BlockSpec(memory_space=pltpu.HBM)
    near = pl.BlockSpec(memory_space=pltpu.VMEM)
    weight_bytes = 8 * own_x * own_y * modes_z * width
    held = jnp.stack([phase, solute, undercool])
    head, tail = call(
        edge_kernel,
        (like(5, cells_y, depth), like(5, cells_y, depth)),
        [],
        1000,
        40 * tile * depth,
    )(held)

    def ring(values, axis, step):
        count = lax.axis_size(axis)
        return lax.ppermute(values, axis, [(i, (i + step) % count) for i in range(count)])

    head, tail, lift = lax.optimization_barrier((head, tail, lift_weight.T))
    before, after = ring(tail, "gx", 1), ring(head, "gx", -1)
    planes = 2
    mixed_weights = call(
        functools.partial(contract_kernel, planes),
        like(modes_z * (own_x * own_y + 2), LANES),
        [
            pltpu.VMEM(spectral_weight.shape, real),
            pltpu.SemaphoreType.DMA((own_x // planes,)),
        ],
        weight_bytes * LANES,
        weight_bytes,
        limit=LARGE_VMEM,
        in_specs=[near, far],
    )(lift, spectral_weight)
    head, tail = call(
        pack_kernel,
        (like(cells_x + 2, 8, depth), like(cells_x + 2, 8, depth)),
        [],
        PACK_COST,
        40 * tile * depth,
    )(held, before, after)
    low, high = ring(tail, "gy", 1), ring(head, "gy", -1)
    extended_shape = pltpu.VMEM((cells_x + 4, cells_y + 16, depth), real)
    stepped, spectra = call(
        step_kernel,
        (like(2, *phase.shape), like(*mixed_weights.shape)),
        [extended_shape] * 4 + [pltpu.VMEM((depth // LANES, 2 * tile, LANES), real)],
        400 * tile * depth,
        80 * tile * depth,
    )(held, before, after, low, high, table["z_plain"], mixed_weights)
    gathered = exchange(spectra.reshape(-1, 2, LANES)).reshape(spectra.shape)
    spread_shape = (cells_x, depth, cells_y * WIDTH)
    modes, fields, vectors, base, weight, lines = call(
        functools.partial(spectral_kernel, shape),
        (
            like(devices, LANES),
            like(devices * 2 * cells_x * (cells_y // SPREAD), LANES),
            like(4, cells_y * WIDTH),
            like(*spread_shape),
            like(*spread_shape),
            jax.ShapeDtypeStruct((cells_x, 4 * cells_y, depth), NARROW),
        ),
        [
            pltpu.VMEM((modes_x // SPREAD, 2 * total_y, LANES), real),
            pltpu.VMEM((2 * modes_x * (total_y // SPREAD), LANES), real),
            pltpu.VMEM((count_x, modes_y, LANES), real),
            pltpu.VMEM((devices * own_x * own_y, LANES), real),
        ],
        100_000_000,
        2_000_000,
    )(
        gathered,
        table["y_first"],
        table["x_first"],
        table["y_back"],
        table["x_back"],
        stepped,
        cotangent.reshape(tile, depth),
        lift,
        local_weight,
        local_bias.reshape(1, WIDTH),
        proj_weight.reshape(1, WIDTH),
    )
    fields = exchange(fields)
    predicted, spectra = call(
        functools.partial(field_kernel, cells_y),
        (like(tile, depth), like(*fields.shape)),
        [],
        1_000_000_000,
        2_000_000,
    )(fields, base, weight, lines, vectors, table["z_back"], table["z_forth"])
    spectra = exchange(spectra)
    chunk = 2 * own_x * own_y * WIDTH // LANES + 2
    gradients = call(
        functools.partial(gradient_kernel, shape),
        like(devices * chunk, LANES),
        [
            pltpu.VMEM((2 * modes_x * (total_y // SPREAD), LANES), real),
            pltpu.VMEM((modes_x // SPREAD, 2 * total_y, LANES), real),
        ],
        100_000_000,
        2_000_000,
    )(spectra, modes, table["x_forth"], table["y_forth"])
    gradients = exchange(gradients.reshape(-1, 2, LANES)).reshape(gradients.shape)
    grad_local, grad_proj, predicted, phase_next, solute_next, grad_spectral = call(
        functools.partial(outer_kernel, 1.0 / math.sqrt(total_x * total_y * depth)),
        (
            like(WIDTH, WIDTH),
            like(1, WIDTH),
            like(*predicted.shape),
            like(*phase.shape),
            like(*phase.shape),
            like(*spectral_weight.shape),
        ),
        [
            pltpu.VMEM((8 * WIDTH, width), NARROW),
            pltpu.VMEM((WIDTH, WIDTH), real),
            pltpu.VMEM((1, WIDTH), real),
            pltpu.VMEM((2, width), real),
            pltpu.VMEM(spectral_weight.shape, real),
            pltpu.SemaphoreType.DMA((own_x + 5,)),
        ],
        weight_bytes * 4 * WIDTH,
        weight_bytes,
        out_specs=(far,) * 6,
    )(gradients, lift, predicted, stepped)
    return (
        phase_next,
        solute_next,
        predicted.reshape(phase.shape),
        grad_spectral,
        grad_local,
        grad_proj.reshape(WIDTH),
    )


def per_device(*arguments):
    count_x, count_y = lax.axis_size("gx"), lax.axis_size("gy")
    if fits(count_x, count_y, arguments[0], arguments[4]):
        return per_device_fast(*arguments)
    return per_device_plain(*arguments)


def solution(mesh):
    return jax.shard_map(
        per_device,
        mesh=mesh,
        in_specs=(
            P("gx", "gy", None),
            P("gx", "gy", None),
            P("gx", "gy", None),
            P(),
            P(None, "gx", "gy", None, None),
            P(),
            P(),
            P(),
            P("gx", "gy", None),
        ),
        out_specs=(
            P("gx", "gy", None),
            P("gx", "gy", None),
            P("gx", "gy", None),
            P(None, "gx", "gy", None, None),
            P(),
            P(),
        ),
        check_vma=False,
    )
```

```python
import functools
from functools import reduce
import math

import jax
import jax.numpy as jnp
import ml_dtypes
import numpy as np
from jax import lax
from jax.experimental import pallas as pl
from jax.experimental.pallas import tpu as pltpu
from jax.sharding import PartitionSpec as P

WIDTH = 32
KX = 32
KY = 32
KZ = 32


TIME_STEP = 0.05
COUPLING = 2.0
SOLID_DIFF = 0.05
LIQUID_DIFF = 1.0
PARTITION = 0.15
TRAP_RATE = 4.0
SOLUTE_MEAN = 0.5


def extended(cells, sides, width):
    for axis, dim in sides:
        count = lax.axis_size(axis)
        head = lax.slice_in_dim(cells, 0, width, axis=dim)
        tail = lax.slice_in_dim(cells, cells.shape[dim] - width, cells.shape[dim], axis=dim)
        cells = jnp.concatenate(
            [
                lax.ppermute(tail, axis, [(i, (i + 1) % count) for i in range(count)]),
                cells,
                lax.ppermute(head, axis, [((i + 1) % count, i) for i in range(count)]),
            ],
            axis=dim,
        )
    return cells


def diffusivity(phase_now):
    return SOLID_DIFF + (LIQUID_DIFF - SOLID_DIFF) * 0.5 * (1.0 - jnp.tanh(phase_now))


def update(phase_now, solute_now, undercool, phase_nb, solute_nb, diff_now, diff_nb):
    lap = reduce(jnp.add, phase_nb) - 6.0 * phase_now
    squares = 1.0 - phase_now * phase_now
    rate = (
        lap
        + phase_now
        - phase_now * phase_now * phase_now
        + COUPLING * squares * squares * (undercool - solute_now)
    )
    fluxes = [
        0.5 * (diff_now + diff_nb[index]) * (solute_nb[index] - solute_now) for index in range(6)
    ]
    divergence = reduce(jnp.add, fluxes)
    speed = TRAP_RATE * jnp.abs(rate)
    keff = (PARTITION + speed) / (1.0 + speed)
    phase_new = phase_now + TIME_STEP * rate
    solute_new = solute_now + TIME_STEP * (divergence + 0.5 * (1.0 - keff) * solute_now * rate)
    return (phase_new, solute_new)


def beside(padded):
    centre = padded[1:-1, 1:-1]
    return [
        padded[2:, 1:-1],
        padded[:-2, 1:-1],
        padded[1:-1, 2:],
        padded[1:-1, :-2],
        jnp.roll(centre, -1, 2),
        jnp.roll(centre, 1, 2),
    ]


def phase_sweep(phase_now, solute_now, undercool):
    padded = extended(jnp.stack([phase_now, solute_now]), (("gx", 1), ("gy", 2)), 1)
    phase_pad = padded[0]
    solute_pad = padded[1]
    diff_pad = diffusivity(phase_pad)
    return update(
        phase_now,
        solute_now,
        undercool,
        beside(phase_pad),
        beside(solute_pad),
        diff_pad[1:-1, 1:-1],
        beside(diff_pad),
    )


def signed_freq(indices, total):
    return jnp.where(indices < total // 2, indices, indices - total)


def wave_tables(freqs, positions, length, factor):
    product = freqs[:, None] * positions[None, :] % length
    angles = product.astype(jnp.float32) * (2.0 * math.pi / length)
    return (jnp.cos(angles) * factor, jnp.sin(angles) * factor)


def complex_mix(cosines, sines, data, pattern, orient):

    def apply(table, values):
        return jnp.einsum(pattern, table, values, precision=lax.Precision.HIGHEST)

    cos_real = apply(cosines, data[0])
    cos_imag = apply(cosines, data[1])
    sin_real = apply(sines, data[0])
    sin_imag = apply(sines, data[1])
    return jnp.stack([cos_real - orient * sin_imag, cos_imag + orient * sin_real])


def x_forward(data, factor):
    portion = lax.all_to_all(data, "gx", split_axis=1, concat_axis=2, tiled=True)
    length = portion.shape[2]
    cosines, sines = wave_tables(
        signed_freq(jnp.arange(KX, dtype=jnp.int32), KX),
        jnp.arange(length, dtype=jnp.int32),
        length,
        factor,
    )
    lines = complex_mix(cosines, sines, portion, "kx,wxyz->wkyz", -1.0)
    return lax.all_to_all(lines, "gx", split_axis=2, concat_axis=1, tiled=True)


def y_forward(data, factor):
    portion = lax.all_to_all(data, "gy", split_axis=1, concat_axis=3, tiled=True)
    length = portion.shape[3]
    cosines, sines = wave_tables(
        signed_freq(jnp.arange(KY, dtype=jnp.int32), KY),
        jnp.arange(length, dtype=jnp.int32),
        length,
        factor,
    )
    lines = complex_mix(cosines, sines, portion, "ky,wayz->wakz", -1.0)
    return lax.all_to_all(lines, "gy", split_axis=3, concat_axis=1, tiled=True)


def contract(weights, values):
    return jnp.einsum("abzoi,iabz->oabz", weights, values, precision=lax.Precision.HIGHEST)


def outer(left, right):
    return jnp.einsum("oabz,iabz->abzoi", left, right, precision=lax.Precision.HIGHEST)


def per_device_plain(
    phase,
    solute,
    undercool,
    lift_weight,
    spectral_weight,
    local_weight,
    local_bias,
    proj_weight,
    cotangent,
):
    phase_mid, solute_mid = phase_sweep(phase, solute, undercool)
    phase_next, solute_next = phase_sweep(phase_mid, solute_mid, undercool)
    cells_x, cells_y, depth = phase.shape
    total_x = cells_x * lax.axis_size("gx")
    total_y = cells_y * lax.axis_size("gy")
    fields = jnp.stack([phase_next, solute_next - SOLUTE_MEAN])
    modes_z = jnp.arange(KZ, dtype=jnp.int32)
    zpos = jnp.arange(depth, dtype=jnp.int32)
    unit_z = jnp.ones((KZ,), jnp.float32)
    weights_z = jnp.where(modes_z == 0, 1.0, 2.0).astype(jnp.float32) / depth

    def z_forward(field, zfactor):
        cosines, sines = wave_tables(modes_z, zpos, depth, zfactor[:, None])
        tables = jnp.stack([cosines, -sines])
        return jnp.einsum("wxyz,rkz->rwxyk", field, tables, precision=lax.Precision.HIGHEST)

    def spectral_forward(field, zfactor, xfactor, yfactor):
        return y_forward(x_forward(z_forward(field, zfactor), xfactor), yfactor)

    lifted = jnp.einsum("wc,cxyz->wxyz", lift_weight, fields, precision=lax.Precision.HIGHEST)
    spectrum = spectral_forward(lifted, unit_z, 1.0, 1.0)
    own_x = spectrum.shape[2]
    own_y = spectrum.shape[3]
    shaped = spectral_weight.reshape(2, own_x, own_y, KZ, WIDTH, WIDTH)
    out_real = contract(shaped[0], spectrum[0]) - contract(shaped[1], spectrum[1])
    out_imag = contract(shaped[0], spectrum[1]) + contract(shaped[1], spectrum[0])
    spectral_out = jnp.stack([out_real, out_imag])
    ypos = lax.axis_index("gy") * cells_y + jnp.arange(cells_y, dtype=jnp.int32)
    portion = lax.all_gather(spectral_out, "gy", axis=3, tiled=True)
    freqs = signed_freq(jnp.arange(portion.shape[3], dtype=jnp.int32), KY)
    cosines, sines = wave_tables(ypos, freqs, total_y, 1.0 / total_y)
    back_y = complex_mix(cosines, sines, portion, "yk,wakz->wayz", 1.0)
    cosines, sines = wave_tables(
        jnp.arange(total_x, dtype=jnp.int32),
        signed_freq(jnp.arange(KX, dtype=jnp.int32), KX),
        total_x,
        1.0 / total_x,
    )
    inverted = complex_mix(
        cosines,
        sines,
        lax.all_to_all(back_y, "gx", split_axis=1, concat_axis=2, tiled=True),
        "xk,wkyz->wxyz",
        1.0,
    )
    back_x = lax.all_to_all(inverted, "gx", split_axis=2, concat_axis=1, tiled=True)
    cos_back, sin_back = wave_tables(modes_z, zpos, depth, weights_z[:, None])
    back_tables = jnp.stack([cos_back, -sin_back])
    spectral_field = jnp.einsum(
        "rwxyk,rkz->wxyz", back_x, back_tables, precision=lax.Precision.HIGHEST
    )
    mixed = jnp.dot(local_weight, lift_weight, precision=lax.Precision.HIGHEST)
    pre_act = (
        spectral_field
        + jnp.einsum("wc,cxyz->wxyz", mixed, fields, precision=lax.Precision.HIGHEST)
        + local_bias[:, None, None, None]
    )
    activated, gelu_back = jax.vjp(jax.nn.gelu, pre_act)
    predicted = jnp.einsum("w,wxyz->xyz", proj_weight, activated, precision=lax.Precision.HIGHEST)
    grad_pre = gelu_back(proj_weight[:, None, None, None] * cotangent[None])[0]
    field_sums = jnp.einsum("wxyz,cxyz->wc", grad_pre, fields, precision=lax.Precision.HIGHEST)
    proj_sums = jnp.einsum("wxyz,xyz->w", activated, cotangent, precision=lax.Precision.HIGHEST)
    field_sums, proj_sums = lax.psum((field_sums, proj_sums), ("gx", "gy"))
    grad_modes = spectral_forward(grad_pre, weights_z, 1.0 / total_x, 1.0 / total_y)
    grad_real = outer(grad_modes[0], spectrum[0]) + outer(grad_modes[1], spectrum[1])
    grad_imag = outer(grad_modes[1], spectrum[0]) - outer(grad_modes[0], spectrum[1])
    grad_spectral = jnp.stack([grad_real, grad_imag]).reshape(2, own_x, own_y, KZ, WIDTH * WIDTH)
    scale = 1.0 / math.sqrt(total_x * total_y * depth)
    grad_local = jnp.dot(field_sums, lift_weight.T, precision=lax.Precision.HIGHEST) * scale
    grad_proj = proj_sums * scale
    return (phase_next, solute_next, predicted, grad_spectral, grad_local, grad_proj)


LANES = 128
SMALL_VMEM = 24 * 1024 * 1024
PACK_COST = 50_000_000_000
SPREAD = LANES // WIDTH
NARROW = jnp.bfloat16
EXACT = lax.Precision.HIGHEST


def halves(table):
    head = table.astype(np.float32).astype(ml_dtypes.bfloat16)
    rest = (table - head.astype(np.float64)).astype(np.float32).astype(ml_dtypes.bfloat16)
    return head, rest


def left_table(table):
    head, rest = halves(table)
    return np.concatenate([head, head, rest], axis=1)


def right_table(table):
    head, rest = halves(table)
    return np.concatenate([head, head, rest], axis=0)


def parts_of(values):
    head = values.astype(NARROW)
    return head, (values - head.astype(jnp.float32)).astype(NARROW)


def thrice(values, axis):
    head, rest = parts_of(values)
    return jnp.concatenate([head, rest, head], axis=axis)


def one_where(mask):
    return mask.astype(jnp.float32).astype(NARROW)


def mul(left, right):
    return jnp.dot(left, right, preferred_element_type=jnp.float32)


def mul_rows(left, right):
    return lax.dot_general(
        left, right, (((1,), (1,)), ((), ())), preferred_element_type=jnp.float32
    )


def angles(freqs, positions, length):
    return 2.0 * np.pi * ((freqs[:, None] * positions[None, :]) % length) / length


def signed(count):
    index = np.arange(count)
    return np.where(index < count // 2, index, index - count)


def rotation(theta, orient):
    cosines, sines = np.cos(theta), orient * np.sin(theta)
    return np.block([[cosines, -sines], [sines, cosines]])


def group_of(shape):
    return lax.broadcasted_iota(jnp.int32, shape, len(shape) - 1) // WIDTH


def pick(groups, choices):
    result = choices[-1]
    for index in range(len(choices) - 2, -1, -1):
        result = jnp.where(groups == index, choices[index], result)
    return result


def turn(values, shift):
    shift = shift % LANES
    return values if shift == 0 else pltpu.roll(values, shift, 1)


def swap_groups(pieces):
    groups = group_of(pieces[0].shape)
    return [
        pick(groups, [turn(pieces[i], WIDTH * (i - j)) for i in range(SPREAD)])
        for j in range(SPREAD)
    ]


def spread_cells(
    lift_ref, local_ref, bias_ref, proj_ref, cotangent_ref, vector_ref, mix_ref, spread_ref
):
    planes, depth, wide = spread_ref.shape
    tile = cotangent_ref.shape[0]
    cells_y = tile // planes
    lift, lift_rest = parts_of(lift_ref[...])
    local, local_rest = parts_of(local_ref[...])
    mixed = mul_rows(lift, local) + mul_rows(lift_rest, local) + mul_rows(lift, local_rest)
    for index in range(wide // WIDTH):
        place = slice(index * WIDTH, (index + 1) * WIDTH)
        vector_ref[0:2, place] = mixed
        vector_ref[2:3, place] = bias_ref[...]
        vector_ref[3:4, place] = proj_ref[...]
    head, rest = parts_of(vector_ref[...])
    row = lax.broadcasted_iota(jnp.int32, (cells_y, wide), 0)
    own = row == lax.broadcasted_iota(jnp.int32, (cells_y, wide), 1) // WIDTH

    def diagonal(line):
        return jnp.where(own, line.astype(jnp.float32), 0.0)

    mixing = [diagonal(part[k : k + 1]) for k in range(2) for part in (head, head, rest)]
    blank = jnp.zeros((2 * cells_y, wide), jnp.float32)
    mix_ref[...] = jnp.concatenate(mixing + [blank], axis=0).astype(NARROW)
    spread = jnp.concatenate(parts_of(cotangent_ref[...].T), axis=1)
    cell = lax.broadcasted_iota(jnp.int32, (2 * tile, wide), 0) % tile
    row = lax.broadcasted_iota(jnp.int32, (2 * tile, wide), 1) // WIDTH
    for plane in range(planes):
        spread_ref[plane] = mul(spread, one_where(cell == plane * cells_y + row))


def contract_kernel(
    planes,
    lift_ref,
    weight_ref,
    local_ref,
    bias_ref,
    proj_ref,
    cotangent_ref,
    out_ref,
    vector_ref,
    mix_ref,
    spread_ref,
):
    _, own_x, own_y, modes_z, width = weight_ref.shape
    chunk = out_ref.shape[0] // modes_z
    steps = own_x // planes

    square = (WIDTH, WIDTH)
    diagonal = lax.broadcasted_iota(jnp.int32, square, 0) == lax.broadcasted_iota(
        jnp.int32, square, 1
    )
    columns = [
        jnp.sum(
            jnp.where(diagonal, jnp.broadcast_to(lift_ref[k : k + 1, :], square), 0.0),
            axis=1,
            keepdims=True,
        )
        for k in range(2)
    ]
    lane = lax.broadcasted_iota(jnp.int32, (WIDTH, LANES), 1)
    base = jnp.where(
        lane % (2 * WIDTH) < WIDTH,
        jnp.broadcast_to(columns[0], lane.shape),
        jnp.broadcast_to(columns[1], lane.shape),
    )
    head, rest = parts_of(base)
    base = jnp.where(lane < 2 * WIDTH, head.astype(jnp.float32), rest.astype(jnp.float32))
    mixing = jnp.concatenate(
        [jnp.where(lane % WIDTH == channel, base, 0.0) for channel in range(WIDTH)], axis=0
    ).astype(NARROW)
    rows = planes * own_y * modes_z
    low = lax.broadcasted_iota(jnp.int32, (rows, LANES), 1) < 2 * WIDTH
    for step in range(steps):
        sums = []
        for part in range(2):
            block = weight_ref[part, step * planes : (step + 1) * planes]
            head, rest = parts_of(block.reshape(rows, width))
            total = mul(head, mixing) + mul(rest, mixing)
            sums.append(total + turn(total, 2 * WIDTH))
        result = jnp.where(low, sums[0], sums[1])
        for plane in range(planes):
            for row in range(own_y):
                first = (plane * own_y + row) * modes_z
                place = row * own_x + step * planes + plane
                out_ref[pl.ds(place, modes_z, stride=chunk), :] = result[
                    first : first + modes_z
                ]
    spread_cells(
        lift_ref,
        local_ref,
        bias_ref,
        proj_ref,
        cotangent_ref,
        vector_ref,
        mix_ref,
        spread_ref,
    )


def edge_kernel(held_ref, head_ref, tail_ref):
    cells_x = held_ref.shape[1]
    for index, reach in enumerate((2, 2, 1)):
        head_ref[2 * index : 2 * index + reach] = held_ref[index, 0:reach]
        tail_ref[2 * index : 2 * index + reach] = held_ref[index, cells_x - reach : cells_x]


def pack_kernel(held_ref, before_ref, after_ref, head_ref, tail_ref):
    _, cells_x, cells_y, _ = held_ref.shape
    for out, near, far in ((head_ref, 0, 1), (tail_ref, cells_y - 1, cells_y - 2)):
        for plane in range(cells_x):
            line = slice(plane, plane + 1)
            for index in range(2):
                out[2 * index, line] = held_ref[index, plane, near : near + 1]
                out[2 * index + 1, line] = held_ref[index, plane, far : far + 1]
            out[4, line] = held_ref[2, plane, near : near + 1]
        for index in range(2):
            out[5, 2 * index : 2 * index + 1] = before_ref[2 * index + 1, near : near + 1]
            out[5, 2 * index + 1 : 2 * index + 2] = after_ref[2 * index, near : near + 1]


def step_kernel(
    held_ref,
    before_ref,
    after_ref,
    low_ref,
    high_ref,
    table_ref,
    mixed_ref,
    fields_ref,
    send_ref,
    phase_ext,
    solute_ext,
    cool_ext,
    diff_ext,
    lines,
):
    _, cells_x, cells_y, depth = held_ref.shape
    base = 8
    end = base + cells_y
    for index, ext in enumerate((phase_ext, solute_ext)):
        first = 2 * index
        ext[2 : cells_x + 2, base:end] = held_ref[index]
        ext[0:2, base:end] = before_ref[first : first + 2]
        ext[cells_x + 2 : cells_x + 4, base:end] = after_ref[first : first + 2]
        for source, near, far in ((low_ref, base - 1, base - 2), (high_ref, end, end + 1)):
            for plane in range(cells_x):
                line = slice(plane, plane + 1)
                ext[plane + 2, near : near + 1] = source[first, line]
                ext[plane + 2, far : far + 1] = source[first + 1, line]
            ext[1, near : near + 1] = source[5, first : first + 1]
            ext[cells_x + 2, near : near + 1] = source[5, first + 1 : first + 2]
    cool_ext[2 : cells_x + 2, base:end] = held_ref[2]
    cool_ext[1:2, base:end] = before_ref[4:5]
    cool_ext[cells_x + 2 : cells_x + 3, base:end] = after_ref[4:5]
    for plane in range(cells_x):
        line = slice(plane, plane + 1)
        cool_ext[plane + 2, base - 1 : base] = low_ref[4, line]
        cool_ext[plane + 2, end : end + 1] = high_ref[4, line]

    def sweep(reach):
        diff_ext[...] = diffusivity(phase_ext[...])

        def window(ext, move_x, move_y):
            return ext[
                2 - reach + move_x : cells_x + 2 + reach + move_x,
                base - reach + move_y : end + reach + move_y,
            ]

        def around(ext, now):
            return [
                window(ext, 1, 0),
                window(ext, -1, 0),
                window(ext, 0, 1),
                window(ext, 0, -1),
                pltpu.roll(now, depth - 1, 2),
                pltpu.roll(now, 1, 2),
            ]

        phase_now = window(phase_ext, 0, 0)
        solute_now = window(solute_ext, 0, 0)
        diff_now = window(diff_ext, 0, 0)
        return update(
            phase_now,
            solute_now,
            window(cool_ext, 0, 0),
            around(phase_ext, phase_now),
            around(solute_ext, solute_now),
            diff_now,
            around(diff_ext, diff_now),
        )

    phase_mid, solute_mid = sweep(1)
    phase_ext[1 : cells_x + 3, base - 1 : end + 1] = phase_mid
    solute_ext[1 : cells_x + 3, base - 1 : end + 1] = solute_mid
    phase_next, solute_next = sweep(0)
    fields_ref[0] = phase_next
    fields_ref[1] = solute_next
    tile = cells_x * cells_y
    both = (phase_next.reshape(tile, depth), solute_next.reshape(tile, depth) - SOLUTE_MEAN)
    ordered = []
    for part in range(depth // LANES):
        for index, values in enumerate(both):
            lines[part, index * tile : (index + 1) * tile] = values[
                :, part * LANES : (part + 1) * LANES
            ]
        ordered.append(
            jnp.concatenate(
                [
                    lines[part, pl.ds(row, 2 * cells_x, stride=cells_y), :]
                    for row in range(cells_y)
                ],
                axis=0,
            )
        )
    ordered = jnp.concatenate(ordered, axis=1)
    spectra = mul_rows(table_ref[...], thrice(ordered, 1))
    send_ref[...] = mixed_ref[...]
    modes_z = spectra.shape[0] // 2
    chunk = send_ref.shape[0] // modes_z
    for part in range(2):
        send_ref[pl.ds(chunk - 2 + part, modes_z, stride=chunk), :] = spectra[
            part * modes_z : (part + 1) * modes_z
        ]


def pack_modes(shape, modes, modes_ref, rows_ref):
    count_x, count_y, _, _, own_x, own_y = shape
    modes_x, modes_y = count_x * own_x, count_y * own_y
    lane = lax.broadcasted_iota(jnp.int32, (modes_y, LANES), 1)
    for index in range(count_x):
        block = modes
        for k in range(4):
            shift = k * own_x - k * modes_x - index * own_x
            block = jnp.where(lane // own_x == k, turn(modes, shift), block)
        rows_ref[index] = block
        line = rows_ref[index, pl.ds(0, count_y, stride=own_y), :]
        groups = group_of(line.shape)
        for row in range(1, own_y):
            piece = rows_ref[index, pl.ds(row, count_y, stride=own_y), :]
            line = jnp.where(groups == row, turn(piece, row * WIDTH), line)
        modes_ref[index * count_y : (index + 1) * count_y] = line


def spectral_kernel(
    shape,
    mixed_ref,
    y_in_ref,
    x_in_ref,
    y_out_ref,
    x_out_ref,
    fields_ref,
    forth_ref,
    chosen_ref,
    gather_ref,
    modes_ref,
    send_ref,
    table_ref,
    line_ref,
    lines_y,
    lines_x,
    rows_ref,
    weight_ref,
):
    count_x, count_y, cells_x, cells_y, own_x, own_y = shape
    modes_x, modes_y = count_x * own_x, count_y * own_y
    total_x, total_y = count_x * cells_x, count_y * cells_y
    tile = cells_x * cells_y
    narrow = 2 * cells_x
    rows = 2 * count_y
    devices = count_x * count_y
    own = own_x * own_y
    chunk = mixed_ref.shape[0] // devices
    spectra = [mixed_ref[pl.ds(own + part, devices, stride=chunk), :] for part in range(2)]
    for index in range(devices):
        weight_ref[index * own : (index + 1) * own, :] = mixed_ref[
            index * chunk : index * chunk + own, :
        ]
    lane = lax.broadcasted_iota(jnp.int32, (rows, LANES), 1)
    blocks = []
    for row in range(cells_y):
        block = jnp.zeros((rows, LANES), jnp.float32)
        for index in range(count_x):
            piece = jnp.concatenate(
                [values[index * count_y : (index + 1) * count_y] for values in spectra], axis=0
            )
            piece = turn(piece, narrow * (index - row))
            block = jnp.where(lane // narrow == index, piece, block)
        blocks.append(block)
    along_y = mul(y_in_ref[...], thrice(jnp.concatenate(blocks, axis=0), 0))
    half = lax.broadcasted_iota(jnp.int32, (modes_y, LANES), 1) < LANES // 2
    joined = jnp.where(half, along_y[0:modes_y], turn(along_y[modes_y:], LANES // 2))
    modes = mul(thrice(joined, 1), x_in_ref[...])
    quads_y = total_y // SPREAD
    quads_x = modes_x // SPREAD
    lane = lax.broadcasted_iota(jnp.int32, (modes_y, LANES), 1) % modes_x
    chosen = jnp.concatenate(
        [jnp.where(lane == freq, modes, 0.0) for freq in range(modes_x)], axis=0
    )
    columns = mul(jnp.concatenate(parts_of(chosen), axis=1), chosen_ref[...])
    low = lax.broadcasted_iota(jnp.int32, (modes_y, LANES), 1) < 2 * WIDTH
    products = [[], []]
    for quad in range(quads_x):
        lines = [[], []]
        for index in range(SPREAD):
            freq = SPREAD * quad + index
            start = (freq // own_x) * count_y * own_y * own_x + freq % own_x
            weights = weight_ref[pl.ds(start, modes_y, stride=own_x), :]
            for part in range(2):
                column = columns[
                    freq * modes_y : (freq + 1) * modes_y, part * LANES : (part + 1) * LANES
                ]
                line = weights * column
                lines[part].append(line + turn(line, 2 * WIDTH))
        for part in range(2):
            pairs = [
                jnp.where(low, lines[part][index], lines[part][index + 1])
                for index in range(0, SPREAD, 2)
            ]
            products[part].append(jnp.concatenate(pairs, axis=1))
    products = jnp.concatenate(products[0] + products[1], axis=0)
    products = mul(jnp.concatenate(parts_of(products), axis=1), gather_ref[...])
    stacked = [
        jnp.concatenate(
            [
                products[(part * quads_x + quad) * modes_y : (part * quads_x + quad + 1) * modes_y]
                for part in range(2)
            ],
            axis=0,
        )
        for quad in range(quads_x)
    ]
    back = mul(y_out_ref[...], thrice(jnp.concatenate(stacked, axis=1), 0))
    for quad in range(quads_x):
        lines_y[quad] = back[:, quad * LANES : (quad + 1) * LANES]
    for quad in range(quads_x):
        for part in range(2):
            pieces = [
                lines_y[quad, pl.ds(part * total_y + i, quads_y, stride=SPREAD), :]
                for i in range(SPREAD)
            ]
            for index, piece in enumerate(swap_groups(pieces)):
                place = part * modes_x + SPREAD * quad + index
                lines_x[pl.ds(place, quads_y, stride=2 * modes_x), :] = piece
    per_tile = cells_y // SPREAD
    blocks = [
        lines_x[quad * 2 * modes_x : (quad + 1) * 2 * modes_x, :] for quad in range(quads_y)
    ]
    back = mul(x_out_ref[...], thrice(jnp.concatenate(blocks, axis=1), 0))
    for quad in range(quads_y):
        for part in range(2):
            for index in range(count_x):
                device = index * count_y + quad // per_tile
                place = (device * 2 + part) * per_tile + quad % per_tile
                first = part * total_x + index * cells_x
                send_ref[place * cells_x : (place + 1) * cells_x, :] = back[
                    first : first + cells_x, quad * LANES : (quad + 1) * LANES
                ]
    pack_modes(shape, modes, modes_ref, rows_ref)
    prepare(fields_ref, forth_ref, table_ref, line_ref)


def prepare(fields_ref, forth_ref, table_ref, line_ref):
    planes, depth, _ = table_ref.shape
    cells_y = fields_ref.shape[2]
    tile = planes * cells_y
    rows = forth_ref.shape[0] // 2
    fields = (fields_ref[0].reshape(tile, depth), fields_ref[1].reshape(tile, depth) - SOLUTE_MEAN)
    blank = jnp.zeros((2 * cells_y, depth), jnp.float32)
    table = forth_ref[rows:].astype(jnp.float32)
    for plane in range(planes):
        lines = [values[plane * cells_y : (plane + 1) * cells_y] for values in fields]
        pieces = [[part.astype(jnp.float32) for part in parts_of(values)] for values in lines]
        both = [piece for head, rest in pieces for piece in (head, rest, head)]
        both = jnp.concatenate([table] + both + [blank], axis=0)
        table_ref[plane] = both.T.astype(NARROW)
        pieces = [piece for pair in zip(*pieces) for piece in pair]
        line_ref[plane] = jnp.concatenate(pieces, axis=0).astype(NARROW)


def fold_channels(values):
    quarter = values.shape[0] // SPREAD
    parts = []
    for first in range(0, values.shape[1], LANES):
        pieces = [
            values[index * quarter : (index + 1) * quarter, first : first + LANES]
            for index in range(SPREAD)
        ]
        channel = lax.broadcasted_iota(jnp.int32, pieces[0].shape, 1) % WIDTH
        span = WIDTH // 2
        while len(pieces) > 1:
            low = channel % (2 * span) < span
            pieces = [
                jnp.where(low, left + turn(left, -span), right + turn(right, span))
                for left, right in zip(pieces[: len(pieces) // 2], pieces[len(pieces) // 2 :])
            ]
            span //= 2
        parts.append(pieces[0])
    return jnp.concatenate(parts, axis=1)


def field_kernel(
    cells_y,
    field_ref,
    table_ref,
    mix_ref,
    weight_ref,
    line_ref,
    vector_ref,
    back_ref,
    forth_ref,
    predicted_ref,
    send_ref,
    shares_ref,
):
    planes, depth, wide = weight_ref.shape
    rows = forth_ref.shape[0] // 2
    halves_y = cells_y // SPREAD
    stride = halves_y * planes
    bias = vector_ref[2:3, :]
    proj = vector_ref[3:4, :]
    root = math.sqrt(2.0 / math.pi)
    curve = 0.044715
    picker = one_where(
        lax.broadcasted_iota(jnp.int32, (SPREAD * cells_y, 2 * wide), 0)
        == lax.broadcasted_iota(jnp.int32, (SPREAD * cells_y, 2 * wide), 1)
        % wide
        // (WIDTH // SPREAD)
    )
    line_sums = jnp.zeros((2 * cells_y, wide), jnp.float32)
    proj_sums = jnp.zeros((8, wide), jnp.float32)
    for plane in range(planes):
        spectra = jnp.concatenate(
            [
                field_ref[pl.ds(part * planes + plane, rows, stride=stride), :]
                for part in range(halves_y)
            ],
            axis=1,
        )
        spectra = jnp.concatenate([thrice(spectra, 0), mix_ref[...]], axis=0)
        back = jnp.concatenate([back_ref[...], table_ref[plane]], axis=1)
        pre = mul(back, spectra) + bias
        square = pre * pre
        bent = jnp.tanh(pre * (root + (root * curve) * square))
        upper = 0.5 + 0.5 * bent
        active = pre * upper
        slope = upper + (active - active * bent) * (root + (3.0 * root * curve) * square)
        cotangent = weight_ref[plane]
        weighted = proj * cotangent
        grad = weighted * slope
        share = mul_rows(
            picker, jnp.concatenate(parts_of(fold_channels(proj * active)), axis=1)
        )
        shares_ref[plane, :, 0 : depth // SPREAD] = share
        for index in range(SPREAD):
            predicted_ref[
                plane * cells_y : (plane + 1) * cells_y,
                index * (depth // SPREAD) : (index + 1) * (depth // SPREAD),
            ] = shares_ref[plane, pl.ds(index, cells_y, stride=SPREAD), 0 : depth // SPREAD]
        head, rest = parts_of(grad)
        lines = line_ref[plane]
        top = jnp.concatenate([forth_ref[0:rows], lines[0 : 2 * cells_y]], axis=0)
        low = jnp.concatenate([forth_ref[rows:], lines[2 * cells_y :]], axis=0)
        spectra = mul(jnp.concatenate([top, low], axis=0), head)
        spectra = spectra[0 : rows + 2 * cells_y] + spectra[rows + 2 * cells_y :] + mul(top, rest)
        for part in range(halves_y):
            send_ref[pl.ds(part * planes + plane, rows, stride=stride), :] = spectra[
                0:rows, part * LANES : (part + 1) * LANES
            ]
        line_sums = line_sums + spectra[rows:]
        proj_sums = proj_sums + jnp.sum(
            (active * cotangent).reshape(depth // 8, 8, wide), axis=0
        )
    shape = (cells_y, wide)
    own = lax.broadcasted_iota(jnp.int32, shape, 0) == (
        lax.broadcasted_iota(jnp.int32, shape, 1) // WIDTH
    )
    sums = [
        jnp.where(own, line_sums[0:cells_y], 0.0),
        jnp.where(own, line_sums[cells_y:], 0.0),
        proj_sums,
    ]
    for index, values in enumerate(sums):
        line = jnp.sum(values, axis=0, keepdims=True)
        line = sum(line[:, part * LANES : (part + 1) * LANES] for part in range(halves_y))
        send_ref[stride + index : stride + index + 1, :] = line


def gradient_kernel(
    shape, spectra_ref, modes_ref, x_in_ref, y_in_ref, send_ref, lines_x, lines_y
):
    count_x, count_y, cells_x, cells_y, own_x, own_y = shape
    modes_x, modes_y = count_x * own_x, count_y * own_y
    total_x, total_y = count_x * cells_x, count_y * cells_y
    per_tile = cells_y // SPREAD
    quads_y = total_y // SPREAD
    chunk = 2 * per_tile * cells_x
    first_device = (lax.axis_index("gx") == 0) & (lax.axis_index("gy") == 0)
    keep = jnp.where(first_device, 0.0, 1.0)
    blocks = []
    for quad in range(quads_y):
        block = []
        for part in range(2):
            for index in range(count_x):
                device = index * count_y + quad // per_tile
                place = (device * 2 + part) * per_tile + quad % per_tile
                piece = spectra_ref[place * cells_x : (place + 1) * cells_x, :]
                block.append(piece * keep if part else piece)
        blocks.append(jnp.concatenate(block, axis=0))
    forth = mul(x_in_ref[...], thrice(jnp.concatenate(blocks, axis=1), 0))
    for quad in range(quads_y):
        lines_x[quad * 2 * modes_x : (quad + 1) * 2 * modes_x, :] = forth[
            :, quad * LANES : (quad + 1) * LANES
        ]
    devices = count_x * count_y
    out_chunk = send_ref.shape[0] // devices
    per_own = own_x // SPREAD
    quads_x = modes_x // SPREAD
    for quad in range(quads_x):
        for part in range(2):
            pieces = [
                lines_x[
                    pl.ds(part * modes_x + SPREAD * quad + j, quads_y, stride=2 * modes_x), :
                ]
                for j in range(SPREAD)
            ]
            for index, piece in enumerate(swap_groups(pieces)):
                lines_y[quad, pl.ds(part * total_y + index, quads_y, stride=SPREAD), :] = piece
    lines = jnp.concatenate([lines_y[quad] for quad in range(quads_x)], axis=1)
    modes = mul(y_in_ref[...], thrice(lines, 0))
    for quad in range(quads_x):
        for part in range(2):
            for index in range(count_y):
                device = (quad // per_own) * count_y + index
                place = device * out_chunk + (part * per_own + quad % per_own) * own_y
                first = part * modes_y + index * own_y
                send_ref[place : place + own_y, :] = modes[
                    first : first + own_y, quad * LANES : (quad + 1) * LANES
                ]
    extra = 2 * per_own * own_y
    send_ref[pl.ds(extra, devices, stride=out_chunk), :] = modes_ref[...]
    groups = group_of((1, LANES))
    total = jnp.zeros((1, LANES), jnp.float32)
    for index in range(3):
        start = chunk // 2 + index
        line = jnp.sum(
            spectra_ref[pl.ds(start, devices, stride=chunk), :], axis=0, keepdims=True
        )
        line = line + turn(line, 2 * WIDTH)
        total = jnp.where(groups == index, line + turn(line, WIDTH), total)
    send_ref[pl.ds(extra + 1, devices, stride=out_chunk), :] = jnp.broadcast_to(
        total, (devices, LANES)
    )


def outer_kernel(
    scale,
    modes_ref,
    narrow_ref,
    predicted_ref,
    fields_ref,
    repeat_ref,
    spread_ref,
    local_out,
    proj_out,
    predicted_out,
    phase_out,
    solute_out,
    grad_ref,
    mix_ref,
    local_ref,
    proj_ref,
    lift_ref,
    held,
    sent,
):
    _, own_x, own_y, modes_z, width = held.shape
    chunk = modes_ref.shape[0] // modes_z
    per_own = own_x // SPREAD
    extra = 2 * per_own * own_y
    copies = [
        pltpu.make_async_copy(predicted_ref, predicted_out, sent.at[own_x]),
        pltpu.make_async_copy(fields_ref.at[0], phase_out, sent.at[own_x + 1]),
        pltpu.make_async_copy(fields_ref.at[1], solute_out, sent.at[own_x + 2]),
    ]
    for copy in copies:
        copy.start()
    for index in range(SPREAD):
        lift_ref[:, index * WIDTH : (index + 1) * WIDTH] = narrow_ref[...]
    for index in range(1, width // LANES):
        lift_ref[:, index * LANES : (index + 1) * LANES] = lift_ref[:, 0:LANES]
    shape = (2 * WIDTH, width)
    row = lax.broadcasted_iota(jnp.int32, shape, 0)
    column = lax.broadcasted_iota(jnp.int32, shape, 1)
    lift = jnp.where(row < WIDTH, lift_ref[0:1, :], lift_ref[1:2, :])
    head, rest = parts_of(jnp.where(column // WIDTH == row % WIDTH, lift, 0.0))
    mix_ref[0 : 2 * WIDTH] = head
    mix_ref[2 * WIDTH : 4 * WIDTH] = head
    mix_ref[4 * WIDTH : 6 * WIDTH] = rest
    mix_ref[6 * WIDTH : 8 * WIDTH] = jnp.zeros_like(rest)
    lane = lax.broadcasted_iota(jnp.int32, (modes_z, LANES), 1)
    low = lane < 2 * WIDTH

    def rows_of(values):
        head, rest = parts_of(values)
        both = jnp.where(low, head.astype(jnp.float32), rest.astype(jnp.float32)).astype(NARROW)
        return jnp.concatenate([both, head], axis=1)

    line = modes_ref[extra + 1 : extra + 2, :]
    square = (WIDTH, WIDTH)
    diagonal = lax.broadcasted_iota(jnp.int32, square, 0) == lax.broadcasted_iota(
        jnp.int32, square, 1
    )
    local = jnp.zeros(square, jnp.float32)
    for k in range(2):
        sums = jnp.broadcast_to(line[:, k * WIDTH : (k + 1) * WIDTH], square)
        sums = jnp.sum(jnp.where(diagonal, sums, 0.0), axis=1, keepdims=True)
        local = local + sums * narrow_ref[k : k + 1, :]
    local_ref[...] = scale * local
    proj_ref[...] = scale * line[:, 2 * WIDTH : 3 * WIDTH]
    copies.append(pltpu.make_async_copy(local_ref, local_out, sent.at[own_x + 3]))
    copies.append(pltpu.make_async_copy(proj_ref, proj_out, sent.at[own_x + 4]))
    copies[3].start()
    copies[4].start()
    grads = jnp.concatenate(
        [modes_ref[pl.ds(place, modes_z, stride=chunk), :] for place in range(extra)], axis=0
    )
    grads = mul(jnp.concatenate(parts_of(grads), axis=1), repeat_ref[...])
    modes = modes_ref[pl.ds(extra, modes_z, stride=chunk), :]
    own = lane // (4 * own_x) * own_x + lane % own_x
    for plane in range(own_x):
        chosen = jnp.concatenate(
            [jnp.where(own == row * own_x + plane, modes, 0.0) for row in range(own_y)], axis=0
        )
        columns = mul(jnp.concatenate(parts_of(chosen), axis=1), spread_ref[...])
        reals, imags = [], []
        for row in range(own_y):
            real = columns[row * modes_z : (row + 1) * modes_z, 0:LANES]
            imag = columns[row * modes_z : (row + 1) * modes_z, LANES:]
            pair = []
            for part in range(2):
                first = ((part * per_own + plane // SPREAD) * own_y + row) * modes_z
                group = plane % SPREAD * LANES
                pair.append(grads[first : first + modes_z, group : group + LANES])
            reals.append(rows_of(pair[0] * real + pair[1] * imag))
            imags.append(rows_of(pair[1] * real - pair[0] * imag))
        result = mul(jnp.concatenate(reals + imags, axis=0), mix_ref[...])
        held[:, plane] = result.reshape(2, own_y, modes_z, width)
        copies.append(
            pltpu.make_async_copy(held.at[:, plane], grad_ref.at[:, plane], sent.at[plane])
        )
        copies[-1].start()
    for copy in copies:
        copy.wait()


def tables(shape, depth, modes_z):
    count_x, count_y, cells_x, cells_y, own_x, own_y = shape
    modes_x, modes_y = count_x * own_x, count_y * own_y
    total_x, total_y = count_x * cells_x, count_y * cells_y
    theta_z = angles(np.arange(modes_z), np.arange(depth), depth)
    theta_x = angles(signed(modes_x), np.arange(total_x), total_x)
    theta_y = angles(signed(modes_y), np.arange(total_y), total_y)
    plain_z = np.concatenate([np.cos(theta_z), -np.sin(theta_z)], axis=0)
    forth_z = plain_z.reshape(2, modes_z, depth).transpose(1, 0, 2).reshape(2 * modes_z, depth)
    weight = np.where(np.arange(modes_z) == 0, 1.0, 2.0) / (total_x * total_y * depth)
    weighted_z = np.repeat(weight, 2)[:, None] * forth_z
    forth_x, back_x = rotation(theta_x, -1.0), rotation(theta_x.T, 1.0)
    forth_y, back_y = rotation(theta_y, -1.0), rotation(theta_y.T, 1.0)
    order_y = forth_y.reshape(2 * modes_y, 2, count_y, cells_y)
    order_y = order_y.transpose(0, 3, 1, 2).reshape(2 * modes_y, 2 * total_y)
    lines = forth_x.reshape(2, modes_x, 2, count_x, cells_x)
    both = np.zeros((2, count_x, 2, cells_x, 2, 2, modes_x))
    for field in range(2):
        both[:, :, field, :, :, field, :] = lines.transpose(2, 3, 4, 0, 1)
    both = both.reshape(4 * total_x, 4 * modes_x)
    index = np.arange(4 * LANES)
    line = index[: 2 * LANES, None] % LANES
    group = index[None, : 2 * LANES] // WIDTH
    same = np.where(group < 4, group, (group + 2) % 4)
    signs = np.where((group == 2) | (group == 3), -1.0, 1.0)
    chosen = np.where(line // modes_x == same, signs, 0.0)
    half = 2 * WIDTH
    row, column = index[:, None] % (SPREAD * half), index[None, :LANES]
    gather = row // half * WIDTH + row % WIDTH == column
    repeat = line == index[None, :] // LANES * WIDTH + index[None, :] % WIDTH
    spread = line // own_x % 4 == group // 4 * 2 + group % 2
    masks = {"chosen": chosen, "gather": gather, "repeat": repeat, "spread": spread}
    masks = {name: mask.astype(ml_dtypes.bfloat16) for name, mask in masks.items()}
    return masks | {
        "z_plain": left_table(plain_z),
        "z_forth": np.concatenate(halves(weighted_z), axis=0),
        "z_back": left_table(weighted_z.T)[:, : 4 * modes_z],
        "y_first": left_table(order_y),
        "x_first": right_table(both),
        "y_back": left_table(back_y),
        "x_back": left_table(back_x),
        "x_forth": left_table(forth_x),
        "y_forth": left_table(forth_y),
    }


def fits(count_x, count_y, phase, spectral_weight):
    cells_x, cells_y, depth = phase.shape
    _, own_x, own_y, modes_z, width = spectral_weight.shape
    return (
        width == WIDTH * WIDTH
        and modes_z == count_x * count_y
        and 4 * modes_z == LANES
        and 4 * count_x * cells_x == LANES
        and 4 * count_x * own_x == LANES
        and 2 * cells_x * cells_y == LANES
        and cells_x == 8
        and cells_y % SPREAD == 0
        and own_x % SPREAD == 0
        and own_y * 4 * own_x == LANES
        and 3 * WIDTH <= LANES
        and cells_y == 8
        and depth % LANES == 0
    )


def call(kernel, outs, scratch, flops, moved, limit=SMALL_VMEM, **more):
    return pl.pallas_call(
        kernel,
        out_shape=outs,
        scratch_shapes=scratch,
        compiler_params=pltpu.CompilerParams(vmem_limit_bytes=limit),
        cost_estimate=pl.CostEstimate(flops=flops, bytes_accessed=moved, transcendentals=0),
        **more,
    )


def exchange(values):
    return lax.all_to_all(values, ("gx", "gy"), split_axis=0, concat_axis=0, tiled=True)


def per_device_fast(
    phase,
    solute,
    undercool,
    lift_weight,
    spectral_weight,
    local_weight,
    local_bias,
    proj_weight,
    cotangent,
):
    count_x, count_y = lax.axis_size("gx"), lax.axis_size("gy")
    cells_x, cells_y, depth = phase.shape
    _, own_x, own_y, modes_z, width = spectral_weight.shape
    shape = (count_x, count_y, cells_x, cells_y, own_x, own_y)
    devices = count_x * count_y
    tile = cells_x * cells_y
    modes_x, modes_y = count_x * own_x, count_y * own_y
    total_x, total_y = count_x * cells_x, count_y * cells_y
    table = tables(shape, depth, modes_z)
    real = jnp.float32

    def like(*dims):
        return jax.ShapeDtypeStruct(dims, real)

    far = pl.BlockSpec(memory_space=pltpu.HBM)
    weight_bytes = 8 * own_x * own_y * modes_z * width
    held = jnp.stack([phase, solute, undercool])
    head, tail = call(
        edge_kernel,
        (like(5, cells_y, depth), like(5, cells_y, depth)),
        [],
        1000,
        40 * tile * depth,
    )(held)

    def ring(values, axis, step):
        count = lax.axis_size(axis)
        return lax.ppermute(values, axis, [(i, (i + step) % count) for i in range(count)])

    head, tail, lift = lax.optimization_barrier((head, tail, lift_weight.T))
    before, after = ring(tail, "gx", 1), ring(head, "gx", -1)
    planes = 2
    spread_shape = (cells_x, depth, cells_y * WIDTH)
    mixed_weights, vectors, mixing, weight = call(
        functools.partial(contract_kernel, planes),
        (
            like(modes_z * (own_x * own_y + 2), LANES),
            like(4, cells_y * WIDTH),
            jax.ShapeDtypeStruct((8 * cells_y, cells_y * WIDTH), NARROW),
            like(*spread_shape),
        ),
        [],
        weight_bytes * LANES,
        weight_bytes,
    )(
        lift,
        spectral_weight,
        local_weight,
        local_bias.reshape(1, WIDTH),
        proj_weight.reshape(1, WIDTH),
        cotangent.reshape(tile, depth),
    )
    head, tail = call(
        pack_kernel,
        (like(6, cells_x, depth), like(6, cells_x, depth)),
        [],
        PACK_COST,
        40 * tile * depth,
    )(held, before, after)
    low, high = ring(tail, "gy", 1), ring(head, "gy", -1)
    extended_shape = pltpu.VMEM((cells_x + 4, cells_y + 16, depth), real)
    stepped, spectra = call(
        step_kernel,
        (like(2, *phase.shape), like(*mixed_weights.shape)),
        [extended_shape] * 4 + [pltpu.VMEM((depth // LANES, 2 * tile, LANES), real)],
        400 * tile * depth,
        80 * tile * depth,
    )(held, before, after, low, high, table["z_plain"], mixed_weights)
    gathered = exchange(spectra.reshape(-1, 2, LANES)).reshape(spectra.shape)
    modes, fields, lines, own_lines = call(
        functools.partial(spectral_kernel, shape),
        (
            like(devices, LANES),
            like(devices * 2 * cells_x * (cells_y // SPREAD), LANES),
            jax.ShapeDtypeStruct((cells_x, depth, LANES), NARROW),
            jax.ShapeDtypeStruct((cells_x, 4 * cells_y, depth), NARROW),
        ),
        [
            pltpu.VMEM((modes_x // SPREAD, 2 * total_y, LANES), real),
            pltpu.VMEM((2 * modes_x * (total_y // SPREAD), LANES), real),
            pltpu.VMEM((count_x, modes_y, LANES), real),
            pltpu.VMEM((devices * own_x * own_y, LANES), real),
        ],
        100_000_000,
        2_000_000,
    )(
        gathered,
        table["y_first"],
        table["x_first"],
        table["y_back"],
        table["x_back"],
        stepped,
        table["z_forth"],
        table["chosen"],
        table["gather"],
    )
    fields = exchange(fields)
    predicted, spectra = call(
        functools.partial(field_kernel, cells_y),
        (like(tile, depth), like(*fields.shape)),
        [pltpu.VMEM((cells_x, SPREAD * cells_y, LANES), real)],
        1_000_000_000,
        2_000_000,
    )(fields, lines, mixing, weight, own_lines, vectors, table["z_back"], table["z_forth"])
    spectra = exchange(spectra)
    chunk = 2 * own_x * own_y * WIDTH // LANES + 2
    gradients = call(
        functools.partial(gradient_kernel, shape),
        like(devices * chunk, LANES),
        [
            pltpu.VMEM((2 * modes_x * (total_y // SPREAD), LANES), real),
            pltpu.VMEM((modes_x // SPREAD, 2 * total_y, LANES), real),
        ],
        100_000_000,
        2_000_000,
    )(spectra, modes, table["x_forth"], table["y_forth"])
    gradients = exchange(gradients.reshape(-1, 2, LANES)).reshape(gradients.shape)
    grad_local, grad_proj, predicted, phase_next, solute_next, grad_spectral = call(
        functools.partial(outer_kernel, 1.0 / math.sqrt(total_x * total_y * depth)),
        (
            like(WIDTH, WIDTH),
            like(1, WIDTH),
            like(*predicted.shape),
            like(*phase.shape),
            like(*phase.shape),
            like(*spectral_weight.shape),
        ),
        [
            pltpu.VMEM((8 * WIDTH, width), NARROW),
            pltpu.VMEM((WIDTH, WIDTH), real),
            pltpu.VMEM((1, WIDTH), real),
            pltpu.VMEM((2, width), real),
            pltpu.VMEM(spectral_weight.shape, real),
            pltpu.SemaphoreType.DMA((own_x + 5,)),
        ],
        weight_bytes * 4 * WIDTH,
        weight_bytes,
        out_specs=(far,) * 6,
    )(gradients, lift, predicted, stepped, table["repeat"], table["spread"])
    return (
        phase_next,
        solute_next,
        predicted.reshape(phase.shape),
        grad_spectral,
        grad_local,
        grad_proj.reshape(WIDTH),
    )


def per_device(*arguments):
    count_x, count_y = lax.axis_size("gx"), lax.axis_size("gy")
    if fits(count_x, count_y, arguments[0], arguments[4]):
        return per_device_fast(*arguments)
    return per_device_plain(*arguments)


def solution(mesh):
    return jax.shard_map(
        per_device,
        mesh=mesh,
        in_specs=(
            P("gx", "gy", None),
            P("gx", "gy", None),
            P("gx", "gy", None),
            P(),
            P(None, "gx", "gy", None, None),
            P(),
            P(),
            P(),
            P("gx", "gy", None),
        ),
        out_specs=(
            P("gx", "gy", None),
            P("gx", "gy", None),
            P("gx", "gy", None),
            P(None, "gx", "gy", None, None),
            P(),
            P(),
        ),
        check_vma=False,
    )
```

```python
import functools
from functools import reduce
import math

import jax
import jax.numpy as jnp
import ml_dtypes
import numpy as np
from jax import lax
from jax.experimental import pallas as pl
from jax.experimental.pallas import tpu as pltpu
from jax.sharding import PartitionSpec as P

WIDTH = 32
KX = 32
KY = 32
KZ = 32


TIME_STEP = 0.05
COUPLING = 2.0
SOLID_DIFF = 0.05
LIQUID_DIFF = 1.0
PARTITION = 0.15
TRAP_RATE = 4.0
SOLUTE_MEAN = 0.5


def extended(cells, sides, width):
    for axis, dim in sides:
        count = lax.axis_size(axis)
        head = lax.slice_in_dim(cells, 0, width, axis=dim)
        tail = lax.slice_in_dim(cells, cells.shape[dim] - width, cells.shape[dim], axis=dim)
        cells = jnp.concatenate(
            [
                lax.ppermute(tail, axis, [(i, (i + 1) % count) for i in range(count)]),
                cells,
                lax.ppermute(head, axis, [((i + 1) % count, i) for i in range(count)]),
            ],
            axis=dim,
        )
    return cells


def diffusivity(phase_now):
    return SOLID_DIFF + (LIQUID_DIFF - SOLID_DIFF) * 0.5 * (1.0 - jnp.tanh(phase_now))


def update(phase_now, solute_now, undercool, phase_nb, solute_nb, diff_now, diff_nb):
    lap = reduce(jnp.add, phase_nb) - 6.0 * phase_now
    squares = 1.0 - phase_now * phase_now
    rate = (
        lap
        + phase_now
        - phase_now * phase_now * phase_now
        + COUPLING * squares * squares * (undercool - solute_now)
    )
    fluxes = [
        0.5 * (diff_now + diff_nb[index]) * (solute_nb[index] - solute_now) for index in range(6)
    ]
    divergence = reduce(jnp.add, fluxes)
    speed = TRAP_RATE * jnp.abs(rate)
    keff = (PARTITION + speed) / (1.0 + speed)
    phase_new = phase_now + TIME_STEP * rate
    solute_new = solute_now + TIME_STEP * (divergence + 0.5 * (1.0 - keff) * solute_now * rate)
    return (phase_new, solute_new)


def beside(padded):
    centre = padded[1:-1, 1:-1]
    return [
        padded[2:, 1:-1],
        padded[:-2, 1:-1],
        padded[1:-1, 2:],
        padded[1:-1, :-2],
        jnp.roll(centre, -1, 2),
        jnp.roll(centre, 1, 2),
    ]


def phase_sweep(phase_now, solute_now, undercool):
    padded = extended(jnp.stack([phase_now, solute_now]), (("gx", 1), ("gy", 2)), 1)
    phase_pad = padded[0]
    solute_pad = padded[1]
    diff_pad = diffusivity(phase_pad)
    return update(
        phase_now,
        solute_now,
        undercool,
        beside(phase_pad),
        beside(solute_pad),
        diff_pad[1:-1, 1:-1],
        beside(diff_pad),
    )


def signed_freq(indices, total):
    return jnp.where(indices < total // 2, indices, indices - total)


def wave_tables(freqs, positions, length, factor):
    product = freqs[:, None] * positions[None, :] % length
    angles = product.astype(jnp.float32) * (2.0 * math.pi / length)
    return (jnp.cos(angles) * factor, jnp.sin(angles) * factor)


def complex_mix(cosines, sines, data, pattern, orient):

    def apply(table, values):
        return jnp.einsum(pattern, table, values, precision=lax.Precision.HIGHEST)

    cos_real = apply(cosines, data[0])
    cos_imag = apply(cosines, data[1])
    sin_real = apply(sines, data[0])
    sin_imag = apply(sines, data[1])
    return jnp.stack([cos_real - orient * sin_imag, cos_imag + orient * sin_real])


def x_forward(data, factor):
    portion = lax.all_to_all(data, "gx", split_axis=1, concat_axis=2, tiled=True)
    length = portion.shape[2]
    cosines, sines = wave_tables(
        signed_freq(jnp.arange(KX, dtype=jnp.int32), KX),
        jnp.arange(length, dtype=jnp.int32),
        length,
        factor,
    )
    lines = complex_mix(cosines, sines, portion, "kx,wxyz->wkyz", -1.0)
    return lax.all_to_all(lines, "gx", split_axis=2, concat_axis=1, tiled=True)


def y_forward(data, factor):
    portion = lax.all_to_all(data, "gy", split_axis=1, concat_axis=3, tiled=True)
    length = portion.shape[3]
    cosines, sines = wave_tables(
        signed_freq(jnp.arange(KY, dtype=jnp.int32), KY),
        jnp.arange(length, dtype=jnp.int32),
        length,
        factor,
    )
    lines = complex_mix(cosines, sines, portion, "ky,wayz->wakz", -1.0)
    return lax.all_to_all(lines, "gy", split_axis=3, concat_axis=1, tiled=True)


def contract(weights, values):
    return jnp.einsum("abzoi,iabz->oabz", weights, values, precision=lax.Precision.HIGHEST)


def outer(left, right):
    return jnp.einsum("oabz,iabz->abzoi", left, right, precision=lax.Precision.HIGHEST)


def per_device_plain(
    phase,
    solute,
    undercool,
    lift_weight,
    spectral_weight,
    local_weight,
    local_bias,
    proj_weight,
    cotangent,
):
    phase_mid, solute_mid = phase_sweep(phase, solute, undercool)
    phase_next, solute_next = phase_sweep(phase_mid, solute_mid, undercool)
    cells_x, cells_y, depth = phase.shape
    total_x = cells_x * lax.axis_size("gx")
    total_y = cells_y * lax.axis_size("gy")
    fields = jnp.stack([phase_next, solute_next - SOLUTE_MEAN])
    modes_z = jnp.arange(KZ, dtype=jnp.int32)
    zpos = jnp.arange(depth, dtype=jnp.int32)
    unit_z = jnp.ones((KZ,), jnp.float32)
    weights_z = jnp.where(modes_z == 0, 1.0, 2.0).astype(jnp.float32) / depth

    def z_forward(field, zfactor):
        cosines, sines = wave_tables(modes_z, zpos, depth, zfactor[:, None])
        tables = jnp.stack([cosines, -sines])
        return jnp.einsum("wxyz,rkz->rwxyk", field, tables, precision=lax.Precision.HIGHEST)

    def spectral_forward(field, zfactor, xfactor, yfactor):
        return y_forward(x_forward(z_forward(field, zfactor), xfactor), yfactor)

    lifted = jnp.einsum("wc,cxyz->wxyz", lift_weight, fields, precision=lax.Precision.HIGHEST)
    spectrum = spectral_forward(lifted, unit_z, 1.0, 1.0)
    own_x = spectrum.shape[2]
    own_y = spectrum.shape[3]
    shaped = spectral_weight.reshape(2, own_x, own_y, KZ, WIDTH, WIDTH)
    out_real = contract(shaped[0], spectrum[0]) - contract(shaped[1], spectrum[1])
    out_imag = contract(shaped[0], spectrum[1]) + contract(shaped[1], spectrum[0])
    spectral_out = jnp.stack([out_real, out_imag])
    ypos = lax.axis_index("gy") * cells_y + jnp.arange(cells_y, dtype=jnp.int32)
    portion = lax.all_gather(spectral_out, "gy", axis=3, tiled=True)
    freqs = signed_freq(jnp.arange(portion.shape[3], dtype=jnp.int32), KY)
    cosines, sines = wave_tables(ypos, freqs, total_y, 1.0 / total_y)
    back_y = complex_mix(cosines, sines, portion, "yk,wakz->wayz", 1.0)
    cosines, sines = wave_tables(
        jnp.arange(total_x, dtype=jnp.int32),
        signed_freq(jnp.arange(KX, dtype=jnp.int32), KX),
        total_x,
        1.0 / total_x,
    )
    inverted = complex_mix(
        cosines,
        sines,
        lax.all_to_all(back_y, "gx", split_axis=1, concat_axis=2, tiled=True),
        "xk,wkyz->wxyz",
        1.0,
    )
    back_x = lax.all_to_all(inverted, "gx", split_axis=2, concat_axis=1, tiled=True)
    cos_back, sin_back = wave_tables(modes_z, zpos, depth, weights_z[:, None])
    back_tables = jnp.stack([cos_back, -sin_back])
    spectral_field = jnp.einsum(
        "rwxyk,rkz->wxyz", back_x, back_tables, precision=lax.Precision.HIGHEST
    )
    mixed = jnp.dot(local_weight, lift_weight, precision=lax.Precision.HIGHEST)
    pre_act = (
        spectral_field
        + jnp.einsum("wc,cxyz->wxyz", mixed, fields, precision=lax.Precision.HIGHEST)
        + local_bias[:, None, None, None]
    )
    activated, gelu_back = jax.vjp(jax.nn.gelu, pre_act)
    predicted = jnp.einsum("w,wxyz->xyz", proj_weight, activated, precision=lax.Precision.HIGHEST)
    grad_pre = gelu_back(proj_weight[:, None, None, None] * cotangent[None])[0]
    field_sums = jnp.einsum("wxyz,cxyz->wc", grad_pre, fields, precision=lax.Precision.HIGHEST)
    proj_sums = jnp.einsum("wxyz,xyz->w", activated, cotangent, precision=lax.Precision.HIGHEST)
    field_sums, proj_sums = lax.psum((field_sums, proj_sums), ("gx", "gy"))
    grad_modes = spectral_forward(grad_pre, weights_z, 1.0 / total_x, 1.0 / total_y)
    grad_real = outer(grad_modes[0], spectrum[0]) + outer(grad_modes[1], spectrum[1])
    grad_imag = outer(grad_modes[1], spectrum[0]) - outer(grad_modes[0], spectrum[1])
    grad_spectral = jnp.stack([grad_real, grad_imag]).reshape(2, own_x, own_y, KZ, WIDTH * WIDTH)
    scale = 1.0 / math.sqrt(total_x * total_y * depth)
    grad_local = jnp.dot(field_sums, lift_weight.T, precision=lax.Precision.HIGHEST) * scale
    grad_proj = proj_sums * scale
    return (phase_next, solute_next, predicted, grad_spectral, grad_local, grad_proj)


LANES = 128
SMALL_VMEM = 24 * 1024 * 1024
PACK_COST = 50_000_000_000
SPREAD = LANES // WIDTH
NARROW = jnp.bfloat16
EXACT = lax.Precision.HIGHEST


def halves(table):
    head = table.astype(np.float32).astype(ml_dtypes.bfloat16)
    rest = (table - head.astype(np.float64)).astype(np.float32).astype(ml_dtypes.bfloat16)
    return head, rest


def left_table(table):
    head, rest = halves(table)
    return np.concatenate([head, head, rest], axis=1)


def right_table(table):
    head, rest = halves(table)
    return np.concatenate([head, head, rest], axis=0)


def parts_of(values):
    head = values.astype(NARROW)
    return head, (values - head.astype(jnp.float32)).astype(NARROW)


def thrice(values, axis):
    head, rest = parts_of(values)
    return jnp.concatenate([head, rest, head], axis=axis)


def one_where(mask):
    return mask.astype(jnp.float32).astype(NARROW)


def mul(left, right):
    return jnp.dot(left, right, preferred_element_type=jnp.float32)


def mul_rows(left, right):
    return lax.dot_general(
        left, right, (((1,), (1,)), ((), ())), preferred_element_type=jnp.float32
    )


def angles(freqs, positions, length):
    return 2.0 * np.pi * ((freqs[:, None] * positions[None, :]) % length) / length


def signed(count):
    index = np.arange(count)
    return np.where(index < count // 2, index, index - count)


def rotation(theta, orient):
    cosines, sines = np.cos(theta), orient * np.sin(theta)
    return np.block([[cosines, -sines], [sines, cosines]])


def group_of(shape):
    return lax.broadcasted_iota(jnp.int32, shape, len(shape) - 1) // WIDTH


def pick(groups, choices):
    result = choices[-1]
    for index in range(len(choices) - 2, -1, -1):
        result = jnp.where(groups == index, choices[index], result)
    return result


def turn(values, shift):
    shift = shift % LANES
    return values if shift == 0 else pltpu.roll(values, shift, 1)


def swap_groups(pieces):
    groups = group_of(pieces[0].shape)
    return [
        pick(groups, [turn(pieces[i], WIDTH * (i - j)) for i in range(SPREAD)])
        for j in range(SPREAD)
    ]


def spread_cells(
    lift_ref, local_ref, bias_ref, proj_ref, cotangent_ref, vector_ref, mix_ref, spread_ref
):
    planes, depth, wide = spread_ref.shape
    tile = cotangent_ref.shape[0]
    cells_y = tile // planes
    lift, lift_rest = parts_of(lift_ref[...])
    local, local_rest = parts_of(local_ref[...])
    mixed = mul_rows(lift, local) + mul_rows(lift_rest, local) + mul_rows(lift, local_rest)
    for index in range(wide // WIDTH):
        place = slice(index * WIDTH, (index + 1) * WIDTH)
        vector_ref[0:2, place] = mixed
        vector_ref[2:3, place] = bias_ref[...]
        vector_ref[3:4, place] = proj_ref[...]
    head, rest = parts_of(vector_ref[...])
    row = lax.broadcasted_iota(jnp.int32, (cells_y, wide), 0)
    own = row == lax.broadcasted_iota(jnp.int32, (cells_y, wide), 1) // WIDTH

    def diagonal(line):
        return jnp.where(own, line.astype(jnp.float32), 0.0)

    mixing = [diagonal(part[k : k + 1]) for k in range(2) for part in (head, head, rest)]
    blank = jnp.zeros((2 * cells_y, wide), jnp.float32)
    mix_ref[...] = jnp.concatenate(mixing + [blank], axis=0).astype(NARROW)
    spread = jnp.concatenate(parts_of(cotangent_ref[...].T), axis=1)
    cell = lax.broadcasted_iota(jnp.int32, (2 * tile, wide), 0) % tile
    row = lax.broadcasted_iota(jnp.int32, (2 * tile, wide), 1) // WIDTH
    for plane in range(planes):
        spread_ref[plane] = mul(spread, one_where(cell == plane * cells_y + row))


def contract_kernel(
    planes,
    lift_ref,
    weight_ref,
    local_ref,
    bias_ref,
    proj_ref,
    cotangent_ref,
    out_ref,
    vector_ref,
    mix_ref,
    spread_ref,
    outer_ref,
    wide_ref,
):
    _, own_x, own_y, modes_z, width = weight_ref.shape
    chunk = out_ref.shape[0] // modes_z
    steps = own_x // planes

    square = (WIDTH, WIDTH)
    diagonal = lax.broadcasted_iota(jnp.int32, square, 0) == lax.broadcasted_iota(
        jnp.int32, square, 1
    )
    columns = [
        jnp.sum(
            jnp.where(diagonal, jnp.broadcast_to(lift_ref[k : k + 1, :], square), 0.0),
            axis=1,
            keepdims=True,
        )
        for k in range(2)
    ]
    lane = lax.broadcasted_iota(jnp.int32, (WIDTH, LANES), 1)
    base = jnp.where(
        lane % (2 * WIDTH) < WIDTH,
        jnp.broadcast_to(columns[0], lane.shape),
        jnp.broadcast_to(columns[1], lane.shape),
    )
    head, rest = parts_of(base)
    base = jnp.where(lane < 2 * WIDTH, head.astype(jnp.float32), rest.astype(jnp.float32))
    mixing = jnp.concatenate(
        [jnp.where(lane % WIDTH == channel, base, 0.0) for channel in range(WIDTH)], axis=0
    ).astype(NARROW)
    rows = planes * own_y * modes_z
    low = lax.broadcasted_iota(jnp.int32, (rows, LANES), 1) < 2 * WIDTH
    for step in range(steps):
        sums = []
        for part in range(2):
            block = weight_ref[part, step * planes : (step + 1) * planes]
            head, rest = parts_of(block.reshape(rows, width))
            total = mul(head, mixing) + mul(rest, mixing)
            sums.append(total + turn(total, 2 * WIDTH))
        result = jnp.where(low, sums[0], sums[1])
        for plane in range(planes):
            for row in range(own_y):
                first = (plane * own_y + row) * modes_z
                place = row * own_x + step * planes + plane
                out_ref[pl.ds(place, modes_z, stride=chunk), :] = result[
                    first : first + modes_z
                ]
    spread_cells(
        lift_ref,
        local_ref,
        bias_ref,
        proj_ref,
        cotangent_ref,
        vector_ref,
        mix_ref,
        spread_ref,
    )
    for index in range(SPREAD):
        wide_ref[:, index * WIDTH : (index + 1) * WIDTH] = lift_ref[...]
    for index in range(1, width // LANES):
        wide_ref[:, index * LANES : (index + 1) * LANES] = wide_ref[:, 0:LANES]
    shape = (2 * WIDTH, width)
    row = lax.broadcasted_iota(jnp.int32, shape, 0)
    column = lax.broadcasted_iota(jnp.int32, shape, 1)
    lift = jnp.where(row < WIDTH, wide_ref[0:1, :], wide_ref[1:2, :])
    head, rest = parts_of(jnp.where(column // WIDTH == row % WIDTH, lift, 0.0))
    outer_ref[0 : 2 * WIDTH] = head
    outer_ref[2 * WIDTH : 4 * WIDTH] = head
    outer_ref[4 * WIDTH : 6 * WIDTH] = rest
    outer_ref[6 * WIDTH : 8 * WIDTH] = jnp.zeros_like(rest)


def edge_kernel(held_ref, head_ref, tail_ref):
    cells_x = held_ref.shape[1]
    for index, reach in enumerate((2, 2, 1)):
        head_ref[2 * index : 2 * index + reach] = held_ref[index, 0:reach]
        tail_ref[2 * index : 2 * index + reach] = held_ref[index, cells_x - reach : cells_x]


def pack_kernel(held_ref, before_ref, after_ref, head_ref, tail_ref):
    _, cells_x, cells_y, _ = held_ref.shape
    for out, near, far in ((head_ref, 0, 1), (tail_ref, cells_y - 1, cells_y - 2)):
        for plane in range(cells_x):
            line = slice(plane, plane + 1)
            for index in range(2):
                out[2 * index, line] = held_ref[index, plane, near : near + 1]
                out[2 * index + 1, line] = held_ref[index, plane, far : far + 1]
            out[4, line] = held_ref[2, plane, near : near + 1]
        for index in range(2):
            out[5, 2 * index : 2 * index + 1] = before_ref[2 * index + 1, near : near + 1]
            out[5, 2 * index + 1 : 2 * index + 2] = after_ref[2 * index, near : near + 1]


def step_kernel(
    held_ref,
    before_ref,
    after_ref,
    low_ref,
    high_ref,
    table_ref,
    mixed_ref,
    fields_ref,
    send_ref,
    phase_ext,
    solute_ext,
    cool_ext,
    diff_ext,
    lines,
):
    _, cells_x, cells_y, depth = held_ref.shape
    base = 8
    end = base + cells_y
    for index, ext in enumerate((phase_ext, solute_ext)):
        first = 2 * index
        ext[2 : cells_x + 2, base:end] = held_ref[index]
        ext[0:2, base:end] = before_ref[first : first + 2]
        ext[cells_x + 2 : cells_x + 4, base:end] = after_ref[first : first + 2]
        for source, near, far in ((low_ref, base - 1, base - 2), (high_ref, end, end + 1)):
            for plane in range(cells_x):
                line = slice(plane, plane + 1)
                ext[plane + 2, near : near + 1] = source[first, line]
                ext[plane + 2, far : far + 1] = source[first + 1, line]
            ext[1, near : near + 1] = source[5, first : first + 1]
            ext[cells_x + 2, near : near + 1] = source[5, first + 1 : first + 2]
    cool_ext[2 : cells_x + 2, base:end] = held_ref[2]
    cool_ext[1:2, base:end] = before_ref[4:5]
    cool_ext[cells_x + 2 : cells_x + 3, base:end] = after_ref[4:5]
    for plane in range(cells_x):
        line = slice(plane, plane + 1)
        cool_ext[plane + 2, base - 1 : base] = low_ref[4, line]
        cool_ext[plane + 2, end : end + 1] = high_ref[4, line]

    send_ref[...] = mixed_ref[...]

    def sweep(reach):
        diff_ext[...] = diffusivity(phase_ext[...])

        def window(ext, move_x, move_y):
            return ext[
                2 - reach + move_x : cells_x + 2 + reach + move_x,
                base - reach + move_y : end + reach + move_y,
            ]

        def around(ext, now):
            return [
                window(ext, 1, 0),
                window(ext, -1, 0),
                window(ext, 0, 1),
                window(ext, 0, -1),
                pltpu.roll(now, depth - 1, 2),
                pltpu.roll(now, 1, 2),
            ]

        phase_now = window(phase_ext, 0, 0)
        solute_now = window(solute_ext, 0, 0)
        diff_now = window(diff_ext, 0, 0)
        return update(
            phase_now,
            solute_now,
            window(cool_ext, 0, 0),
            around(phase_ext, phase_now),
            around(solute_ext, solute_now),
            diff_now,
            around(diff_ext, diff_now),
        )

    phase_mid, solute_mid = sweep(1)
    phase_ext[1 : cells_x + 3, base - 1 : end + 1] = phase_mid
    solute_ext[1 : cells_x + 3, base - 1 : end + 1] = solute_mid
    phase_next, solute_next = sweep(0)
    fields_ref[0] = phase_next
    fields_ref[1] = solute_next
    tile = cells_x * cells_y
    both = (phase_next.reshape(tile, depth), solute_next.reshape(tile, depth) - SOLUTE_MEAN)
    ordered = []
    for part in range(depth // LANES):
        for index, values in enumerate(both):
            lines[part, index * tile : (index + 1) * tile] = values[
                :, part * LANES : (part + 1) * LANES
            ]
        ordered.append(
            jnp.concatenate(
                [
                    lines[part, pl.ds(row, 2 * cells_x, stride=cells_y), :]
                    for row in range(cells_y)
                ],
                axis=0,
            )
        )
    ordered = jnp.concatenate(ordered, axis=1)
    spectra = mul_rows(table_ref[...], thrice(ordered, 1))
    modes_z = spectra.shape[0] // 2
    chunk = send_ref.shape[0] // modes_z
    for part in range(2):
        send_ref[pl.ds(chunk - 2 + part, modes_z, stride=chunk), :] = spectra[
            part * modes_z : (part + 1) * modes_z
        ]


def pack_modes(shape, modes, modes_ref, rows_ref):
    count_x, count_y, _, _, own_x, own_y = shape
    modes_x, modes_y = count_x * own_x, count_y * own_y
    lane = lax.broadcasted_iota(jnp.int32, (modes_y, LANES), 1)
    for index in range(count_x):
        block = modes
        for k in range(4):
            shift = k * own_x - k * modes_x - index * own_x
            block = jnp.where(lane // own_x == k, turn(modes, shift), block)
        rows_ref[index] = block
        line = rows_ref[index, pl.ds(0, count_y, stride=own_y), :]
        groups = group_of(line.shape)
        for row in range(1, own_y):
            piece = rows_ref[index, pl.ds(row, count_y, stride=own_y), :]
            line = jnp.where(groups == row, turn(piece, row * WIDTH), line)
        modes_ref[index * count_y : (index + 1) * count_y] = line


def spectral_kernel(
    shape,
    mixed_ref,
    y_in_ref,
    x_in_ref,
    y_out_ref,
    x_out_ref,
    fields_ref,
    forth_ref,
    chosen_ref,
    gather_ref,
    modes_ref,
    send_ref,
    table_ref,
    line_ref,
    lines_y,
    lines_x,
    rows_ref,
    weight_ref,
):
    count_x, count_y, cells_x, cells_y, own_x, own_y = shape
    modes_x, modes_y = count_x * own_x, count_y * own_y
    total_x, total_y = count_x * cells_x, count_y * cells_y
    tile = cells_x * cells_y
    narrow = 2 * cells_x
    rows = 2 * count_y
    devices = count_x * count_y
    own = own_x * own_y
    chunk = mixed_ref.shape[0] // devices
    spectra = [mixed_ref[pl.ds(own + part, devices, stride=chunk), :] for part in range(2)]
    for index in range(devices):
        weight_ref[index * own : (index + 1) * own, :] = mixed_ref[
            index * chunk : index * chunk + own, :
        ]
    lane = lax.broadcasted_iota(jnp.int32, (rows, LANES), 1)
    blocks = []
    for row in range(cells_y):
        block = jnp.zeros((rows, LANES), jnp.float32)
        for index in range(count_x):
            piece = jnp.concatenate(
                [values[index * count_y : (index + 1) * count_y] for values in spectra], axis=0
            )
            piece = turn(piece, narrow * (index - row))
            block = jnp.where(lane // narrow == index, piece, block)
        blocks.append(block)
    along_y = mul(y_in_ref[...], thrice(jnp.concatenate(blocks, axis=0), 0))
    prepare(fields_ref, forth_ref, table_ref, line_ref)
    half = lax.broadcasted_iota(jnp.int32, (modes_y, LANES), 1) < LANES // 2
    joined = jnp.where(half, along_y[0:modes_y], turn(along_y[modes_y:], LANES // 2))
    modes = mul(thrice(joined, 1), x_in_ref[...])
    quads_y = total_y // SPREAD
    quads_x = modes_x // SPREAD
    lane = lax.broadcasted_iota(jnp.int32, (modes_y, LANES), 1) % modes_x
    chosen = jnp.concatenate(
        [jnp.where(lane == freq, modes, 0.0) for freq in range(modes_x)], axis=0
    )
    columns = mul(jnp.concatenate(parts_of(chosen), axis=1), chosen_ref[...])
    low = lax.broadcasted_iota(jnp.int32, (modes_y, LANES), 1) < 2 * WIDTH
    def gathered(quads):
        products = [[], []]
        for quad in quads:
            lines = [[], []]
            for index in range(SPREAD):
                freq = SPREAD * quad + index
                start = (freq // own_x) * count_y * own_y * own_x + freq % own_x
                weights = weight_ref[pl.ds(start, modes_y, stride=own_x), :]
                for part in range(2):
                    column = columns[
                        freq * modes_y : (freq + 1) * modes_y, part * LANES : (part + 1) * LANES
                    ]
                    line = weights * column
                    lines[part].append(line + turn(line, 2 * WIDTH))
            for part in range(2):
                pairs = [
                    jnp.where(low, lines[part][index], lines[part][index + 1])
                    for index in range(0, SPREAD, 2)
                ]
                products[part].append(jnp.concatenate(pairs, axis=1))
        products = jnp.concatenate(products[0] + products[1], axis=0)
        products = mul(jnp.concatenate(parts_of(products), axis=1), gather_ref[...])
        stacked = []
        for index in range(len(quads)):
            places = [(part * len(quads) + index) * modes_y for part in range(2)]
            stacked.append(
                jnp.concatenate([products[place : place + modes_y] for place in places], axis=0)
            )
        return thrice(jnp.concatenate(stacked, axis=1), 0)

    def along_lines(quads, stacked):
        back = mul(y_out_ref[...], stacked)
        for index, quad in enumerate(quads):
            lines_y[quad] = back[:, index * LANES : (index + 1) * LANES]
        for quad in quads:
            for part in range(2):
                pieces = [
                    lines_y[quad, pl.ds(part * total_y + i, quads_y, stride=SPREAD), :]
                    for i in range(SPREAD)
                ]
                for index, piece in enumerate(swap_groups(pieces)):
                    place = part * modes_x + SPREAD * quad + index
                    lines_x[pl.ds(place, quads_y, stride=2 * modes_x), :] = piece

    batches = [range(first, first + 2) for first in range(0, quads_x, 2)]
    following = gathered(batches[0])
    for index, quads in enumerate(batches):
        stacked = following
        if index + 1 < len(batches):
            following = gathered(batches[index + 1])
        along_lines(quads, stacked)
    per_tile = cells_y // SPREAD
    for start in range(0, quads_y, 4):
        blocks = [
            lines_x[quad * 2 * modes_x : (quad + 1) * 2 * modes_x, :]
            for quad in range(start, start + 4)
        ]
        back = mul(x_out_ref[...], thrice(jnp.concatenate(blocks, axis=1), 0))
        for quad in range(start, start + 4):
            lanes = slice((quad - start) * LANES, (quad - start + 1) * LANES)
            for part in range(2):
                for index in range(count_x):
                    device = index * count_y + quad // per_tile
                    place = (device * 2 + part) * per_tile + quad % per_tile
                    first = part * total_x + index * cells_x
                    send_ref[place * cells_x : (place + 1) * cells_x, :] = back[
                        first : first + cells_x, lanes
                    ]
    pack_modes(shape, modes, modes_ref, rows_ref)


def prepare(fields_ref, forth_ref, table_ref, line_ref):
    planes, depth, _ = table_ref.shape
    cells_y = fields_ref.shape[2]
    tile = planes * cells_y
    rows = forth_ref.shape[0] // 2
    fields = (fields_ref[0].reshape(tile, depth), fields_ref[1].reshape(tile, depth) - SOLUTE_MEAN)
    blank = jnp.zeros((2 * cells_y, depth), jnp.float32)
    table = forth_ref[rows:].astype(jnp.float32)
    for plane in range(planes):
        lines = [values[plane * cells_y : (plane + 1) * cells_y] for values in fields]
        pieces = [[part.astype(jnp.float32) for part in parts_of(values)] for values in lines]
        both = [piece for head, rest in pieces for piece in (head, rest, head)]
        both = jnp.concatenate([table] + both + [blank], axis=0)
        table_ref[plane] = both.T.astype(NARROW)
        pieces = [piece for pair in zip(*pieces) for piece in pair]
        line_ref[plane] = jnp.concatenate(pieces, axis=0).astype(NARROW)


def fold_channels(values):
    quarter = values.shape[0] // SPREAD
    parts = []
    for first in range(0, values.shape[1], LANES):
        pieces = [
            values[index * quarter : (index + 1) * quarter, first : first + LANES]
            for index in range(SPREAD)
        ]
        channel = lax.broadcasted_iota(jnp.int32, pieces[0].shape, 1) % WIDTH
        span = WIDTH // 2
        while len(pieces) > 1:
            low = channel % (2 * span) < span
            pieces = [
                jnp.where(low, left + turn(left, -span), right + turn(right, span))
                for left, right in zip(pieces[: len(pieces) // 2], pieces[len(pieces) // 2 :])
            ]
            span //= 2
        parts.append(pieces[0])
    return jnp.concatenate(parts, axis=1)


def field_kernel(
    cells_y,
    field_ref,
    table_ref,
    mix_ref,
    weight_ref,
    line_ref,
    vector_ref,
    back_ref,
    forth_ref,
    predicted_ref,
    send_ref,
    shares_ref,
):
    planes, depth, wide = weight_ref.shape
    rows = forth_ref.shape[0] // 2
    halves_y = cells_y // SPREAD
    stride = halves_y * planes
    bias = vector_ref[2:3, :]
    proj = vector_ref[3:4, :]
    root = math.sqrt(2.0 / math.pi)
    curve = 0.044715
    picker = one_where(
        lax.broadcasted_iota(jnp.int32, (SPREAD * cells_y, 2 * wide), 0)
        == lax.broadcasted_iota(jnp.int32, (SPREAD * cells_y, 2 * wide), 1)
        % wide
        // (WIDTH // SPREAD)
    )
    line_sums = jnp.zeros((2 * cells_y, wide), jnp.float32)
    proj_sums = jnp.zeros((8, wide), jnp.float32)
    def back(plane):
        spectra = jnp.concatenate(
            [
                field_ref[pl.ds(part * planes + plane, rows, stride=stride), :]
                for part in range(halves_y)
            ],
            axis=1,
        )
        spectra = jnp.concatenate([thrice(spectra, 0), mix_ref[...]], axis=0)
        table = jnp.concatenate([back_ref[...], table_ref[plane]], axis=1)
        return mul(table, spectra) + bias

    def activate(pre, plane):
        square = pre * pre
        bent = jnp.tanh(pre * (root + (root * curve) * square))
        upper = 0.5 + 0.5 * bent
        active = pre * upper
        slope = upper + (active - active * bent) * (root + (3.0 * root * curve) * square)
        cotangent = weight_ref[plane]
        grad = proj * cotangent * slope
        sums = jnp.sum((active * cotangent).reshape(depth // 8, 8, wide), axis=0)
        return sums, parts_of(fold_channels(proj * active)), parts_of(grad)

    def forth(shared, grad, plane):
        shares_ref[plane, :, 0 : depth // SPREAD] = mul_rows(
            picker, jnp.concatenate(shared, axis=1)
        )
        for index in range(SPREAD):
            predicted_ref[
                plane * cells_y : (plane + 1) * cells_y,
                index * (depth // SPREAD) : (index + 1) * (depth // SPREAD),
            ] = shares_ref[plane, pl.ds(index, cells_y, stride=SPREAD), 0 : depth // SPREAD]
        head, rest = grad
        lines = line_ref[plane]
        top = jnp.concatenate([forth_ref[0:rows], lines[0 : 2 * cells_y]], axis=0)
        low = jnp.concatenate([forth_ref[rows:], lines[2 * cells_y :]], axis=0)
        spectra = mul(jnp.concatenate([top, low], axis=0), head)
        spectra = spectra[0 : rows + 2 * cells_y] + spectra[rows + 2 * cells_y :] + mul(top, rest)
        for part in range(halves_y):
            send_ref[pl.ds(part * planes + plane, rows, stride=stride), :] = spectra[
                0:rows, part * LANES : (part + 1) * LANES
            ]
        return spectra[rows:]

    following = back(0)
    previous = None
    for plane in range(planes + 1):
        pre = following
        if plane + 1 < planes:
            following = back(plane + 1)
        if plane < planes:
            sums, *current = activate(pre, plane)
            proj_sums = proj_sums + sums
        if plane > 0:
            line_sums = line_sums + forth(*previous, plane - 1)
        previous = current
    shape = (cells_y, wide)
    own = lax.broadcasted_iota(jnp.int32, shape, 0) == (
        lax.broadcasted_iota(jnp.int32, shape, 1) // WIDTH
    )
    sums = [
        jnp.where(own, line_sums[0:cells_y], 0.0),
        jnp.where(own, line_sums[cells_y:], 0.0),
        proj_sums,
    ]
    for index, values in enumerate(sums):
        line = jnp.sum(values, axis=0, keepdims=True)
        line = sum(line[:, part * LANES : (part + 1) * LANES] for part in range(halves_y))
        send_ref[stride + index : stride + index + 1, :] = line


def gradient_kernel(
    shape, spectra_ref, modes_ref, x_in_ref, y_in_ref, send_ref, lines_x, lines_y
):
    count_x, count_y, cells_x, cells_y, own_x, own_y = shape
    modes_x, modes_y = count_x * own_x, count_y * own_y
    total_x, total_y = count_x * cells_x, count_y * cells_y
    per_tile = cells_y // SPREAD
    quads_y = total_y // SPREAD
    chunk = 2 * per_tile * cells_x
    first_device = (lax.axis_index("gx") == 0) & (lax.axis_index("gy") == 0)
    keep = jnp.where(first_device, 0.0, 1.0)
    devices = count_x * count_y
    out_chunk = send_ref.shape[0] // devices
    per_own = own_x // SPREAD
    quads_x = modes_x // SPREAD
    for start in range(0, quads_y, SPREAD):
        blocks = []
        for quad in range(start, start + SPREAD):
            block = []
            for part in range(2):
                for index in range(count_x):
                    device = index * count_y + quad // per_tile
                    place = (device * 2 + part) * per_tile + quad % per_tile
                    piece = spectra_ref[place * cells_x : (place + 1) * cells_x, :]
                    block.append(piece * keep if part else piece)
            blocks.append(jnp.concatenate(block, axis=0))
        forth = mul(x_in_ref[...], thrice(jnp.concatenate(blocks, axis=1), 0))
        for quad in range(start, start + SPREAD):
            lines_x[quad * 2 * modes_x : (quad + 1) * 2 * modes_x, :] = forth[
                :, (quad - start) * LANES : (quad - start + 1) * LANES
            ]
    extra = 2 * per_own * own_y
    send_ref[pl.ds(extra, devices, stride=out_chunk), :] = modes_ref[...]
    groups = group_of((1, LANES))
    total = jnp.zeros((1, LANES), jnp.float32)
    for index in range(3):
        start = chunk // 2 + index
        line = jnp.sum(
            spectra_ref[pl.ds(start, devices, stride=chunk), :], axis=0, keepdims=True
        )
        line = line + turn(line, 2 * WIDTH)
        total = jnp.where(groups == index, line + turn(line, WIDTH), total)
    send_ref[pl.ds(extra + 1, devices, stride=out_chunk), :] = jnp.broadcast_to(
        total, (devices, LANES)
    )
    for start in range(0, quads_x, 2):
        for quad in range(start, start + 2):
            for part in range(2):
                pieces = [
                    lines_x[
                        pl.ds(part * modes_x + SPREAD * quad + j, quads_y, stride=2 * modes_x), :
                    ]
                    for j in range(SPREAD)
                ]
                for index, piece in enumerate(swap_groups(pieces)):
                    lines_y[quad, pl.ds(part * total_y + index, quads_y, stride=SPREAD), :] = piece
        lines = jnp.concatenate([lines_y[start], lines_y[start + 1]], axis=1)
        modes = mul(y_in_ref[...], thrice(lines, 0))
        for quad in range(start, start + 2):
            for part in range(2):
                for index in range(count_y):
                    device = (quad // per_own) * count_y + index
                    place = device * out_chunk + (part * per_own + quad % per_own) * own_y
                    first = part * modes_y + index * own_y
                    send_ref[place : place + own_y, :] = modes[
                        first : first + own_y, (quad - start) * LANES : (quad - start + 1) * LANES
                    ]


def outer_kernel(
    scale,
    modes_ref,
    narrow_ref,
    predicted_ref,
    fields_ref,
    mix_ref,
    repeat_ref,
    spread_ref,
    local_out,
    proj_out,
    predicted_out,
    phase_out,
    solute_out,
    grad_ref,
    local_ref,
    proj_ref,
    held,
    sent,
):
    _, own_x, own_y, modes_z, width = held.shape
    chunk = modes_ref.shape[0] // modes_z
    per_own = own_x // SPREAD
    extra = 2 * per_own * own_y
    copies = [
        pltpu.make_async_copy(predicted_ref, predicted_out, sent.at[own_x]),
        pltpu.make_async_copy(fields_ref.at[0], phase_out, sent.at[own_x + 1]),
        pltpu.make_async_copy(fields_ref.at[1], solute_out, sent.at[own_x + 2]),
    ]
    for copy in copies:
        copy.start()
    lane = lax.broadcasted_iota(jnp.int32, (modes_z, LANES), 1)
    low = lane < 2 * WIDTH

    def rows_of(values):
        head, rest = parts_of(values)
        both = jnp.where(low, head.astype(jnp.float32), rest.astype(jnp.float32)).astype(NARROW)
        return jnp.concatenate([both, head], axis=1)

    def repeated(half):
        grads = [
            modes_ref[pl.ds((part * per_own + half) * own_y + row, modes_z, stride=chunk), :]
            for part in range(2)
            for row in range(own_y)
        ]
        grads = jnp.concatenate(grads, axis=0)
        return mul(jnp.concatenate(parts_of(grads), axis=1), repeat_ref[...])

    modes = modes_ref[pl.ds(extra, modes_z, stride=chunk), :]
    own = lane // (4 * own_x) * own_x + lane % own_x
    for plane in range(own_x):
        if plane % SPREAD == 0:
            grads = repeated(plane // SPREAD)
        chosen = jnp.concatenate(
            [jnp.where(own == row * own_x + plane, modes, 0.0) for row in range(own_y)], axis=0
        )
        columns = mul(jnp.concatenate(parts_of(chosen), axis=1), spread_ref[...])
        reals, imags = [], []
        for row in range(own_y):
            real = columns[row * modes_z : (row + 1) * modes_z, 0:LANES]
            imag = columns[row * modes_z : (row + 1) * modes_z, LANES:]
            pair = []
            for part in range(2):
                first = (part * own_y + row) * modes_z
                group = plane % SPREAD * LANES
                pair.append(grads[first : first + modes_z, group : group + LANES])
            reals.append(rows_of(pair[0] * real + pair[1] * imag))
            imags.append(rows_of(pair[1] * real - pair[0] * imag))
        result = mul(jnp.concatenate(reals + imags, axis=0), mix_ref[...])
        held[:, plane] = result.reshape(2, own_y, modes_z, width)
        copies.append(
            pltpu.make_async_copy(held.at[:, plane], grad_ref.at[:, plane], sent.at[plane])
        )
        copies[-1].start()
    line = modes_ref[extra + 1 : extra + 2, :]
    square = (WIDTH, WIDTH)
    diagonal = lax.broadcasted_iota(jnp.int32, square, 0) == lax.broadcasted_iota(
        jnp.int32, square, 1
    )
    local = jnp.zeros(square, jnp.float32)
    for k in range(2):
        sums = jnp.broadcast_to(line[:, k * WIDTH : (k + 1) * WIDTH], square)
        sums = jnp.sum(jnp.where(diagonal, sums, 0.0), axis=1, keepdims=True)
        local = local + sums * narrow_ref[k : k + 1, :]
    local_ref[...] = scale * local
    proj_ref[...] = scale * line[:, 2 * WIDTH : 3 * WIDTH]
    copies.append(pltpu.make_async_copy(local_ref, local_out, sent.at[own_x + 3]))
    copies.append(pltpu.make_async_copy(proj_ref, proj_out, sent.at[own_x + 4]))
    copies[-2].start()
    copies[-1].start()
    for copy in copies:
        copy.wait()


def tables(shape, depth, modes_z):
    count_x, count_y, cells_x, cells_y, own_x, own_y = shape
    modes_x, modes_y = count_x * own_x, count_y * own_y
    total_x, total_y = count_x * cells_x, count_y * cells_y
    theta_z = angles(np.arange(modes_z), np.arange(depth), depth)
    theta_x = angles(signed(modes_x), np.arange(total_x), total_x)
    theta_y = angles(signed(modes_y), np.arange(total_y), total_y)
    plain_z = np.concatenate([np.cos(theta_z), -np.sin(theta_z)], axis=0)
    forth_z = plain_z.reshape(2, modes_z, depth).transpose(1, 0, 2).reshape(2 * modes_z, depth)
    weight = np.where(np.arange(modes_z) == 0, 1.0, 2.0) / (total_x * total_y * depth)
    weighted_z = np.repeat(weight, 2)[:, None] * forth_z
    forth_x, back_x = rotation(theta_x, -1.0), rotation(theta_x.T, 1.0)
    forth_y, back_y = rotation(theta_y, -1.0), rotation(theta_y.T, 1.0)
    order_y = forth_y.reshape(2 * modes_y, 2, count_y, cells_y)
    order_y = order_y.transpose(0, 3, 1, 2).reshape(2 * modes_y, 2 * total_y)
    lines = forth_x.reshape(2, modes_x, 2, count_x, cells_x)
    both = np.zeros((2, count_x, 2, cells_x, 2, 2, modes_x))
    for field in range(2):
        both[:, :, field, :, :, field, :] = lines.transpose(2, 3, 4, 0, 1)
    both = both.reshape(4 * total_x, 4 * modes_x)
    index = np.arange(4 * LANES)
    line = index[: 2 * LANES, None] % LANES
    group = index[None, : 2 * LANES] // WIDTH
    same = np.where(group < 4, group, (group + 2) % 4)
    signs = np.where((group == 2) | (group == 3), -1.0, 1.0)
    chosen = np.where(line // modes_x == same, signs, 0.0)
    half = 2 * WIDTH
    row, column = index[:, None] % (SPREAD * half), index[None, :LANES]
    gather = row // half * WIDTH + row % WIDTH == column
    repeat = line == index[None, :] // LANES * WIDTH + index[None, :] % WIDTH
    spread = line // own_x % 4 == group // 4 * 2 + group % 2
    masks = {"chosen": chosen, "gather": gather, "repeat": repeat, "spread": spread}
    masks = {name: mask.astype(ml_dtypes.bfloat16) for name, mask in masks.items()}
    return masks | {
        "z_plain": left_table(plain_z),
        "z_forth": np.concatenate(halves(weighted_z), axis=0),
        "z_back": left_table(weighted_z.T)[:, : 4 * modes_z],
        "y_first": left_table(order_y),
        "x_first": right_table(both),
        "y_back": left_table(back_y),
        "x_back": left_table(back_x),
        "x_forth": left_table(forth_x),
        "y_forth": left_table(forth_y),
    }


def fits(count_x, count_y, phase, spectral_weight):
    cells_x, cells_y, depth = phase.shape
    _, own_x, own_y, modes_z, width = spectral_weight.shape
    return (
        width == WIDTH * WIDTH
        and modes_z == count_x * count_y
        and 4 * modes_z == LANES
        and 4 * count_x * cells_x == LANES
        and 4 * count_x * own_x == LANES
        and 2 * cells_x * cells_y == LANES
        and cells_x == 8
        and cells_y % SPREAD == 0
        and own_x % SPREAD == 0
        and own_y * 4 * own_x == LANES
        and 3 * WIDTH <= LANES
        and cells_y == 8
        and depth % LANES == 0
    )


def call(kernel, outs, scratch, flops, moved, limit=SMALL_VMEM, **more):
    return pl.pallas_call(
        kernel,
        out_shape=outs,
        scratch_shapes=scratch,
        compiler_params=pltpu.CompilerParams(vmem_limit_bytes=limit),
        cost_estimate=pl.CostEstimate(flops=flops, bytes_accessed=moved, transcendentals=0),
        **more,
    )


def exchange(values):
    return lax.all_to_all(values, ("gx", "gy"), split_axis=0, concat_axis=0, tiled=True)


def per_device_fast(
    phase,
    solute,
    undercool,
    lift_weight,
    spectral_weight,
    local_weight,
    local_bias,
    proj_weight,
    cotangent,
):
    count_x, count_y = lax.axis_size("gx"), lax.axis_size("gy")
    cells_x, cells_y, depth = phase.shape
    _, own_x, own_y, modes_z, width = spectral_weight.shape
    shape = (count_x, count_y, cells_x, cells_y, own_x, own_y)
    devices = count_x * count_y
    tile = cells_x * cells_y
    modes_x, modes_y = count_x * own_x, count_y * own_y
    total_x, total_y = count_x * cells_x, count_y * cells_y
    table = tables(shape, depth, modes_z)
    real = jnp.float32

    def like(*dims):
        return jax.ShapeDtypeStruct(dims, real)

    far = pl.BlockSpec(memory_space=pltpu.HBM)
    weight_bytes = 8 * own_x * own_y * modes_z * width
    held = jnp.stack([phase, solute, undercool])
    head, tail = call(
        edge_kernel,
        (like(5, cells_y, depth), like(5, cells_y, depth)),
        [],
        1000,
        40 * tile * depth,
    )(held)

    def ring(values, axis, step):
        count = lax.axis_size(axis)
        return lax.ppermute(values, axis, [(i, (i + step) % count) for i in range(count)])

    head, tail, lift = lax.optimization_barrier((head, tail, lift_weight.T))
    before, after = ring(tail, "gx", 1), ring(head, "gx", -1)
    planes = 2
    spread_shape = (cells_x, depth, cells_y * WIDTH)
    mixed_weights, vectors, mixing, weight, outer_mix = call(
        functools.partial(contract_kernel, planes),
        (
            like(modes_z * (own_x * own_y + 2), LANES),
            like(4, cells_y * WIDTH),
            jax.ShapeDtypeStruct((8 * cells_y, cells_y * WIDTH), NARROW),
            like(*spread_shape),
            jax.ShapeDtypeStruct((8 * WIDTH, width), NARROW),
        ),
        [pltpu.VMEM((2, width), real)],
        weight_bytes * LANES,
        weight_bytes,
    )(
        lift,
        spectral_weight,
        local_weight,
        local_bias.reshape(1, WIDTH),
        proj_weight.reshape(1, WIDTH),
        cotangent.reshape(tile, depth),
    )
    head, tail = call(
        pack_kernel,
        (like(6, cells_x, depth), like(6, cells_x, depth)),
        [],
        PACK_COST,
        40 * tile * depth,
    )(held, before, after)
    low, high = ring(tail, "gy", 1), ring(head, "gy", -1)
    extended_shape = pltpu.VMEM((cells_x + 4, cells_y + 16, depth), real)
    stepped, spectra = call(
        step_kernel,
        (like(2, *phase.shape), like(*mixed_weights.shape)),
        [extended_shape] * 4 + [pltpu.VMEM((depth // LANES, 2 * tile, LANES), real)],
        400 * tile * depth,
        80 * tile * depth,
    )(held, before, after, low, high, table["z_plain"], mixed_weights)
    gathered = exchange(spectra.reshape(-1, 2, LANES)).reshape(spectra.shape)
    modes, fields, lines, own_lines = call(
        functools.partial(spectral_kernel, shape),
        (
            like(devices, LANES),
            like(devices * 2 * cells_x * (cells_y // SPREAD), LANES),
            jax.ShapeDtypeStruct((cells_x, depth, LANES), NARROW),
            jax.ShapeDtypeStruct((cells_x, 4 * cells_y, depth), NARROW),
        ),
        [
            pltpu.VMEM((modes_x // SPREAD, 2 * total_y, LANES), real),
            pltpu.VMEM((2 * modes_x * (total_y // SPREAD), LANES), real),
            pltpu.VMEM((count_x, modes_y, LANES), real),
            pltpu.VMEM((devices * own_x * own_y, LANES), real),
        ],
        100_000_000,
        2_000_000,
    )(
        gathered,
        table["y_first"],
        table["x_first"],
        table["y_back"],
        table["x_back"],
        stepped,
        table["z_forth"],
        table["chosen"],
        table["gather"],
    )
    fields = exchange(fields)
    predicted, spectra = call(
        functools.partial(field_kernel, cells_y),
        (like(tile, depth), like(*fields.shape)),
        [pltpu.VMEM((cells_x, SPREAD * cells_y, LANES), real)],
        1_000_000_000,
        2_000_000,
    )(fields, lines, mixing, weight, own_lines, vectors, table["z_back"], table["z_forth"])
    spectra = exchange(spectra)
    chunk = 2 * own_x * own_y * WIDTH // LANES + 2
    gradients = call(
        functools.partial(gradient_kernel, shape),
        like(devices * chunk, LANES),
        [
            pltpu.VMEM((2 * modes_x * (total_y // SPREAD), LANES), real),
            pltpu.VMEM((modes_x // SPREAD, 2 * total_y, LANES), real),
        ],
        100_000_000,
        2_000_000,
    )(spectra, modes, table["x_forth"], table["y_forth"])
    gradients = exchange(gradients.reshape(-1, 2, LANES)).reshape(gradients.shape)
    grad_local, grad_proj, predicted, phase_next, solute_next, grad_spectral = call(
        functools.partial(outer_kernel, 1.0 / math.sqrt(total_x * total_y * depth)),
        (
            like(WIDTH, WIDTH),
            like(1, WIDTH),
            like(*predicted.shape),
            like(*phase.shape),
            like(*phase.shape),
            like(*spectral_weight.shape),
        ),
        [
            pltpu.VMEM((WIDTH, WIDTH), real),
            pltpu.VMEM((1, WIDTH), real),
            pltpu.VMEM(spectral_weight.shape, real),
            pltpu.SemaphoreType.DMA((own_x + 5,)),
        ],
        weight_bytes * 4 * WIDTH,
        weight_bytes,
        out_specs=(far,) * 6,
    )(gradients, lift, predicted, stepped, outer_mix, table["repeat"], table["spread"])
    return (
        phase_next,
        solute_next,
        predicted.reshape(phase.shape),
        grad_spectral,
        grad_local,
        grad_proj.reshape(WIDTH),
    )


def per_device(*arguments):
    count_x, count_y = lax.axis_size("gx"), lax.axis_size("gy")
    if fits(count_x, count_y, arguments[0], arguments[4]):
        return per_device_fast(*arguments)
    return per_device_plain(*arguments)


def solution(mesh):
    return jax.shard_map(
        per_device,
        mesh=mesh,
        in_specs=(
            P("gx", "gy", None),
            P("gx", "gy", None),
            P("gx", "gy", None),
            P(),
            P(None, "gx", "gy", None, None),
            P(),
            P(),
            P(),
            P("gx", "gy", None),
        ),
        out_specs=(
            P("gx", "gy", None),
            P("gx", "gy", None),
            P("gx", "gy", None),
            P(None, "gx", "gy", None, None),
            P(),
            P(),
        ),
        check_vma=False,
    )
```

```python
import functools
from functools import reduce
import math

import jax
import jax.numpy as jnp
import ml_dtypes
import numpy as np
from jax import lax
from jax.experimental import pallas as pl
from jax.experimental.pallas import tpu as pltpu
from jax.sharding import PartitionSpec as P

WIDTH = 32
KX = 32
KY = 32
KZ = 32


TIME_STEP = 0.05
COUPLING = 2.0
SOLID_DIFF = 0.05
LIQUID_DIFF = 1.0
PARTITION = 0.15
TRAP_RATE = 4.0
SOLUTE_MEAN = 0.5


def extended(cells, sides, width):
    for axis, dim in sides:
        count = lax.axis_size(axis)
        head = lax.slice_in_dim(cells, 0, width, axis=dim)
        tail = lax.slice_in_dim(cells, cells.shape[dim] - width, cells.shape[dim], axis=dim)
        cells = jnp.concatenate(
            [
                lax.ppermute(tail, axis, [(i, (i + 1) % count) for i in range(count)]),
                cells,
                lax.ppermute(head, axis, [((i + 1) % count, i) for i in range(count)]),
            ],
            axis=dim,
        )
    return cells


def diffusivity(phase_now):
    return SOLID_DIFF + (LIQUID_DIFF - SOLID_DIFF) * 0.5 * (1.0 - jnp.tanh(phase_now))


def update(phase_now, solute_now, undercool, phase_nb, solute_nb, diff_now, diff_nb):
    lap = reduce(jnp.add, phase_nb) - 6.0 * phase_now
    squares = 1.0 - phase_now * phase_now
    rate = (
        lap
        + phase_now
        - phase_now * phase_now * phase_now
        + COUPLING * squares * squares * (undercool - solute_now)
    )
    fluxes = [
        0.5 * (diff_now + diff_nb[index]) * (solute_nb[index] - solute_now) for index in range(6)
    ]
    divergence = reduce(jnp.add, fluxes)
    speed = TRAP_RATE * jnp.abs(rate)
    keff = (PARTITION + speed) / (1.0 + speed)
    phase_new = phase_now + TIME_STEP * rate
    solute_new = solute_now + TIME_STEP * (divergence + 0.5 * (1.0 - keff) * solute_now * rate)
    return (phase_new, solute_new)


def beside(padded):
    centre = padded[1:-1, 1:-1]
    return [
        padded[2:, 1:-1],
        padded[:-2, 1:-1],
        padded[1:-1, 2:],
        padded[1:-1, :-2],
        jnp.roll(centre, -1, 2),
        jnp.roll(centre, 1, 2),
    ]


def phase_sweep(phase_now, solute_now, undercool):
    padded = extended(jnp.stack([phase_now, solute_now]), (("gx", 1), ("gy", 2)), 1)
    phase_pad = padded[0]
    solute_pad = padded[1]
    diff_pad = diffusivity(phase_pad)
    return update(
        phase_now,
        solute_now,
        undercool,
        beside(phase_pad),
        beside(solute_pad),
        diff_pad[1:-1, 1:-1],
        beside(diff_pad),
    )


def signed_freq(indices, total):
    return jnp.where(indices < total // 2, indices, indices - total)


def wave_tables(freqs, positions, length, factor):
    product = freqs[:, None] * positions[None, :] % length
    angles = product.astype(jnp.float32) * (2.0 * math.pi / length)
    return (jnp.cos(angles) * factor, jnp.sin(angles) * factor)


def complex_mix(cosines, sines, data, pattern, orient):

    def apply(table, values):
        return jnp.einsum(pattern, table, values, precision=lax.Precision.HIGHEST)

    cos_real = apply(cosines, data[0])
    cos_imag = apply(cosines, data[1])
    sin_real = apply(sines, data[0])
    sin_imag = apply(sines, data[1])
    return jnp.stack([cos_real - orient * sin_imag, cos_imag + orient * sin_real])


def x_forward(data, factor):
    portion = lax.all_to_all(data, "gx", split_axis=1, concat_axis=2, tiled=True)
    length = portion.shape[2]
    cosines, sines = wave_tables(
        signed_freq(jnp.arange(KX, dtype=jnp.int32), KX),
        jnp.arange(length, dtype=jnp.int32),
        length,
        factor,
    )
    lines = complex_mix(cosines, sines, portion, "kx,wxyz->wkyz", -1.0)
    return lax.all_to_all(lines, "gx", split_axis=2, concat_axis=1, tiled=True)


def y_forward(data, factor):
    portion = lax.all_to_all(data, "gy", split_axis=1, concat_axis=3, tiled=True)
    length = portion.shape[3]
    cosines, sines = wave_tables(
        signed_freq(jnp.arange(KY, dtype=jnp.int32), KY),
        jnp.arange(length, dtype=jnp.int32),
        length,
        factor,
    )
    lines = complex_mix(cosines, sines, portion, "ky,wayz->wakz", -1.0)
    return lax.all_to_all(lines, "gy", split_axis=3, concat_axis=1, tiled=True)


def contract(weights, values):
    return jnp.einsum("abzoi,iabz->oabz", weights, values, precision=lax.Precision.HIGHEST)


def outer(left, right):
    return jnp.einsum("oabz,iabz->abzoi", left, right, precision=lax.Precision.HIGHEST)


def per_device_plain(
    phase,
    solute,
    undercool,
    lift_weight,
    spectral_weight,
    local_weight,
    local_bias,
    proj_weight,
    cotangent,
):
    phase_mid, solute_mid = phase_sweep(phase, solute, undercool)
    phase_next, solute_next = phase_sweep(phase_mid, solute_mid, undercool)
    cells_x, cells_y, depth = phase.shape
    total_x = cells_x * lax.axis_size("gx")
    total_y = cells_y * lax.axis_size("gy")
    fields = jnp.stack([phase_next, solute_next - SOLUTE_MEAN])
    modes_z = jnp.arange(KZ, dtype=jnp.int32)
    zpos = jnp.arange(depth, dtype=jnp.int32)
    unit_z = jnp.ones((KZ,), jnp.float32)
    weights_z = jnp.where(modes_z == 0, 1.0, 2.0).astype(jnp.float32) / depth

    def z_forward(field, zfactor):
        cosines, sines = wave_tables(modes_z, zpos, depth, zfactor[:, None])
        tables = jnp.stack([cosines, -sines])
        return jnp.einsum("wxyz,rkz->rwxyk", field, tables, precision=lax.Precision.HIGHEST)

    def spectral_forward(field, zfactor, xfactor, yfactor):
        return y_forward(x_forward(z_forward(field, zfactor), xfactor), yfactor)

    lifted = jnp.einsum("wc,cxyz->wxyz", lift_weight, fields, precision=lax.Precision.HIGHEST)
    spectrum = spectral_forward(lifted, unit_z, 1.0, 1.0)
    own_x = spectrum.shape[2]
    own_y = spectrum.shape[3]
    shaped = spectral_weight.reshape(2, own_x, own_y, KZ, WIDTH, WIDTH)
    out_real = contract(shaped[0], spectrum[0]) - contract(shaped[1], spectrum[1])
    out_imag = contract(shaped[0], spectrum[1]) + contract(shaped[1], spectrum[0])
    spectral_out = jnp.stack([out_real, out_imag])
    ypos = lax.axis_index("gy") * cells_y + jnp.arange(cells_y, dtype=jnp.int32)
    portion = lax.all_gather(spectral_out, "gy", axis=3, tiled=True)
    freqs = signed_freq(jnp.arange(portion.shape[3], dtype=jnp.int32), KY)
    cosines, sines = wave_tables(ypos, freqs, total_y, 1.0 / total_y)
    back_y = complex_mix(cosines, sines, portion, "yk,wakz->wayz", 1.0)
    cosines, sines = wave_tables(
        jnp.arange(total_x, dtype=jnp.int32),
        signed_freq(jnp.arange(KX, dtype=jnp.int32), KX),
        total_x,
        1.0 / total_x,
    )
    inverted = complex_mix(
        cosines,
        sines,
        lax.all_to_all(back_y, "gx", split_axis=1, concat_axis=2, tiled=True),
        "xk,wkyz->wxyz",
        1.0,
    )
    back_x = lax.all_to_all(inverted, "gx", split_axis=2, concat_axis=1, tiled=True)
    cos_back, sin_back = wave_tables(modes_z, zpos, depth, weights_z[:, None])
    back_tables = jnp.stack([cos_back, -sin_back])
    spectral_field = jnp.einsum(
        "rwxyk,rkz->wxyz", back_x, back_tables, precision=lax.Precision.HIGHEST
    )
    mixed = jnp.dot(local_weight, lift_weight, precision=lax.Precision.HIGHEST)
    pre_act = (
        spectral_field
        + jnp.einsum("wc,cxyz->wxyz", mixed, fields, precision=lax.Precision.HIGHEST)
        + local_bias[:, None, None, None]
    )
    activated, gelu_back = jax.vjp(jax.nn.gelu, pre_act)
    predicted = jnp.einsum("w,wxyz->xyz", proj_weight, activated, precision=lax.Precision.HIGHEST)
    grad_pre = gelu_back(proj_weight[:, None, None, None] * cotangent[None])[0]
    field_sums = jnp.einsum("wxyz,cxyz->wc", grad_pre, fields, precision=lax.Precision.HIGHEST)
    proj_sums = jnp.einsum("wxyz,xyz->w", activated, cotangent, precision=lax.Precision.HIGHEST)
    field_sums, proj_sums = lax.psum((field_sums, proj_sums), ("gx", "gy"))
    grad_modes = spectral_forward(grad_pre, weights_z, 1.0 / total_x, 1.0 / total_y)
    grad_real = outer(grad_modes[0], spectrum[0]) + outer(grad_modes[1], spectrum[1])
    grad_imag = outer(grad_modes[1], spectrum[0]) - outer(grad_modes[0], spectrum[1])
    grad_spectral = jnp.stack([grad_real, grad_imag]).reshape(2, own_x, own_y, KZ, WIDTH * WIDTH)
    scale = 1.0 / math.sqrt(total_x * total_y * depth)
    grad_local = jnp.dot(field_sums, lift_weight.T, precision=lax.Precision.HIGHEST) * scale
    grad_proj = proj_sums * scale
    return (phase_next, solute_next, predicted, grad_spectral, grad_local, grad_proj)


LANES = 128
SMALL_VMEM = 24 * 1024 * 1024
PACK_COST = 50_000_000_000
SPREAD = LANES // WIDTH
NARROW = jnp.bfloat16
EXACT = lax.Precision.HIGHEST


def halves(table):
    head = table.astype(np.float32).astype(ml_dtypes.bfloat16)
    rest = (table - head.astype(np.float64)).astype(np.float32).astype(ml_dtypes.bfloat16)
    return head, rest


def left_table(table):
    head, rest = halves(table)
    return np.concatenate([head, head, rest], axis=1)


def right_table(table):
    head, rest = halves(table)
    return np.concatenate([head, head, rest], axis=0)


def parts_of(values):
    head = values.astype(NARROW)
    return head, (values - head.astype(jnp.float32)).astype(NARROW)


def thrice(values, axis):
    head, rest = parts_of(values)
    return jnp.concatenate([head, rest, head], axis=axis)


def one_where(mask):
    return mask.astype(jnp.float32).astype(NARROW)


def mul(left, right):
    return jnp.dot(left, right, preferred_element_type=jnp.float32)


def mul_rows(left, right):
    return lax.dot_general(
        left, right, (((1,), (1,)), ((), ())), preferred_element_type=jnp.float32
    )


def angles(freqs, positions, length):
    return 2.0 * np.pi * ((freqs[:, None] * positions[None, :]) % length) / length


def signed(count):
    index = np.arange(count)
    return np.where(index < count // 2, index, index - count)


def rotation(theta, orient):
    cosines, sines = np.cos(theta), orient * np.sin(theta)
    return np.block([[cosines, -sines], [sines, cosines]])


def group_of(shape):
    return lax.broadcasted_iota(jnp.int32, shape, len(shape) - 1) // WIDTH


def pick(groups, choices):
    result = choices[-1]
    for index in range(len(choices) - 2, -1, -1):
        result = jnp.where(groups == index, choices[index], result)
    return result


def turn(values, shift):
    shift = shift % LANES
    return values if shift == 0 else pltpu.roll(values, shift, 1)


def swap_groups(pieces):
    groups = group_of(pieces[0].shape)
    return [
        pick(groups, [turn(pieces[i], WIDTH * (i - j)) for i in range(SPREAD)])
        for j in range(SPREAD)
    ]


def spread_cells(
    lift_ref, local_ref, bias_ref, proj_ref, cotangent_ref, vector_ref, mix_ref, spread_ref
):
    planes, depth, wide = spread_ref.shape
    tile = cotangent_ref.shape[0]
    cells_y = tile // planes
    lift, lift_rest = parts_of(lift_ref[...])
    local, local_rest = parts_of(local_ref[...])
    mixed = mul_rows(lift, local) + mul_rows(lift_rest, local) + mul_rows(lift, local_rest)
    for index in range(wide // WIDTH):
        place = slice(index * WIDTH, (index + 1) * WIDTH)
        vector_ref[0:2, place] = mixed
        vector_ref[2:3, place] = bias_ref[...]
        vector_ref[3:4, place] = proj_ref[...]
    head, rest = parts_of(vector_ref[...])
    row = lax.broadcasted_iota(jnp.int32, (cells_y, wide), 0)
    own = row == lax.broadcasted_iota(jnp.int32, (cells_y, wide), 1) // WIDTH

    def diagonal(line):
        return jnp.where(own, line.astype(jnp.float32), 0.0)

    mixing = [diagonal(part[k : k + 1]) for k in range(2) for part in (head, head, rest)]
    blank = jnp.zeros((2 * cells_y, wide), jnp.float32)
    mix_ref[...] = jnp.concatenate(mixing + [blank], axis=0).astype(NARROW)
    spread = jnp.concatenate(parts_of(cotangent_ref[...].T), axis=1)
    cell = lax.broadcasted_iota(jnp.int32, (2 * tile, wide), 0) % tile
    row = lax.broadcasted_iota(jnp.int32, (2 * tile, wide), 1) // WIDTH
    for plane in range(planes):
        spread_ref[plane] = mul(spread, one_where(cell == plane * cells_y + row))


def contract_kernel(
    planes,
    lift_ref,
    weight_ref,
    local_ref,
    bias_ref,
    proj_ref,
    cotangent_ref,
    out_ref,
    vector_ref,
    mix_ref,
    spread_ref,
    outer_ref,
    wide_ref,
):
    _, own_x, own_y, modes_z, width = weight_ref.shape
    chunk = out_ref.shape[0] // modes_z
    steps = own_x // planes

    square = (WIDTH, WIDTH)
    diagonal = lax.broadcasted_iota(jnp.int32, square, 0) == lax.broadcasted_iota(
        jnp.int32, square, 1
    )
    columns = [
        jnp.sum(
            jnp.where(diagonal, jnp.broadcast_to(lift_ref[k : k + 1, :], square), 0.0),
            axis=1,
            keepdims=True,
        )
        for k in range(2)
    ]
    lane = lax.broadcasted_iota(jnp.int32, (WIDTH, LANES), 1)
    base = jnp.where(
        lane % (2 * WIDTH) < WIDTH,
        jnp.broadcast_to(columns[0], lane.shape),
        jnp.broadcast_to(columns[1], lane.shape),
    )
    head, rest = parts_of(base)
    base = jnp.where(lane < 2 * WIDTH, head.astype(jnp.float32), rest.astype(jnp.float32))
    mixing = jnp.concatenate(
        [jnp.where(lane % WIDTH == channel, base, 0.0) for channel in range(WIDTH)], axis=0
    ).astype(NARROW)
    rows = planes * own_y * modes_z
    low = lax.broadcasted_iota(jnp.int32, (rows, LANES), 1) < 2 * WIDTH
    for step in range(steps):
        sums = []
        for part in range(2):
            block = weight_ref[part, step * planes : (step + 1) * planes]
            head, rest = parts_of(block.reshape(rows, width))
            total = mul(head, mixing) + mul(rest, mixing)
            sums.append(total + turn(total, 2 * WIDTH))
        result = jnp.where(low, sums[0], sums[1])
        for plane in range(planes):
            for row in range(own_y):
                first = (plane * own_y + row) * modes_z
                place = row * own_x + step * planes + plane
                out_ref[pl.ds(place, modes_z, stride=chunk), :] = result[
                    first : first + modes_z
                ]
    spread_cells(
        lift_ref,
        local_ref,
        bias_ref,
        proj_ref,
        cotangent_ref,
        vector_ref,
        mix_ref,
        spread_ref,
    )
    for index in range(SPREAD):
        wide_ref[:, index * WIDTH : (index + 1) * WIDTH] = lift_ref[...]
    for index in range(1, width // LANES):
        wide_ref[:, index * LANES : (index + 1) * LANES] = wide_ref[:, 0:LANES]
    shape = (2 * WIDTH, width)
    row = lax.broadcasted_iota(jnp.int32, shape, 0)
    column = lax.broadcasted_iota(jnp.int32, shape, 1)
    lift = jnp.where(row < WIDTH, wide_ref[0:1, :], wide_ref[1:2, :])
    head, rest = parts_of(jnp.where(column // WIDTH == row % WIDTH, lift, 0.0))
    outer_ref[0 : 2 * WIDTH] = head
    outer_ref[2 * WIDTH : 4 * WIDTH] = head
    outer_ref[4 * WIDTH : 6 * WIDTH] = rest
    outer_ref[6 * WIDTH : 8 * WIDTH] = jnp.zeros_like(rest)


def edge_kernel(held_ref, head_ref, tail_ref):
    cells_x = held_ref.shape[1]
    for index, reach in enumerate((2, 2, 1)):
        head_ref[2 * index : 2 * index + reach] = held_ref[index, 0:reach]
        tail_ref[2 * index : 2 * index + reach] = held_ref[index, cells_x - reach : cells_x]


def pack_kernel(held_ref, before_ref, after_ref, head_ref, tail_ref):
    _, cells_x, cells_y, _ = held_ref.shape
    for out, near, far in ((head_ref, 0, 1), (tail_ref, cells_y - 1, cells_y - 2)):
        for plane in range(cells_x):
            line = slice(plane, plane + 1)
            for index in range(2):
                out[2 * index, line] = held_ref[index, plane, near : near + 1]
                out[2 * index + 1, line] = held_ref[index, plane, far : far + 1]
            out[4, line] = held_ref[2, plane, near : near + 1]
        for index in range(2):
            out[5, 2 * index : 2 * index + 1] = before_ref[2 * index + 1, near : near + 1]
            out[5, 2 * index + 1 : 2 * index + 2] = after_ref[2 * index, near : near + 1]


def step_kernel(
    held_ref,
    before_ref,
    after_ref,
    low_ref,
    high_ref,
    table_ref,
    mixed_ref,
    fields_ref,
    send_ref,
    phase_ext,
    solute_ext,
    cool_ext,
    diff_ext,
    lines,
):
    _, cells_x, cells_y, depth = held_ref.shape
    base = 8
    end = base + cells_y
    for index, ext in enumerate((phase_ext, solute_ext)):
        first = 2 * index
        ext[2 : cells_x + 2, base:end] = held_ref[index]
        ext[0:2, base:end] = before_ref[first : first + 2]
        ext[cells_x + 2 : cells_x + 4, base:end] = after_ref[first : first + 2]
        for source, near in ((low_ref, base - 1), (high_ref, end)):
            for plane in range(cells_x):
                ext[plane + 2, near : near + 1] = source[first, plane : plane + 1]
            ext[1, near : near + 1] = source[5, first : first + 1]
            ext[cells_x + 2, near : near + 1] = source[5, first + 1 : first + 2]
    cool_ext[2 : cells_x + 2, base:end] = held_ref[2]
    cool_ext[1:2, base:end] = before_ref[4:5]
    cool_ext[cells_x + 2 : cells_x + 3, base:end] = after_ref[4:5]

    send_ref[...] = mixed_ref[...]

    def sweep(reach):
        diff_ext[...] = diffusivity(phase_ext[...])

        def window(ext, move_x, move_y):
            return ext[
                2 - reach + move_x : cells_x + 2 + reach + move_x, base + move_y : end + move_y
            ]

        def around(ext, now):
            return [
                window(ext, 1, 0),
                window(ext, -1, 0),
                window(ext, 0, 1),
                window(ext, 0, -1),
                pltpu.roll(now, depth - 1, 2),
                pltpu.roll(now, 1, 2),
            ]

        phase_now = window(phase_ext, 0, 0)
        solute_now = window(solute_ext, 0, 0)
        diff_now = window(diff_ext, 0, 0)
        return update(
            phase_now,
            solute_now,
            window(cool_ext, 0, 0),
            around(phase_ext, phase_now),
            around(solute_ext, solute_now),
            diff_now,
            around(diff_ext, diff_now),
        )

    def edge(source, row, sign):
        values, sides = [], []
        for index in range(2):
            near, far = source[2 * index], source[2 * index + 1]
            inner = jnp.concatenate(
                [held_ref[index, plane, row : row + 1] for plane in range(cells_x)], axis=0
            )
            before = source[5, 2 * index : 2 * index + 1]
            after = source[5, 2 * index + 1 : 2 * index + 2]
            values.append(near)
            sides.append(
                [
                    jnp.concatenate([near[1:], after], axis=0),
                    jnp.concatenate([before, near[:-1]], axis=0),
                    *((inner, far) if sign < 0 else (far, inner)),
                    pltpu.roll(near, depth - 1, 1),
                    pltpu.roll(near, 1, 1),
                ]
            )
        diffs = [diffusivity(side) for side in sides[0]]
        return update(*values, source[4], *sides, diffusivity(values[0]), diffs)

    phase_mid, solute_mid = sweep(1)
    edges = (edge(low_ref, 0, -1), edge(high_ref, cells_y - 1, 1))
    phase_ext[1 : cells_x + 3, base:end] = phase_mid
    solute_ext[1 : cells_x + 3, base:end] = solute_mid
    for place, moved in zip((base - 1, end), edges):
        for ext, line in zip((phase_ext, solute_ext), moved):
            for plane in range(cells_x):
                ext[plane + 2, place : place + 1] = line[plane : plane + 1]
    phase_next, solute_next = sweep(0)
    fields_ref[0] = phase_next
    fields_ref[1] = solute_next
    tile = cells_x * cells_y
    both = (phase_next.reshape(tile, depth), solute_next.reshape(tile, depth) - SOLUTE_MEAN)
    ordered = []
    for part in range(depth // LANES):
        for index, values in enumerate(both):
            lines[part, index * tile : (index + 1) * tile] = values[
                :, part * LANES : (part + 1) * LANES
            ]
        ordered.append(
            jnp.concatenate(
                [
                    lines[part, pl.ds(row, 2 * cells_x, stride=cells_y), :]
                    for row in range(cells_y)
                ],
                axis=0,
            )
        )
    ordered = jnp.concatenate(ordered, axis=1)
    spectra = mul_rows(table_ref[...], thrice(ordered, 1))
    modes_z = spectra.shape[0] // 2
    chunk = send_ref.shape[0] // modes_z
    for part in range(2):
        send_ref[pl.ds(chunk - 2 + part, modes_z, stride=chunk), :] = spectra[
            part * modes_z : (part + 1) * modes_z
        ]


def pack_modes(shape, modes, modes_ref, rows_ref):
    count_x, count_y, _, _, own_x, own_y = shape
    modes_x, modes_y = count_x * own_x, count_y * own_y
    lane = lax.broadcasted_iota(jnp.int32, (modes_y, LANES), 1)
    for index in range(count_x):
        block = modes
        for k in range(4):
            shift = k * own_x - k * modes_x - index * own_x
            block = jnp.where(lane // own_x == k, turn(modes, shift), block)
        rows_ref[index] = block
        line = rows_ref[index, pl.ds(0, count_y, stride=own_y), :]
        groups = group_of(line.shape)
        for row in range(1, own_y):
            piece = rows_ref[index, pl.ds(row, count_y, stride=own_y), :]
            line = jnp.where(groups == row, turn(piece, row * WIDTH), line)
        modes_ref[index * count_y : (index + 1) * count_y] = line


def spectral_kernel(
    shape,
    mixed_ref,
    y_in_ref,
    x_in_ref,
    y_out_ref,
    x_out_ref,
    fields_ref,
    forth_ref,
    chosen_ref,
    gather_ref,
    modes_ref,
    send_ref,
    table_ref,
    line_ref,
    lines_y,
    lines_x,
    rows_ref,
    weight_ref,
):
    count_x, count_y, cells_x, cells_y, own_x, own_y = shape
    modes_x, modes_y = count_x * own_x, count_y * own_y
    total_x, total_y = count_x * cells_x, count_y * cells_y
    tile = cells_x * cells_y
    narrow = 2 * cells_x
    rows = 2 * count_y
    devices = count_x * count_y
    own = own_x * own_y
    chunk = mixed_ref.shape[0] // devices
    spectra = [mixed_ref[pl.ds(own + part, devices, stride=chunk), :] for part in range(2)]
    for index in range(devices):
        weight_ref[index * own : (index + 1) * own, :] = mixed_ref[
            index * chunk : index * chunk + own, :
        ]
    lane = lax.broadcasted_iota(jnp.int32, (rows, LANES), 1)
    blocks = []
    for row in range(cells_y):
        block = jnp.zeros((rows, LANES), jnp.float32)
        for index in range(count_x):
            piece = jnp.concatenate(
                [values[index * count_y : (index + 1) * count_y] for values in spectra], axis=0
            )
            piece = turn(piece, narrow * (index - row))
            block = jnp.where(lane // narrow == index, piece, block)
        blocks.append(block)
    along_y = mul(y_in_ref[...], thrice(jnp.concatenate(blocks, axis=0), 0))
    prepare(fields_ref, forth_ref, table_ref, line_ref)
    half = lax.broadcasted_iota(jnp.int32, (modes_y, LANES), 1) < LANES // 2
    joined = jnp.where(half, along_y[0:modes_y], turn(along_y[modes_y:], LANES // 2))
    modes = mul(thrice(joined, 1), x_in_ref[...])
    quads_y = total_y // SPREAD
    quads_x = modes_x // SPREAD
    lane = lax.broadcasted_iota(jnp.int32, (modes_y, LANES), 1) % modes_x
    chosen = jnp.concatenate(
        [jnp.where(lane == freq, modes, 0.0) for freq in range(modes_x)], axis=0
    )
    columns = mul(jnp.concatenate(parts_of(chosen), axis=1), chosen_ref[...])
    low = lax.broadcasted_iota(jnp.int32, (modes_y, LANES), 1) < 2 * WIDTH
    def gathered(quads):
        products = [[], []]
        for quad in quads:
            lines = [[], []]
            for index in range(SPREAD):
                freq = SPREAD * quad + index
                start = (freq // own_x) * count_y * own_y * own_x + freq % own_x
                weights = weight_ref[pl.ds(start, modes_y, stride=own_x), :]
                for part in range(2):
                    column = columns[
                        freq * modes_y : (freq + 1) * modes_y, part * LANES : (part + 1) * LANES
                    ]
                    line = weights * column
                    lines[part].append(line + turn(line, 2 * WIDTH))
            for part in range(2):
                pairs = [
                    jnp.where(low, lines[part][index], lines[part][index + 1])
                    for index in range(0, SPREAD, 2)
                ]
                products[part].append(jnp.concatenate(pairs, axis=1))
        products = jnp.concatenate(products[0] + products[1], axis=0)
        products = mul(jnp.concatenate(parts_of(products), axis=1), gather_ref[...])
        stacked = []
        for index in range(len(quads)):
            places = [(part * len(quads) + index) * modes_y for part in range(2)]
            stacked.append(
                jnp.concatenate([products[place : place + modes_y] for place in places], axis=0)
            )
        return thrice(jnp.concatenate(stacked, axis=1), 0)

    def along_lines(quads, stacked):
        back = mul(y_out_ref[...], stacked)
        for index, quad in enumerate(quads):
            lines_y[quad] = back[:, index * LANES : (index + 1) * LANES]
        for quad in quads:
            for part in range(2):
                pieces = [
                    lines_y[quad, pl.ds(part * total_y + i, quads_y, stride=SPREAD), :]
                    for i in range(SPREAD)
                ]
                for index, piece in enumerate(swap_groups(pieces)):
                    place = part * modes_x + SPREAD * quad + index
                    lines_x[pl.ds(place, quads_y, stride=2 * modes_x), :] = piece

    batches = [range(first, first + 2) for first in range(0, quads_x, 2)]
    following = gathered(batches[0])
    for index, quads in enumerate(batches):
        stacked = following
        if index + 1 < len(batches):
            following = gathered(batches[index + 1])
        along_lines(quads, stacked)
    per_tile = cells_y // SPREAD
    for start in range(0, quads_y, 4):
        blocks = [
            lines_x[quad * 2 * modes_x : (quad + 1) * 2 * modes_x, :]
            for quad in range(start, start + 4)
        ]
        back = mul(x_out_ref[...], thrice(jnp.concatenate(blocks, axis=1), 0))
        for quad in range(start, start + 4):
            lanes = slice((quad - start) * LANES, (quad - start + 1) * LANES)
            for part in range(2):
                for index in range(count_x):
                    device = index * count_y + quad // per_tile
                    place = (device * 2 + part) * per_tile + quad % per_tile
                    first = part * total_x + index * cells_x
                    send_ref[place * cells_x : (place + 1) * cells_x, :] = back[
                        first : first + cells_x, lanes
                    ]
    pack_modes(shape, modes, modes_ref, rows_ref)


def prepare(fields_ref, forth_ref, table_ref, line_ref):
    planes, depth, _ = table_ref.shape
    cells_y = fields_ref.shape[2]
    tile = planes * cells_y
    rows = forth_ref.shape[0] // 2
    fields = (fields_ref[0].reshape(tile, depth), fields_ref[1].reshape(tile, depth) - SOLUTE_MEAN)
    blank = jnp.zeros((2 * cells_y, depth), jnp.float32)
    table = forth_ref[rows:].astype(jnp.float32)
    for plane in range(planes):
        lines = [values[plane * cells_y : (plane + 1) * cells_y] for values in fields]
        pieces = [[part.astype(jnp.float32) for part in parts_of(values)] for values in lines]
        both = [piece for head, rest in pieces for piece in (head, rest, head)]
        both = jnp.concatenate([table] + both + [blank], axis=0)
        table_ref[plane] = both.T.astype(NARROW)
        pieces = [piece for pair in zip(*pieces) for piece in pair]
        line_ref[plane] = jnp.concatenate(pieces, axis=0).astype(NARROW)


def fold_channels(values):
    quarter = values.shape[0] // SPREAD
    parts = []
    for first in range(0, values.shape[1], LANES):
        pieces = [
            values[index * quarter : (index + 1) * quarter, first : first + LANES]
            for index in range(SPREAD)
        ]
        channel = lax.broadcasted_iota(jnp.int32, pieces[0].shape, 1) % WIDTH
        span = WIDTH // 2
        while len(pieces) > 1:
            low = channel % (2 * span) < span
            pieces = [
                jnp.where(low, left + turn(left, -span), right + turn(right, span))
                for left, right in zip(pieces[: len(pieces) // 2], pieces[len(pieces) // 2 :])
            ]
            span //= 2
        parts.append(pieces[0])
    return jnp.concatenate(parts, axis=1)


def field_kernel(
    cells_y,
    field_ref,
    table_ref,
    mix_ref,
    weight_ref,
    line_ref,
    vector_ref,
    back_ref,
    forth_ref,
    predicted_ref,
    send_ref,
    shares_ref,
):
    planes, depth, wide = weight_ref.shape
    rows = forth_ref.shape[0] // 2
    halves_y = cells_y // SPREAD
    stride = halves_y * planes
    bias = vector_ref[2:3, :]
    proj = vector_ref[3:4, :]
    root = math.sqrt(2.0 / math.pi)
    curve = 0.044715
    picker = one_where(
        lax.broadcasted_iota(jnp.int32, (SPREAD * cells_y, 2 * wide), 0)
        == lax.broadcasted_iota(jnp.int32, (SPREAD * cells_y, 2 * wide), 1)
        % wide
        // (WIDTH // SPREAD)
    )
    line_sums = jnp.zeros((2 * cells_y, wide), jnp.float32)
    proj_sums = jnp.zeros((8, wide), jnp.float32)
    def back(plane):
        spectra = jnp.concatenate(
            [
                field_ref[pl.ds(part * planes + plane, rows, stride=stride), :]
                for part in range(halves_y)
            ],
            axis=1,
        )
        spectra = jnp.concatenate([thrice(spectra, 0), mix_ref[...]], axis=0)
        table = jnp.concatenate([back_ref[...], table_ref[plane]], axis=1)
        return mul(table, spectra) + bias

    def activate(pre, plane):
        square = pre * pre
        bent = jnp.tanh(pre * (root + (root * curve) * square))
        upper = 0.5 + 0.5 * bent
        active = pre * upper
        slope = upper + (active - active * bent) * (root + (3.0 * root * curve) * square)
        cotangent = weight_ref[plane]
        grad = proj * cotangent * slope
        sums = jnp.sum((active * cotangent).reshape(depth // 8, 8, wide), axis=0)
        return sums, parts_of(fold_channels(proj * active)), parts_of(grad)

    def forth(shared, grad, plane):
        shares_ref[plane, :, 0 : depth // SPREAD] = mul_rows(
            picker, jnp.concatenate(shared, axis=1)
        )
        for index in range(SPREAD):
            predicted_ref[
                plane * cells_y : (plane + 1) * cells_y,
                index * (depth // SPREAD) : (index + 1) * (depth // SPREAD),
            ] = shares_ref[plane, pl.ds(index, cells_y, stride=SPREAD), 0 : depth // SPREAD]
        head, rest = grad
        lines = line_ref[plane]
        top = jnp.concatenate([forth_ref[0:rows], lines[0 : 2 * cells_y]], axis=0)
        low = jnp.concatenate([forth_ref[rows:], lines[2 * cells_y :]], axis=0)
        spectra = mul(jnp.concatenate([top, low], axis=0), head)
        spectra = spectra[0 : rows + 2 * cells_y] + spectra[rows + 2 * cells_y :] + mul(top, rest)
        for part in range(halves_y):
            send_ref[pl.ds(part * planes + plane, rows, stride=stride), :] = spectra[
                0:rows, part * LANES : (part + 1) * LANES
            ]
        return spectra[rows:]

    following = back(0)
    previous = None
    for plane in range(planes + 1):
        pre = following
        if plane + 1 < planes:
            following = back(plane + 1)
        if plane < planes:
            sums, *current = activate(pre, plane)
            proj_sums = proj_sums + sums
        if plane > 0:
            line_sums = line_sums + forth(*previous, plane - 1)
        previous = current
    shape = (cells_y, wide)
    own = lax.broadcasted_iota(jnp.int32, shape, 0) == (
        lax.broadcasted_iota(jnp.int32, shape, 1) // WIDTH
    )
    sums = [
        jnp.where(own, line_sums[0:cells_y], 0.0),
        jnp.where(own, line_sums[cells_y:], 0.0),
        proj_sums,
    ]
    for index, values in enumerate(sums):
        line = jnp.sum(values, axis=0, keepdims=True)
        line = sum(line[:, part * LANES : (part + 1) * LANES] for part in range(halves_y))
        send_ref[stride + index : stride + index + 1, :] = line


def gradient_kernel(
    shape, spectra_ref, modes_ref, x_in_ref, y_in_ref, send_ref, lines_x, lines_y
):
    count_x, count_y, cells_x, cells_y, own_x, own_y = shape
    modes_x, modes_y = count_x * own_x, count_y * own_y
    total_x, total_y = count_x * cells_x, count_y * cells_y
    per_tile = cells_y // SPREAD
    quads_y = total_y // SPREAD
    chunk = 2 * per_tile * cells_x
    first_device = (lax.axis_index("gx") == 0) & (lax.axis_index("gy") == 0)
    keep = jnp.where(first_device, 0.0, 1.0)
    devices = count_x * count_y
    out_chunk = send_ref.shape[0] // devices
    per_own = own_x // SPREAD
    quads_x = modes_x // SPREAD
    for start in range(0, quads_y, SPREAD):
        blocks = []
        for quad in range(start, start + SPREAD):
            block = []
            for part in range(2):
                for index in range(count_x):
                    device = index * count_y + quad // per_tile
                    place = (device * 2 + part) * per_tile + quad % per_tile
                    piece = spectra_ref[place * cells_x : (place + 1) * cells_x, :]
                    block.append(piece * keep if part else piece)
            blocks.append(jnp.concatenate(block, axis=0))
        forth = mul(x_in_ref[...], thrice(jnp.concatenate(blocks, axis=1), 0))
        for quad in range(start, start + SPREAD):
            lines_x[quad * 2 * modes_x : (quad + 1) * 2 * modes_x, :] = forth[
                :, (quad - start) * LANES : (quad - start + 1) * LANES
            ]
    extra = 2 * per_own * own_y
    send_ref[pl.ds(extra, devices, stride=out_chunk), :] = modes_ref[...]
    groups = group_of((1, LANES))
    total = jnp.zeros((1, LANES), jnp.float32)
    for index in range(3):
        start = chunk // 2 + index
        line = jnp.sum(
            spectra_ref[pl.ds(start, devices, stride=chunk), :], axis=0, keepdims=True
        )
        line = line + turn(line, 2 * WIDTH)
        total = jnp.where(groups == index, line + turn(line, WIDTH), total)
    send_ref[pl.ds(extra + 1, devices, stride=out_chunk), :] = jnp.broadcast_to(
        total, (devices, LANES)
    )
    for start in range(0, quads_x, 2):
        for quad in range(start, start + 2):
            for part in range(2):
                pieces = [
                    lines_x[
                        pl.ds(part * modes_x + SPREAD * quad + j, quads_y, stride=2 * modes_x), :
                    ]
                    for j in range(SPREAD)
                ]
                for index, piece in enumerate(swap_groups(pieces)):
                    lines_y[quad, pl.ds(part * total_y + index, quads_y, stride=SPREAD), :] = piece
        lines = jnp.concatenate([lines_y[start], lines_y[start + 1]], axis=1)
        modes = mul(y_in_ref[...], thrice(lines, 0))
        for quad in range(start, start + 2):
            for part in range(2):
                for index in range(count_y):
                    device = (quad // per_own) * count_y + index
                    place = device * out_chunk + (part * per_own + quad % per_own) * own_y
                    first = part * modes_y + index * own_y
                    send_ref[place : place + own_y, :] = modes[
                        first : first + own_y, (quad - start) * LANES : (quad - start + 1) * LANES
                    ]


def outer_kernel(
    scale,
    modes_ref,
    narrow_ref,
    predicted_ref,
    fields_ref,
    mix_ref,
    repeat_ref,
    spread_ref,
    local_out,
    proj_out,
    predicted_out,
    phase_out,
    solute_out,
    grad_ref,
    local_ref,
    proj_ref,
    held,
    sent,
):
    _, own_x, own_y, modes_z, width = held.shape
    chunk = modes_ref.shape[0] // modes_z
    per_own = own_x // SPREAD
    extra = 2 * per_own * own_y
    copies = [
        pltpu.make_async_copy(predicted_ref, predicted_out, sent.at[own_x]),
        pltpu.make_async_copy(fields_ref.at[0], phase_out, sent.at[own_x + 1]),
        pltpu.make_async_copy(fields_ref.at[1], solute_out, sent.at[own_x + 2]),
    ]
    for copy in copies:
        copy.start()
    lane = lax.broadcasted_iota(jnp.int32, (modes_z, LANES), 1)
    low = lane < 2 * WIDTH

    def rows_of(values):
        head, rest = parts_of(values)
        both = jnp.where(low, head.astype(jnp.float32), rest.astype(jnp.float32)).astype(NARROW)
        return jnp.concatenate([both, head], axis=1)

    def repeated(half):
        grads = [
            modes_ref[pl.ds((part * per_own + half) * own_y + row, modes_z, stride=chunk), :]
            for part in range(2)
            for row in range(own_y)
        ]
        grads = jnp.concatenate(grads, axis=0)
        return mul(jnp.concatenate(parts_of(grads), axis=1), repeat_ref[...])

    modes = modes_ref[pl.ds(extra, modes_z, stride=chunk), :]
    own = lane // (4 * own_x) * own_x + lane % own_x
    for plane in range(own_x):
        if plane % SPREAD == 0:
            grads = repeated(plane // SPREAD)
        chosen = jnp.concatenate(
            [jnp.where(own == row * own_x + plane, modes, 0.0) for row in range(own_y)], axis=0
        )
        columns = mul(jnp.concatenate(parts_of(chosen), axis=1), spread_ref[...])
        reals, imags = [], []
        for row in range(own_y):
            real = columns[row * modes_z : (row + 1) * modes_z, 0:LANES]
            imag = columns[row * modes_z : (row + 1) * modes_z, LANES:]
            pair = []
            for part in range(2):
                first = (part * own_y + row) * modes_z
                group = plane % SPREAD * LANES
                pair.append(grads[first : first + modes_z, group : group + LANES])
            reals.append(rows_of(pair[0] * real + pair[1] * imag))
            imags.append(rows_of(pair[1] * real - pair[0] * imag))
        result = mul(jnp.concatenate(reals + imags, axis=0), mix_ref[...])
        held[:, plane] = result.reshape(2, own_y, modes_z, width)
        copies.append(
            pltpu.make_async_copy(held.at[:, plane], grad_ref.at[:, plane], sent.at[plane])
        )
        copies[-1].start()
    line = modes_ref[extra + 1 : extra + 2, :]
    square = (WIDTH, WIDTH)
    diagonal = lax.broadcasted_iota(jnp.int32, square, 0) == lax.broadcasted_iota(
        jnp.int32, square, 1
    )
    local = jnp.zeros(square, jnp.float32)
    for k in range(2):
        sums = jnp.broadcast_to(line[:, k * WIDTH : (k + 1) * WIDTH], square)
        sums = jnp.sum(jnp.where(diagonal, sums, 0.0), axis=1, keepdims=True)
        local = local + sums * narrow_ref[k : k + 1, :]
    local_ref[...] = scale * local
    proj_ref[...] = scale * line[:, 2 * WIDTH : 3 * WIDTH]
    copies.append(pltpu.make_async_copy(local_ref, local_out, sent.at[own_x + 3]))
    copies.append(pltpu.make_async_copy(proj_ref, proj_out, sent.at[own_x + 4]))
    copies[-2].start()
    copies[-1].start()
    for copy in copies:
        copy.wait()


def tables(shape, depth, modes_z):
    count_x, count_y, cells_x, cells_y, own_x, own_y = shape
    modes_x, modes_y = count_x * own_x, count_y * own_y
    total_x, total_y = count_x * cells_x, count_y * cells_y
    theta_z = angles(np.arange(modes_z), np.arange(depth), depth)
    theta_x = angles(signed(modes_x), np.arange(total_x), total_x)
    theta_y = angles(signed(modes_y), np.arange(total_y), total_y)
    plain_z = np.concatenate([np.cos(theta_z), -np.sin(theta_z)], axis=0)
    forth_z = plain_z.reshape(2, modes_z, depth).transpose(1, 0, 2).reshape(2 * modes_z, depth)
    weight = np.where(np.arange(modes_z) == 0, 1.0, 2.0) / (total_x * total_y * depth)
    weighted_z = np.repeat(weight, 2)[:, None] * forth_z
    forth_x, back_x = rotation(theta_x, -1.0), rotation(theta_x.T, 1.0)
    forth_y, back_y = rotation(theta_y, -1.0), rotation(theta_y.T, 1.0)
    order_y = forth_y.reshape(2 * modes_y, 2, count_y, cells_y)
    order_y = order_y.transpose(0, 3, 1, 2).reshape(2 * modes_y, 2 * total_y)
    lines = forth_x.reshape(2, modes_x, 2, count_x, cells_x)
    both = np.zeros((2, count_x, 2, cells_x, 2, 2, modes_x))
    for field in range(2):
        both[:, :, field, :, :, field, :] = lines.transpose(2, 3, 4, 0, 1)
    both = both.reshape(4 * total_x, 4 * modes_x)
    index = np.arange(4 * LANES)
    line = index[: 2 * LANES, None] % LANES
    group = index[None, : 2 * LANES] // WIDTH
    same = np.where(group < 4, group, (group + 2) % 4)
    signs = np.where((group == 2) | (group == 3), -1.0, 1.0)
    chosen = np.where(line // modes_x == same, signs, 0.0)
    half = 2 * WIDTH
    row, column = index[:, None] % (SPREAD * half), index[None, :LANES]
    gather = row // half * WIDTH + row % WIDTH == column
    repeat = line == index[None, :] // LANES * WIDTH + index[None, :] % WIDTH
    spread = line // own_x % 4 == group // 4 * 2 + group % 2
    masks = {"chosen": chosen, "gather": gather, "repeat": repeat, "spread": spread}
    masks = {name: mask.astype(ml_dtypes.bfloat16) for name, mask in masks.items()}
    return masks | {
        "z_plain": left_table(plain_z),
        "z_forth": np.concatenate(halves(weighted_z), axis=0),
        "z_back": left_table(weighted_z.T)[:, : 4 * modes_z],
        "y_first": left_table(order_y),
        "x_first": right_table(both),
        "y_back": left_table(back_y),
        "x_back": left_table(back_x),
        "x_forth": left_table(forth_x),
        "y_forth": left_table(forth_y),
    }


def fits(count_x, count_y, phase, spectral_weight):
    cells_x, cells_y, depth = phase.shape
    _, own_x, own_y, modes_z, width = spectral_weight.shape
    return (
        width == WIDTH * WIDTH
        and modes_z == count_x * count_y
        and 4 * modes_z == LANES
        and 4 * count_x * cells_x == LANES
        and 4 * count_x * own_x == LANES
        and 2 * cells_x * cells_y == LANES
        and cells_x == 8
        and cells_y % SPREAD == 0
        and own_x % SPREAD == 0
        and own_y * 4 * own_x == LANES
        and 3 * WIDTH <= LANES
        and cells_y == 8
        and depth % LANES == 0
    )


def call(kernel, outs, scratch, flops, moved, limit=SMALL_VMEM, **more):
    return pl.pallas_call(
        kernel,
        out_shape=outs,
        scratch_shapes=scratch,
        compiler_params=pltpu.CompilerParams(vmem_limit_bytes=limit),
        cost_estimate=pl.CostEstimate(flops=flops, bytes_accessed=moved, transcendentals=0),
        **more,
    )


def exchange(values):
    return lax.all_to_all(values, ("gx", "gy"), split_axis=0, concat_axis=0, tiled=True)


def per_device_fast(
    phase,
    solute,
    undercool,
    lift_weight,
    spectral_weight,
    local_weight,
    local_bias,
    proj_weight,
    cotangent,
):
    count_x, count_y = lax.axis_size("gx"), lax.axis_size("gy")
    cells_x, cells_y, depth = phase.shape
    _, own_x, own_y, modes_z, width = spectral_weight.shape
    shape = (count_x, count_y, cells_x, cells_y, own_x, own_y)
    devices = count_x * count_y
    tile = cells_x * cells_y
    modes_x, modes_y = count_x * own_x, count_y * own_y
    total_x, total_y = count_x * cells_x, count_y * cells_y
    table = tables(shape, depth, modes_z)
    real = jnp.float32

    def like(*dims):
        return jax.ShapeDtypeStruct(dims, real)

    far = pl.BlockSpec(memory_space=pltpu.HBM)
    weight_bytes = 8 * own_x * own_y * modes_z * width
    held = jnp.stack([phase, solute, undercool])
    head, tail = call(
        edge_kernel,
        (like(5, cells_y, depth), like(5, cells_y, depth)),
        [],
        1000,
        40 * tile * depth,
    )(held)

    def ring(values, axis, step):
        count = lax.axis_size(axis)
        return lax.ppermute(values, axis, [(i, (i + step) % count) for i in range(count)])

    head, tail, lift = lax.optimization_barrier((head, tail, lift_weight.T))
    before, after = ring(tail, "gx", 1), ring(head, "gx", -1)
    planes = 2
    spread_shape = (cells_x, depth, cells_y * WIDTH)
    mixed_weights, vectors, mixing, weight, outer_mix = call(
        functools.partial(contract_kernel, planes),
        (
            like(modes_z * (own_x * own_y + 2), LANES),
            like(4, cells_y * WIDTH),
            jax.ShapeDtypeStruct((8 * cells_y, cells_y * WIDTH), NARROW),
            like(*spread_shape),
            jax.ShapeDtypeStruct((8 * WIDTH, width), NARROW),
        ),
        [pltpu.VMEM((2, width), real)],
        weight_bytes * LANES,
        weight_bytes,
    )(
        lift,
        spectral_weight,
        local_weight,
        local_bias.reshape(1, WIDTH),
        proj_weight.reshape(1, WIDTH),
        cotangent.reshape(tile, depth),
    )
    head, tail = call(
        pack_kernel,
        (like(6, cells_x, depth), like(6, cells_x, depth)),
        [],
        PACK_COST,
        40 * tile * depth,
    )(held, before, after)
    low, high = ring(tail, "gy", 1), ring(head, "gy", -1)
    extended_shape = pltpu.VMEM((cells_x + 4, cells_y + 16, depth), real)
    stepped, spectra = call(
        step_kernel,
        (like(2, *phase.shape), like(*mixed_weights.shape)),
        [extended_shape] * 4 + [pltpu.VMEM((depth // LANES, 2 * tile, LANES), real)],
        400 * tile * depth,
        80 * tile * depth,
    )(held, before, after, low, high, table["z_plain"], mixed_weights)
    gathered = exchange(spectra.reshape(-1, 2, LANES)).reshape(spectra.shape)
    modes, fields, lines, own_lines = call(
        functools.partial(spectral_kernel, shape),
        (
            like(devices, LANES),
            like(devices * 2 * cells_x * (cells_y // SPREAD), LANES),
            jax.ShapeDtypeStruct((cells_x, depth, LANES), NARROW),
            jax.ShapeDtypeStruct((cells_x, 4 * cells_y, depth), NARROW),
        ),
        [
            pltpu.VMEM((modes_x // SPREAD, 2 * total_y, LANES), real),
            pltpu.VMEM((2 * modes_x * (total_y // SPREAD), LANES), real),
            pltpu.VMEM((count_x, modes_y, LANES), real),
            pltpu.VMEM((devices * own_x * own_y, LANES), real),
        ],
        100_000_000,
        2_000_000,
    )(
        gathered,
        table["y_first"],
        table["x_first"],
        table["y_back"],
        table["x_back"],
        stepped,
        table["z_forth"],
        table["chosen"],
        table["gather"],
    )
    fields = exchange(fields)
    predicted, spectra = call(
        functools.partial(field_kernel, cells_y),
        (like(tile, depth), like(*fields.shape)),
        [pltpu.VMEM((cells_x, SPREAD * cells_y, LANES), real)],
        1_000_000_000,
        2_000_000,
    )(fields, lines, mixing, weight, own_lines, vectors, table["z_back"], table["z_forth"])
    spectra = exchange(spectra)
    chunk = 2 * own_x * own_y * WIDTH // LANES + 2
    gradients = call(
        functools.partial(gradient_kernel, shape),
        like(devices * chunk, LANES),
        [
            pltpu.VMEM((2 * modes_x * (total_y // SPREAD), LANES), real),
            pltpu.VMEM((modes_x // SPREAD, 2 * total_y, LANES), real),
        ],
        100_000_000,
        2_000_000,
    )(spectra, modes, table["x_forth"], table["y_forth"])
    gradients = exchange(gradients.reshape(-1, 2, LANES)).reshape(gradients.shape)
    grad_local, grad_proj, predicted, phase_next, solute_next, grad_spectral = call(
        functools.partial(outer_kernel, 1.0 / math.sqrt(total_x * total_y * depth)),
        (
            like(WIDTH, WIDTH),
            like(1, WIDTH),
            like(*predicted.shape),
            like(*phase.shape),
            like(*phase.shape),
            like(*spectral_weight.shape),
        ),
        [
            pltpu.VMEM((WIDTH, WIDTH), real),
            pltpu.VMEM((1, WIDTH), real),
            pltpu.VMEM(spectral_weight.shape, real),
            pltpu.SemaphoreType.DMA((own_x + 5,)),
        ],
        weight_bytes * 4 * WIDTH,
        weight_bytes,
        out_specs=(far,) * 6,
    )(gradients, lift, predicted, stepped, outer_mix, table["repeat"], table["spread"])
    return (
        phase_next,
        solute_next,
        predicted.reshape(phase.shape),
        grad_spectral,
        grad_local,
        grad_proj.reshape(WIDTH),
    )


def per_device(*arguments):
    count_x, count_y = lax.axis_size("gx"), lax.axis_size("gy")
    if fits(count_x, count_y, arguments[0], arguments[4]):
        return per_device_fast(*arguments)
    return per_device_plain(*arguments)


def solution(mesh):
    return jax.shard_map(
        per_device,
        mesh=mesh,
        in_specs=(
            P("gx", "gy", None),
            P("gx", "gy", None),
            P("gx", "gy", None),
            P(),
            P(None, "gx", "gy", None, None),
            P(),
            P(),
            P(),
            P("gx", "gy", None),
        ),
        out_specs=(
            P("gx", "gy", None),
            P("gx", "gy", None),
            P("gx", "gy", None),
            P(None, "gx", "gy", None, None),
            P(),
            P(),
        ),
        check_vma=False,
    )
```

```python
import functools
from functools import reduce
import math

import jax
import jax.numpy as jnp
import ml_dtypes
import numpy as np
from jax import lax
from jax.experimental import pallas as pl
from jax.experimental.pallas import tpu as pltpu
from jax.sharding import PartitionSpec as P

WIDTH = 32
KX = 32
KY = 32
KZ = 32


TIME_STEP = 0.05
COUPLING = 2.0
SOLID_DIFF = 0.05
LIQUID_DIFF = 1.0
PARTITION = 0.15
TRAP_RATE = 4.0
SOLUTE_MEAN = 0.5


def extended(cells, sides, width):
    for axis, dim in sides:
        count = lax.axis_size(axis)
        head = lax.slice_in_dim(cells, 0, width, axis=dim)
        tail = lax.slice_in_dim(cells, cells.shape[dim] - width, cells.shape[dim], axis=dim)
        cells = jnp.concatenate(
            [
                lax.ppermute(tail, axis, [(i, (i + 1) % count) for i in range(count)]),
                cells,
                lax.ppermute(head, axis, [((i + 1) % count, i) for i in range(count)]),
            ],
            axis=dim,
        )
    return cells


def diffusivity(phase_now):
    return SOLID_DIFF + (LIQUID_DIFF - SOLID_DIFF) * 0.5 * (1.0 - jnp.tanh(phase_now))


def update(phase_now, solute_now, undercool, phase_nb, solute_nb, diff_now, diff_nb):
    lap = reduce(jnp.add, phase_nb) - 6.0 * phase_now
    squares = 1.0 - phase_now * phase_now
    rate = (
        lap
        + phase_now
        - phase_now * phase_now * phase_now
        + COUPLING * squares * squares * (undercool - solute_now)
    )
    fluxes = [
        0.5 * (diff_now + diff_nb[index]) * (solute_nb[index] - solute_now) for index in range(6)
    ]
    divergence = reduce(jnp.add, fluxes)
    speed = TRAP_RATE * jnp.abs(rate)
    keff = (PARTITION + speed) / (1.0 + speed)
    phase_new = phase_now + TIME_STEP * rate
    solute_new = solute_now + TIME_STEP * (divergence + 0.5 * (1.0 - keff) * solute_now * rate)
    return (phase_new, solute_new)


def beside(padded):
    centre = padded[1:-1, 1:-1]
    return [
        padded[2:, 1:-1],
        padded[:-2, 1:-1],
        padded[1:-1, 2:],
        padded[1:-1, :-2],
        jnp.roll(centre, -1, 2),
        jnp.roll(centre, 1, 2),
    ]


def phase_sweep(phase_now, solute_now, undercool):
    padded = extended(jnp.stack([phase_now, solute_now]), (("gx", 1), ("gy", 2)), 1)
    phase_pad = padded[0]
    solute_pad = padded[1]
    diff_pad = diffusivity(phase_pad)
    return update(
        phase_now,
        solute_now,
        undercool,
        beside(phase_pad),
        beside(solute_pad),
        diff_pad[1:-1, 1:-1],
        beside(diff_pad),
    )


def signed_freq(indices, total):
    return jnp.where(indices < total // 2, indices, indices - total)


def wave_tables(freqs, positions, length, factor):
    product = freqs[:, None] * positions[None, :] % length
    angles = product.astype(jnp.float32) * (2.0 * math.pi / length)
    return (jnp.cos(angles) * factor, jnp.sin(angles) * factor)


def complex_mix(cosines, sines, data, pattern, orient):

    def apply(table, values):
        return jnp.einsum(pattern, table, values, precision=lax.Precision.HIGHEST)

    cos_real = apply(cosines, data[0])
    cos_imag = apply(cosines, data[1])
    sin_real = apply(sines, data[0])
    sin_imag = apply(sines, data[1])
    return jnp.stack([cos_real - orient * sin_imag, cos_imag + orient * sin_real])


def x_forward(data, factor):
    portion = lax.all_to_all(data, "gx", split_axis=1, concat_axis=2, tiled=True)
    length = portion.shape[2]
    cosines, sines = wave_tables(
        signed_freq(jnp.arange(KX, dtype=jnp.int32), KX),
        jnp.arange(length, dtype=jnp.int32),
        length,
        factor,
    )
    lines = complex_mix(cosines, sines, portion, "kx,wxyz->wkyz", -1.0)
    return lax.all_to_all(lines, "gx", split_axis=2, concat_axis=1, tiled=True)


def y_forward(data, factor):
    portion = lax.all_to_all(data, "gy", split_axis=1, concat_axis=3, tiled=True)
    length = portion.shape[3]
    cosines, sines = wave_tables(
        signed_freq(jnp.arange(KY, dtype=jnp.int32), KY),
        jnp.arange(length, dtype=jnp.int32),
        length,
        factor,
    )
    lines = complex_mix(cosines, sines, portion, "ky,wayz->wakz", -1.0)
    return lax.all_to_all(lines, "gy", split_axis=3, concat_axis=1, tiled=True)


def contract(weights, values):
    return jnp.einsum("abzoi,iabz->oabz", weights, values, precision=lax.Precision.HIGHEST)


def outer(left, right):
    return jnp.einsum("oabz,iabz->abzoi", left, right, precision=lax.Precision.HIGHEST)


def per_device_plain(
    phase,
    solute,
    undercool,
    lift_weight,
    spectral_weight,
    local_weight,
    local_bias,
    proj_weight,
    cotangent,
):
    phase_mid, solute_mid = phase_sweep(phase, solute, undercool)
    phase_next, solute_next = phase_sweep(phase_mid, solute_mid, undercool)
    cells_x, cells_y, depth = phase.shape
    total_x = cells_x * lax.axis_size("gx")
    total_y = cells_y * lax.axis_size("gy")
    fields = jnp.stack([phase_next, solute_next - SOLUTE_MEAN])
    modes_z = jnp.arange(KZ, dtype=jnp.int32)
    zpos = jnp.arange(depth, dtype=jnp.int32)
    unit_z = jnp.ones((KZ,), jnp.float32)
    weights_z = jnp.where(modes_z == 0, 1.0, 2.0).astype(jnp.float32) / depth

    def z_forward(field, zfactor):
        cosines, sines = wave_tables(modes_z, zpos, depth, zfactor[:, None])
        tables = jnp.stack([cosines, -sines])
        return jnp.einsum("wxyz,rkz->rwxyk", field, tables, precision=lax.Precision.HIGHEST)

    def spectral_forward(field, zfactor, xfactor, yfactor):
        return y_forward(x_forward(z_forward(field, zfactor), xfactor), yfactor)

    lifted = jnp.einsum("wc,cxyz->wxyz", lift_weight, fields, precision=lax.Precision.HIGHEST)
    spectrum = spectral_forward(lifted, unit_z, 1.0, 1.0)
    own_x = spectrum.shape[2]
    own_y = spectrum.shape[3]
    shaped = spectral_weight.reshape(2, own_x, own_y, KZ, WIDTH, WIDTH)
    out_real = contract(shaped[0], spectrum[0]) - contract(shaped[1], spectrum[1])
    out_imag = contract(shaped[0], spectrum[1]) + contract(shaped[1], spectrum[0])
    spectral_out = jnp.stack([out_real, out_imag])
    ypos = lax.axis_index("gy") * cells_y + jnp.arange(cells_y, dtype=jnp.int32)
    portion = lax.all_gather(spectral_out, "gy", axis=3, tiled=True)
    freqs = signed_freq(jnp.arange(portion.shape[3], dtype=jnp.int32), KY)
    cosines, sines = wave_tables(ypos, freqs, total_y, 1.0 / total_y)
    back_y = complex_mix(cosines, sines, portion, "yk,wakz->wayz", 1.0)
    cosines, sines = wave_tables(
        jnp.arange(total_x, dtype=jnp.int32),
        signed_freq(jnp.arange(KX, dtype=jnp.int32), KX),
        total_x,
        1.0 / total_x,
    )
    inverted = complex_mix(
        cosines,
        sines,
        lax.all_to_all(back_y, "gx", split_axis=1, concat_axis=2, tiled=True),
        "xk,wkyz->wxyz",
        1.0,
    )
    back_x = lax.all_to_all(inverted, "gx", split_axis=2, concat_axis=1, tiled=True)
    cos_back, sin_back = wave_tables(modes_z, zpos, depth, weights_z[:, None])
    back_tables = jnp.stack([cos_back, -sin_back])
    spectral_field = jnp.einsum(
        "rwxyk,rkz->wxyz", back_x, back_tables, precision=lax.Precision.HIGHEST
    )
    mixed = jnp.dot(local_weight, lift_weight, precision=lax.Precision.HIGHEST)
    pre_act = (
        spectral_field
        + jnp.einsum("wc,cxyz->wxyz", mixed, fields, precision=lax.Precision.HIGHEST)
        + local_bias[:, None, None, None]
    )
    activated, gelu_back = jax.vjp(jax.nn.gelu, pre_act)
    predicted = jnp.einsum("w,wxyz->xyz", proj_weight, activated, precision=lax.Precision.HIGHEST)
    grad_pre = gelu_back(proj_weight[:, None, None, None] * cotangent[None])[0]
    field_sums = jnp.einsum("wxyz,cxyz->wc", grad_pre, fields, precision=lax.Precision.HIGHEST)
    proj_sums = jnp.einsum("wxyz,xyz->w", activated, cotangent, precision=lax.Precision.HIGHEST)
    field_sums, proj_sums = lax.psum((field_sums, proj_sums), ("gx", "gy"))
    grad_modes = spectral_forward(grad_pre, weights_z, 1.0 / total_x, 1.0 / total_y)
    grad_real = outer(grad_modes[0], spectrum[0]) + outer(grad_modes[1], spectrum[1])
    grad_imag = outer(grad_modes[1], spectrum[0]) - outer(grad_modes[0], spectrum[1])
    grad_spectral = jnp.stack([grad_real, grad_imag]).reshape(2, own_x, own_y, KZ, WIDTH * WIDTH)
    scale = 1.0 / math.sqrt(total_x * total_y * depth)
    grad_local = jnp.dot(field_sums, lift_weight.T, precision=lax.Precision.HIGHEST) * scale
    grad_proj = proj_sums * scale
    return (phase_next, solute_next, predicted, grad_spectral, grad_local, grad_proj)


LANES = 128
SMALL_VMEM = 24 * 1024 * 1024
PACK_COST = 50_000_000_000
SPREAD = LANES // WIDTH
NARROW = jnp.bfloat16
EXACT = lax.Precision.HIGHEST


def halves(table):
    head = table.astype(np.float32).astype(ml_dtypes.bfloat16)
    rest = (table - head.astype(np.float64)).astype(np.float32).astype(ml_dtypes.bfloat16)
    return head, rest


def left_table(table):
    head, rest = halves(table)
    return np.concatenate([head, head, rest], axis=1)


def right_table(table):
    head, rest = halves(table)
    return np.concatenate([head, head, rest], axis=0)


def parts_of(values):
    head = values.astype(NARROW)
    return head, (values - head.astype(jnp.float32)).astype(NARROW)


def thrice(values, axis):
    head, rest = parts_of(values)
    return jnp.concatenate([head, rest, head], axis=axis)


def one_where(mask):
    return mask.astype(jnp.float32).astype(NARROW)


def mul(left, right):
    return jnp.dot(left, right, preferred_element_type=jnp.float32)


def mul_rows(left, right):
    return lax.dot_general(
        left, right, (((1,), (1,)), ((), ())), preferred_element_type=jnp.float32
    )


def angles(freqs, positions, length):
    return 2.0 * np.pi * ((freqs[:, None] * positions[None, :]) % length) / length


def signed(count):
    index = np.arange(count)
    return np.where(index < count // 2, index, index - count)


def rotation(theta, orient):
    cosines, sines = np.cos(theta), orient * np.sin(theta)
    return np.block([[cosines, -sines], [sines, cosines]])


def group_of(shape):
    return lax.broadcasted_iota(jnp.int32, shape, len(shape) - 1) // WIDTH


def pick(groups, choices):
    result = choices[-1]
    for index in range(len(choices) - 2, -1, -1):
        result = jnp.where(groups == index, choices[index], result)
    return result


def turn(values, shift):
    shift = shift % LANES
    return values if shift == 0 else pltpu.roll(values, shift, 1)


def swap_groups(pieces):
    groups = group_of(pieces[0].shape)
    return [
        pick(groups, [turn(pieces[i], WIDTH * (i - j)) for i in range(SPREAD)])
        for j in range(SPREAD)
    ]


def spread_cells(
    lift_ref, local_ref, bias_ref, proj_ref, cotangent_ref, vector_ref, mix_ref, spread_ref
):
    planes, depth, wide = spread_ref.shape
    tile = cotangent_ref.shape[0]
    cells_y = tile // planes
    lift, lift_rest = parts_of(lift_ref[...])
    local, local_rest = parts_of(local_ref[...])
    mixed = mul_rows(lift, local) + mul_rows(lift_rest, local) + mul_rows(lift, local_rest)
    for index in range(wide // WIDTH):
        place = slice(index * WIDTH, (index + 1) * WIDTH)
        vector_ref[0:2, place] = mixed
        vector_ref[2:3, place] = bias_ref[...]
        vector_ref[3:4, place] = proj_ref[...]
    head, rest = parts_of(vector_ref[...])
    row = lax.broadcasted_iota(jnp.int32, (cells_y, wide), 0)
    own = row == lax.broadcasted_iota(jnp.int32, (cells_y, wide), 1) // WIDTH

    def diagonal(line):
        return jnp.where(own, line.astype(jnp.float32), 0.0)

    mixing = [diagonal(part[k : k + 1]) for k in range(2) for part in (head, head, rest)]
    mixing += [part[2:3].astype(jnp.float32) for part in (head, rest)]
    mixing.append(jnp.zeros((2 * cells_y - 2, wide), jnp.float32))
    mix_ref[...] = jnp.concatenate(mixing, axis=0).astype(NARROW)
    spread = jnp.concatenate(parts_of(cotangent_ref[...].T), axis=1)
    cell = lax.broadcasted_iota(jnp.int32, (2 * tile, wide), 0) % tile
    row = lax.broadcasted_iota(jnp.int32, (2 * tile, wide), 1) // WIDTH
    for plane in range(planes):
        spread_ref[plane] = mul(spread, one_where(cell == plane * cells_y + row))


def contract_kernel(
    planes,
    lift_ref,
    weight_ref,
    local_ref,
    bias_ref,
    proj_ref,
    cotangent_ref,
    out_ref,
    vector_ref,
    mix_ref,
    spread_ref,
    outer_ref,
    wide_ref,
):
    _, own_x, own_y, modes_z, width = weight_ref.shape
    chunk = out_ref.shape[0] // modes_z
    steps = own_x // planes

    square = (WIDTH, WIDTH)
    diagonal = lax.broadcasted_iota(jnp.int32, square, 0) == lax.broadcasted_iota(
        jnp.int32, square, 1
    )
    columns = [
        jnp.sum(
            jnp.where(diagonal, jnp.broadcast_to(lift_ref[k : k + 1, :], square), 0.0),
            axis=1,
            keepdims=True,
        )
        for k in range(2)
    ]
    lane = lax.broadcasted_iota(jnp.int32, (WIDTH, LANES), 1)
    base = jnp.where(
        lane % (2 * WIDTH) < WIDTH,
        jnp.broadcast_to(columns[0], lane.shape),
        jnp.broadcast_to(columns[1], lane.shape),
    )
    head, rest = parts_of(base)
    base = jnp.where(lane < 2 * WIDTH, head.astype(jnp.float32), rest.astype(jnp.float32))
    mixing = jnp.concatenate(
        [jnp.where(lane % WIDTH == channel, base, 0.0) for channel in range(WIDTH)], axis=0
    ).astype(NARROW)
    rows = planes * own_y * modes_z
    low = lax.broadcasted_iota(jnp.int32, (rows, LANES), 1) < 2 * WIDTH
    for step in range(steps):
        sums = []
        for part in range(2):
            block = weight_ref[part, step * planes : (step + 1) * planes]
            head, rest = parts_of(block.reshape(rows, width))
            total = mul(head, mixing) + mul(rest, mixing)
            sums.append(total + turn(total, 2 * WIDTH))
        result = jnp.where(low, sums[0], sums[1])
        for plane in range(planes):
            for row in range(own_y):
                first = (plane * own_y + row) * modes_z
                place = row * own_x + step * planes + plane
                out_ref[pl.ds(place, modes_z, stride=chunk), :] = result[
                    first : first + modes_z
                ]
    spread_cells(
        lift_ref,
        local_ref,
        bias_ref,
        proj_ref,
        cotangent_ref,
        vector_ref,
        mix_ref,
        spread_ref,
    )
    for index in range(SPREAD):
        wide_ref[:, index * WIDTH : (index + 1) * WIDTH] = lift_ref[...]
    for index in range(1, width // LANES):
        wide_ref[:, index * LANES : (index + 1) * LANES] = wide_ref[:, 0:LANES]
    shape = (2 * WIDTH, width)
    row = lax.broadcasted_iota(jnp.int32, shape, 0)
    column = lax.broadcasted_iota(jnp.int32, shape, 1)
    lift = jnp.where(row < WIDTH, wide_ref[0:1, :], wide_ref[1:2, :])
    head, rest = parts_of(jnp.where(column // WIDTH == row % WIDTH, lift, 0.0))
    outer_ref[0 : 2 * WIDTH] = head
    outer_ref[2 * WIDTH : 4 * WIDTH] = head
    outer_ref[4 * WIDTH : 6 * WIDTH] = rest
    outer_ref[6 * WIDTH : 8 * WIDTH] = jnp.zeros_like(rest)


def edge_kernel(held_ref, head_ref, tail_ref):
    cells_x = held_ref.shape[1]
    for index, reach in enumerate((2, 2, 1)):
        head_ref[2 * index : 2 * index + reach] = held_ref[index, 0:reach]
        tail_ref[2 * index : 2 * index + reach] = held_ref[index, cells_x - reach : cells_x]


def pack_kernel(held_ref, before_ref, after_ref, head_ref, tail_ref):
    _, cells_x, cells_y, _ = held_ref.shape
    for out, near, far in ((head_ref, 0, 1), (tail_ref, cells_y - 1, cells_y - 2)):
        for plane in range(cells_x):
            line = slice(plane, plane + 1)
            for index in range(2):
                out[2 * index, line] = held_ref[index, plane, near : near + 1]
                out[2 * index + 1, line] = held_ref[index, plane, far : far + 1]
            out[4, line] = held_ref[2, plane, near : near + 1]
        for index in range(2):
            out[5, 2 * index : 2 * index + 1] = before_ref[2 * index + 1, near : near + 1]
            out[5, 2 * index + 1 : 2 * index + 2] = after_ref[2 * index, near : near + 1]


def step_kernel(
    held_ref,
    before_ref,
    after_ref,
    low_ref,
    high_ref,
    table_ref,
    mixed_ref,
    fields_ref,
    send_ref,
    phase_ext,
    solute_ext,
    cool_ext,
    diff_ext,
    lines,
):
    _, cells_x, cells_y, depth = held_ref.shape
    base = 8
    end = base + cells_y
    for index, ext in enumerate((phase_ext, solute_ext)):
        first = 2 * index
        ext[2 : cells_x + 2, base:end] = held_ref[index]
        ext[0:2, base:end] = before_ref[first : first + 2]
        ext[cells_x + 2 : cells_x + 4, base:end] = after_ref[first : first + 2]
        for source, near in ((low_ref, base - 1), (high_ref, end)):
            for plane in range(cells_x):
                ext[plane + 2, near : near + 1] = source[first, plane : plane + 1]
            ext[1, near : near + 1] = source[5, first : first + 1]
            ext[cells_x + 2, near : near + 1] = source[5, first + 1 : first + 2]
    cool_ext[2 : cells_x + 2, base:end] = held_ref[2]
    cool_ext[1:2, base:end] = before_ref[4:5]
    cool_ext[cells_x + 2 : cells_x + 3, base:end] = after_ref[4:5]

    send_ref[...] = mixed_ref[...]

    def sweep(reach):
        diff_ext[...] = diffusivity(phase_ext[...])

        def window(ext, move_x, move_y):
            return ext[
                2 - reach + move_x : cells_x + 2 + reach + move_x, base + move_y : end + move_y
            ]

        def around(ext, now):
            return [
                window(ext, 1, 0),
                window(ext, -1, 0),
                window(ext, 0, 1),
                window(ext, 0, -1),
                pltpu.roll(now, depth - 1, 2),
                pltpu.roll(now, 1, 2),
            ]

        phase_now = window(phase_ext, 0, 0)
        solute_now = window(solute_ext, 0, 0)
        diff_now = window(diff_ext, 0, 0)
        return update(
            phase_now,
            solute_now,
            window(cool_ext, 0, 0),
            around(phase_ext, phase_now),
            around(solute_ext, solute_now),
            diff_now,
            around(diff_ext, diff_now),
        )

    def edge(source, row, sign):
        values, sides = [], []
        for index in range(2):
            near, far = source[2 * index], source[2 * index + 1]
            inner = jnp.concatenate(
                [held_ref[index, plane, row : row + 1] for plane in range(cells_x)], axis=0
            )
            before = source[5, 2 * index : 2 * index + 1]
            after = source[5, 2 * index + 1 : 2 * index + 2]
            values.append(near)
            sides.append(
                [
                    jnp.concatenate([near[1:], after], axis=0),
                    jnp.concatenate([before, near[:-1]], axis=0),
                    *((inner, far) if sign < 0 else (far, inner)),
                    pltpu.roll(near, depth - 1, 1),
                    pltpu.roll(near, 1, 1),
                ]
            )
        diffs = [diffusivity(side) for side in sides[0]]
        return update(*values, source[4], *sides, diffusivity(values[0]), diffs)

    phase_mid, solute_mid = sweep(1)
    edges = (edge(low_ref, 0, -1), edge(high_ref, cells_y - 1, 1))
    phase_ext[1 : cells_x + 3, base:end] = phase_mid
    solute_ext[1 : cells_x + 3, base:end] = solute_mid
    for place, moved in zip((base - 1, end), edges):
        for ext, line in zip((phase_ext, solute_ext), moved):
            for plane in range(cells_x):
                ext[plane + 2, place : place + 1] = line[plane : plane + 1]
    phase_next, solute_next = sweep(0)
    fields_ref[0] = phase_next
    fields_ref[1] = solute_next
    tile = cells_x * cells_y
    both = (phase_next.reshape(tile, depth), solute_next.reshape(tile, depth) - SOLUTE_MEAN)
    ordered = []
    for part in range(depth // LANES):
        for index, values in enumerate(both):
            lines[part, index * tile : (index + 1) * tile] = values[
                :, part * LANES : (part + 1) * LANES
            ]
        ordered.append(
            jnp.concatenate(
                [
                    lines[part, pl.ds(row, 2 * cells_x, stride=cells_y), :]
                    for row in range(cells_y)
                ],
                axis=0,
            )
        )
    ordered = jnp.concatenate(ordered, axis=1)
    spectra = mul_rows(table_ref[...], thrice(ordered, 1))
    modes_z = spectra.shape[0] // 2
    chunk = send_ref.shape[0] // modes_z
    for part in range(2):
        send_ref[pl.ds(chunk - 2 + part, modes_z, stride=chunk), :] = spectra[
            part * modes_z : (part + 1) * modes_z
        ]


def pack_modes(shape, modes, modes_ref, rows_ref):
    count_x, count_y, _, _, own_x, own_y = shape
    modes_x, modes_y = count_x * own_x, count_y * own_y
    lane = lax.broadcasted_iota(jnp.int32, (modes_y, LANES), 1)
    for index in range(count_x):
        block = modes
        for k in range(4):
            shift = k * own_x - k * modes_x - index * own_x
            block = jnp.where(lane // own_x == k, turn(modes, shift), block)
        rows_ref[index] = block
        line = rows_ref[index, pl.ds(0, count_y, stride=own_y), :]
        groups = group_of(line.shape)
        for row in range(1, own_y):
            piece = rows_ref[index, pl.ds(row, count_y, stride=own_y), :]
            line = jnp.where(groups == row, turn(piece, row * WIDTH), line)
        modes_ref[index * count_y : (index + 1) * count_y] = line


def spectral_kernel(
    shape,
    mixed_ref,
    y_in_ref,
    x_in_ref,
    y_out_ref,
    x_out_ref,
    fields_ref,
    forth_ref,
    chosen_ref,
    gather_ref,
    modes_ref,
    send_ref,
    table_ref,
    line_ref,
    lines_y,
    lines_x,
    rows_ref,
    weight_ref,
):
    count_x, count_y, cells_x, cells_y, own_x, own_y = shape
    modes_x, modes_y = count_x * own_x, count_y * own_y
    total_x, total_y = count_x * cells_x, count_y * cells_y
    tile = cells_x * cells_y
    narrow = 2 * cells_x
    rows = 2 * count_y
    devices = count_x * count_y
    own = own_x * own_y
    chunk = mixed_ref.shape[0] // devices
    spectra = [mixed_ref[pl.ds(own + part, devices, stride=chunk), :] for part in range(2)]
    for index in range(devices):
        weight_ref[index * own : (index + 1) * own, :] = mixed_ref[
            index * chunk : index * chunk + own, :
        ]
    lane = lax.broadcasted_iota(jnp.int32, (rows, LANES), 1)
    blocks = []
    for row in range(cells_y):
        block = jnp.zeros((rows, LANES), jnp.float32)
        for index in range(count_x):
            piece = jnp.concatenate(
                [values[index * count_y : (index + 1) * count_y] for values in spectra], axis=0
            )
            piece = turn(piece, narrow * (index - row))
            block = jnp.where(lane // narrow == index, piece, block)
        blocks.append(block)
    along_y = mul(y_in_ref[...], thrice(jnp.concatenate(blocks, axis=0), 0))
    prepare(fields_ref, forth_ref, table_ref, line_ref)
    half = lax.broadcasted_iota(jnp.int32, (modes_y, LANES), 1) < LANES // 2
    joined = jnp.where(half, along_y[0:modes_y], turn(along_y[modes_y:], LANES // 2))
    modes = mul(thrice(joined, 1), x_in_ref[...])
    quads_y = total_y // SPREAD
    quads_x = modes_x // SPREAD
    lane = lax.broadcasted_iota(jnp.int32, (modes_y, LANES), 1) % modes_x
    chosen = jnp.concatenate(
        [jnp.where(lane == freq, modes, 0.0) for freq in range(modes_x)], axis=0
    )
    columns = mul(jnp.concatenate(parts_of(chosen), axis=1), chosen_ref[...])
    low = lax.broadcasted_iota(jnp.int32, (modes_y, LANES), 1) < 2 * WIDTH
    def gathered(quads):
        products = [[], []]
        for quad in quads:
            lines = [[], []]
            for index in range(SPREAD):
                freq = SPREAD * quad + index
                start = (freq // own_x) * count_y * own_y * own_x + freq % own_x
                weights = weight_ref[pl.ds(start, modes_y, stride=own_x), :]
                for part in range(2):
                    column = columns[
                        freq * modes_y : (freq + 1) * modes_y, part * LANES : (part + 1) * LANES
                    ]
                    line = weights * column
                    lines[part].append(line + turn(line, 2 * WIDTH))
            for part in range(2):
                pairs = [
                    jnp.where(low, lines[part][index], lines[part][index + 1])
                    for index in range(0, SPREAD, 2)
                ]
                products[part].append(jnp.concatenate(pairs, axis=1))
        products = jnp.concatenate(products[0] + products[1], axis=0)
        products = mul(jnp.concatenate(parts_of(products), axis=1), gather_ref[...])
        stacked = []
        for index in range(len(quads)):
            places = [(part * len(quads) + index) * modes_y for part in range(2)]
            stacked.append(
                jnp.concatenate([products[place : place + modes_y] for place in places], axis=0)
            )
        return thrice(jnp.concatenate(stacked, axis=1), 0)

    def along_lines(quads, stacked):
        back = mul(y_out_ref[...], stacked)
        for index, quad in enumerate(quads):
            lines_y[quad] = back[:, index * LANES : (index + 1) * LANES]
        for quad in quads:
            for part in range(2):
                pieces = [
                    lines_y[quad, pl.ds(part * total_y + i, quads_y, stride=SPREAD), :]
                    for i in range(SPREAD)
                ]
                for index, piece in enumerate(swap_groups(pieces)):
                    place = part * modes_x + SPREAD * quad + index
                    lines_x[pl.ds(place, quads_y, stride=2 * modes_x), :] = piece

    batches = [range(first, first + 2) for first in range(0, quads_x, 2)]
    following = gathered(batches[0])
    for index, quads in enumerate(batches):
        stacked = following
        if index + 1 < len(batches):
            following = gathered(batches[index + 1])
        along_lines(quads, stacked)
    per_tile = cells_y // SPREAD
    for start in range(0, quads_y, 4):
        blocks = [
            lines_x[quad * 2 * modes_x : (quad + 1) * 2 * modes_x, :]
            for quad in range(start, start + 4)
        ]
        back = mul(x_out_ref[...], thrice(jnp.concatenate(blocks, axis=1), 0))
        for quad in range(start, start + 4):
            lanes = slice((quad - start) * LANES, (quad - start + 1) * LANES)
            for part in range(2):
                for index in range(count_x):
                    device = index * count_y + quad // per_tile
                    place = (device * 2 + part) * per_tile + quad % per_tile
                    first = part * total_x + index * cells_x
                    send_ref[place * cells_x : (place + 1) * cells_x, :] = back[
                        first : first + cells_x, lanes
                    ]
    pack_modes(shape, modes, modes_ref, rows_ref)


def prepare(fields_ref, forth_ref, table_ref, line_ref):
    planes, depth, _ = table_ref.shape
    cells_y = fields_ref.shape[2]
    tile = planes * cells_y
    rows = forth_ref.shape[0] // 2
    fields = (fields_ref[0].reshape(tile, depth), fields_ref[1].reshape(tile, depth) - SOLUTE_MEAN)
    ones = jnp.where(lax.broadcasted_iota(jnp.int32, (2 * cells_y, depth), 0) < 2, 1.0, 0.0)
    table = forth_ref[rows:].astype(jnp.float32)
    for plane in range(planes):
        lines = [values[plane * cells_y : (plane + 1) * cells_y] for values in fields]
        pieces = [[part.astype(jnp.float32) for part in parts_of(values)] for values in lines]
        both = [piece for head, rest in pieces for piece in (head, rest, head)]
        both = jnp.concatenate([table] + both + [ones], axis=0)
        table_ref[plane] = both.T.astype(NARROW)
        pieces = [piece for pair in zip(*pieces) for piece in pair]
        line_ref[plane] = jnp.concatenate(pieces, axis=0).astype(NARROW)


def fold_channels(values):
    quarter = values.shape[0] // SPREAD
    parts = []
    for first in range(0, values.shape[1], LANES):
        pieces = [
            values[index * quarter : (index + 1) * quarter, first : first + LANES]
            for index in range(SPREAD)
        ]
        channel = lax.broadcasted_iota(jnp.int32, pieces[0].shape, 1) % WIDTH
        span = WIDTH // 2
        while len(pieces) > 1:
            low = channel % (2 * span) < span
            pieces = [
                jnp.where(low, left + turn(left, -span), right + turn(right, span))
                for left, right in zip(pieces[: len(pieces) // 2], pieces[len(pieces) // 2 :])
            ]
            span //= 2
        parts.append(pieces[0])
    return jnp.concatenate(parts, axis=1)


def field_kernel(
    cells_y,
    field_ref,
    table_ref,
    mix_ref,
    weight_ref,
    line_ref,
    vector_ref,
    back_ref,
    forth_ref,
    predicted_ref,
    send_ref,
    shares_ref,
):
    planes, depth, wide = weight_ref.shape
    rows = forth_ref.shape[0] // 2
    halves_y = cells_y // SPREAD
    stride = halves_y * planes
    proj = 0.5 * vector_ref[3:4, :]
    root = math.sqrt(2.0 / math.pi)
    curve = 0.044715
    picker = one_where(
        lax.broadcasted_iota(jnp.int32, (SPREAD * cells_y, 2 * wide), 0)
        == lax.broadcasted_iota(jnp.int32, (SPREAD * cells_y, 2 * wide), 1)
        % wide
        // (WIDTH // SPREAD)
    )
    line_sums = jnp.zeros((2 * cells_y, wide), jnp.float32)
    proj_sums = jnp.zeros((8, wide), jnp.float32)
    def back(plane):
        spectra = jnp.concatenate(
            [
                field_ref[pl.ds(part * planes + plane, rows, stride=stride), :]
                for part in range(halves_y)
            ],
            axis=1,
        )
        spectra = jnp.concatenate([thrice(spectra, 0), mix_ref[...]], axis=0)
        table = jnp.concatenate([back_ref[...], table_ref[plane]], axis=1)
        return mul(table, spectra)

    def activate(pre, plane):
        square = pre * pre
        bent = jnp.tanh(pre * (root + (root * curve) * square))
        upper = 1.0 + bent
        active = pre * upper
        slope = upper + (active - active * bent) * (root + (3.0 * root * curve) * square)
        cotangent = weight_ref[plane]
        grad = cotangent * slope
        sums = jnp.sum((active * cotangent).reshape(depth // 8, 8, wide), axis=0)
        return sums, parts_of(fold_channels(proj * active)), parts_of(grad)

    def forth(shared, grad, plane):
        shares_ref[plane, :, 0 : depth // SPREAD] = mul_rows(
            picker, jnp.concatenate(shared, axis=1)
        )
        for index in range(SPREAD):
            predicted_ref[
                plane * cells_y : (plane + 1) * cells_y,
                index * (depth // SPREAD) : (index + 1) * (depth // SPREAD),
            ] = shares_ref[plane, pl.ds(index, cells_y, stride=SPREAD), 0 : depth // SPREAD]
        head, rest = grad
        lines = line_ref[plane]
        top = jnp.concatenate([forth_ref[0:rows], lines[0 : 2 * cells_y]], axis=0)
        low = jnp.concatenate([forth_ref[rows:], lines[2 * cells_y :]], axis=0)
        spectra = mul(jnp.concatenate([top, low], axis=0), head)
        spectra = spectra[0 : rows + 2 * cells_y] + spectra[rows + 2 * cells_y :] + mul(top, rest)
        spectra = spectra * proj
        for part in range(halves_y):
            send_ref[pl.ds(part * planes + plane, rows, stride=stride), :] = spectra[
                0:rows, part * LANES : (part + 1) * LANES
            ]
        return spectra[rows:]

    following = back(0)
    previous = None
    for plane in range(planes + 1):
        pre = following
        if plane + 1 < planes:
            following = back(plane + 1)
        if plane < planes:
            sums, *current = activate(pre, plane)
            proj_sums = proj_sums + sums
        if plane > 0:
            line_sums = line_sums + forth(*previous, plane - 1)
        previous = current
    shape = (cells_y, wide)
    own = lax.broadcasted_iota(jnp.int32, shape, 0) == (
        lax.broadcasted_iota(jnp.int32, shape, 1) // WIDTH
    )
    sums = [
        jnp.where(own, line_sums[0:cells_y], 0.0),
        jnp.where(own, line_sums[cells_y:], 0.0),
        0.5 * proj_sums,
    ]
    for index, values in enumerate(sums):
        line = jnp.sum(values, axis=0, keepdims=True)
        line = sum(line[:, part * LANES : (part + 1) * LANES] for part in range(halves_y))
        send_ref[stride + index : stride + index + 1, :] = line


def gradient_kernel(
    shape, spectra_ref, modes_ref, x_in_ref, y_in_ref, send_ref, lines_x, lines_y
):
    count_x, count_y, cells_x, cells_y, own_x, own_y = shape
    modes_x, modes_y = count_x * own_x, count_y * own_y
    total_x, total_y = count_x * cells_x, count_y * cells_y
    per_tile = cells_y // SPREAD
    quads_y = total_y // SPREAD
    chunk = 2 * per_tile * cells_x
    first_device = (lax.axis_index("gx") == 0) & (lax.axis_index("gy") == 0)
    keep = jnp.where(first_device, 0.0, 1.0)
    devices = count_x * count_y
    out_chunk = send_ref.shape[0] // devices
    per_own = own_x // SPREAD
    quads_x = modes_x // SPREAD
    for start in range(0, quads_y, SPREAD):
        blocks = []
        for quad in range(start, start + SPREAD):
            block = []
            for part in range(2):
                for index in range(count_x):
                    device = index * count_y + quad // per_tile
                    place = (device * 2 + part) * per_tile + quad % per_tile
                    piece = spectra_ref[place * cells_x : (place + 1) * cells_x, :]
                    block.append(piece * keep if part else piece)
            blocks.append(jnp.concatenate(block, axis=0))
        forth = mul(x_in_ref[...], thrice(jnp.concatenate(blocks, axis=1), 0))
        for quad in range(start, start + SPREAD):
            lines_x[quad * 2 * modes_x : (quad + 1) * 2 * modes_x, :] = forth[
                :, (quad - start) * LANES : (quad - start + 1) * LANES
            ]
    extra = 2 * per_own * own_y
    send_ref[pl.ds(extra, devices, stride=out_chunk), :] = modes_ref[...]
    groups = group_of((1, LANES))
    total = jnp.zeros((1, LANES), jnp.float32)
    for index in range(3):
        start = chunk // 2 + index
        line = jnp.sum(
            spectra_ref[pl.ds(start, devices, stride=chunk), :], axis=0, keepdims=True
        )
        line = line + turn(line, 2 * WIDTH)
        total = jnp.where(groups == index, line + turn(line, WIDTH), total)
    send_ref[pl.ds(extra + 1, devices, stride=out_chunk), :] = jnp.broadcast_to(
        total, (devices, LANES)
    )
    for start in range(0, quads_x, 2):
        for quad in range(start, start + 2):
            for part in range(2):
                pieces = [
                    lines_x[
                        pl.ds(part * modes_x + SPREAD * quad + j, quads_y, stride=2 * modes_x), :
                    ]
                    for j in range(SPREAD)
                ]
                for index, piece in enumerate(swap_groups(pieces)):
                    lines_y[quad, pl.ds(part * total_y + index, quads_y, stride=SPREAD), :] = piece
        lines = jnp.concatenate([lines_y[start], lines_y[start + 1]], axis=1)
        modes = mul(y_in_ref[...], thrice(lines, 0))
        for quad in range(start, start + 2):
            for part in range(2):
                for index in range(count_y):
                    device = (quad // per_own) * count_y + index
                    place = device * out_chunk + (part * per_own + quad % per_own) * own_y
                    first = part * modes_y + index * own_y
                    send_ref[place : place + own_y, :] = modes[
                        first : first + own_y, (quad - start) * LANES : (quad - start + 1) * LANES
                    ]


def outer_kernel(
    scale,
    modes_ref,
    narrow_ref,
    predicted_ref,
    fields_ref,
    mix_ref,
    repeat_ref,
    spread_ref,
    local_out,
    proj_out,
    predicted_out,
    phase_out,
    solute_out,
    grad_ref,
    local_ref,
    proj_ref,
    held,
    sent,
):
    _, own_x, own_y, modes_z, width = held.shape
    chunk = modes_ref.shape[0] // modes_z
    per_own = own_x // SPREAD
    extra = 2 * per_own * own_y
    copies = [
        pltpu.make_async_copy(predicted_ref, predicted_out, sent.at[own_x]),
        pltpu.make_async_copy(fields_ref.at[0], phase_out, sent.at[own_x + 1]),
        pltpu.make_async_copy(fields_ref.at[1], solute_out, sent.at[own_x + 2]),
    ]
    for copy in copies:
        copy.start()
    lane = lax.broadcasted_iota(jnp.int32, (modes_z, LANES), 1)
    low = lane < 2 * WIDTH

    def rows_of(values):
        head, rest = parts_of(values)
        both = jnp.where(low, head.astype(jnp.float32), rest.astype(jnp.float32)).astype(NARROW)
        return jnp.concatenate([both, head], axis=1)

    def repeated(half):
        grads = [
            modes_ref[pl.ds((part * per_own + half) * own_y + row, modes_z, stride=chunk), :]
            for part in range(2)
            for row in range(own_y)
        ]
        grads = jnp.concatenate(grads, axis=0)
        return mul(jnp.concatenate(parts_of(grads), axis=1), repeat_ref[...])

    modes = modes_ref[pl.ds(extra, modes_z, stride=chunk), :]
    own = lane // (4 * own_x) * own_x + lane % own_x
    for plane in range(own_x):
        if plane % SPREAD == 0:
            grads = repeated(plane // SPREAD)
        chosen = jnp.concatenate(
            [jnp.where(own == row * own_x + plane, modes, 0.0) for row in range(own_y)], axis=0
        )
        columns = mul(jnp.concatenate(parts_of(chosen), axis=1), spread_ref[...])
        reals, imags = [], []
        for row in range(own_y):
            real = columns[row * modes_z : (row + 1) * modes_z, 0:LANES]
            imag = columns[row * modes_z : (row + 1) * modes_z, LANES:]
            pair = []
            for part in range(2):
                first = (part * own_y + row) * modes_z
                group = plane % SPREAD * LANES
                pair.append(grads[first : first + modes_z, group : group + LANES])
            reals.append(rows_of(pair[0] * real + pair[1] * imag))
            imags.append(rows_of(pair[1] * real - pair[0] * imag))
        result = mul(jnp.concatenate(reals + imags, axis=0), mix_ref[...])
        held[:, plane] = result.reshape(2, own_y, modes_z, width)
        copies.append(
            pltpu.make_async_copy(held.at[:, plane], grad_ref.at[:, plane], sent.at[plane])
        )
        copies[-1].start()
    line = modes_ref[extra + 1 : extra + 2, :]
    square = (WIDTH, WIDTH)
    diagonal = lax.broadcasted_iota(jnp.int32, square, 0) == lax.broadcasted_iota(
        jnp.int32, square, 1
    )
    local = jnp.zeros(square, jnp.float32)
    for k in range(2):
        sums = jnp.broadcast_to(line[:, k * WIDTH : (k + 1) * WIDTH], square)
        sums = jnp.sum(jnp.where(diagonal, sums, 0.0), axis=1, keepdims=True)
        local = local + sums * narrow_ref[k : k + 1, :]
    local_ref[...] = scale * local
    proj_ref[...] = scale * line[:, 2 * WIDTH : 3 * WIDTH]
    copies.append(pltpu.make_async_copy(local_ref, local_out, sent.at[own_x + 3]))
    copies.append(pltpu.make_async_copy(proj_ref, proj_out, sent.at[own_x + 4]))
    copies[-2].start()
    copies[-1].start()
    for copy in copies:
        copy.wait()


def tables(shape, depth, modes_z):
    count_x, count_y, cells_x, cells_y, own_x, own_y = shape
    modes_x, modes_y = count_x * own_x, count_y * own_y
    total_x, total_y = count_x * cells_x, count_y * cells_y
    theta_z = angles(np.arange(modes_z), np.arange(depth), depth)
    theta_x = angles(signed(modes_x), np.arange(total_x), total_x)
    theta_y = angles(signed(modes_y), np.arange(total_y), total_y)
    plain_z = np.concatenate([np.cos(theta_z), -np.sin(theta_z)], axis=0)
    forth_z = plain_z.reshape(2, modes_z, depth).transpose(1, 0, 2).reshape(2 * modes_z, depth)
    weight = np.where(np.arange(modes_z) == 0, 1.0, 2.0) / (total_x * total_y * depth)
    weighted_z = np.repeat(weight, 2)[:, None] * forth_z
    forth_x, back_x = rotation(theta_x, -1.0), rotation(theta_x.T, 1.0)
    forth_y, back_y = rotation(theta_y, -1.0), rotation(theta_y.T, 1.0)
    order_y = forth_y.reshape(2 * modes_y, 2, count_y, cells_y)
    order_y = order_y.transpose(0, 3, 1, 2).reshape(2 * modes_y, 2 * total_y)
    lines = forth_x.reshape(2, modes_x, 2, count_x, cells_x)
    both = np.zeros((2, count_x, 2, cells_x, 2, 2, modes_x))
    for field in range(2):
        both[:, :, field, :, :, field, :] = lines.transpose(2, 3, 4, 0, 1)
    both = both.reshape(4 * total_x, 4 * modes_x)
    index = np.arange(4 * LANES)
    line = index[: 2 * LANES, None] % LANES
    group = index[None, : 2 * LANES] // WIDTH
    same = np.where(group < 4, group, (group + 2) % 4)
    signs = np.where((group == 2) | (group == 3), -1.0, 1.0)
    chosen = np.where(line // modes_x == same, signs, 0.0)
    half = 2 * WIDTH
    row, column = index[:, None] % (SPREAD * half), index[None, :LANES]
    gather = row // half * WIDTH + row % WIDTH == column
    repeat = line == index[None, :] // LANES * WIDTH + index[None, :] % WIDTH
    spread = line // own_x % 4 == group // 4 * 2 + group % 2
    masks = {"chosen": chosen, "gather": gather, "repeat": repeat, "spread": spread}
    masks = {name: mask.astype(ml_dtypes.bfloat16) for name, mask in masks.items()}
    return masks | {
        "z_plain": left_table(plain_z),
        "z_forth": np.concatenate(halves(weighted_z), axis=0),
        "z_back": left_table(weighted_z.T)[:, : 4 * modes_z],
        "y_first": left_table(order_y),
        "x_first": right_table(both),
        "y_back": left_table(back_y),
        "x_back": left_table(back_x),
        "x_forth": left_table(forth_x),
        "y_forth": left_table(forth_y),
    }


def fits(count_x, count_y, phase, spectral_weight):
    cells_x, cells_y, depth = phase.shape
    _, own_x, own_y, modes_z, width = spectral_weight.shape
    return (
        width == WIDTH * WIDTH
        and modes_z == count_x * count_y
        and 4 * modes_z == LANES
        and 4 * count_x * cells_x == LANES
        and 4 * count_x * own_x == LANES
        and 2 * cells_x * cells_y == LANES
        and cells_x == 8
        and cells_y % SPREAD == 0
        and own_x % SPREAD == 0
        and own_y * 4 * own_x == LANES
        and 3 * WIDTH <= LANES
        and cells_y == 8
        and depth % LANES == 0
    )


def call(kernel, outs, scratch, flops, moved, limit=SMALL_VMEM, **more):
    return pl.pallas_call(
        kernel,
        out_shape=outs,
        scratch_shapes=scratch,
        compiler_params=pltpu.CompilerParams(vmem_limit_bytes=limit),
        cost_estimate=pl.CostEstimate(flops=flops, bytes_accessed=moved, transcendentals=0),
        **more,
    )


def exchange(values):
    return lax.all_to_all(values, ("gx", "gy"), split_axis=0, concat_axis=0, tiled=True)


def per_device_fast(
    phase,
    solute,
    undercool,
    lift_weight,
    spectral_weight,
    local_weight,
    local_bias,
    proj_weight,
    cotangent,
):
    count_x, count_y = lax.axis_size("gx"), lax.axis_size("gy")
    cells_x, cells_y, depth = phase.shape
    _, own_x, own_y, modes_z, width = spectral_weight.shape
    shape = (count_x, count_y, cells_x, cells_y, own_x, own_y)
    devices = count_x * count_y
    tile = cells_x * cells_y
    modes_x, modes_y = count_x * own_x, count_y * own_y
    total_x, total_y = count_x * cells_x, count_y * cells_y
    table = tables(shape, depth, modes_z)
    real = jnp.float32

    def like(*dims):
        return jax.ShapeDtypeStruct(dims, real)

    far = pl.BlockSpec(memory_space=pltpu.HBM)
    weight_bytes = 8 * own_x * own_y * modes_z * width
    held = jnp.stack([phase, solute, undercool])
    head, tail = call(
        edge_kernel,
        (like(5, cells_y, depth), like(5, cells_y, depth)),
        [],
        1000,
        40 * tile * depth,
    )(held)

    def ring(values, axis, step):
        count = lax.axis_size(axis)
        return lax.ppermute(values, axis, [(i, (i + step) % count) for i in range(count)])

    head, tail, lift = lax.optimization_barrier((head, tail, lift_weight.T))
    before, after = ring(tail, "gx", 1), ring(head, "gx", -1)
    planes = 2
    spread_shape = (cells_x, depth, cells_y * WIDTH)
    mixed_weights, vectors, mixing, weight, outer_mix = call(
        functools.partial(contract_kernel, planes),
        (
            like(modes_z * (own_x * own_y + 2), LANES),
            like(4, cells_y * WIDTH),
            jax.ShapeDtypeStruct((8 * cells_y, cells_y * WIDTH), NARROW),
            like(*spread_shape),
            jax.ShapeDtypeStruct((8 * WIDTH, width), NARROW),
        ),
        [pltpu.VMEM((2, width), real)],
        weight_bytes * LANES,
        weight_bytes,
    )(
        lift,
        spectral_weight,
        local_weight,
        local_bias.reshape(1, WIDTH),
        proj_weight.reshape(1, WIDTH),
        cotangent.reshape(tile, depth),
    )
    head, tail = call(
        pack_kernel,
        (like(6, cells_x, depth), like(6, cells_x, depth)),
        [],
        PACK_COST,
        40 * tile * depth,
    )(held, before, after)
    low, high = ring(tail, "gy", 1), ring(head, "gy", -1)
    extended_shape = pltpu.VMEM((cells_x + 4, cells_y + 16, depth), real)
    stepped, spectra = call(
        step_kernel,
        (like(2, *phase.shape), like(*mixed_weights.shape)),
        [extended_shape] * 4 + [pltpu.VMEM((depth // LANES, 2 * tile, LANES), real)],
        400 * tile * depth,
        80 * tile * depth,
    )(held, before, after, low, high, table["z_plain"], mixed_weights)
    gathered = exchange(spectra.reshape(-1, 2, LANES)).reshape(spectra.shape)
    modes, fields, lines, own_lines = call(
        functools.partial(spectral_kernel, shape),
        (
            like(devices, LANES),
            like(devices * 2 * cells_x * (cells_y // SPREAD), LANES),
            jax.ShapeDtypeStruct((cells_x, depth, LANES), NARROW),
            jax.ShapeDtypeStruct((cells_x, 4 * cells_y, depth), NARROW),
        ),
        [
            pltpu.VMEM((modes_x // SPREAD, 2 * total_y, LANES), real),
            pltpu.VMEM((2 * modes_x * (total_y // SPREAD), LANES), real),
            pltpu.VMEM((count_x, modes_y, LANES), real),
            pltpu.VMEM((devices * own_x * own_y, LANES), real),
        ],
        100_000_000,
        2_000_000,
    )(
        gathered,
        table["y_first"],
        table["x_first"],
        table["y_back"],
        table["x_back"],
        stepped,
        table["z_forth"],
        table["chosen"],
        table["gather"],
    )
    fields = exchange(fields)
    predicted, spectra = call(
        functools.partial(field_kernel, cells_y),
        (like(tile, depth), like(*fields.shape)),
        [pltpu.VMEM((cells_x, SPREAD * cells_y, LANES), real)],
        1_000_000_000,
        2_000_000,
    )(fields, lines, mixing, weight, own_lines, vectors, table["z_back"], table["z_forth"])
    spectra = exchange(spectra)
    chunk = 2 * own_x * own_y * WIDTH // LANES + 2
    gradients = call(
        functools.partial(gradient_kernel, shape),
        like(devices * chunk, LANES),
        [
            pltpu.VMEM((2 * modes_x * (total_y // SPREAD), LANES), real),
            pltpu.VMEM((modes_x // SPREAD, 2 * total_y, LANES), real),
        ],
        100_000_000,
        2_000_000,
    )(spectra, modes, table["x_forth"], table["y_forth"])
    gradients = exchange(gradients.reshape(-1, 2, LANES)).reshape(gradients.shape)
    grad_local, grad_proj, predicted, phase_next, solute_next, grad_spectral = call(
        functools.partial(outer_kernel, 1.0 / math.sqrt(total_x * total_y * depth)),
        (
            like(WIDTH, WIDTH),
            like(1, WIDTH),
            like(*predicted.shape),
            like(*phase.shape),
            like(*phase.shape),
            like(*spectral_weight.shape),
        ),
        [
            pltpu.VMEM((WIDTH, WIDTH), real),
            pltpu.VMEM((1, WIDTH), real),
            pltpu.VMEM(spectral_weight.shape, real),
            pltpu.SemaphoreType.DMA((own_x + 5,)),
        ],
        weight_bytes * 4 * WIDTH,
        weight_bytes,
        out_specs=(far,) * 6,
    )(gradients, lift, predicted, stepped, outer_mix, table["repeat"], table["spread"])
    return (
        phase_next,
        solute_next,
        predicted.reshape(phase.shape),
        grad_spectral,
        grad_local,
        grad_proj.reshape(WIDTH),
    )


def per_device(*arguments):
    count_x, count_y = lax.axis_size("gx"), lax.axis_size("gy")
    if fits(count_x, count_y, arguments[0], arguments[4]):
        return per_device_fast(*arguments)
    return per_device_plain(*arguments)


def solution(mesh):
    return jax.shard_map(
        per_device,
        mesh=mesh,
        in_specs=(
            P("gx", "gy", None),
            P("gx", "gy", None),
            P("gx", "gy", None),
            P(),
            P(None, "gx", "gy", None, None),
            P(),
            P(),
            P(),
            P("gx", "gy", None),
        ),
        out_specs=(
            P("gx", "gy", None),
            P("gx", "gy", None),
            P("gx", "gy", None),
            P(None, "gx", "gy", None, None),
            P(),
            P(),
        ),
        check_vma=False,
    )
```

```python
import functools
from functools import reduce
import math

import jax
import jax.numpy as jnp
import ml_dtypes
import numpy as np
from jax import lax
from jax.experimental import pallas as pl
from jax.experimental.pallas import tpu as pltpu
from jax.sharding import PartitionSpec as P

WIDTH = 32
KX = 32
KY = 32
KZ = 32


TIME_STEP = 0.05
COUPLING = 2.0
SOLID_DIFF = 0.05
LIQUID_DIFF = 1.0
PARTITION = 0.15
TRAP_RATE = 4.0
SOLUTE_MEAN = 0.5


def extended(cells, sides, width):
    for axis, dim in sides:
        count = lax.axis_size(axis)
        head = lax.slice_in_dim(cells, 0, width, axis=dim)
        tail = lax.slice_in_dim(cells, cells.shape[dim] - width, cells.shape[dim], axis=dim)
        cells = jnp.concatenate(
            [
                lax.ppermute(tail, axis, [(i, (i + 1) % count) for i in range(count)]),
                cells,
                lax.ppermute(head, axis, [((i + 1) % count, i) for i in range(count)]),
            ],
            axis=dim,
        )
    return cells


def diffusivity(phase_now):
    return SOLID_DIFF + (LIQUID_DIFF - SOLID_DIFF) * 0.5 * (1.0 - jnp.tanh(phase_now))


def update(phase_now, solute_now, undercool, phase_nb, solute_nb, diff_now, diff_nb):
    lap = reduce(jnp.add, phase_nb) - 6.0 * phase_now
    squares = 1.0 - phase_now * phase_now
    rate = (
        lap
        + phase_now
        - phase_now * phase_now * phase_now
        + COUPLING * squares * squares * (undercool - solute_now)
    )
    fluxes = [
        0.5 * (diff_now + diff_nb[index]) * (solute_nb[index] - solute_now) for index in range(6)
    ]
    divergence = reduce(jnp.add, fluxes)
    speed = TRAP_RATE * jnp.abs(rate)
    keff = (PARTITION + speed) / (1.0 + speed)
    phase_new = phase_now + TIME_STEP * rate
    solute_new = solute_now + TIME_STEP * (divergence + 0.5 * (1.0 - keff) * solute_now * rate)
    return (phase_new, solute_new)


def beside(padded):
    centre = padded[1:-1, 1:-1]
    return [
        padded[2:, 1:-1],
        padded[:-2, 1:-1],
        padded[1:-1, 2:],
        padded[1:-1, :-2],
        jnp.roll(centre, -1, 2),
        jnp.roll(centre, 1, 2),
    ]


def phase_sweep(phase_now, solute_now, undercool):
    padded = extended(jnp.stack([phase_now, solute_now]), (("gx", 1), ("gy", 2)), 1)
    phase_pad = padded[0]
    solute_pad = padded[1]
    diff_pad = diffusivity(phase_pad)
    return update(
        phase_now,
        solute_now,
        undercool,
        beside(phase_pad),
        beside(solute_pad),
        diff_pad[1:-1, 1:-1],
        beside(diff_pad),
    )


def signed_freq(indices, total):
    return jnp.where(indices < total // 2, indices, indices - total)


def wave_tables(freqs, positions, length, factor):
    product = freqs[:, None] * positions[None, :] % length
    angles = product.astype(jnp.float32) * (2.0 * math.pi / length)
    return (jnp.cos(angles) * factor, jnp.sin(angles) * factor)


def complex_mix(cosines, sines, data, pattern, orient):

    def apply(table, values):
        return jnp.einsum(pattern, table, values, precision=lax.Precision.HIGHEST)

    cos_real = apply(cosines, data[0])
    cos_imag = apply(cosines, data[1])
    sin_real = apply(sines, data[0])
    sin_imag = apply(sines, data[1])
    return jnp.stack([cos_real - orient * sin_imag, cos_imag + orient * sin_real])


def x_forward(data, factor):
    portion = lax.all_to_all(data, "gx", split_axis=1, concat_axis=2, tiled=True)
    length = portion.shape[2]
    cosines, sines = wave_tables(
        signed_freq(jnp.arange(KX, dtype=jnp.int32), KX),
        jnp.arange(length, dtype=jnp.int32),
        length,
        factor,
    )
    lines = complex_mix(cosines, sines, portion, "kx,wxyz->wkyz", -1.0)
    return lax.all_to_all(lines, "gx", split_axis=2, concat_axis=1, tiled=True)


def y_forward(data, factor):
    portion = lax.all_to_all(data, "gy", split_axis=1, concat_axis=3, tiled=True)
    length = portion.shape[3]
    cosines, sines = wave_tables(
        signed_freq(jnp.arange(KY, dtype=jnp.int32), KY),
        jnp.arange(length, dtype=jnp.int32),
        length,
        factor,
    )
    lines = complex_mix(cosines, sines, portion, "ky,wayz->wakz", -1.0)
    return lax.all_to_all(lines, "gy", split_axis=3, concat_axis=1, tiled=True)


def contract(weights, values):
    return jnp.einsum("abzoi,iabz->oabz", weights, values, precision=lax.Precision.HIGHEST)


def outer(left, right):
    return jnp.einsum("oabz,iabz->abzoi", left, right, precision=lax.Precision.HIGHEST)


def per_device_plain(
    phase,
    solute,
    undercool,
    lift_weight,
    spectral_weight,
    local_weight,
    local_bias,
    proj_weight,
    cotangent,
):
    phase_mid, solute_mid = phase_sweep(phase, solute, undercool)
    phase_next, solute_next = phase_sweep(phase_mid, solute_mid, undercool)
    cells_x, cells_y, depth = phase.shape
    total_x = cells_x * lax.axis_size("gx")
    total_y = cells_y * lax.axis_size("gy")
    fields = jnp.stack([phase_next, solute_next - SOLUTE_MEAN])
    modes_z = jnp.arange(KZ, dtype=jnp.int32)
    zpos = jnp.arange(depth, dtype=jnp.int32)
    unit_z = jnp.ones((KZ,), jnp.float32)
    weights_z = jnp.where(modes_z == 0, 1.0, 2.0).astype(jnp.float32) / depth

    def z_forward(field, zfactor):
        cosines, sines = wave_tables(modes_z, zpos, depth, zfactor[:, None])
        tables = jnp.stack([cosines, -sines])
        return jnp.einsum("wxyz,rkz->rwxyk", field, tables, precision=lax.Precision.HIGHEST)

    def spectral_forward(field, zfactor, xfactor, yfactor):
        return y_forward(x_forward(z_forward(field, zfactor), xfactor), yfactor)

    lifted = jnp.einsum("wc,cxyz->wxyz", lift_weight, fields, precision=lax.Precision.HIGHEST)
    spectrum = spectral_forward(lifted, unit_z, 1.0, 1.0)
    own_x = spectrum.shape[2]
    own_y = spectrum.shape[3]
    shaped = spectral_weight.reshape(2, own_x, own_y, KZ, WIDTH, WIDTH)
    out_real = contract(shaped[0], spectrum[0]) - contract(shaped[1], spectrum[1])
    out_imag = contract(shaped[0], spectrum[1]) + contract(shaped[1], spectrum[0])
    spectral_out = jnp.stack([out_real, out_imag])
    ypos = lax.axis_index("gy") * cells_y + jnp.arange(cells_y, dtype=jnp.int32)
    portion = lax.all_gather(spectral_out, "gy", axis=3, tiled=True)
    freqs = signed_freq(jnp.arange(portion.shape[3], dtype=jnp.int32), KY)
    cosines, sines = wave_tables(ypos, freqs, total_y, 1.0 / total_y)
    back_y = complex_mix(cosines, sines, portion, "yk,wakz->wayz", 1.0)
    cosines, sines = wave_tables(
        jnp.arange(total_x, dtype=jnp.int32),
        signed_freq(jnp.arange(KX, dtype=jnp.int32), KX),
        total_x,
        1.0 / total_x,
    )
    inverted = complex_mix(
        cosines,
        sines,
        lax.all_to_all(back_y, "gx", split_axis=1, concat_axis=2, tiled=True),
        "xk,wkyz->wxyz",
        1.0,
    )
    back_x = lax.all_to_all(inverted, "gx", split_axis=2, concat_axis=1, tiled=True)
    cos_back, sin_back = wave_tables(modes_z, zpos, depth, weights_z[:, None])
    back_tables = jnp.stack([cos_back, -sin_back])
    spectral_field = jnp.einsum(
        "rwxyk,rkz->wxyz", back_x, back_tables, precision=lax.Precision.HIGHEST
    )
    mixed = jnp.dot(local_weight, lift_weight, precision=lax.Precision.HIGHEST)
    pre_act = (
        spectral_field
        + jnp.einsum("wc,cxyz->wxyz", mixed, fields, precision=lax.Precision.HIGHEST)
        + local_bias[:, None, None, None]
    )
    activated, gelu_back = jax.vjp(jax.nn.gelu, pre_act)
    predicted = jnp.einsum("w,wxyz->xyz", proj_weight, activated, precision=lax.Precision.HIGHEST)
    grad_pre = gelu_back(proj_weight[:, None, None, None] * cotangent[None])[0]
    field_sums = jnp.einsum("wxyz,cxyz->wc", grad_pre, fields, precision=lax.Precision.HIGHEST)
    proj_sums = jnp.einsum("wxyz,xyz->w", activated, cotangent, precision=lax.Precision.HIGHEST)
    field_sums, proj_sums = lax.psum((field_sums, proj_sums), ("gx", "gy"))
    grad_modes = spectral_forward(grad_pre, weights_z, 1.0 / total_x, 1.0 / total_y)
    grad_real = outer(grad_modes[0], spectrum[0]) + outer(grad_modes[1], spectrum[1])
    grad_imag = outer(grad_modes[1], spectrum[0]) - outer(grad_modes[0], spectrum[1])
    grad_spectral = jnp.stack([grad_real, grad_imag]).reshape(2, own_x, own_y, KZ, WIDTH * WIDTH)
    scale = 1.0 / math.sqrt(total_x * total_y * depth)
    grad_local = jnp.dot(field_sums, lift_weight.T, precision=lax.Precision.HIGHEST) * scale
    grad_proj = proj_sums * scale
    return (phase_next, solute_next, predicted, grad_spectral, grad_local, grad_proj)


LANES = 128
SMALL_VMEM = 24 * 1024 * 1024
PACK_COST = 50_000_000_000
SPREAD = LANES // WIDTH
NARROW = jnp.bfloat16
EXACT = lax.Precision.HIGHEST


def halves(table):
    head = table.astype(np.float32).astype(ml_dtypes.bfloat16)
    rest = (table - head.astype(np.float64)).astype(np.float32).astype(ml_dtypes.bfloat16)
    return head, rest


def left_table(table):
    head, rest = halves(table)
    return np.concatenate([head, head, rest], axis=1)


def right_table(table):
    head, rest = halves(table)
    return np.concatenate([head, head, rest], axis=0)


def parts_of(values):
    head = values.astype(NARROW)
    return head, (values - head.astype(jnp.float32)).astype(NARROW)


def thrice(values, axis):
    head, rest = parts_of(values)
    return jnp.concatenate([head, rest, head], axis=axis)


def one_where(mask):
    return mask.astype(jnp.float32).astype(NARROW)


def mul(left, right):
    return jnp.dot(left, right, preferred_element_type=jnp.float32)


def mul_rows(left, right):
    return lax.dot_general(
        left, right, (((1,), (1,)), ((), ())), preferred_element_type=jnp.float32
    )


def angles(freqs, positions, length):
    return 2.0 * np.pi * ((freqs[:, None] * positions[None, :]) % length) / length


def signed(count):
    index = np.arange(count)
    return np.where(index < count // 2, index, index - count)


def rotation(theta, orient):
    cosines, sines = np.cos(theta), orient * np.sin(theta)
    return np.block([[cosines, -sines], [sines, cosines]])


def group_of(shape):
    return lax.broadcasted_iota(jnp.int32, shape, len(shape) - 1) // WIDTH


def pick(groups, choices):
    result = choices[-1]
    for index in range(len(choices) - 2, -1, -1):
        result = jnp.where(groups == index, choices[index], result)
    return result


def turn(values, shift):
    shift = shift % LANES
    return values if shift == 0 else pltpu.roll(values, shift, 1)


def swap_groups(pieces):
    groups = group_of(pieces[0].shape)
    return [
        pick(groups, [turn(pieces[i], WIDTH * (i - j)) for i in range(SPREAD)])
        for j in range(SPREAD)
    ]


def spread_cells(
    lift_ref, local_ref, bias_ref, proj_ref, cotangent_ref, vector_ref, mix_ref, spread_ref
):
    planes, depth, wide = spread_ref.shape
    tile = cotangent_ref.shape[0]
    cells_y = tile // planes
    lift, lift_rest = parts_of(lift_ref[...])
    local, local_rest = parts_of(local_ref[...])
    mixed = mul_rows(lift, local) + mul_rows(lift_rest, local) + mul_rows(lift, local_rest)
    for index in range(wide // WIDTH):
        place = slice(index * WIDTH, (index + 1) * WIDTH)
        vector_ref[0:2, place] = mixed
        vector_ref[2:3, place] = bias_ref[...]
        vector_ref[3:4, place] = proj_ref[...]
    head, rest = parts_of(vector_ref[...])
    row = lax.broadcasted_iota(jnp.int32, (cells_y, wide), 0)
    own = row == lax.broadcasted_iota(jnp.int32, (cells_y, wide), 1) // WIDTH

    def diagonal(line):
        return jnp.where(own, line.astype(jnp.float32), 0.0)

    mixing = [diagonal(part[k : k + 1]) for k in range(2) for part in (head, head, rest)]
    blank = jnp.zeros((2 * cells_y, wide), jnp.float32)
    mix_ref[...] = jnp.concatenate(mixing + [blank], axis=0).astype(NARROW)
    spread = jnp.concatenate(parts_of(cotangent_ref[...].T), axis=1)
    cell = lax.broadcasted_iota(jnp.int32, (2 * tile, wide), 0) % tile
    row = lax.broadcasted_iota(jnp.int32, (2 * tile, wide), 1) // WIDTH
    for plane in range(planes):
        spread_ref[plane] = mul(spread, one_where(cell == plane * cells_y + row))


def contract_kernel(
    planes,
    lift_ref,
    weight_ref,
    local_ref,
    bias_ref,
    proj_ref,
    cotangent_ref,
    out_ref,
    vector_ref,
    mix_ref,
    spread_ref,
    outer_ref,
    wide_ref,
):
    _, own_x, own_y, modes_z, width = weight_ref.shape
    chunk = out_ref.shape[0] // modes_z
    steps = own_x // planes

    square = (WIDTH, WIDTH)
    diagonal = lax.broadcasted_iota(jnp.int32, square, 0) == lax.broadcasted_iota(
        jnp.int32, square, 1
    )
    columns = [
        jnp.sum(
            jnp.where(diagonal, jnp.broadcast_to(lift_ref[k : k + 1, :], square), 0.0),
            axis=1,
            keepdims=True,
        )
        for k in range(2)
    ]
    lane = lax.broadcasted_iota(jnp.int32, (WIDTH, LANES), 1)
    base = jnp.where(
        lane % (2 * WIDTH) < WIDTH,
        jnp.broadcast_to(columns[0], lane.shape),
        jnp.broadcast_to(columns[1], lane.shape),
    )
    head, rest = parts_of(base)
    base = jnp.where(lane < 2 * WIDTH, head.astype(jnp.float32), rest.astype(jnp.float32))
    mixing = jnp.concatenate(
        [jnp.where(lane % WIDTH == channel, base, 0.0) for channel in range(WIDTH)], axis=0
    ).astype(NARROW)
    rows = planes * own_y * modes_z
    low = lax.broadcasted_iota(jnp.int32, (rows, LANES), 1) < 2 * WIDTH
    for step in range(steps):
        sums = []
        for part in range(2):
            block = weight_ref[part, step * planes : (step + 1) * planes]
            head, rest = parts_of(block.reshape(rows, width))
            total = mul(head, mixing) + mul(rest, mixing)
            sums.append(total + turn(total, 2 * WIDTH))
        result = jnp.where(low, sums[0], sums[1])
        for plane in range(planes):
            for row in range(own_y):
                first = (plane * own_y + row) * modes_z
                place = row * own_x + step * planes + plane
                out_ref[pl.ds(place, modes_z, stride=chunk), :] = result[
                    first : first + modes_z
                ]
    spread_cells(
        lift_ref,
        local_ref,
        bias_ref,
        proj_ref,
        cotangent_ref,
        vector_ref,
        mix_ref,
        spread_ref,
    )
    for index in range(SPREAD):
        wide_ref[:, index * WIDTH : (index + 1) * WIDTH] = lift_ref[...]
    for index in range(1, width // LANES):
        wide_ref[:, index * LANES : (index + 1) * LANES] = wide_ref[:, 0:LANES]
    shape = (2 * WIDTH, width)
    row = lax.broadcasted_iota(jnp.int32, shape, 0)
    column = lax.broadcasted_iota(jnp.int32, shape, 1)
    lift = jnp.where(row < WIDTH, wide_ref[0:1, :], wide_ref[1:2, :])
    head, rest = parts_of(jnp.where(column // WIDTH == row % WIDTH, lift, 0.0))
    outer_ref[0 : 2 * WIDTH] = head
    outer_ref[2 * WIDTH : 4 * WIDTH] = head
    outer_ref[4 * WIDTH : 6 * WIDTH] = rest
    outer_ref[6 * WIDTH : 8 * WIDTH] = jnp.zeros_like(rest)


def edge_kernel(held_ref, head_ref, tail_ref):
    cells_x = held_ref.shape[1]
    for index, reach in enumerate((2, 2, 1)):
        head_ref[2 * index : 2 * index + reach] = held_ref[index, 0:reach]
        tail_ref[2 * index : 2 * index + reach] = held_ref[index, cells_x - reach : cells_x]


def pack_kernel(held_ref, before_ref, after_ref, head_ref, tail_ref):
    _, cells_x, cells_y, _ = held_ref.shape
    for out, near, far in ((head_ref, 0, 1), (tail_ref, cells_y - 1, cells_y - 2)):
        for plane in range(cells_x):
            line = slice(plane, plane + 1)
            for index in range(2):
                out[2 * index, line] = held_ref[index, plane, near : near + 1]
                out[2 * index + 1, line] = held_ref[index, plane, far : far + 1]
            out[4, line] = held_ref[2, plane, near : near + 1]
        for index in range(2):
            out[5, 2 * index : 2 * index + 1] = before_ref[2 * index + 1, near : near + 1]
            out[5, 2 * index + 1 : 2 * index + 2] = after_ref[2 * index, near : near + 1]


def step_kernel(
    held_ref,
    before_ref,
    after_ref,
    low_ref,
    high_ref,
    table_ref,
    mixed_ref,
    fields_ref,
    send_ref,
    phase_ext,
    solute_ext,
    cool_ext,
    diff_ext,
    lines,
):
    _, cells_x, cells_y, depth = held_ref.shape
    base = 8
    end = base + cells_y
    for index, ext in enumerate((phase_ext, solute_ext)):
        first = 2 * index
        ext[2 : cells_x + 2, base:end] = held_ref[index]
        ext[0:2, base:end] = before_ref[first : first + 2]
        ext[cells_x + 2 : cells_x + 4, base:end] = after_ref[first : first + 2]
        for source, near in ((low_ref, base - 1), (high_ref, end)):
            for plane in range(cells_x):
                ext[plane + 2, near : near + 1] = source[first, plane : plane + 1]
            ext[1, near : near + 1] = source[5, first : first + 1]
            ext[cells_x + 2, near : near + 1] = source[5, first + 1 : first + 2]
    cool_ext[2 : cells_x + 2, base:end] = held_ref[2]
    cool_ext[1:2, base:end] = before_ref[4:5]
    cool_ext[cells_x + 2 : cells_x + 3, base:end] = after_ref[4:5]

    send_ref[...] = mixed_ref[...]

    def sweep(reach):
        diff_ext[...] = diffusivity(phase_ext[...])

        def window(ext, move_x, move_y):
            return ext[
                2 - reach + move_x : cells_x + 2 + reach + move_x, base + move_y : end + move_y
            ]

        def around(ext, now):
            return [
                window(ext, 1, 0),
                window(ext, -1, 0),
                window(ext, 0, 1),
                window(ext, 0, -1),
                pltpu.roll(now, depth - 1, 2),
                pltpu.roll(now, 1, 2),
            ]

        phase_now = window(phase_ext, 0, 0)
        solute_now = window(solute_ext, 0, 0)
        diff_now = window(diff_ext, 0, 0)
        return update(
            phase_now,
            solute_now,
            window(cool_ext, 0, 0),
            around(phase_ext, phase_now),
            around(solute_ext, solute_now),
            diff_now,
            around(diff_ext, diff_now),
        )

    def edge(source, row, sign):
        values, sides = [], []
        for index in range(2):
            near, far = source[2 * index], source[2 * index + 1]
            inner = jnp.concatenate(
                [held_ref[index, plane, row : row + 1] for plane in range(cells_x)], axis=0
            )
            before = source[5, 2 * index : 2 * index + 1]
            after = source[5, 2 * index + 1 : 2 * index + 2]
            values.append(near)
            sides.append(
                [
                    jnp.concatenate([near[1:], after], axis=0),
                    jnp.concatenate([before, near[:-1]], axis=0),
                    *((inner, far) if sign < 0 else (far, inner)),
                    pltpu.roll(near, depth - 1, 1),
                    pltpu.roll(near, 1, 1),
                ]
            )
        diffs = [diffusivity(side) for side in sides[0]]
        return update(*values, source[4], *sides, diffusivity(values[0]), diffs)

    phase_mid, solute_mid = sweep(1)
    edges = (edge(low_ref, 0, -1), edge(high_ref, cells_y - 1, 1))
    phase_ext[1 : cells_x + 3, base:end] = phase_mid
    solute_ext[1 : cells_x + 3, base:end] = solute_mid
    for place, moved in zip((base - 1, end), edges):
        for ext, line in zip((phase_ext, solute_ext), moved):
            for plane in range(cells_x):
                ext[plane + 2, place : place + 1] = line[plane : plane + 1]
    phase_next, solute_next = sweep(0)
    fields_ref[0] = phase_next
    fields_ref[1] = solute_next
    tile = cells_x * cells_y
    both = (phase_next.reshape(tile, depth), solute_next.reshape(tile, depth) - SOLUTE_MEAN)
    ordered = []
    for part in range(depth // LANES):
        for index, values in enumerate(both):
            lines[part, index * tile : (index + 1) * tile] = values[
                :, part * LANES : (part + 1) * LANES
            ]
        ordered.append(
            jnp.concatenate(
                [
                    lines[part, pl.ds(row, 2 * cells_x, stride=cells_y), :]
                    for row in range(cells_y)
                ],
                axis=0,
            )
        )
    ordered = jnp.concatenate(ordered, axis=1)
    spectra = mul_rows(table_ref[...], thrice(ordered, 1))
    modes_z = spectra.shape[0] // 2
    chunk = send_ref.shape[0] // modes_z
    for part in range(2):
        send_ref[pl.ds(chunk - 2 + part, modes_z, stride=chunk), :] = spectra[
            part * modes_z : (part + 1) * modes_z
        ]


def pack_modes(shape, modes, modes_ref, rows_ref):
    count_x, count_y, _, _, own_x, own_y = shape
    modes_x, modes_y = count_x * own_x, count_y * own_y
    lane = lax.broadcasted_iota(jnp.int32, (modes_y, LANES), 1)
    for index in range(count_x):
        block = modes
        for k in range(4):
            shift = k * own_x - k * modes_x - index * own_x
            block = jnp.where(lane // own_x == k, turn(modes, shift), block)
        rows_ref[index] = block
        line = rows_ref[index, pl.ds(0, count_y, stride=own_y), :]
        groups = group_of(line.shape)
        for row in range(1, own_y):
            piece = rows_ref[index, pl.ds(row, count_y, stride=own_y), :]
            line = jnp.where(groups == row, turn(piece, row * WIDTH), line)
        modes_ref[pl.ds(index, count_y, stride=count_x), :] = line


def spectral_kernel(
    shape,
    mixed_ref,
    y_in_ref,
    x_in_ref,
    y_out_ref,
    x_out_ref,
    fields_ref,
    forth_ref,
    chosen_ref,
    gather_ref,
    modes_ref,
    send_ref,
    table_ref,
    line_ref,
    lines_y,
    lines_x,
    rows_ref,
    weight_ref,
):
    count_x, count_y, cells_x, cells_y, own_x, own_y = shape
    modes_x, modes_y = count_x * own_x, count_y * own_y
    total_x, total_y = count_x * cells_x, count_y * cells_y
    tile = cells_x * cells_y
    narrow = 2 * cells_x
    rows = 2 * count_y
    devices = count_x * count_y
    own = own_x * own_y
    chunk = mixed_ref.shape[0] // devices
    for index_x in range(count_x):
        for index_y in range(count_y):
            place = (index_x * count_y + index_y) * own
            start = (index_y * count_x + index_x) * chunk
            weight_ref[place : place + own, :] = mixed_ref[start : start + own, :]
    pieces = [
        jnp.concatenate(
            [
                mixed_ref[pl.ds(index * chunk + own + part, count_y, stride=count_x * chunk), :]
                for part in range(2)
            ],
            axis=0,
        )
        for index in range(count_x)
    ]
    lane = lax.broadcasted_iota(jnp.int32, (rows, LANES), 1)
    blocks = []
    for row in range(cells_y):
        block = jnp.zeros((rows, LANES), jnp.float32)
        for index in range(count_x):
            piece = turn(pieces[index], narrow * (index - row))
            block = jnp.where(lane // narrow == index, piece, block)
        blocks.append(block)
    along_y = mul(y_in_ref[...], thrice(jnp.concatenate(blocks, axis=0), 0))
    prepare(fields_ref, forth_ref, table_ref, line_ref)
    half = lax.broadcasted_iota(jnp.int32, (modes_y, LANES), 1) < LANES // 2
    joined = jnp.where(half, along_y[0:modes_y], turn(along_y[modes_y:], LANES // 2))
    modes = mul(thrice(joined, 1), x_in_ref[...])
    quads_y = total_y // SPREAD
    quads_x = modes_x // SPREAD
    lane = lax.broadcasted_iota(jnp.int32, (modes_y, LANES), 1) % modes_x
    chosen = jnp.concatenate(
        [jnp.where(lane == freq, modes, 0.0) for freq in range(modes_x)], axis=0
    )
    columns = mul(jnp.concatenate(parts_of(chosen), axis=1), chosen_ref[...])
    low = lax.broadcasted_iota(jnp.int32, (modes_y, LANES), 1) < 2 * WIDTH
    def gathered(quads):
        products = [[], []]
        for quad in quads:
            lines = [[], []]
            for index in range(SPREAD):
                freq = SPREAD * quad + index
                start = (freq // own_x) * count_y * own_y * own_x + freq % own_x
                weights = weight_ref[pl.ds(start, modes_y, stride=own_x), :]
                for part in range(2):
                    column = columns[
                        freq * modes_y : (freq + 1) * modes_y, part * LANES : (part + 1) * LANES
                    ]
                    line = weights * column
                    lines[part].append(line + turn(line, 2 * WIDTH))
            for part in range(2):
                pairs = [
                    jnp.where(low, lines[part][index], lines[part][index + 1])
                    for index in range(0, SPREAD, 2)
                ]
                products[part].append(jnp.concatenate(pairs, axis=1))
        products = jnp.concatenate(products[0] + products[1], axis=0)
        products = mul(jnp.concatenate(parts_of(products), axis=1), gather_ref[...])
        stacked = []
        for index in range(len(quads)):
            places = [(part * len(quads) + index) * modes_y for part in range(2)]
            stacked.append(
                jnp.concatenate([products[place : place + modes_y] for place in places], axis=0)
            )
        return thrice(jnp.concatenate(stacked, axis=1), 0)

    def along_lines(quads, stacked):
        back = mul(y_out_ref[...], stacked)
        for index, quad in enumerate(quads):
            lines_y[quad] = back[:, index * LANES : (index + 1) * LANES]
        for quad in quads:
            for part in range(2):
                pieces = [
                    lines_y[quad, pl.ds(part * total_y + i, quads_y, stride=SPREAD), :]
                    for i in range(SPREAD)
                ]
                for index, piece in enumerate(swap_groups(pieces)):
                    place = part * modes_x + SPREAD * quad + index
                    lines_x[pl.ds(place, quads_y, stride=2 * modes_x), :] = piece

    batches = [range(first, first + 2) for first in range(0, quads_x, 2)]
    following = gathered(batches[0])
    for index, quads in enumerate(batches):
        stacked = following
        if index + 1 < len(batches):
            following = gathered(batches[index + 1])
        along_lines(quads, stacked)
    per_tile = cells_y // SPREAD
    for start in range(0, quads_y, 4):
        blocks = [
            lines_x[quad * 2 * modes_x : (quad + 1) * 2 * modes_x, :]
            for quad in range(start, start + 4)
        ]
        back = mul(x_out_ref[...], thrice(jnp.concatenate(blocks, axis=1), 0))
        for quad in range(start, start + 4):
            lanes = slice((quad - start) * LANES, (quad - start + 1) * LANES)
            for part in range(2):
                for index in range(count_x):
                    device = quad // per_tile * count_x + index
                    place = (device * 2 + part) * per_tile + quad % per_tile
                    first = part * total_x + index * cells_x
                    send_ref[place * cells_x : (place + 1) * cells_x, :] = back[
                        first : first + cells_x, lanes
                    ]
    pack_modes(shape, modes, modes_ref, rows_ref)


def prepare(fields_ref, forth_ref, table_ref, line_ref):
    planes, depth, _ = table_ref.shape
    cells_y = fields_ref.shape[2]
    tile = planes * cells_y
    rows = forth_ref.shape[0] // 2
    fields = (fields_ref[0].reshape(tile, depth), fields_ref[1].reshape(tile, depth) - SOLUTE_MEAN)
    blank = jnp.zeros((2 * cells_y, depth), jnp.float32)
    table = forth_ref[rows:].astype(jnp.float32)
    for plane in range(planes):
        lines = [values[plane * cells_y : (plane + 1) * cells_y] for values in fields]
        pieces = [[part.astype(jnp.float32) for part in parts_of(values)] for values in lines]
        both = [piece for head, rest in pieces for piece in (head, rest, head)]
        both = jnp.concatenate([table] + both + [blank], axis=0)
        table_ref[plane] = both.T.astype(NARROW)
        pieces = [piece for pair in zip(*pieces) for piece in pair]
        line_ref[plane] = jnp.concatenate(pieces, axis=0).astype(NARROW)


def fold_channels(values):
    quarter = values.shape[0] // SPREAD
    parts = []
    for first in range(0, values.shape[1], LANES):
        pieces = [
            values[index * quarter : (index + 1) * quarter, first : first + LANES]
            for index in range(SPREAD)
        ]
        channel = lax.broadcasted_iota(jnp.int32, pieces[0].shape, 1) % WIDTH
        span = WIDTH // 2
        while len(pieces) > 1:
            low = channel % (2 * span) < span
            pieces = [
                jnp.where(low, left + turn(left, -span), right + turn(right, span))
                for left, right in zip(pieces[: len(pieces) // 2], pieces[len(pieces) // 2 :])
            ]
            span //= 2
        parts.append(pieces[0])
    return jnp.concatenate(parts, axis=1)


def field_kernel(
    cells_y,
    field_ref,
    table_ref,
    mix_ref,
    weight_ref,
    line_ref,
    vector_ref,
    back_ref,
    forth_ref,
    predicted_ref,
    send_ref,
    shares_ref,
):
    planes, depth, wide = weight_ref.shape
    rows = forth_ref.shape[0] // 2
    halves_y = cells_y // SPREAD
    stride = halves_y * planes
    bias = vector_ref[2:3, :]
    proj = vector_ref[3:4, :]
    root = math.sqrt(2.0 / math.pi)
    curve = 0.044715
    picker = one_where(
        lax.broadcasted_iota(jnp.int32, (SPREAD * cells_y, 2 * wide), 0)
        == lax.broadcasted_iota(jnp.int32, (SPREAD * cells_y, 2 * wide), 1)
        % wide
        // (WIDTH // SPREAD)
    )
    line_sums = jnp.zeros((2 * cells_y, wide), jnp.float32)
    proj_sums = jnp.zeros((8, wide), jnp.float32)
    def back(plane):
        spectra = jnp.concatenate(
            [
                field_ref[pl.ds(part * planes + plane, rows, stride=stride), :]
                for part in range(halves_y)
            ],
            axis=1,
        )
        spectra = jnp.concatenate([thrice(spectra, 0), mix_ref[...]], axis=0)
        table = jnp.concatenate([back_ref[...], table_ref[plane]], axis=1)
        return mul(table, spectra) + bias

    def activate(pre, plane):
        square = pre * pre
        bent = jnp.tanh(pre * (root + (root * curve) * square))
        upper = 0.5 + 0.5 * bent
        active = pre * upper
        slope = upper + (active - active * bent) * (root + (3.0 * root * curve) * square)
        cotangent = weight_ref[plane]
        grad = proj * cotangent * slope
        sums = jnp.sum((active * cotangent).reshape(depth // 8, 8, wide), axis=0)
        return sums, parts_of(fold_channels(proj * active)), parts_of(grad)

    def forth(shared, grad, plane):
        shares_ref[plane, :, 0 : depth // SPREAD] = mul_rows(
            picker, jnp.concatenate(shared, axis=1)
        )
        for index in range(SPREAD):
            predicted_ref[
                plane * cells_y : (plane + 1) * cells_y,
                index * (depth // SPREAD) : (index + 1) * (depth // SPREAD),
            ] = shares_ref[plane, pl.ds(index, cells_y, stride=SPREAD), 0 : depth // SPREAD]
        head, rest = grad
        lines = line_ref[plane]
        top = jnp.concatenate([forth_ref[0:rows], lines[0 : 2 * cells_y]], axis=0)
        low = jnp.concatenate([forth_ref[rows:], lines[2 * cells_y :]], axis=0)
        spectra = mul(jnp.concatenate([top, low], axis=0), head)
        spectra = spectra[0 : rows + 2 * cells_y] + spectra[rows + 2 * cells_y :] + mul(top, rest)
        for part in range(halves_y):
            send_ref[pl.ds(part * planes + plane, rows, stride=stride), :] = spectra[
                0:rows, part * LANES : (part + 1) * LANES
            ]
        return spectra[rows:]

    following = back(0)
    previous = None
    for plane in range(planes + 1):
        pre = following
        if plane + 1 < planes:
            following = back(plane + 1)
        if plane < planes:
            sums, *current = activate(pre, plane)
            proj_sums = proj_sums + sums
        if plane > 0:
            line_sums = line_sums + forth(*previous, plane - 1)
        previous = current
    shape = (cells_y, wide)
    own = lax.broadcasted_iota(jnp.int32, shape, 0) == (
        lax.broadcasted_iota(jnp.int32, shape, 1) // WIDTH
    )
    sums = [
        jnp.where(own, line_sums[0:cells_y], 0.0),
        jnp.where(own, line_sums[cells_y:], 0.0),
        proj_sums,
    ]
    for index, values in enumerate(sums):
        line = jnp.sum(values, axis=0, keepdims=True)
        line = sum(line[:, part * LANES : (part + 1) * LANES] for part in range(halves_y))
        send_ref[stride + index : stride + index + 1, :] = line


def gradient_kernel(
    shape, spectra_ref, modes_ref, x_in_ref, y_in_ref, send_ref, lines_x, lines_y
):
    count_x, count_y, cells_x, cells_y, own_x, own_y = shape
    modes_x, modes_y = count_x * own_x, count_y * own_y
    total_x, total_y = count_x * cells_x, count_y * cells_y
    per_tile = cells_y // SPREAD
    quads_y = total_y // SPREAD
    chunk = 2 * per_tile * cells_x
    first_device = (lax.axis_index("gx") == 0) & (lax.axis_index("gy") == 0)
    keep = jnp.where(first_device, 0.0, 1.0)
    devices = count_x * count_y
    out_chunk = send_ref.shape[0] // devices
    per_own = own_x // SPREAD
    quads_x = modes_x // SPREAD
    for start in range(0, quads_y, SPREAD):
        blocks = []
        for quad in range(start, start + SPREAD):
            block = []
            for part in range(2):
                for index in range(count_x):
                    device = quad // per_tile * count_x + index
                    place = (device * 2 + part) * per_tile + quad % per_tile
                    piece = spectra_ref[place * cells_x : (place + 1) * cells_x, :]
                    block.append(piece * keep if part else piece)
            blocks.append(jnp.concatenate(block, axis=0))
        forth = mul(x_in_ref[...], thrice(jnp.concatenate(blocks, axis=1), 0))
        for quad in range(start, start + SPREAD):
            lines_x[quad * 2 * modes_x : (quad + 1) * 2 * modes_x, :] = forth[
                :, (quad - start) * LANES : (quad - start + 1) * LANES
            ]
    extra = 2 * per_own * own_y
    send_ref[pl.ds(extra, devices, stride=out_chunk), :] = modes_ref[...]
    groups = group_of((1, LANES))
    total = jnp.zeros((1, LANES), jnp.float32)
    for index in range(3):
        start = chunk // 2 + index
        line = jnp.sum(
            spectra_ref[pl.ds(start, devices, stride=chunk), :], axis=0, keepdims=True
        )
        line = line + turn(line, 2 * WIDTH)
        total = jnp.where(groups == index, line + turn(line, WIDTH), total)
    send_ref[pl.ds(extra + 1, devices, stride=out_chunk), :] = jnp.broadcast_to(
        total, (devices, LANES)
    )
    for start in range(0, quads_x, 2):
        for quad in range(start, start + 2):
            for part in range(2):
                pieces = [
                    lines_x[
                        pl.ds(part * modes_x + SPREAD * quad + j, quads_y, stride=2 * modes_x), :
                    ]
                    for j in range(SPREAD)
                ]
                for index, piece in enumerate(swap_groups(pieces)):
                    lines_y[quad, pl.ds(part * total_y + index, quads_y, stride=SPREAD), :] = piece
        lines = jnp.concatenate([lines_y[start], lines_y[start + 1]], axis=1)
        modes = mul(y_in_ref[...], thrice(lines, 0))
        for quad in range(start, start + 2):
            for part in range(2):
                for index in range(count_y):
                    device = index * count_x + quad // per_own
                    place = device * out_chunk + (part * per_own + quad % per_own) * own_y
                    first = part * modes_y + index * own_y
                    send_ref[place : place + own_y, :] = modes[
                        first : first + own_y, (quad - start) * LANES : (quad - start + 1) * LANES
                    ]


def outer_kernel(
    scale,
    modes_ref,
    narrow_ref,
    predicted_ref,
    fields_ref,
    mix_ref,
    repeat_ref,
    spread_ref,
    local_out,
    proj_out,
    predicted_out,
    phase_out,
    solute_out,
    grad_ref,
    local_ref,
    proj_ref,
    held,
    sent,
):
    _, own_x, own_y, modes_z, width = held.shape
    chunk = modes_ref.shape[0] // modes_z
    per_own = own_x // SPREAD
    extra = 2 * per_own * own_y
    copies = [
        pltpu.make_async_copy(predicted_ref, predicted_out, sent.at[2 * own_x]),
        pltpu.make_async_copy(fields_ref.at[0], phase_out, sent.at[2 * own_x + 1]),
        pltpu.make_async_copy(fields_ref.at[1], solute_out, sent.at[2 * own_x + 2]),
    ]
    for copy in copies:
        copy.start()
    lane = lax.broadcasted_iota(jnp.int32, (modes_z, LANES), 1)
    low = lane < 2 * WIDTH

    def rows_of(values):
        head, rest = parts_of(values)
        both = jnp.where(low, head.astype(jnp.float32), rest.astype(jnp.float32)).astype(NARROW)
        return jnp.concatenate([both, head], axis=1)

    def repeated(half):
        grads = [
            modes_ref[pl.ds((part * per_own + half) * own_y + row, modes_z, stride=chunk), :]
            for part in range(2)
            for row in range(own_y)
        ]
        grads = jnp.concatenate(grads, axis=0)
        return mul(jnp.concatenate(parts_of(grads), axis=1), repeat_ref[...])

    modes = modes_ref[pl.ds(extra, modes_z, stride=chunk), :]
    own = lane // (4 * own_x) * own_x + lane % own_x
    for plane in range(own_x):
        if plane % SPREAD == 0:
            grads = repeated(plane // SPREAD)
        chosen = jnp.concatenate(
            [jnp.where(own == row * own_x + plane, modes, 0.0) for row in range(own_y)], axis=0
        )
        columns = mul(jnp.concatenate(parts_of(chosen), axis=1), spread_ref[...])
        reals, imags = [], []
        for row in range(own_y):
            real = columns[row * modes_z : (row + 1) * modes_z, 0:LANES]
            imag = columns[row * modes_z : (row + 1) * modes_z, LANES:]
            pair = []
            for part in range(2):
                first = (part * own_y + row) * modes_z
                group = plane % SPREAD * LANES
                pair.append(grads[first : first + modes_z, group : group + LANES])
            reals.append(rows_of(pair[0] * real + pair[1] * imag))
            imags.append(rows_of(pair[1] * real - pair[0] * imag))
        for part, factors in enumerate((reals, imags)):
            result = mul(jnp.concatenate(factors, axis=0), mix_ref[...])
            held[part, plane] = result.reshape(own_y, modes_z, width)
            copies.append(
                pltpu.make_async_copy(
                    held.at[part, plane], grad_ref.at[part, plane], sent.at[2 * plane + part]
                )
            )
            copies[-1].start()
    line = modes_ref[extra + 1 : extra + 2, :]
    square = (WIDTH, WIDTH)
    diagonal = lax.broadcasted_iota(jnp.int32, square, 0) == lax.broadcasted_iota(
        jnp.int32, square, 1
    )
    local = jnp.zeros(square, jnp.float32)
    for k in range(2):
        sums = jnp.broadcast_to(line[:, k * WIDTH : (k + 1) * WIDTH], square)
        sums = jnp.sum(jnp.where(diagonal, sums, 0.0), axis=1, keepdims=True)
        local = local + sums * narrow_ref[k : k + 1, :]
    local_ref[...] = scale * local
    proj_ref[...] = scale * line[:, 2 * WIDTH : 3 * WIDTH]
    copies.append(pltpu.make_async_copy(local_ref, local_out, sent.at[2 * own_x + 3]))
    copies.append(pltpu.make_async_copy(proj_ref, proj_out, sent.at[2 * own_x + 4]))
    copies[-2].start()
    copies[-1].start()
    for copy in copies:
        copy.wait()


def tables(shape, depth, modes_z):
    count_x, count_y, cells_x, cells_y, own_x, own_y = shape
    modes_x, modes_y = count_x * own_x, count_y * own_y
    total_x, total_y = count_x * cells_x, count_y * cells_y
    theta_z = angles(np.arange(modes_z), np.arange(depth), depth)
    theta_x = angles(signed(modes_x), np.arange(total_x), total_x)
    theta_y = angles(signed(modes_y), np.arange(total_y), total_y)
    plain_z = np.concatenate([np.cos(theta_z), -np.sin(theta_z)], axis=0)
    forth_z = plain_z.reshape(2, modes_z, depth).transpose(1, 0, 2).reshape(2 * modes_z, depth)
    weight = np.where(np.arange(modes_z) == 0, 1.0, 2.0) / (total_x * total_y * depth)
    weighted_z = np.repeat(weight, 2)[:, None] * forth_z
    forth_x, back_x = rotation(theta_x, -1.0), rotation(theta_x.T, 1.0)
    forth_y, back_y = rotation(theta_y, -1.0), rotation(theta_y.T, 1.0)
    order_y = forth_y.reshape(2 * modes_y, 2, count_y, cells_y)
    order_y = order_y.transpose(0, 3, 1, 2).reshape(2 * modes_y, 2 * total_y)
    lines = forth_x.reshape(2, modes_x, 2, count_x, cells_x)
    both = np.zeros((2, count_x, 2, cells_x, 2, 2, modes_x))
    for field in range(2):
        both[:, :, field, :, :, field, :] = lines.transpose(2, 3, 4, 0, 1)
    both = both.reshape(4 * total_x, 4 * modes_x)
    index = np.arange(4 * LANES)
    line = index[: 2 * LANES, None] % LANES
    group = index[None, : 2 * LANES] // WIDTH
    same = np.where(group < 4, group, (group + 2) % 4)
    signs = np.where((group == 2) | (group == 3), -1.0, 1.0)
    chosen = np.where(line // modes_x == same, signs, 0.0)
    half = 2 * WIDTH
    row, column = index[:, None] % (SPREAD * half), index[None, :LANES]
    gather = row // half * WIDTH + row % WIDTH == column
    repeat = line == index[None, :] // LANES * WIDTH + index[None, :] % WIDTH
    spread = line // own_x % 4 == group // 4 * 2 + group % 2
    masks = {"chosen": chosen, "gather": gather, "repeat": repeat, "spread": spread}
    masks = {name: mask.astype(ml_dtypes.bfloat16) for name, mask in masks.items()}
    return masks | {
        "z_plain": left_table(plain_z),
        "z_forth": np.concatenate(halves(weighted_z), axis=0),
        "z_back": left_table(weighted_z.T)[:, : 4 * modes_z],
        "y_first": left_table(order_y),
        "x_first": right_table(both),
        "y_back": left_table(back_y),
        "x_back": left_table(back_x),
        "x_forth": left_table(forth_x),
        "y_forth": left_table(forth_y),
    }


def fits(count_x, count_y, phase, spectral_weight):
    cells_x, cells_y, depth = phase.shape
    _, own_x, own_y, modes_z, width = spectral_weight.shape
    return (
        width == WIDTH * WIDTH
        and modes_z == count_x * count_y
        and 4 * modes_z == LANES
        and 4 * count_x * cells_x == LANES
        and 4 * count_x * own_x == LANES
        and 2 * cells_x * cells_y == LANES
        and cells_x == 8
        and cells_y % SPREAD == 0
        and own_x % SPREAD == 0
        and own_y * 4 * own_x == LANES
        and 3 * WIDTH <= LANES
        and cells_y == 8
        and depth % LANES == 0
    )


def call(kernel, outs, scratch, flops, moved, limit=SMALL_VMEM, **more):
    return pl.pallas_call(
        kernel,
        out_shape=outs,
        scratch_shapes=scratch,
        compiler_params=pltpu.CompilerParams(vmem_limit_bytes=limit),
        cost_estimate=pl.CostEstimate(flops=flops, bytes_accessed=moved, transcendentals=0),
        **more,
    )


def exchange(values):
    return lax.all_to_all(values, ("gy", "gx"), split_axis=0, concat_axis=0, tiled=True)


def per_device_fast(
    phase,
    solute,
    undercool,
    lift_weight,
    spectral_weight,
    local_weight,
    local_bias,
    proj_weight,
    cotangent,
):
    count_x, count_y = lax.axis_size("gx"), lax.axis_size("gy")
    cells_x, cells_y, depth = phase.shape
    _, own_x, own_y, modes_z, width = spectral_weight.shape
    shape = (count_x, count_y, cells_x, cells_y, own_x, own_y)
    devices = count_x * count_y
    tile = cells_x * cells_y
    modes_x, modes_y = count_x * own_x, count_y * own_y
    total_x, total_y = count_x * cells_x, count_y * cells_y
    table = tables(shape, depth, modes_z)
    real = jnp.float32

    def like(*dims):
        return jax.ShapeDtypeStruct(dims, real)

    far = pl.BlockSpec(memory_space=pltpu.HBM)
    weight_bytes = 8 * own_x * own_y * modes_z * width
    held = jnp.stack([phase, solute, undercool])
    head, tail = call(
        edge_kernel,
        (like(5, cells_y, depth), like(5, cells_y, depth)),
        [],
        1000,
        40 * tile * depth,
    )(held)

    def ring(values, axis, step):
        count = lax.axis_size(axis)
        return lax.ppermute(values, axis, [(i, (i + step) % count) for i in range(count)])

    head, tail, lift = lax.optimization_barrier((head, tail, lift_weight.T))
    before, after = ring(tail, "gx", 1), ring(head, "gx", -1)
    planes = 2
    spread_shape = (cells_x, depth, cells_y * WIDTH)
    mixed_weights, vectors, mixing, weight, outer_mix = call(
        functools.partial(contract_kernel, planes),
        (
            like(modes_z * (own_x * own_y + 2), LANES),
            like(4, cells_y * WIDTH),
            jax.ShapeDtypeStruct((8 * cells_y, cells_y * WIDTH), NARROW),
            like(*spread_shape),
            jax.ShapeDtypeStruct((8 * WIDTH, width), NARROW),
        ),
        [pltpu.VMEM((2, width), real)],
        weight_bytes * LANES,
        weight_bytes,
    )(
        lift,
        spectral_weight,
        local_weight,
        local_bias.reshape(1, WIDTH),
        proj_weight.reshape(1, WIDTH),
        cotangent.reshape(tile, depth),
    )
    head, tail = call(
        pack_kernel,
        (like(6, cells_x, depth), like(6, cells_x, depth)),
        [],
        PACK_COST,
        40 * tile * depth,
    )(held, before, after)
    low, high = ring(tail, "gy", 1), ring(head, "gy", -1)
    extended_shape = pltpu.VMEM((cells_x + 4, cells_y + 16, depth), real)
    stepped, spectra = call(
        step_kernel,
        (like(2, *phase.shape), like(*mixed_weights.shape)),
        [extended_shape] * 4 + [pltpu.VMEM((depth // LANES, 2 * tile, LANES), real)],
        400 * tile * depth,
        80 * tile * depth,
    )(held, before, after, low, high, table["z_plain"], mixed_weights)
    gathered = exchange(spectra.reshape(-1, 2, LANES)).reshape(spectra.shape)
    modes, fields, lines, own_lines = call(
        functools.partial(spectral_kernel, shape),
        (
            like(devices, LANES),
            like(devices * 2 * cells_x * (cells_y // SPREAD), LANES),
            jax.ShapeDtypeStruct((cells_x, depth, LANES), NARROW),
            jax.ShapeDtypeStruct((cells_x, 4 * cells_y, depth), NARROW),
        ),
        [
            pltpu.VMEM((modes_x // SPREAD, 2 * total_y, LANES), real),
            pltpu.VMEM((2 * modes_x * (total_y // SPREAD), LANES), real),
            pltpu.VMEM((count_x, modes_y, LANES), real),
            pltpu.VMEM((devices * own_x * own_y, LANES), real),
        ],
        100_000_000,
        2_000_000,
    )(
        gathered,
        table["y_first"],
        table["x_first"],
        table["y_back"],
        table["x_back"],
        stepped,
        table["z_forth"],
        table["chosen"],
        table["gather"],
    )
    fields = exchange(fields)
    predicted, spectra = call(
        functools.partial(field_kernel, cells_y),
        (like(tile, depth), like(*fields.shape)),
        [pltpu.VMEM((cells_x, SPREAD * cells_y, LANES), real)],
        1_000_000_000,
        2_000_000,
    )(fields, lines, mixing, weight, own_lines, vectors, table["z_back"], table["z_forth"])
    spectra = exchange(spectra)
    chunk = 2 * own_x * own_y * WIDTH // LANES + 2
    gradients = call(
        functools.partial(gradient_kernel, shape),
        like(devices * chunk, LANES),
        [
            pltpu.VMEM((2 * modes_x * (total_y // SPREAD), LANES), real),
            pltpu.VMEM((modes_x // SPREAD, 2 * total_y, LANES), real),
        ],
        100_000_000,
        2_000_000,
    )(spectra, modes, table["x_forth"], table["y_forth"])
    gradients = exchange(gradients.reshape(-1, 2, LANES)).reshape(gradients.shape)
    grad_local, grad_proj, predicted, phase_next, solute_next, grad_spectral = call(
        functools.partial(outer_kernel, 1.0 / math.sqrt(total_x * total_y * depth)),
        (
            like(WIDTH, WIDTH),
            like(1, WIDTH),
            like(*predicted.shape),
            like(*phase.shape),
            like(*phase.shape),
            like(*spectral_weight.shape),
        ),
        [
            pltpu.VMEM((WIDTH, WIDTH), real),
            pltpu.VMEM((1, WIDTH), real),
            pltpu.VMEM(spectral_weight.shape, real),
            pltpu.SemaphoreType.DMA((2 * own_x + 5,)),
        ],
        weight_bytes * 4 * WIDTH,
        weight_bytes,
        out_specs=(far,) * 6,
    )(gradients, lift, predicted, stepped, outer_mix, table["repeat"], table["spread"])
    return (
        phase_next,
        solute_next,
        predicted.reshape(phase.shape),
        grad_spectral,
        grad_local,
        grad_proj.reshape(WIDTH),
    )


def per_device(*arguments):
    count_x, count_y = lax.axis_size("gx"), lax.axis_size("gy")
    if fits(count_x, count_y, arguments[0], arguments[4]):
        return per_device_fast(*arguments)
    return per_device_plain(*arguments)


def solution(mesh):
    return jax.shard_map(
        per_device,
        mesh=mesh,
        in_specs=(
            P("gx", "gy", None),
            P("gx", "gy", None),
            P("gx", "gy", None),
            P(),
            P(None, "gx", "gy", None, None),
            P(),
            P(),
            P(),
            P("gx", "gy", None),
        ),
        out_specs=(
            P("gx", "gy", None),
            P("gx", "gy", None),
            P("gx", "gy", None),
            P(None, "gx", "gy", None, None),
            P(),
            P(),
        ),
        check_vma=False,
    )
```

```python
import functools
from functools import reduce
import math

import jax
import jax.numpy as jnp
import ml_dtypes
import numpy as np
from jax import lax
from jax.experimental import pallas as pl
from jax.experimental.pallas import tpu as pltpu
from jax.sharding import PartitionSpec as P

WIDTH = 32
KX = 32
KY = 32
KZ = 32


TIME_STEP = 0.05
COUPLING = 2.0
SOLID_DIFF = 0.05
LIQUID_DIFF = 1.0
PARTITION = 0.15
TRAP_RATE = 4.0
SOLUTE_MEAN = 0.5


def extended(cells, sides, width):
    for axis, dim in sides:
        count = lax.axis_size(axis)
        head = lax.slice_in_dim(cells, 0, width, axis=dim)
        tail = lax.slice_in_dim(cells, cells.shape[dim] - width, cells.shape[dim], axis=dim)
        cells = jnp.concatenate(
            [
                lax.ppermute(tail, axis, [(i, (i + 1) % count) for i in range(count)]),
                cells,
                lax.ppermute(head, axis, [((i + 1) % count, i) for i in range(count)]),
            ],
            axis=dim,
        )
    return cells


def diffusivity(phase_now):
    return SOLID_DIFF + (LIQUID_DIFF - SOLID_DIFF) * 0.5 * (1.0 - jnp.tanh(phase_now))


def update(phase_now, solute_now, undercool, phase_nb, solute_nb, diff_now, diff_nb):
    lap = reduce(jnp.add, phase_nb) - 6.0 * phase_now
    squares = 1.0 - phase_now * phase_now
    rate = (
        lap
        + phase_now
        - phase_now * phase_now * phase_now
        + COUPLING * squares * squares * (undercool - solute_now)
    )
    fluxes = [
        0.5 * (diff_now + diff_nb[index]) * (solute_nb[index] - solute_now) for index in range(6)
    ]
    divergence = reduce(jnp.add, fluxes)
    speed = TRAP_RATE * jnp.abs(rate)
    keff = (PARTITION + speed) / (1.0 + speed)
    phase_new = phase_now + TIME_STEP * rate
    solute_new = solute_now + TIME_STEP * (divergence + 0.5 * (1.0 - keff) * solute_now * rate)
    return (phase_new, solute_new)


def beside(padded):
    centre = padded[1:-1, 1:-1]
    return [
        padded[2:, 1:-1],
        padded[:-2, 1:-1],
        padded[1:-1, 2:],
        padded[1:-1, :-2],
        jnp.roll(centre, -1, 2),
        jnp.roll(centre, 1, 2),
    ]


def phase_sweep(phase_now, solute_now, undercool):
    padded = extended(jnp.stack([phase_now, solute_now]), (("gx", 1), ("gy", 2)), 1)
    phase_pad = padded[0]
    solute_pad = padded[1]
    diff_pad = diffusivity(phase_pad)
    return update(
        phase_now,
        solute_now,
        undercool,
        beside(phase_pad),
        beside(solute_pad),
        diff_pad[1:-1, 1:-1],
        beside(diff_pad),
    )


def signed_freq(indices, total):
    return jnp.where(indices < total // 2, indices, indices - total)


def wave_tables(freqs, positions, length, factor):
    product = freqs[:, None] * positions[None, :] % length
    angles = product.astype(jnp.float32) * (2.0 * math.pi / length)
    return (jnp.cos(angles) * factor, jnp.sin(angles) * factor)


def complex_mix(cosines, sines, data, pattern, orient):

    def apply(table, values):
        return jnp.einsum(pattern, table, values, precision=lax.Precision.HIGHEST)

    cos_real = apply(cosines, data[0])
    cos_imag = apply(cosines, data[1])
    sin_real = apply(sines, data[0])
    sin_imag = apply(sines, data[1])
    return jnp.stack([cos_real - orient * sin_imag, cos_imag + orient * sin_real])


def x_forward(data, factor):
    portion = lax.all_to_all(data, "gx", split_axis=1, concat_axis=2, tiled=True)
    length = portion.shape[2]
    cosines, sines = wave_tables(
        signed_freq(jnp.arange(KX, dtype=jnp.int32), KX),
        jnp.arange(length, dtype=jnp.int32),
        length,
        factor,
    )
    lines = complex_mix(cosines, sines, portion, "kx,wxyz->wkyz", -1.0)
    return lax.all_to_all(lines, "gx", split_axis=2, concat_axis=1, tiled=True)


def y_forward(data, factor):
    portion = lax.all_to_all(data, "gy", split_axis=1, concat_axis=3, tiled=True)
    length = portion.shape[3]
    cosines, sines = wave_tables(
        signed_freq(jnp.arange(KY, dtype=jnp.int32), KY),
        jnp.arange(length, dtype=jnp.int32),
        length,
        factor,
    )
    lines = complex_mix(cosines, sines, portion, "ky,wayz->wakz", -1.0)
    return lax.all_to_all(lines, "gy", split_axis=3, concat_axis=1, tiled=True)


def contract(weights, values):
    return jnp.einsum("abzoi,iabz->oabz", weights, values, precision=lax.Precision.HIGHEST)


def outer(left, right):
    return jnp.einsum("oabz,iabz->abzoi", left, right, precision=lax.Precision.HIGHEST)


def per_device_plain(
    phase,
    solute,
    undercool,
    lift_weight,
    spectral_weight,
    local_weight,
    local_bias,
    proj_weight,
    cotangent,
):
    phase_mid, solute_mid = phase_sweep(phase, solute, undercool)
    phase_next, solute_next = phase_sweep(phase_mid, solute_mid, undercool)
    cells_x, cells_y, depth = phase.shape
    total_x = cells_x * lax.axis_size("gx")
    total_y = cells_y * lax.axis_size("gy")
    fields = jnp.stack([phase_next, solute_next - SOLUTE_MEAN])
    modes_z = jnp.arange(KZ, dtype=jnp.int32)
    zpos = jnp.arange(depth, dtype=jnp.int32)
    unit_z = jnp.ones((KZ,), jnp.float32)
    weights_z = jnp.where(modes_z == 0, 1.0, 2.0).astype(jnp.float32) / depth

    def z_forward(field, zfactor):
        cosines, sines = wave_tables(modes_z, zpos, depth, zfactor[:, None])
        tables = jnp.stack([cosines, -sines])
        return jnp.einsum("wxyz,rkz->rwxyk", field, tables, precision=lax.Precision.HIGHEST)

    def spectral_forward(field, zfactor, xfactor, yfactor):
        return y_forward(x_forward(z_forward(field, zfactor), xfactor), yfactor)

    lifted = jnp.einsum("wc,cxyz->wxyz", lift_weight, fields, precision=lax.Precision.HIGHEST)
    spectrum = spectral_forward(lifted, unit_z, 1.0, 1.0)
    own_x = spectrum.shape[2]
    own_y = spectrum.shape[3]
    shaped = spectral_weight.reshape(2, own_x, own_y, KZ, WIDTH, WIDTH)
    out_real = contract(shaped[0], spectrum[0]) - contract(shaped[1], spectrum[1])
    out_imag = contract(shaped[0], spectrum[1]) + contract(shaped[1], spectrum[0])
    spectral_out = jnp.stack([out_real, out_imag])
    ypos = lax.axis_index("gy") * cells_y + jnp.arange(cells_y, dtype=jnp.int32)
    portion = lax.all_gather(spectral_out, "gy", axis=3, tiled=True)
    freqs = signed_freq(jnp.arange(portion.shape[3], dtype=jnp.int32), KY)
    cosines, sines = wave_tables(ypos, freqs, total_y, 1.0 / total_y)
    back_y = complex_mix(cosines, sines, portion, "yk,wakz->wayz", 1.0)
    cosines, sines = wave_tables(
        jnp.arange(total_x, dtype=jnp.int32),
        signed_freq(jnp.arange(KX, dtype=jnp.int32), KX),
        total_x,
        1.0 / total_x,
    )
    inverted = complex_mix(
        cosines,
        sines,
        lax.all_to_all(back_y, "gx", split_axis=1, concat_axis=2, tiled=True),
        "xk,wkyz->wxyz",
        1.0,
    )
    back_x = lax.all_to_all(inverted, "gx", split_axis=2, concat_axis=1, tiled=True)
    cos_back, sin_back = wave_tables(modes_z, zpos, depth, weights_z[:, None])
    back_tables = jnp.stack([cos_back, -sin_back])
    spectral_field = jnp.einsum(
        "rwxyk,rkz->wxyz", back_x, back_tables, precision=lax.Precision.HIGHEST
    )
    mixed = jnp.dot(local_weight, lift_weight, precision=lax.Precision.HIGHEST)
    pre_act = (
        spectral_field
        + jnp.einsum("wc,cxyz->wxyz", mixed, fields, precision=lax.Precision.HIGHEST)
        + local_bias[:, None, None, None]
    )
    activated, gelu_back = jax.vjp(jax.nn.gelu, pre_act)
    predicted = jnp.einsum("w,wxyz->xyz", proj_weight, activated, precision=lax.Precision.HIGHEST)
    grad_pre = gelu_back(proj_weight[:, None, None, None] * cotangent[None])[0]
    field_sums = jnp.einsum("wxyz,cxyz->wc", grad_pre, fields, precision=lax.Precision.HIGHEST)
    proj_sums = jnp.einsum("wxyz,xyz->w", activated, cotangent, precision=lax.Precision.HIGHEST)
    field_sums, proj_sums = lax.psum((field_sums, proj_sums), ("gx", "gy"))
    grad_modes = spectral_forward(grad_pre, weights_z, 1.0 / total_x, 1.0 / total_y)
    grad_real = outer(grad_modes[0], spectrum[0]) + outer(grad_modes[1], spectrum[1])
    grad_imag = outer(grad_modes[1], spectrum[0]) - outer(grad_modes[0], spectrum[1])
    grad_spectral = jnp.stack([grad_real, grad_imag]).reshape(2, own_x, own_y, KZ, WIDTH * WIDTH)
    scale = 1.0 / math.sqrt(total_x * total_y * depth)
    grad_local = jnp.dot(field_sums, lift_weight.T, precision=lax.Precision.HIGHEST) * scale
    grad_proj = proj_sums * scale
    return (phase_next, solute_next, predicted, grad_spectral, grad_local, grad_proj)


LANES = 128
SMALL_VMEM = 24 * 1024 * 1024
PACK_COST = 50_000_000_000
SPREAD = LANES // WIDTH
NARROW = jnp.bfloat16
EXACT = lax.Precision.HIGHEST


def halves(table):
    head = table.astype(np.float32).astype(ml_dtypes.bfloat16)
    rest = (table - head.astype(np.float64)).astype(np.float32).astype(ml_dtypes.bfloat16)
    return head, rest


def left_table(table):
    head, rest = halves(table)
    return np.concatenate([head, head, rest], axis=1)


def right_table(table):
    head, rest = halves(table)
    return np.concatenate([head, head, rest], axis=0)


def parts_of(values):
    head = values.astype(NARROW)
    return head, (values - head.astype(jnp.float32)).astype(NARROW)


def thrice(values, axis):
    head, rest = parts_of(values)
    return jnp.concatenate([head, rest, head], axis=axis)


def one_where(mask):
    return mask.astype(jnp.float32).astype(NARROW)


def mul(left, right):
    return jnp.dot(left, right, preferred_element_type=jnp.float32)


def mul_rows(left, right):
    return lax.dot_general(
        left, right, (((1,), (1,)), ((), ())), preferred_element_type=jnp.float32
    )


def angles(freqs, positions, length):
    return 2.0 * np.pi * ((freqs[:, None] * positions[None, :]) % length) / length


def signed(count):
    index = np.arange(count)
    return np.where(index < count // 2, index, index - count)


def rotation(theta, orient):
    cosines, sines = np.cos(theta), orient * np.sin(theta)
    return np.block([[cosines, -sines], [sines, cosines]])


def group_of(shape):
    return lax.broadcasted_iota(jnp.int32, shape, len(shape) - 1) // WIDTH


def pick(groups, choices):
    result = choices[-1]
    for index in range(len(choices) - 2, -1, -1):
        result = jnp.where(groups == index, choices[index], result)
    return result


def turn(values, shift):
    shift = shift % LANES
    return values if shift == 0 else pltpu.roll(values, shift, 1)


def swap_groups(pieces):
    groups = group_of(pieces[0].shape)
    return [
        pick(groups, [turn(pieces[i], WIDTH * (i - j)) for i in range(SPREAD)])
        for j in range(SPREAD)
    ]


def spread_cells(
    lift_ref, local_ref, bias_ref, proj_ref, cotangent_ref, vector_ref, mix_ref, spread_ref
):
    planes, depth, wide = spread_ref.shape
    tile = cotangent_ref.shape[0]
    cells_y = tile // planes
    lift, lift_rest = parts_of(lift_ref[...])
    local, local_rest = parts_of(local_ref[...])
    mixed = mul_rows(lift, local) + mul_rows(lift_rest, local) + mul_rows(lift, local_rest)
    for index in range(wide // WIDTH):
        place = slice(index * WIDTH, (index + 1) * WIDTH)
        vector_ref[0:2, place] = mixed
        vector_ref[2:3, place] = bias_ref[...]
        vector_ref[3:4, place] = proj_ref[...]
    head, rest = parts_of(vector_ref[...])
    row = lax.broadcasted_iota(jnp.int32, (cells_y, wide), 0)
    own = row == lax.broadcasted_iota(jnp.int32, (cells_y, wide), 1) // WIDTH

    def diagonal(line):
        return jnp.where(own, line.astype(jnp.float32), 0.0)

    mixing = [diagonal(part[k : k + 1]) for k in range(2) for part in (head, head, rest)]
    mixing += [part[2:3].astype(jnp.float32) for part in (head, rest)]
    mixing.append(jnp.zeros((2 * cells_y - 2, wide), jnp.float32))
    mix_ref[...] = jnp.concatenate(mixing, axis=0).astype(NARROW)
    spread = jnp.concatenate(parts_of(cotangent_ref[...].T), axis=1)
    cell = lax.broadcasted_iota(jnp.int32, (2 * tile, wide), 0) % tile
    row = lax.broadcasted_iota(jnp.int32, (2 * tile, wide), 1) // WIDTH
    for plane in range(planes):
        spread_ref[plane] = mul(spread, one_where(cell == plane * cells_y + row))


def contract_kernel(
    planes,
    lift_ref,
    weight_ref,
    local_ref,
    bias_ref,
    proj_ref,
    cotangent_ref,
    out_ref,
    vector_ref,
    mix_ref,
    spread_ref,
    outer_ref,
    wide_ref,
):
    _, own_x, own_y, modes_z, width = weight_ref.shape
    chunk = out_ref.shape[0] // modes_z
    steps = own_x // planes

    square = (WIDTH, WIDTH)
    diagonal = lax.broadcasted_iota(jnp.int32, square, 0) == lax.broadcasted_iota(
        jnp.int32, square, 1
    )
    columns = [
        jnp.sum(
            jnp.where(diagonal, jnp.broadcast_to(lift_ref[k : k + 1, :], square), 0.0),
            axis=1,
            keepdims=True,
        )
        for k in range(2)
    ]
    lane = lax.broadcasted_iota(jnp.int32, (WIDTH, LANES), 1)
    base = jnp.where(
        lane % (2 * WIDTH) < WIDTH,
        jnp.broadcast_to(columns[0], lane.shape),
        jnp.broadcast_to(columns[1], lane.shape),
    )
    head, rest = parts_of(base)
    base = jnp.where(lane < 2 * WIDTH, head.astype(jnp.float32), rest.astype(jnp.float32))
    mixing = jnp.concatenate(
        [jnp.where(lane % WIDTH == channel, base, 0.0) for channel in range(WIDTH)], axis=0
    ).astype(NARROW)
    rows = planes * own_y * modes_z
    low = lax.broadcasted_iota(jnp.int32, (rows, LANES), 1) < 2 * WIDTH
    for step in range(steps):
        sums = []
        for part in range(2):
            block = weight_ref[part, step * planes : (step + 1) * planes]
            head, rest = parts_of(block.reshape(rows, width))
            total = mul(head, mixing) + mul(rest, mixing)
            sums.append(total + turn(total, 2 * WIDTH))
        result = jnp.where(low, sums[0], sums[1])
        for plane in range(planes):
            for row in range(own_y):
                first = (plane * own_y + row) * modes_z
                place = row * own_x + step * planes + plane
                out_ref[pl.ds(place, modes_z, stride=chunk), :] = result[
                    first : first + modes_z
                ]
    spread_cells(
        lift_ref,
        local_ref,
        bias_ref,
        proj_ref,
        cotangent_ref,
        vector_ref,
        mix_ref,
        spread_ref,
    )
    for index in range(SPREAD):
        wide_ref[:, index * WIDTH : (index + 1) * WIDTH] = lift_ref[...]
    for index in range(1, width // LANES):
        wide_ref[:, index * LANES : (index + 1) * LANES] = wide_ref[:, 0:LANES]
    shape = (2 * WIDTH, width)
    row = lax.broadcasted_iota(jnp.int32, shape, 0)
    column = lax.broadcasted_iota(jnp.int32, shape, 1)
    lift = jnp.where(row < WIDTH, wide_ref[0:1, :], wide_ref[1:2, :])
    head, rest = parts_of(jnp.where(column // WIDTH == row % WIDTH, lift, 0.0))
    outer_ref[0 : 2 * WIDTH] = head
    outer_ref[2 * WIDTH : 4 * WIDTH] = head
    outer_ref[4 * WIDTH : 6 * WIDTH] = rest
    outer_ref[6 * WIDTH : 8 * WIDTH] = jnp.zeros_like(rest)


def edge_kernel(held_ref, head_ref, tail_ref):
    cells_x = held_ref.shape[1]
    for index, reach in enumerate((2, 2, 1)):
        head_ref[2 * index : 2 * index + reach] = held_ref[index, 0:reach]
        tail_ref[2 * index : 2 * index + reach] = held_ref[index, cells_x - reach : cells_x]


def pack_kernel(held_ref, before_ref, after_ref, head_ref, tail_ref):
    _, cells_x, cells_y, _ = held_ref.shape
    for out, near, far in ((head_ref, 0, 1), (tail_ref, cells_y - 1, cells_y - 2)):
        for plane in range(cells_x):
            line = slice(plane, plane + 1)
            for index in range(2):
                out[2 * index, line] = held_ref[index, plane, near : near + 1]
                out[2 * index + 1, line] = held_ref[index, plane, far : far + 1]
            out[4, line] = held_ref[2, plane, near : near + 1]
        for index in range(2):
            out[5, 2 * index : 2 * index + 1] = before_ref[2 * index + 1, near : near + 1]
            out[5, 2 * index + 1 : 2 * index + 2] = after_ref[2 * index, near : near + 1]


def step_kernel(
    held_ref,
    before_ref,
    after_ref,
    low_ref,
    high_ref,
    table_ref,
    mixed_ref,
    fields_ref,
    send_ref,
    phase_ext,
    solute_ext,
    cool_ext,
    diff_ext,
    lines,
):
    _, cells_x, cells_y, depth = held_ref.shape
    base = 8
    end = base + cells_y
    for index, ext in enumerate((phase_ext, solute_ext)):
        first = 2 * index
        ext[2 : cells_x + 2, base:end] = held_ref[index]
        ext[0:2, base:end] = before_ref[first : first + 2]
        ext[cells_x + 2 : cells_x + 4, base:end] = after_ref[first : first + 2]
        for source, near in ((low_ref, base - 1), (high_ref, end)):
            for plane in range(cells_x):
                ext[plane + 2, near : near + 1] = source[first, plane : plane + 1]
            ext[1, near : near + 1] = source[5, first : first + 1]
            ext[cells_x + 2, near : near + 1] = source[5, first + 1 : first + 2]
    cool_ext[2 : cells_x + 2, base:end] = held_ref[2]
    cool_ext[1:2, base:end] = before_ref[4:5]
    cool_ext[cells_x + 2 : cells_x + 3, base:end] = after_ref[4:5]

    send_ref[...] = mixed_ref[...]

    def sweep(reach):
        diff_ext[...] = diffusivity(phase_ext[...])

        def window(ext, move_x, move_y):
            return ext[
                2 - reach + move_x : cells_x + 2 + reach + move_x, base + move_y : end + move_y
            ]

        def around(ext, now):
            return [
                window(ext, 1, 0),
                window(ext, -1, 0),
                window(ext, 0, 1),
                window(ext, 0, -1),
                pltpu.roll(now, depth - 1, 2),
                pltpu.roll(now, 1, 2),
            ]

        phase_now = window(phase_ext, 0, 0)
        solute_now = window(solute_ext, 0, 0)
        diff_now = window(diff_ext, 0, 0)
        return update(
            phase_now,
            solute_now,
            window(cool_ext, 0, 0),
            around(phase_ext, phase_now),
            around(solute_ext, solute_now),
            diff_now,
            around(diff_ext, diff_now),
        )

    def edge(source, row, sign):
        values, sides = [], []
        for index in range(2):
            near, far = source[2 * index], source[2 * index + 1]
            inner = jnp.concatenate(
                [held_ref[index, plane, row : row + 1] for plane in range(cells_x)], axis=0
            )
            before = source[5, 2 * index : 2 * index + 1]
            after = source[5, 2 * index + 1 : 2 * index + 2]
            values.append(near)
            sides.append(
                [
                    jnp.concatenate([near[1:], after], axis=0),
                    jnp.concatenate([before, near[:-1]], axis=0),
                    *((inner, far) if sign < 0 else (far, inner)),
                    pltpu.roll(near, depth - 1, 1),
                    pltpu.roll(near, 1, 1),
                ]
            )
        diffs = [diffusivity(side) for side in sides[0]]
        return update(*values, source[4], *sides, diffusivity(values[0]), diffs)

    phase_mid, solute_mid = sweep(1)
    edges = (edge(low_ref, 0, -1), edge(high_ref, cells_y - 1, 1))
    phase_ext[1 : cells_x + 3, base:end] = phase_mid
    solute_ext[1 : cells_x + 3, base:end] = solute_mid
    for place, moved in zip((base - 1, end), edges):
        for ext, line in zip((phase_ext, solute_ext), moved):
            for plane in range(cells_x):
                ext[plane + 2, place : place + 1] = line[plane : plane + 1]
    phase_next, solute_next = sweep(0)
    fields_ref[0] = phase_next
    fields_ref[1] = solute_next
    tile = cells_x * cells_y
    both = (phase_next.reshape(tile, depth), solute_next.reshape(tile, depth) - SOLUTE_MEAN)
    ordered = []
    for part in range(depth // LANES):
        for index, values in enumerate(both):
            lines[part, index * tile : (index + 1) * tile] = values[
                :, part * LANES : (part + 1) * LANES
            ]
        ordered.append(
            jnp.concatenate(
                [
                    lines[part, pl.ds(row, 2 * cells_x, stride=cells_y), :]
                    for row in range(cells_y)
                ],
                axis=0,
            )
        )
    ordered = jnp.concatenate(ordered, axis=1)
    spectra = mul_rows(table_ref[...], thrice(ordered, 1))
    modes_z = spectra.shape[0] // 2
    chunk = send_ref.shape[0] // modes_z
    for part in range(2):
        send_ref[pl.ds(chunk - 2 + part, modes_z, stride=chunk), :] = spectra[
            part * modes_z : (part + 1) * modes_z
        ]


def pack_modes(shape, modes, modes_ref, rows_ref):
    count_x, count_y, _, _, own_x, own_y = shape
    modes_x, modes_y = count_x * own_x, count_y * own_y
    lane = lax.broadcasted_iota(jnp.int32, (modes_y, LANES), 1)
    for index in range(count_x):
        block = modes
        for k in range(4):
            shift = k * own_x - k * modes_x - index * own_x
            block = jnp.where(lane // own_x == k, turn(modes, shift), block)
        rows_ref[index] = block
        line = rows_ref[index, pl.ds(0, count_y, stride=own_y), :]
        groups = group_of(line.shape)
        for row in range(1, own_y):
            piece = rows_ref[index, pl.ds(row, count_y, stride=own_y), :]
            line = jnp.where(groups == row, turn(piece, row * WIDTH), line)
        modes_ref[pl.ds(index, count_y, stride=count_x), :] = line


def spectral_kernel(
    shape,
    mixed_ref,
    y_in_ref,
    x_in_ref,
    y_out_ref,
    x_out_ref,
    fields_ref,
    forth_ref,
    chosen_ref,
    gather_ref,
    modes_ref,
    send_ref,
    table_ref,
    line_ref,
    lines_y,
    lines_x,
    rows_ref,
    weight_ref,
):
    count_x, count_y, cells_x, cells_y, own_x, own_y = shape
    modes_x, modes_y = count_x * own_x, count_y * own_y
    total_x, total_y = count_x * cells_x, count_y * cells_y
    tile = cells_x * cells_y
    narrow = 2 * cells_x
    rows = 2 * count_y
    devices = count_x * count_y
    own = own_x * own_y
    chunk = mixed_ref.shape[0] // devices
    for index_x in range(count_x):
        for index_y in range(count_y):
            place = (index_x * count_y + index_y) * own
            start = (index_y * count_x + index_x) * chunk
            weight_ref[place : place + own, :] = mixed_ref[start : start + own, :]
    pieces = [
        jnp.concatenate(
            [
                mixed_ref[pl.ds(index * chunk + own + part, count_y, stride=count_x * chunk), :]
                for part in range(2)
            ],
            axis=0,
        )
        for index in range(count_x)
    ]
    lane = lax.broadcasted_iota(jnp.int32, (rows, LANES), 1)
    blocks = []
    for row in range(cells_y):
        block = jnp.zeros((rows, LANES), jnp.float32)
        for index in range(count_x):
            piece = turn(pieces[index], narrow * (index - row))
            block = jnp.where(lane // narrow == index, piece, block)
        blocks.append(block)
    along_y = mul(y_in_ref[...], thrice(jnp.concatenate(blocks, axis=0), 0))
    prepare(fields_ref, forth_ref, table_ref, line_ref)
    half = lax.broadcasted_iota(jnp.int32, (modes_y, LANES), 1) < LANES // 2
    joined = jnp.where(half, along_y[0:modes_y], turn(along_y[modes_y:], LANES // 2))
    modes = mul(thrice(joined, 1), x_in_ref[...])
    quads_y = total_y // SPREAD
    quads_x = modes_x // SPREAD
    lane = lax.broadcasted_iota(jnp.int32, (modes_y, LANES), 1) % modes_x
    chosen = jnp.concatenate(
        [jnp.where(lane == freq, modes, 0.0) for freq in range(modes_x)], axis=0
    )
    columns = mul(jnp.concatenate(parts_of(chosen), axis=1), chosen_ref[...])
    low = lax.broadcasted_iota(jnp.int32, (modes_y, LANES), 1) < 2 * WIDTH
    def gathered(quads):
        products = [[], []]
        for quad in quads:
            lines = [[], []]
            for index in range(SPREAD):
                freq = SPREAD * quad + index
                start = (freq // own_x) * count_y * own_y * own_x + freq % own_x
                weights = weight_ref[pl.ds(start, modes_y, stride=own_x), :]
                for part in range(2):
                    column = columns[
                        freq * modes_y : (freq + 1) * modes_y, part * LANES : (part + 1) * LANES
                    ]
                    line = weights * column
                    lines[part].append(line + turn(line, 2 * WIDTH))
            for part in range(2):
                pairs = [
                    jnp.where(low, lines[part][index], lines[part][index + 1])
                    for index in range(0, SPREAD, 2)
                ]
                products[part].append(jnp.concatenate(pairs, axis=1))
        products = jnp.concatenate(products[0] + products[1], axis=0)
        products = mul(jnp.concatenate(parts_of(products), axis=1), gather_ref[...])
        stacked = []
        for index in range(len(quads)):
            places = [(part * len(quads) + index) * modes_y for part in range(2)]
            stacked.append(
                jnp.concatenate([products[place : place + modes_y] for place in places], axis=0)
            )
        return thrice(jnp.concatenate(stacked, axis=1), 0)

    def along_lines(quads, stacked):
        back = mul(y_out_ref[...], stacked)
        for index, quad in enumerate(quads):
            lines_y[quad] = back[:, index * LANES : (index + 1) * LANES]
        for quad in quads:
            for part in range(2):
                pieces = [
                    lines_y[quad, pl.ds(part * total_y + i, quads_y, stride=SPREAD), :]
                    for i in range(SPREAD)
                ]
                for index, piece in enumerate(swap_groups(pieces)):
                    place = part * modes_x + SPREAD * quad + index
                    lines_x[pl.ds(place, quads_y, stride=2 * modes_x), :] = piece

    batches = [range(first, first + 2) for first in range(0, quads_x, 2)]
    following = gathered(batches[0])
    for index, quads in enumerate(batches):
        stacked = following
        if index + 1 < len(batches):
            following = gathered(batches[index + 1])
        along_lines(quads, stacked)
    per_tile = cells_y // SPREAD
    for start in range(0, quads_y, 4):
        blocks = [
            lines_x[quad * 2 * modes_x : (quad + 1) * 2 * modes_x, :]
            for quad in range(start, start + 4)
        ]
        back = mul(x_out_ref[...], thrice(jnp.concatenate(blocks, axis=1), 0))
        for quad in range(start, start + 4):
            lanes = slice((quad - start) * LANES, (quad - start + 1) * LANES)
            for part in range(2):
                for index in range(count_x):
                    device = quad // per_tile * count_x + index
                    place = (device * 2 + part) * per_tile + quad % per_tile
                    first = part * total_x + index * cells_x
                    send_ref[place * cells_x : (place + 1) * cells_x, :] = back[
                        first : first + cells_x, lanes
                    ]
    pack_modes(shape, modes, modes_ref, rows_ref)


def prepare(fields_ref, forth_ref, table_ref, line_ref):
    planes, depth, _ = table_ref.shape
    cells_y = fields_ref.shape[2]
    tile = planes * cells_y
    rows = forth_ref.shape[0] // 2
    fields = (fields_ref[0].reshape(tile, depth), fields_ref[1].reshape(tile, depth) - SOLUTE_MEAN)
    ones = jnp.where(lax.broadcasted_iota(jnp.int32, (2 * cells_y, depth), 0) < 2, 1.0, 0.0)
    table = forth_ref[rows:].astype(jnp.float32)
    for plane in range(planes):
        lines = [values[plane * cells_y : (plane + 1) * cells_y] for values in fields]
        pieces = [[part.astype(jnp.float32) for part in parts_of(values)] for values in lines]
        both = [piece for head, rest in pieces for piece in (head, rest, head)]
        both = jnp.concatenate([table] + both + [ones], axis=0)
        table_ref[plane] = both.T.astype(NARROW)
        pieces = [piece for pair in zip(*pieces) for piece in pair]
        line_ref[plane] = jnp.concatenate(pieces, axis=0).astype(NARROW)


def fold_channels(values):
    quarter = values.shape[0] // SPREAD
    parts = []
    for first in range(0, values.shape[1], LANES):
        pieces = [
            values[index * quarter : (index + 1) * quarter, first : first + LANES]
            for index in range(SPREAD)
        ]
        channel = lax.broadcasted_iota(jnp.int32, pieces[0].shape, 1) % WIDTH
        span = WIDTH // 2
        while len(pieces) > 1:
            low = channel % (2 * span) < span
            pieces = [
                jnp.where(low, left + turn(left, -span), right + turn(right, span))
                for left, right in zip(pieces[: len(pieces) // 2], pieces[len(pieces) // 2 :])
            ]
            span //= 2
        parts.append(pieces[0])
    return jnp.concatenate(parts, axis=1)


def field_kernel(
    cells_y,
    field_ref,
    table_ref,
    mix_ref,
    weight_ref,
    line_ref,
    vector_ref,
    back_ref,
    forth_ref,
    predicted_ref,
    send_ref,
    shares_ref,
):
    planes, depth, wide = weight_ref.shape
    rows = forth_ref.shape[0] // 2
    halves_y = cells_y // SPREAD
    stride = halves_y * planes
    proj = 0.5 * vector_ref[3:4, :]
    root = math.sqrt(2.0 / math.pi)
    curve = 0.044715
    picker = one_where(
        lax.broadcasted_iota(jnp.int32, (SPREAD * cells_y, 2 * wide), 0)
        == lax.broadcasted_iota(jnp.int32, (SPREAD * cells_y, 2 * wide), 1)
        % wide
        // (WIDTH // SPREAD)
    )
    line_sums = jnp.zeros((2 * cells_y, wide), jnp.float32)
    proj_sums = jnp.zeros((8, wide), jnp.float32)
    def back(plane):
        spectra = jnp.concatenate(
            [
                field_ref[pl.ds(part * planes + plane, rows, stride=stride), :]
                for part in range(halves_y)
            ],
            axis=1,
        )
        spectra = jnp.concatenate([thrice(spectra, 0), mix_ref[...]], axis=0)
        table = jnp.concatenate([back_ref[...], table_ref[plane]], axis=1)
        return mul(table, spectra)

    def activate(pre, plane):
        square = pre * pre
        bent = jnp.tanh(pre * (root + (root * curve) * square))
        upper = 1.0 + bent
        active = pre * upper
        slope = upper + (active - active * bent) * (root + (3.0 * root * curve) * square)
        cotangent = weight_ref[plane]
        grad = cotangent * slope
        sums = jnp.sum((active * cotangent).reshape(depth // 8, 8, wide), axis=0)
        return sums, parts_of(fold_channels(proj * active)), parts_of(grad)

    def forth(shared, grad, plane):
        shares_ref[plane, :, 0 : depth // SPREAD] = mul_rows(
            picker, jnp.concatenate(shared, axis=1)
        )
        for index in range(SPREAD):
            predicted_ref[
                plane * cells_y : (plane + 1) * cells_y,
                index * (depth // SPREAD) : (index + 1) * (depth // SPREAD),
            ] = shares_ref[plane, pl.ds(index, cells_y, stride=SPREAD), 0 : depth // SPREAD]
        head, rest = grad
        lines = line_ref[plane]
        top = jnp.concatenate([forth_ref[0:rows], lines[0 : 2 * cells_y]], axis=0)
        low = jnp.concatenate([forth_ref[rows:], lines[2 * cells_y :]], axis=0)
        spectra = mul(jnp.concatenate([top, low], axis=0), head)
        spectra = spectra[0 : rows + 2 * cells_y] + spectra[rows + 2 * cells_y :] + mul(top, rest)
        spectra = spectra * proj
        for part in range(halves_y):
            send_ref[pl.ds(part * planes + plane, rows, stride=stride), :] = spectra[
                0:rows, part * LANES : (part + 1) * LANES
            ]
        return spectra[rows:]

    following = back(0)
    previous = None
    for plane in range(planes + 1):
        pre = following
        if plane + 1 < planes:
            following = back(plane + 1)
        if plane < planes:
            sums, *current = activate(pre, plane)
            proj_sums = proj_sums + sums
        if plane > 0:
            line_sums = line_sums + forth(*previous, plane - 1)
        previous = current
    shape = (cells_y, wide)
    own = lax.broadcasted_iota(jnp.int32, shape, 0) == (
        lax.broadcasted_iota(jnp.int32, shape, 1) // WIDTH
    )
    sums = [
        jnp.where(own, line_sums[0:cells_y], 0.0),
        jnp.where(own, line_sums[cells_y:], 0.0),
        0.5 * proj_sums,
    ]
    for index, values in enumerate(sums):
        line = jnp.sum(values, axis=0, keepdims=True)
        line = sum(line[:, part * LANES : (part + 1) * LANES] for part in range(halves_y))
        send_ref[stride + index : stride + index + 1, :] = line


def gradient_kernel(
    shape, spectra_ref, modes_ref, x_in_ref, y_in_ref, send_ref, lines_x, lines_y
):
    count_x, count_y, cells_x, cells_y, own_x, own_y = shape
    modes_x, modes_y = count_x * own_x, count_y * own_y
    total_x, total_y = count_x * cells_x, count_y * cells_y
    per_tile = cells_y // SPREAD
    quads_y = total_y // SPREAD
    chunk = 2 * per_tile * cells_x
    first_device = (lax.axis_index("gx") == 0) & (lax.axis_index("gy") == 0)
    keep = jnp.where(first_device, 0.0, 1.0)
    devices = count_x * count_y
    out_chunk = send_ref.shape[0] // devices
    per_own = own_x // SPREAD
    quads_x = modes_x // SPREAD
    for start in range(0, quads_y, SPREAD):
        blocks = []
        for quad in range(start, start + SPREAD):
            block = []
            for part in range(2):
                for index in range(count_x):
                    device = quad // per_tile * count_x + index
                    place = (device * 2 + part) * per_tile + quad % per_tile
                    piece = spectra_ref[place * cells_x : (place + 1) * cells_x, :]
                    block.append(piece * keep if part else piece)
            blocks.append(jnp.concatenate(block, axis=0))
        forth = mul(x_in_ref[...], thrice(jnp.concatenate(blocks, axis=1), 0))
        for quad in range(start, start + SPREAD):
            lines_x[quad * 2 * modes_x : (quad + 1) * 2 * modes_x, :] = forth[
                :, (quad - start) * LANES : (quad - start + 1) * LANES
            ]
    extra = 2 * per_own * own_y
    send_ref[pl.ds(extra, devices, stride=out_chunk), :] = modes_ref[...]
    groups = group_of((1, LANES))
    total = jnp.zeros((1, LANES), jnp.float32)
    for index in range(3):
        start = chunk // 2 + index
        line = jnp.sum(
            spectra_ref[pl.ds(start, devices, stride=chunk), :], axis=0, keepdims=True
        )
        line = line + turn(line, 2 * WIDTH)
        total = jnp.where(groups == index, line + turn(line, WIDTH), total)
    send_ref[pl.ds(extra + 1, devices, stride=out_chunk), :] = jnp.broadcast_to(
        total, (devices, LANES)
    )
    for start in range(0, quads_x, 2):
        for quad in range(start, start + 2):
            for part in range(2):
                pieces = [
                    lines_x[
                        pl.ds(part * modes_x + SPREAD * quad + j, quads_y, stride=2 * modes_x), :
                    ]
                    for j in range(SPREAD)
                ]
                for index, piece in enumerate(swap_groups(pieces)):
                    lines_y[quad, pl.ds(part * total_y + index, quads_y, stride=SPREAD), :] = piece
        lines = jnp.concatenate([lines_y[start], lines_y[start + 1]], axis=1)
        modes = mul(y_in_ref[...], thrice(lines, 0))
        for quad in range(start, start + 2):
            for part in range(2):
                for index in range(count_y):
                    device = index * count_x + quad // per_own
                    place = device * out_chunk + (part * per_own + quad % per_own) * own_y
                    first = part * modes_y + index * own_y
                    send_ref[place : place + own_y, :] = modes[
                        first : first + own_y, (quad - start) * LANES : (quad - start + 1) * LANES
                    ]


def outer_kernel(
    scale,
    modes_ref,
    narrow_ref,
    predicted_ref,
    fields_ref,
    mix_ref,
    repeat_ref,
    spread_ref,
    local_out,
    proj_out,
    predicted_out,
    phase_out,
    solute_out,
    grad_ref,
    local_ref,
    proj_ref,
    held,
    sent,
):
    _, own_x, own_y, modes_z, width = held.shape
    chunk = modes_ref.shape[0] // modes_z
    per_own = own_x // SPREAD
    extra = 2 * per_own * own_y
    copies = [
        pltpu.make_async_copy(predicted_ref, predicted_out, sent.at[own_x]),
        pltpu.make_async_copy(fields_ref.at[0], phase_out, sent.at[own_x + 1]),
        pltpu.make_async_copy(fields_ref.at[1], solute_out, sent.at[own_x + 2]),
    ]
    for copy in copies:
        copy.start()
    lane = lax.broadcasted_iota(jnp.int32, (modes_z, LANES), 1)
    low = lane < 2 * WIDTH

    def rows_of(values):
        head, rest = parts_of(values)
        both = jnp.where(low, head.astype(jnp.float32), rest.astype(jnp.float32)).astype(NARROW)
        return jnp.concatenate([both, head], axis=1)

    def repeated(half):
        grads = [
            modes_ref[pl.ds((part * per_own + half) * own_y + row, modes_z, stride=chunk), :]
            for part in range(2)
            for row in range(own_y)
        ]
        grads = jnp.concatenate(grads, axis=0)
        return mul(jnp.concatenate(parts_of(grads), axis=1), repeat_ref[...])

    modes = modes_ref[pl.ds(extra, modes_z, stride=chunk), :]
    own = lane // (4 * own_x) * own_x + lane % own_x
    for plane in range(own_x):
        if plane % SPREAD == 0:
            grads = repeated(plane // SPREAD)
        chosen = jnp.concatenate(
            [jnp.where(own == row * own_x + plane, modes, 0.0) for row in range(own_y)], axis=0
        )
        columns = mul(jnp.concatenate(parts_of(chosen), axis=1), spread_ref[...])
        reals, imags = [], []
        for row in range(own_y):
            real = columns[row * modes_z : (row + 1) * modes_z, 0:LANES]
            imag = columns[row * modes_z : (row + 1) * modes_z, LANES:]
            pair = []
            for part in range(2):
                first = (part * own_y + row) * modes_z
                group = plane % SPREAD * LANES
                pair.append(grads[first : first + modes_z, group : group + LANES])
            reals.append(rows_of(pair[0] * real + pair[1] * imag))
            imags.append(rows_of(pair[1] * real - pair[0] * imag))
        result = mul(jnp.concatenate(reals + imags, axis=0), mix_ref[...])
        held[:, plane] = result.reshape(2, own_y, modes_z, width)
        copies.append(
            pltpu.make_async_copy(held.at[:, plane], grad_ref.at[:, plane], sent.at[plane])
        )
        copies[-1].start()
    line = modes_ref[extra + 1 : extra + 2, :]
    square = (WIDTH, WIDTH)
    diagonal = lax.broadcasted_iota(jnp.int32, square, 0) == lax.broadcasted_iota(
        jnp.int32, square, 1
    )
    local = jnp.zeros(square, jnp.float32)
    for k in range(2):
        sums = jnp.broadcast_to(line[:, k * WIDTH : (k + 1) * WIDTH], square)
        sums = jnp.sum(jnp.where(diagonal, sums, 0.0), axis=1, keepdims=True)
        local = local + sums * narrow_ref[k : k + 1, :]
    local_ref[...] = scale * local
    proj_ref[...] = scale * line[:, 2 * WIDTH : 3 * WIDTH]
    copies.append(pltpu.make_async_copy(local_ref, local_out, sent.at[own_x + 3]))
    copies.append(pltpu.make_async_copy(proj_ref, proj_out, sent.at[own_x + 4]))
    copies[-2].start()
    copies[-1].start()
    for copy in copies:
        copy.wait()


def tables(shape, depth, modes_z):
    count_x, count_y, cells_x, cells_y, own_x, own_y = shape
    modes_x, modes_y = count_x * own_x, count_y * own_y
    total_x, total_y = count_x * cells_x, count_y * cells_y
    theta_z = angles(np.arange(modes_z), np.arange(depth), depth)
    theta_x = angles(signed(modes_x), np.arange(total_x), total_x)
    theta_y = angles(signed(modes_y), np.arange(total_y), total_y)
    plain_z = np.concatenate([np.cos(theta_z), -np.sin(theta_z)], axis=0)
    forth_z = plain_z.reshape(2, modes_z, depth).transpose(1, 0, 2).reshape(2 * modes_z, depth)
    weight = np.where(np.arange(modes_z) == 0, 1.0, 2.0) / (total_x * total_y * depth)
    weighted_z = np.repeat(weight, 2)[:, None] * forth_z
    forth_x, back_x = rotation(theta_x, -1.0), rotation(theta_x.T, 1.0)
    forth_y, back_y = rotation(theta_y, -1.0), rotation(theta_y.T, 1.0)
    order_y = forth_y.reshape(2 * modes_y, 2, count_y, cells_y)
    order_y = order_y.transpose(0, 3, 1, 2).reshape(2 * modes_y, 2 * total_y)
    lines = forth_x.reshape(2, modes_x, 2, count_x, cells_x)
    both = np.zeros((2, count_x, 2, cells_x, 2, 2, modes_x))
    for field in range(2):
        both[:, :, field, :, :, field, :] = lines.transpose(2, 3, 4, 0, 1)
    both = both.reshape(4 * total_x, 4 * modes_x)
    index = np.arange(4 * LANES)
    line = index[: 2 * LANES, None] % LANES
    group = index[None, : 2 * LANES] // WIDTH
    same = np.where(group < 4, group, (group + 2) % 4)
    signs = np.where((group == 2) | (group == 3), -1.0, 1.0)
    chosen = np.where(line // modes_x == same, signs, 0.0)
    half = 2 * WIDTH
    row, column = index[:, None] % (SPREAD * half), index[None, :LANES]
    gather = row // half * WIDTH + row % WIDTH == column
    repeat = line == index[None, :] // LANES * WIDTH + index[None, :] % WIDTH
    spread = line // own_x % 4 == group // 4 * 2 + group % 2
    masks = {"chosen": chosen, "gather": gather, "repeat": repeat, "spread": spread}
    masks = {name: mask.astype(ml_dtypes.bfloat16) for name, mask in masks.items()}
    return masks | {
        "z_plain": left_table(plain_z),
        "z_forth": np.concatenate(halves(weighted_z), axis=0),
        "z_back": left_table(weighted_z.T)[:, : 4 * modes_z],
        "y_first": left_table(order_y),
        "x_first": right_table(both),
        "y_back": left_table(back_y),
        "x_back": left_table(back_x),
        "x_forth": left_table(forth_x),
        "y_forth": left_table(forth_y),
    }


def fits(count_x, count_y, phase, spectral_weight):
    cells_x, cells_y, depth = phase.shape
    _, own_x, own_y, modes_z, width = spectral_weight.shape
    return (
        width == WIDTH * WIDTH
        and modes_z == count_x * count_y
        and 4 * modes_z == LANES
        and 4 * count_x * cells_x == LANES
        and 4 * count_x * own_x == LANES
        and 2 * cells_x * cells_y == LANES
        and cells_x == 8
        and cells_y % SPREAD == 0
        and own_x % SPREAD == 0
        and own_y * 4 * own_x == LANES
        and 3 * WIDTH <= LANES
        and cells_y == 8
        and depth % LANES == 0
    )


def call(kernel, outs, scratch, flops, moved, limit=SMALL_VMEM, **more):
    return pl.pallas_call(
        kernel,
        out_shape=outs,
        scratch_shapes=scratch,
        compiler_params=pltpu.CompilerParams(vmem_limit_bytes=limit),
        cost_estimate=pl.CostEstimate(flops=flops, bytes_accessed=moved, transcendentals=0),
        **more,
    )


def exchange(values):
    return lax.all_to_all(values, ("gy", "gx"), split_axis=0, concat_axis=0, tiled=True)


def per_device_fast(
    phase,
    solute,
    undercool,
    lift_weight,
    spectral_weight,
    local_weight,
    local_bias,
    proj_weight,
    cotangent,
):
    count_x, count_y = lax.axis_size("gx"), lax.axis_size("gy")
    cells_x, cells_y, depth = phase.shape
    _, own_x, own_y, modes_z, width = spectral_weight.shape
    shape = (count_x, count_y, cells_x, cells_y, own_x, own_y)
    devices = count_x * count_y
    tile = cells_x * cells_y
    modes_x, modes_y = count_x * own_x, count_y * own_y
    total_x, total_y = count_x * cells_x, count_y * cells_y
    table = tables(shape, depth, modes_z)
    real = jnp.float32

    def like(*dims):
        return jax.ShapeDtypeStruct(dims, real)

    far = pl.BlockSpec(memory_space=pltpu.HBM)
    weight_bytes = 8 * own_x * own_y * modes_z * width
    held = jnp.stack([phase, solute, undercool])
    head, tail = call(
        edge_kernel,
        (like(5, cells_y, depth), like(5, cells_y, depth)),
        [],
        1000,
        40 * tile * depth,
    )(held)

    def ring(values, axis, step):
        count = lax.axis_size(axis)
        return lax.ppermute(values, axis, [(i, (i + step) % count) for i in range(count)])

    head, tail, lift = lax.optimization_barrier((head, tail, lift_weight.T))
    before, after = ring(tail, "gx", 1), ring(head, "gx", -1)
    planes = 2
    spread_shape = (cells_x, depth, cells_y * WIDTH)
    mixed_weights, vectors, mixing, weight, outer_mix = call(
        functools.partial(contract_kernel, planes),
        (
            like(modes_z * (own_x * own_y + 2), LANES),
            like(4, cells_y * WIDTH),
            jax.ShapeDtypeStruct((8 * cells_y, cells_y * WIDTH), NARROW),
            like(*spread_shape),
            jax.ShapeDtypeStruct((8 * WIDTH, width), NARROW),
        ),
        [pltpu.VMEM((2, width), real)],
        weight_bytes * LANES,
        weight_bytes,
    )(
        lift,
        spectral_weight,
        local_weight,
        local_bias.reshape(1, WIDTH),
        proj_weight.reshape(1, WIDTH),
        cotangent.reshape(tile, depth),
    )
    head, tail = call(
        pack_kernel,
        (like(6, cells_x, depth), like(6, cells_x, depth)),
        [],
        PACK_COST,
        40 * tile * depth,
    )(held, before, after)
    low, high = ring(tail, "gy", 1), ring(head, "gy", -1)
    extended_shape = pltpu.VMEM((cells_x + 4, cells_y + 16, depth), real)
    stepped, spectra = call(
        step_kernel,
        (like(2, *phase.shape), like(*mixed_weights.shape)),
        [extended_shape] * 4 + [pltpu.VMEM((depth // LANES, 2 * tile, LANES), real)],
        400 * tile * depth,
        80 * tile * depth,
    )(held, before, after, low, high, table["z_plain"], mixed_weights)
    gathered = exchange(spectra.reshape(-1, 2, LANES)).reshape(spectra.shape)
    modes, fields, lines, own_lines = call(
        functools.partial(spectral_kernel, shape),
        (
            like(devices, LANES),
            like(devices * 2 * cells_x * (cells_y // SPREAD), LANES),
            jax.ShapeDtypeStruct((cells_x, depth, LANES), NARROW),
            jax.ShapeDtypeStruct((cells_x, 4 * cells_y, depth), NARROW),
        ),
        [
            pltpu.VMEM((modes_x // SPREAD, 2 * total_y, LANES), real),
            pltpu.VMEM((2 * modes_x * (total_y // SPREAD), LANES), real),
            pltpu.VMEM((count_x, modes_y, LANES), real),
            pltpu.VMEM((devices * own_x * own_y, LANES), real),
        ],
        100_000_000,
        2_000_000,
    )(
        gathered,
        table["y_first"],
        table["x_first"],
        table["y_back"],
        table["x_back"],
        stepped,
        table["z_forth"],
        table["chosen"],
        table["gather"],
    )
    fields = exchange(fields)
    predicted, spectra = call(
        functools.partial(field_kernel, cells_y),
        (like(tile, depth), like(*fields.shape)),
        [pltpu.VMEM((cells_x, SPREAD * cells_y, LANES), real)],
        1_000_000_000,
        2_000_000,
    )(fields, lines, mixing, weight, own_lines, vectors, table["z_back"], table["z_forth"])
    spectra = exchange(spectra)
    chunk = 2 * own_x * own_y * WIDTH // LANES + 2
    gradients = call(
        functools.partial(gradient_kernel, shape),
        like(devices * chunk, LANES),
        [
            pltpu.VMEM((2 * modes_x * (total_y // SPREAD), LANES), real),
            pltpu.VMEM((modes_x // SPREAD, 2 * total_y, LANES), real),
        ],
        100_000_000,
        2_000_000,
    )(spectra, modes, table["x_forth"], table["y_forth"])
    gradients = exchange(gradients.reshape(-1, 2, LANES)).reshape(gradients.shape)
    grad_local, grad_proj, predicted, phase_next, solute_next, grad_spectral = call(
        functools.partial(outer_kernel, 1.0 / math.sqrt(total_x * total_y * depth)),
        (
            like(WIDTH, WIDTH),
            like(1, WIDTH),
            like(*predicted.shape),
            like(*phase.shape),
            like(*phase.shape),
            like(*spectral_weight.shape),
        ),
        [
            pltpu.VMEM((WIDTH, WIDTH), real),
            pltpu.VMEM((1, WIDTH), real),
            pltpu.VMEM(spectral_weight.shape, real),
            pltpu.SemaphoreType.DMA((own_x + 5,)),
        ],
        weight_bytes * 4 * WIDTH,
        weight_bytes,
        out_specs=(far,) * 6,
    )(gradients, lift, predicted, stepped, outer_mix, table["repeat"], table["spread"])
    return (
        phase_next,
        solute_next,
        predicted.reshape(phase.shape),
        grad_spectral,
        grad_local,
        grad_proj.reshape(WIDTH),
    )


def per_device(*arguments):
    count_x, count_y = lax.axis_size("gx"), lax.axis_size("gy")
    if fits(count_x, count_y, arguments[0], arguments[4]):
        return per_device_fast(*arguments)
    return per_device_plain(*arguments)


def solution(mesh):
    return jax.shard_map(
        per_device,
        mesh=mesh,
        in_specs=(
            P("gx", "gy", None),
            P("gx", "gy", None),
            P("gx", "gy", None),
            P(),
            P(None, "gx", "gy", None, None),
            P(),
            P(),
            P(),
            P("gx", "gy", None),
        ),
        out_specs=(
            P("gx", "gy", None),
            P("gx", "gy", None),
            P("gx", "gy", None),
            P(None, "gx", "gy", None, None),
            P(),
            P(),
        ),
        check_vma=False,
    )
```
